32 devices in a mesh: replica: 8 (over z, core), group: 4 (over y, x).
Axes of the slice: x: 2, y: 2, z: 4, core: 2. Of those that a mesh axis runs over, the one named last changes fastest.
Arguments:
- inputs: bfloat16 [16, 1024, 1600], P('replica', 'group'), may hold values from -6 to 6
- segments: int32 [16, 1024], P('replica', 'group'), may hold values from 59 to 1023, as said below
- cotangent: bfloat16 [16, 1024, 1600], P('replica', 'group'), may hold values from -6 to 6
- project_in: bfloat16 [1600, 4800], P('group'), may hold values from -0.15625 to 0.15625
- project_out: bfloat16 [1600, 1600], P('group'), may hold values from -1.25 to 1.25
- expand_weight: bfloat16 [1600, 6400], P('group'), may hold values from -0.15625 to 0.15625
- reduce_weight: bfloat16 [6400, 1600], P('group'), may hold values from -0.078125 to 0.078125
- query_bias: bfloat16 [1600], P('group'), may hold values from -3 to 3
- value_bias: bfloat16 [1600], P('group'), may hold values from -3 to 3
- project_bias: bfloat16 [1600], P('group'), may hold values from -3 to 3
- expand_bias: bfloat16 [6400], P('group'), may hold values from -3 to 3
- reduce_bias: bfloat16 [1600], P('group'), may hold values from -3 to 3
- first_gain: bfloat16 [1600], P('group'), may hold values from 0.5 to 1.5
- first_shift: bfloat16 [1600], P('group'), may hold values from -2 to 2
- second_gain: bfloat16 [1600], P('group'), may hold values from 0.5 to 1.5
- second_shift: bfloat16 [1600], P('group'), may hold values from -2 to 2
Outputs:
- outputs: bfloat16 [16, 1024, 1600], P('replica', 'group')
- input_grad: float32 [16, 1024, 1600], P('replica', 'group')
- project_in_grad: float32 [1600, 4800], P('group')
- project_out_grad: float32 [1600, 1600], P('group')
- expand_weight_grad: float32 [1600, 6400], P('group')
- reduce_weight_grad: float32 [6400, 1600], P('group')
- query_bias_grad: float32 [1600], P('group')
- value_bias_grad: float32 [1600], P('group')
- project_bias_grad: float32 [1600], P('group')
- expand_bias_grad: float32 [6400], P('group')
- reduce_bias_grad: float32 [1600], P('group')
- first_gain_grad: float32 [1600], P('group')
- first_shift_grad: float32 [1600], P('group')
- second_gain_grad: float32 [1600], P('group')
- second_shift_grad: float32 [1600], P('group')
The draws below stay inside these ranges and needn't reach their ends.
Inputs may be any that keep to these rules, and one draw needn't show every extreme that they name: `segments`: within a sequence the numbers never fall; all tokens of a document carry the position of the document's last token in its sequence; a document that ends inside its sequence holds 60 to 800 tokens, the last of a sequence may be shorter; of the 2 sequences on one index of replica, exactly one is a single document.
All inputs are finite; a program needn't handle non-finite values.
Results may differ from the reference program's by a relative error of at most 0.019.
Values may be sent and summed in bfloat16 or wider, within the bound.
A program may use at most 384 MiB of HBM per device.

```python
import math
import jax
import jax.numpy as jnp
from jax import lax

D = 1600
HEADS = 25
HEAD_DIM = 64
FF = 6400
SEQ_DEV = 2
MINDOC = 60
MAXDOC = 800
SEQS = 16
SEQLEN = 1024


def draw_segments(key, part):
    key = jax.random.fold_in(key, 7)
    length_key, whole_key = jax.random.split(key)
    documents = SEQLEN // MINDOC + 1
    lengths = jax.random.randint(length_key, (SEQS, documents), MINDOC, MAXDOC + 1, dtype=jnp.int32)
    finals = jnp.cumsum(lengths, axis=1).astype(jnp.int32) - 1
    positions = jnp.arange(SEQLEN, dtype=jnp.int32)
    covering = jnp.where(finals[:, None, :] >= positions[None, :, None], finals[:, None, :], SEQLEN - 1)
    labels = jnp.minimum(jnp.min(covering, axis=2), SEQLEN - 1)
    chosen = jax.random.randint(whole_key, (SEQS // SEQ_DEV,), 0, SEQ_DEV, dtype=jnp.int32)
    single = jnp.arange(SEQS, dtype=jnp.int32) % SEQ_DEV == jnp.repeat(chosen, SEQ_DEV)
    return jnp.where(single[:, None], SEQLEN - 1, labels).astype(jnp.int32)


def levels(key, dims, cuts, least, top_value):
    level, own = 1.0, jax.random.fold_in(key, 6)
    for axis_at, parts in cuts:
        heights = jnp.exp(jax.random.uniform(jax.random.fold_in(own, axis_at), (parts,), jnp.float32, least / len(cuts), top_value / len(cuts)))
        level = level * jnp.repeat(heights, dims[axis_at] // parts).reshape([-1 if axis == axis_at else 1 for axis in range(len(dims))])
    return level


def noise(stream_key, extent, scale, most, cuts=(), kind=jnp.bfloat16):
    values = jax.random.normal(stream_key, extent, jnp.float32) * scale
    if len(cuts) > 0:
        values = levels(stream_key, extent, cuts, -0.22, 0.18) * values
    return jnp.clip(values, min=-most, max=most).astype(kind)


def setup_inputs(seed: int = 0) -> dict:
    keys = jax.random.split(jax.random.key(seed), 17)
    inputs = noise(keys[0], (SEQS, SEQLEN, D), 1.0, 6.0, ((0, 8), (1, 4)))
    segments = draw_segments(jax.random.fold_in(keys[16], 71), 0)
    cotangent = noise(keys[2], (SEQS, SEQLEN, D), 1.0, 6.0, ((0, 8), (1, 4)))
    project_in = noise(keys[3], (D, 3 * D), D ** -0.5, 0.15625, ((0, 4),))
    project_out = noise(keys[4], (D, D), (max(D // 64, 1)) ** -0.5, 1.25, ((0, 4),))
    expand_weight = noise(keys[5], (D, FF), D ** -0.5, 0.15625, ((0, 4),))
    reduce_weight = noise(keys[6], (FF, D), FF ** -0.5, 0.078125, ((0, 4),))
    query_bias = noise(keys[7], (D,), 0.5, 3.0, ((0, 4),))
    value_bias = noise(keys[8], (D,), 0.5, 3.0, ((0, 4),))
    project_bias = noise(keys[9], (D,), 0.5, 3.0, ((0, 4),))
    expand_bias = noise(keys[10], (FF,), 0.5, 3.0, ((0, 4),))
    reduce_bias = noise(keys[11], (D,), 0.5, 3.0, ((0, 4),))
    first_gain = jnp.clip(1.0 + 0.1 * jax.random.normal(keys[12], (D,), jnp.float32), 0.5, 1.5).astype(jnp.bfloat16)
    first_shift = noise(keys[13], (D,), 0.3, 2.0, ((0, 4),))
    second_gain = jnp.clip(1.0 + 0.1 * jax.random.normal(keys[14], (D,), jnp.float32), 0.5, 1.5).astype(jnp.bfloat16)
    second_shift = noise(keys[15], (D,), 0.3, 2.0, ((0, 4),))
    return {"inputs": inputs, "segments": segments, "cotangent": cotangent, "project_in": project_in, "project_out": project_out, "expand_weight": expand_weight, "reduce_weight": reduce_weight, "query_bias": query_bias, "value_bias": value_bias, "project_bias": project_bias, "expand_bias": expand_bias, "reduce_bias": reduce_bias, "first_gain": first_gain, "first_shift": first_shift, "second_gain": second_gain, "second_shift": second_shift}


@jax.custom_vjp
def low(v):
    return lax.optimization_barrier(v.astype(jnp.bfloat16)).astype(jnp.float32)

@jax.custom_vjp
def low_back(v):
    return v

def low_keep(v):
    return (low(v), None)

def low_pass(kept, grad):
    return (grad,)

def back_keep(v):
    return (v, None)

def back_low(kept, grad):
    return (low(grad),)
low.defvjp(low_keep, low_pass)
low_back.defvjp(back_keep, back_low)
epsilon = 1e-05
very_low = -1e+30
highest = lax.Precision.HIGHEST

def both_ways(tensor):
    return low(low_back(tensor))

def layer_norm(entries, gain, shift):
    center = entries - lax.optimization_barrier(jnp.mean(entries, axis=-1, keepdims=True))
    spread = lax.optimization_barrier(jnp.mean(center * center, axis=-1, keepdims=True))
    return center * lax.rsqrt(spread + epsilon) * gain + shift

def attention(queries, key_rows, value_rows, segment_row):
    block_len = 512 if SEQLEN % 512 == 0 else SEQLEN
    block_count = SEQLEN // block_len
    positions = jnp.arange(SEQLEN, dtype=jnp.int32)
    scaling = 1.0 / math.sqrt(HEAD_DIM)

    def one_block(block):
        query_block, segment_block, position_block = block
        scores = jnp.einsum('qhd,khd->hqk', query_block, key_rows, precision=highest, preferred_element_type=jnp.float32) * scaling
        scores = low_back(scores)
        allowed = (segment_block[:, None] == segment_row[None, :]) & (positions[None, :] <= position_block[:, None])
        scores = jnp.where(allowed[None], scores, very_low)
        largest = lax.optimization_barrier(jnp.max(scores, axis=-1, keepdims=True))
        exponent = jnp.exp(scores - largest)
        shares = low(exponent / lax.optimization_barrier(jnp.sum(exponent, axis=-1, keepdims=True)))
        return jnp.einsum('hqk,khd->qhd', shares, value_rows, precision=highest, preferred_element_type=jnp.float32)
    blocks = (queries.reshape(block_count, block_len, HEADS, HEAD_DIM), segment_row.reshape(block_count, block_len), positions.reshape(block_count, block_len))
    return lax.map(jax.checkpoint(one_block), blocks).reshape(SEQLEN, HEADS * HEAD_DIM)

def forward(params, entries, segment_row):
    project_in, project_out, expand_weight, reduce_weight, query_bias, value_bias, project_bias, expand_bias, reduce_bias, first_gain, first_shift, second_gain, second_shift = params
    normed = low(layer_norm(entries, first_gain, first_shift))
    mixture = jnp.dot(normed, project_in, precision=highest, preferred_element_type=jnp.float32)
    queries = both_ways(mixture[:, :D] + query_bias)
    key_rows = both_ways(mixture[:, D:2 * D])
    value_rows = both_ways(mixture[:, 2 * D:] + value_bias)
    head_shape = (SEQLEN, HEADS, HEAD_DIM)
    attended = both_ways(attention(queries.reshape(head_shape), key_rows.reshape(head_shape), value_rows.reshape(head_shape), segment_row))
    branch = low_back(jnp.dot(attended, project_out, precision=highest, preferred_element_type=jnp.float32) + project_bias)
    middle = entries + branch
    second = low(layer_norm(middle, second_gain, second_shift))
    expanded = low_back(jnp.dot(second, expand_weight, precision=highest, preferred_element_type=jnp.float32) + expand_bias)
    activated = low(jax.nn.gelu(expanded, approximate=True))
    feeding = low_back(jnp.dot(activated, reduce_weight, precision=highest, preferred_element_type=jnp.float32) + reduce_bias)
    return middle + feeding

def reference(inputs, segments, cotangent, project_in, project_out, expand_weight, reduce_weight, query_bias, value_bias, project_bias, expand_bias, reduce_bias, first_gain, first_shift, second_gain, second_shift):
    params = tuple((member.astype(jnp.float32) for member in (project_in, project_out, expand_weight, reduce_weight, query_bias, value_bias, project_bias, expand_bias, reduce_bias, first_gain, first_shift, second_gain, second_shift)))

    def per_sequence(totals, sequence):
        entries, segment_row, grad_rows = sequence
        result, pullback = jax.vjp(lambda weights, entry: forward(weights, entry, segment_row), params, entries)
        weight_grads, entry_grad = pullback(grad_rows)
        totals = jax.tree.map(lambda left, right: left + right, totals, weight_grads)
        return (totals, (result.astype(jnp.bfloat16), entry_grad))
    zeros = jax.tree.map(jnp.zeros_like, params)
    totals, produced = lax.scan(per_sequence, zeros, (inputs.astype(jnp.float32), segments, cotangent.astype(jnp.float32)))
    return (produced[0], produced[1], totals[0], totals[1], totals[2], totals[3], totals[4], totals[5], totals[6], totals[7], totals[8], totals[9], totals[10], totals[11], totals[12])
```

```python
import functools
import math

import jax
import jax.numpy as jnp
from jax import lax
from jax.sharding import PartitionSpec as P

from jax.experimental import pallas as pl
from jax.experimental.pallas import tpu as pltpu

HEADS = 25
HEAD_DIM = 64


epsilon = 1e-05
very_low = -1e30


def carried_in(part, axis, combine, identity):
    place = lax.axis_index(axis)
    gathered = lax.all_gather(part, axis)
    state = jnp.zeros_like(part) + jnp.asarray(identity, part.dtype)

    def one(hop, state):
        return combine(state, lax.dynamic_index_in_dim(gathered, hop, 0, False))

    return lax.fori_loop(0, place, one, state)


def layer_norm(entries, gain, shift):
    center = entries - jnp.mean(entries, axis=-1, keepdims=True)
    spread = jnp.mean(center * center, axis=-1, keepdims=True)
    return center * lax.rsqrt(spread + epsilon) * gain + shift


def product(left, right):
    return jnp.dot(left, right, preferred_element_type=jnp.float32)


def product_back(left, right):
    return lax.dot_general(
        left, right, (((1,), (1,)), ((), ())), preferred_element_type=jnp.float32
    )


def weight_term(left, right):
    return lax.dot_general(
        left, right, (((0,), (0,)), ((), ())), preferred_element_type=jnp.float32
    )


def column_sum(entries):
    return jnp.sum(entries.astype(jnp.float32), axis=0)


def block_scores(queries, key_block, offset, query_pos, doc_start):
    block_count = key_block.shape[0]
    key_count = key_block.shape[2]
    scaling = 1.0 / math.sqrt(HEAD_DIM)
    scores = (
        jnp.einsum("schd,pskhd->shcpk", queries, key_block, preferred_element_type=jnp.float32)
        * scaling
    )
    key_pos = (offset + jnp.arange(block_count, dtype=jnp.int32))[:, None] * key_count + jnp.arange(
        key_count, dtype=jnp.int32
    )[None, :]
    allowed = (key_pos[None, None] <= query_pos[None, :, None, None]) & (
        key_pos[None, None] >= doc_start[:, :, None, None]
    )
    allowed = allowed[:, None]
    return (jnp.where(allowed, scores, very_low), allowed)


def attend(running, key_block, value_block, offset, queries, query_pos, doc_start):
    largest, denominator, summed = running
    masked, allowed = block_scores(queries, key_block, offset, query_pos, doc_start)
    fresh = jnp.maximum(largest, jnp.max(masked, axis=(3, 4)))
    shares = jnp.where(allowed, jnp.exp(masked - fresh[..., None, None]), 0.0)
    rescale = jnp.exp(largest - fresh)
    denominator = denominator * rescale + jnp.sum(shares, axis=(3, 4))
    added = jnp.einsum(
        "shcpk,pskhd->schd",
        shares.astype(jnp.bfloat16),
        value_block,
        preferred_element_type=jnp.float32,
    )
    summed = summed * jnp.transpose(rescale, (0, 2, 1))[..., None] + added
    return (fresh, denominator, summed)


def attend_back(
    grad_query,
    key_block,
    value_block,
    offset,
    queries,
    query_pos,
    doc_start,
    log_total,
    grad_low,
    row_dot,
):
    masked, allowed = block_scores(queries, key_block, offset, query_pos, doc_start)
    shares = jnp.where(allowed, jnp.exp(masked - log_total[..., None, None]), 0.0)
    grad_value = jnp.einsum(
        "shcpk,schd->pskhd",
        shares.astype(jnp.bfloat16),
        grad_low,
        preferred_element_type=jnp.float32,
    )
    grad_share = jnp.einsum(
        "schd,pskhd->shcpk", grad_low, value_block, preferred_element_type=jnp.float32
    )
    grad_score = (shares * (grad_share - row_dot[..., None, None])).astype(jnp.bfloat16)
    grad_query = grad_query + jnp.einsum(
        "shcpk,pskhd->schd", grad_score, key_block, preferred_element_type=jnp.float32
    )
    grad_key = jnp.einsum(
        "shcpk,schd->pskhd", grad_score, queries, preferred_element_type=jnp.float32
    )
    return (grad_query, (grad_key, grad_value))


def on_device_any(
    inputs,
    segments,
    cotangent,
    project_in,
    project_out,
    expand_weight,
    reduce_weight,
    query_bias,
    value_bias,
    project_bias,
    expand_bias,
    reduce_bias,
    first_gain,
    first_shift,
    second_gain,
    second_shift,
):
    seq_here, local_len, width = inputs.shape
    groups = lax.axis_size("group")
    total_rows = seq_here * local_len
    head_shape = (seq_here, local_len, HEADS, HEAD_DIM)
    shards = (
        project_in,
        project_out,
        expand_weight,
        reduce_weight,
        query_bias,
        value_bias,
        project_bias,
        expand_bias,
        reduce_bias,
        first_gain,
        first_shift,
        second_gain,
        second_shift,
    )
    whole = (
        lax.all_gather(shards[0], "group", axis=0, tiled=True),
        lax.all_gather(shards[1], "group", axis=0, tiled=True),
        lax.all_gather(shards[2], "group", axis=0, tiled=True),
        lax.all_gather(shards[3], "group", axis=0, tiled=True),
        lax.all_gather(shards[4], "group", axis=0, tiled=True),
        lax.all_gather(shards[5], "group", axis=0, tiled=True),
        lax.all_gather(shards[6], "group", axis=0, tiled=True),
        lax.all_gather(shards[7], "group", axis=0, tiled=True),
        lax.all_gather(shards[8], "group", axis=0, tiled=True),
        lax.all_gather(shards[9], "group", axis=0, tiled=True),
        lax.all_gather(shards[10], "group", axis=0, tiled=True),
        lax.all_gather(shards[11], "group", axis=0, tiled=True),
        lax.all_gather(shards[12], "group", axis=0, tiled=True),
    )
    (
        full_in,
        full_out,
        full_expand,
        full_reduce,
        bias_query,
        bias_value,
        bias_project,
        bias_expand,
        bias_reduce,
        gain_first,
        shift_first,
        gain_second,
        shift_second,
    ) = whole
    group_rank = lax.axis_index("group")
    query_pos = group_rank * local_len + jnp.arange(local_len, dtype=jnp.int32)
    positions = jnp.broadcast_to(query_pos[None, :], (seq_here, local_len))
    end_marks = jnp.where(segments == positions, positions + 1, 0)
    before = carried_in(
        jnp.max(end_marks, axis=1), "group", jnp.maximum, jnp.zeros((seq_here,), jnp.int32)
    )
    inside = lax.cummax(end_marks, axis=1)
    inside = jnp.concatenate([jnp.zeros((seq_here, 1), jnp.int32), inside[:, :-1]], axis=1)
    doc_start = jnp.maximum(before[:, None], inside)
    flat_input = inputs.reshape(total_rows, width).astype(jnp.float32)
    normed_low = layer_norm(
        flat_input, gain_first.astype(jnp.float32), shift_first.astype(jnp.float32)
    ).astype(jnp.bfloat16)
    mixture = product(normed_low, full_in)
    queries = (
        (mixture[:, :width] + bias_query.astype(jnp.float32))
        .astype(jnp.bfloat16)
        .reshape(head_shape)
    )
    key_rows = (
        mixture[:, width : 2 * width].astype(jnp.bfloat16).reshape(seq_here, local_len, width)
    )
    value_rows = (
        (mixture[:, 2 * width :] + bias_value.astype(jnp.float32))
        .astype(jnp.bfloat16)
        .reshape(seq_here, local_len, width)
    )
    initial = (
        jnp.full((seq_here, HEADS, local_len), very_low, jnp.float32),
        jnp.zeros((seq_here, HEADS, local_len), jnp.float32),
        jnp.zeros(head_shape, jnp.float32),
    )
    block_ids = jnp.arange(groups, dtype=jnp.int32)
    running = initial
    pieces = (
        lax.all_gather(key_rows[None], "group", axis=0, tiled=True),
        lax.all_gather(value_rows[None], "group", axis=0, tiled=True),
    )
    piece_count = pieces[0].shape[0]

    def one_piece(state, members):
        key_piece, value_piece, index = members
        updated = attend(
            state,
            key_piece.reshape((1,) + head_shape),
            value_piece.reshape((1,) + head_shape),
            index,
            queries,
            query_pos,
            doc_start,
        )
        return (updated, None)

    running, unused_steps = lax.scan(
        one_piece, running, (pieces[0], pieces[1], jnp.arange(piece_count, dtype=jnp.int32))
    )
    largest, denominator, summed = running
    attended = summed / jnp.transpose(denominator, (0, 2, 1))[..., None]
    log_total = largest + jnp.log(denominator)
    attended_low = attended.reshape(total_rows, width).astype(jnp.bfloat16)
    middle = flat_input + product(attended_low, full_out) + bias_project.astype(jnp.float32)
    second_low = layer_norm(
        middle, gain_second.astype(jnp.float32), shift_second.astype(jnp.float32)
    ).astype(jnp.bfloat16)
    expanded = product(second_low, full_expand) + bias_expand.astype(jnp.float32)
    activated_low = jax.nn.gelu(expanded, approximate=True).astype(jnp.bfloat16)
    result = middle + product(activated_low, full_reduce) + bias_reduce.astype(jnp.float32)
    outputs = result.astype(jnp.bfloat16).reshape(seq_here, local_len, width)
    whole_back = (
        lax.all_gather(shards[0], "group", axis=0, tiled=True),
        lax.all_gather(shards[1], "group", axis=0, tiled=True),
        lax.all_gather(shards[2], "group", axis=0, tiled=True),
        lax.all_gather(shards[3], "group", axis=0, tiled=True),
        lax.all_gather(shards[4], "group", axis=0, tiled=True),
        lax.all_gather(shards[5], "group", axis=0, tiled=True),
        lax.all_gather(shards[6], "group", axis=0, tiled=True),
        lax.all_gather(shards[7], "group", axis=0, tiled=True),
        lax.all_gather(shards[8], "group", axis=0, tiled=True),
        lax.all_gather(shards[9], "group", axis=0, tiled=True),
        lax.all_gather(shards[10], "group", axis=0, tiled=True),
        lax.all_gather(shards[11], "group", axis=0, tiled=True),
        lax.all_gather(shards[12], "group", axis=0, tiled=True),
    )
    keys_back = (
        lax.all_gather(key_rows[None], "group", axis=0, tiled=True),
        lax.all_gather(value_rows[None], "group", axis=0, tiled=True),
    )
    (
        back_in,
        back_out,
        back_expand,
        back_reduce,
        unused_query,
        unused_value,
        unused_project,
        unused_expand,
        unused_reduce,
        back_gain_first,
        back_shift_first,
        back_gain_second,
        back_shift_second,
    ) = whole_back
    grad_rows = cotangent.reshape(total_rows, width).astype(jnp.float32)
    grad_result_low = cotangent.reshape(total_rows, width)
    reduce_bias_grad = column_sum(grad_result_low)
    grad_activated = product_back(grad_result_low, back_reduce)
    unused_gelu, gelu_back = jax.vjp(lambda entry: jax.nn.gelu(entry, approximate=True), expanded)
    grad_expanded_low = gelu_back(grad_activated)[0].astype(jnp.bfloat16)
    expand_bias_grad = column_sum(grad_expanded_low)
    grad_second = product_back(grad_expanded_low, back_expand)
    unused_second, second_back = jax.vjp(
        layer_norm,
        middle,
        back_gain_second.astype(jnp.float32),
        back_shift_second.astype(jnp.float32),
    )
    grad_middle, second_gain_grad, second_shift_grad = second_back(grad_second)
    grad_middle = grad_middle + grad_rows
    reduce_weight_grad = weight_term(activated_low, grad_result_low)
    expand_weight_grad = weight_term(second_low, grad_expanded_low)
    feed_parts = (
        lax.psum_scatter(
            expand_weight_grad.astype(jnp.bfloat16), "group", scatter_dimension=0, tiled=True
        ).astype(jnp.float32),
        lax.psum_scatter(
            reduce_weight_grad.astype(jnp.bfloat16), "group", scatter_dimension=0, tiled=True
        ).astype(jnp.float32),
        lax.psum_scatter(
            expand_bias_grad.astype(jnp.bfloat16), "group", scatter_dimension=0, tiled=True
        ).astype(jnp.float32),
        lax.psum_scatter(
            reduce_bias_grad.astype(jnp.bfloat16), "group", scatter_dimension=0, tiled=True
        ).astype(jnp.float32),
        lax.psum_scatter(
            second_gain_grad.astype(jnp.bfloat16), "group", scatter_dimension=0, tiled=True
        ).astype(jnp.float32),
        lax.psum_scatter(
            second_shift_grad.astype(jnp.bfloat16), "group", scatter_dimension=0, tiled=True
        ).astype(jnp.float32),
    )
    grad_middle_low = grad_middle.astype(jnp.bfloat16)
    project_bias_grad = column_sum(grad_middle_low)
    grad_attended_low = (
        product_back(grad_middle_low, back_out).astype(jnp.bfloat16).reshape(head_shape)
    )
    row_dot = jnp.einsum("schd,schd->shc", grad_attended_low.astype(jnp.float32), attended)

    def back_step(grad_query, members):
        key_piece, value_piece, offset = members
        return attend_back(
            grad_query,
            key_piece.reshape((1,) + head_shape),
            value_piece.reshape((1,) + head_shape),
            offset,
            queries,
            query_pos,
            doc_start,
            log_total,
            grad_attended_low,
            row_dot,
        )

    grad_query, terms = lax.scan(
        back_step, jnp.zeros(head_shape, jnp.float32), (keys_back[0], keys_back[1], block_ids)
    )
    key_terms = terms[0].reshape(groups, seq_here, local_len, width)
    value_terms = terms[1].reshape(groups, seq_here, local_len, width)
    key_grad, value_grad = (
        lax.psum_scatter(
            key_terms.astype(jnp.bfloat16), "group", scatter_dimension=0, tiled=True
        ).astype(jnp.float32),
        lax.psum_scatter(
            value_terms.astype(jnp.bfloat16), "group", scatter_dimension=0, tiled=True
        ).astype(jnp.float32),
    )
    scaling = 1.0 / math.sqrt(HEAD_DIM)
    grad_query_low = (grad_query * scaling).reshape(total_rows, width).astype(jnp.bfloat16)
    grad_key_low = (key_grad * scaling).reshape(total_rows, width).astype(jnp.bfloat16)
    grad_value_low = value_grad.reshape(total_rows, width).astype(jnp.bfloat16)
    query_bias_grad = column_sum(grad_query_low)
    value_bias_grad = column_sum(grad_value_low)
    grad_mixture_low = jnp.concatenate([grad_query_low, grad_key_low, grad_value_low], axis=1)
    grad_normed = product_back(grad_mixture_low, back_in)
    unused_first, first_back = jax.vjp(
        layer_norm,
        flat_input,
        back_gain_first.astype(jnp.float32),
        back_shift_first.astype(jnp.float32),
    )
    grad_entry, first_gain_grad, first_shift_grad = first_back(grad_normed)
    input_grad = (grad_entry + grad_middle).reshape(seq_here, local_len, width)
    project_weight_grad = weight_term(attended_low, grad_middle_low)
    in_weight_grad = weight_term(normed_low, grad_mixture_low)
    mixer_parts = (
        lax.psum_scatter(
            in_weight_grad.astype(jnp.bfloat16), "group", scatter_dimension=0, tiled=True
        ).astype(jnp.float32),
        lax.psum_scatter(
            project_weight_grad.astype(jnp.bfloat16), "group", scatter_dimension=0, tiled=True
        ).astype(jnp.float32),
        lax.psum_scatter(
            query_bias_grad.astype(jnp.bfloat16), "group", scatter_dimension=0, tiled=True
        ).astype(jnp.float32),
        lax.psum_scatter(
            value_bias_grad.astype(jnp.bfloat16), "group", scatter_dimension=0, tiled=True
        ).astype(jnp.float32),
        lax.psum_scatter(
            project_bias_grad.astype(jnp.bfloat16), "group", scatter_dimension=0, tiled=True
        ).astype(jnp.float32),
        lax.psum_scatter(
            first_gain_grad.astype(jnp.bfloat16), "group", scatter_dimension=0, tiled=True
        ).astype(jnp.float32),
        lax.psum_scatter(
            first_shift_grad.astype(jnp.bfloat16), "group", scatter_dimension=0, tiled=True
        ).astype(jnp.float32),
    )
    share_in, share_out, share_expand, share_reduce = (
        mixer_parts[0],
        mixer_parts[1],
        feed_parts[0],
        feed_parts[1],
    )
    share_query, share_value, share_project = (mixer_parts[2], mixer_parts[3], mixer_parts[4])
    share_expand_bias, share_reduce_bias = (feed_parts[2], feed_parts[3])
    share_first_gain, share_first_shift = (mixer_parts[5], mixer_parts[6])
    share_second_gain, share_second_shift = (feed_parts[4], feed_parts[5])
    totals = (
        lax.psum(share_in.astype(jnp.bfloat16), "replica").astype(jnp.float32),
        lax.psum(share_out.astype(jnp.bfloat16), "replica").astype(jnp.float32),
        lax.psum(share_expand.astype(jnp.bfloat16), "replica").astype(jnp.float32),
        lax.psum(share_reduce.astype(jnp.bfloat16), "replica").astype(jnp.float32),
        lax.psum(share_query.astype(jnp.bfloat16), "replica").astype(jnp.float32),
        lax.psum(share_value.astype(jnp.bfloat16), "replica").astype(jnp.float32),
        lax.psum(share_project.astype(jnp.bfloat16), "replica").astype(jnp.float32),
        lax.psum(share_expand_bias.astype(jnp.bfloat16), "replica").astype(jnp.float32),
        lax.psum(share_reduce_bias.astype(jnp.bfloat16), "replica").astype(jnp.float32),
        lax.psum(share_first_gain.astype(jnp.bfloat16), "replica").astype(jnp.float32),
        lax.psum(share_first_shift.astype(jnp.bfloat16), "replica").astype(jnp.float32),
        lax.psum(share_second_gain.astype(jnp.bfloat16), "replica").astype(jnp.float32),
        lax.psum(share_second_shift.astype(jnp.bfloat16), "replica").astype(jnp.float32),
    )
    return (
        outputs,
        input_grad,
        totals[0],
        totals[1],
        totals[2],
        totals[3],
        totals[4],
        totals[5],
        totals[6],
        totals[7],
        totals[8],
        totals[9],
        totals[10],
        totals[11],
        totals[12],
    )


NT = (((1,), (1,)), ((), ()))

def dot_nt(a, b):
    return lax.dot_general(a, b, NT, preferred_element_type=jnp.float32)

def dot_nn(a, b):
    return jnp.dot(a, b, preferred_element_type=jnp.float32)

BLOCK = 256

def heads_kernel(q_ref, k_ref, v_ref, segc_ref, segr_ref, o_ref, lse_ref, ot_ref, vt_ref):
    tile = pl.program_id(0)
    length = q_ref.shape[0]
    blocks = length // BLOCK
    lane = lax.broadcasted_iota(jnp.int32, (1, 128), 1)
    ot_ref[...] = jnp.zeros_like(ot_ref)
    lse_ref[...] = jnp.zeros_like(lse_ref)
    vt_ref[...] = v_ref[...].T

    def head(h):
        k = jnp.where((lane >= 64 * h) & (lane < 64 * h + 64), k_ref[...], jnp.bfloat16(0))
        for i in range(blocks):
            low, high = i * BLOCK, (i + 1) * BLOCK
            q = q_ref[low:high, :] * jnp.bfloat16(0.125)
            s = dot_nt(k[:high], q)
            same = segc_ref[:high, :] == segr_ref[:, low:high]
            kpos = lax.broadcasted_iota(jnp.int32, (high, BLOCK), 0)
            qpos = lax.broadcasted_iota(jnp.int32, (high, BLOCK), 1) + low
            s = jnp.where(same & (kpos <= qpos), s, -1e30)
            m = jnp.max(s, axis=0, keepdims=True)
            p = jnp.exp(s - m)
            l = jnp.sum(p, axis=0, keepdims=True)
            ot = dot_nn(vt_ref[64 * h : 64 * h + 64, :high], p.astype(jnp.bfloat16))
            ot_ref[64 * h : 64 * h + 64, low:high] = ot / l
            lse_ref[0, h : h + 1, low:high] = m + jnp.log(l)

    head(0)

    @pl.when(tile < 6)
    def _():
        head(1)

    o_ref[...] = ot_ref[...].T.astype(jnp.bfloat16)


def heads(qkv, segc, segr):
    length = qkv.shape[0]
    spec = lambda off: pl.BlockSpec((length, 128), lambda t: (0, t + off))
    return pl.pallas_call(
        heads_kernel,
        grid=(7,),
        in_specs=[spec(0), spec(7), spec(14), pl.BlockSpec((length, 1), lambda t: (0, 0)), pl.BlockSpec((1, length), lambda t: (0, 0))],
        out_specs=[pl.BlockSpec((length, 128), lambda t: (0, t)), pl.BlockSpec((1, 8, length), lambda t: (t, 0, 0))],
        out_shape=[jax.ShapeDtypeStruct((length, 896), jnp.bfloat16), jax.ShapeDtypeStruct((7, 8, length), jnp.float32)],
        scratch_shapes=[pltpu.VMEM((128, length), jnp.float32), pltpu.VMEM((128, length), jnp.bfloat16)],
        compiler_params=pltpu.CompilerParams(vmem_limit_bytes=48 * 2**20),
        cost_estimate=pl.CostEstimate(flops=int(13 * 2 * 2 * length * length * 64 * 2), bytes_accessed=8 * length * 896, transcendentals=13 * length * length // 2),
        name="heads",
    )(qkv, qkv, qkv, segc, segr)


def heads_back_kernel(q_ref, k_ref, v_ref, do_ref, o_ref, lse_ref, segc_ref, segr_ref, dq_ref, dk_ref, dv_ref, dqt_ref, odt_ref):
    tile = pl.program_id(0)
    length = q_ref.shape[0]
    blocks = length // BLOCK
    lane = lax.broadcasted_iota(jnp.int32, (1, 128), 1)
    dqt_ref[...] = jnp.zeros_like(dqt_ref)
    odt_ref[...] = (do_ref[...].astype(jnp.float32) * o_ref[...].astype(jnp.float32)).T

    def head(h):
        mine = (lane >= 64 * h) & (lane < 64 * h + 64)
        dot_row = jnp.sum(odt_ref[64 * h : 64 * h + 64, :], axis=0, keepdims=True)
        for j in range(blocks):
            low, high = j * BLOCK, (j + 1) * BLOCK
            rest = length - low
            q = q_ref[low:, :] * jnp.bfloat16(0.125)
            do = do_ref[low:, :]
            k = jnp.where(mine, k_ref[low:high, :], jnp.bfloat16(0))
            v = jnp.where(mine, v_ref[low:high, :], jnp.bfloat16(0))
            s = dot_nt(k, q)
            same = segc_ref[low:high, :] == segr_ref[:, low:]
            kpos = lax.broadcasted_iota(jnp.int32, (BLOCK, rest), 0)
            qpos = lax.broadcasted_iota(jnp.int32, (BLOCK, rest), 1)
            p = jnp.where(same & (kpos <= qpos), jnp.exp(s - lse_ref[0, h : h + 1, low:]), 0.0)
            dp = dot_nt(v, do)
            ds = (p * (dp - dot_row[:, low:])).astype(jnp.bfloat16)
            dv = dot_nn(p.astype(jnp.bfloat16), do)
            dk = dot_nn(ds, q)
            if h == 0:
                dv_ref[low:high, :] = jnp.where(mine, dv, 0.0).astype(jnp.bfloat16)
                dk_ref[low:high, :] = jnp.where(mine, dk, 0.0).astype(jnp.bfloat16)
            else:
                dv_ref[low:high, :] = jnp.where(mine, dv.astype(jnp.bfloat16), dv_ref[low:high, :])
                dk_ref[low:high, :] = jnp.where(mine, dk.astype(jnp.bfloat16), dk_ref[low:high, :])
            dqt_ref[:, low:] += dot_nn(k.T, ds)

    head(0)

    @pl.when(tile < 6)
    def _():
        head(1)

    dq_ref[...] = (dqt_ref[...].T * 0.125).astype(jnp.bfloat16)


def heads_back(qkv, grad, out, lse, segc, segr):
    length = qkv.shape[0]
    spec = lambda off: pl.BlockSpec((length, 128), lambda t: (0, t + off))
    one = pl.BlockSpec((length, 128), lambda t: (0, t))
    shape = jax.ShapeDtypeStruct((length, 896), jnp.bfloat16)
    return pl.pallas_call(
        heads_back_kernel,
        grid=(7,),
        in_specs=[spec(0), spec(7), spec(14), one, one, pl.BlockSpec((1, 8, length), lambda t: (t, 0, 0)), pl.BlockSpec((length, 1), lambda t: (0, 0)), pl.BlockSpec((1, length), lambda t: (0, 0))],
        out_specs=[one, one, one],
        out_shape=[shape, shape, shape],
        scratch_shapes=[pltpu.VMEM((128, length), jnp.float32), pltpu.VMEM((128, length), jnp.float32)],
        compiler_params=pltpu.CompilerParams(vmem_limit_bytes=48 * 2**20),
        cost_estimate=pl.CostEstimate(flops=int(13 * 5 * 2 * length * length * 64 * 2), bytes_accessed=16 * length * 896, transcendentals=13 * length * length // 2),
        name="heads_back",
    )(qkv, qkv, qkv, grad, out, lse, segc, segr)

MESH = pl.DeviceIdType.MESH


def flipped(z=0, core=0, y=0, x=0):
    pairs = []
    for me in range(32):
        pairs.append((me, me ^ (8 * z + 4 * core + 2 * y + x)))
    return pairs


FLIP_X = flipped(x=1)
FLIP_Y = flipped(y=1)
FLIP_CORE = flipped(core=1)
FLIP_Z = flipped(z=1)
FLIP_PAIR = flipped(z=2)
INWARD = [(me, me + 8) for me in range(8)] + [(me, me - 8) for me in range(24, 32)]
MIDDLE = [(me, me + 8) for me in range(8, 16)] + [(me, me - 8) for me in range(16, 24)]
OUTWARD = [(me, me - 8) for me in range(8, 16)] + [(me, me + 8) for me in range(16, 24)]


def moved(entries, pairs):
    return lax.ppermute(entries, ("replica", "group"), pairs)


def low(entries):
    return entries.astype(jnp.bfloat16)


def wide(entries):
    return entries.astype(jnp.float32)


def at(entries, index):
    return lax.dynamic_index_in_dim(entries, index, 0, False)


def place():
    replica = lax.axis_index("replica")
    group = lax.axis_index("group")
    core = lax.rem(replica, 2)
    z = lax.div(replica, 2)
    return replica, group, z, core, lax.div(group, 2), lax.rem(group, 2)


def partners(replica, group):
    core = lax.rem(replica, 2)
    z = lax.rem(lax.div(replica, 2), 2)
    y = lax.div(group, 2)
    x = lax.rem(group, 2)
    by_x = (replica, group + 1 - 2 * x)
    by_y = (replica, group + 2 - 4 * y)
    by_both = (replica, group + 3 - 4 * y - 2 * x)
    by_core = (replica + 1 - 2 * core, group)
    by_z = (replica + 2 - 4 * z, group)
    return by_x, by_y, by_both, by_core, by_z


def greet(devices):
    barrier = pltpu.get_barrier_semaphore()
    for device in devices:
        pl.semaphore_signal(barrier, inc=1, device_id=device, device_id_type=MESH)
    pl.semaphore_wait(barrier, len(devices))


def first_exchange_kernel(inp, weights, vec, seg, cot, x_seq, w_full, vecs, segs, cots, send, recv, local):
    replica = lax.axis_index("replica")
    group = lax.axis_index("group")
    core = lax.rem(replica, 2)
    y = lax.div(group, 2)
    x = lax.rem(group, 2)
    by_x, by_y, by_both, by_core, by_z = partners(replica, group)
    greet((by_x, by_y, by_both, by_core, by_z))
    other_x = 1 - x
    other_y = 1 - y
    slot_x = group + 1 - 2 * x
    slot_y = group + 2 - 4 * y
    slot_both = group + 3 - 4 * y - 2 * x
    mine = pl.ds(pl.multiple_of(core * 192, 16), 208)
    shared = pl.ds(pl.multiple_of(core * 208, 16), 192)
    count = [0]

    def remote(src, dst, device):
        i = count[0]
        count[0] = i + 1
        copy = pltpu.make_async_remote_copy(src_ref=src, dst_ref=dst, send_sem=send.at[i], recv_sem=recv.at[i], device_id=device, device_id_type=MESH)
        copy.start()
        return copy

    small = [
        remote(vec, vecs.at[group], by_x),
        remote(vec, vecs.at[group], by_y),
        remote(vec, vecs.at[group], by_both),
        remote(seg.at[other_x], segs.at[group], by_x),
        remote(seg.at[x], segs.at[group], by_y),
        remote(seg.at[other_x], segs.at[group], by_both),
    ]
    x_block = remote(inp.at[other_x], x_seq.at[group], by_x)
    y_block = remote(inp.at[x], x_seq.at[group], by_y)
    w_x = remote(weights.at[y, mine], w_full.at[group, mine], by_x)
    w_y = remote(weights.at[other_y, mine], w_full.at[group, mine], by_y)
    cot_core = remote(cot, cots.at[1], by_core)
    cot_z = remote(cot, cots.at[2], by_z)
    own = [
        pltpu.make_async_copy(inp.at[x], x_seq.at[group], local.at[0]),
        pltpu.make_async_copy(weights.at[y], w_full.at[group], local.at[1]),
        pltpu.make_async_copy(vec, vecs.at[group], local.at[2]),
        pltpu.make_async_copy(seg.at[x], segs.at[group], local.at[3]),
        pltpu.make_async_copy(cot, cots.at[0], local.at[4]),
    ]
    for copy in own:
        copy.start()
    x_block.wait_recv()
    y_more = remote(x_seq.at[slot_x], x_seq.at[slot_x], by_y)
    w_y.wait_recv()
    w_more = remote(w_full.at[slot_y, mine], w_full.at[slot_y, mine], by_x)
    w_y_core = remote(w_full.at[slot_y, shared], w_full.at[slot_y, shared], by_core)
    w_x.wait_recv()
    w_x_core = remote(w_full.at[slot_x, shared], w_full.at[slot_x, shared], by_core)
    cot_z.wait_recv()
    cot_more = remote(cots.at[2], cots.at[3], by_core)
    w_more.wait_recv()
    w_more_core = remote(w_full.at[slot_both, shared], w_full.at[slot_both, shared], by_core)
    for copy in small + [y_block, y_more, cot_core, cot_more, w_y_core, w_x_core, w_more_core]:
        copy.wait_recv()
    for copy in small + [x_block, y_block, y_more, w_x, w_y, w_more, cot_core, cot_z, cot_more, w_y_core, w_x_core, w_more_core]:
        copy.wait_send()
    for copy in own:
        copy.wait()


def first_exchange(inp, weights, vec, seg, cot):
    any_space = pl.BlockSpec(memory_space=pl.ANY)
    shape = jax.ShapeDtypeStruct
    return pl.pallas_call(
        first_exchange_kernel,
        in_specs=[any_space] * 5,
        out_specs=[any_space] * 5,
        out_shape=[
            shape((4,) + inp.shape[1:], inp.dtype),
            shape((4,) + weights.shape[1:], weights.dtype),
            shape((4,) + vec.shape, vec.dtype),
            shape((4,) + seg.shape[1:], seg.dtype),
            shape((4,) + cot.shape, cot.dtype),
        ],
        scratch_shapes=[pltpu.SemaphoreType.DMA((18,)), pltpu.SemaphoreType.DMA((18,)), pltpu.SemaphoreType.DMA((5,))],
        compiler_params=pltpu.CompilerParams(collective_id=0, has_side_effects=True),
        name="first_exchange",
    )(inp, weights, vec, seg, cot)


def turn_kernel(forth, src, dst, send, recv, local):
    replica = lax.axis_index("replica")
    group = lax.axis_index("group")
    y = lax.div(group, 2)
    x = lax.rem(group, 2)
    by_x, by_y, by_both, by_core, by_z = partners(replica, group)
    others = (by_both, by_x, by_y)
    greet(others)

    def view(device):
        there = device[1]
        there_y = lax.div(there, 2)
        there_x = lax.rem(there, 2)
        if forth:
            return src.at[there], dst.at[x, y]
        return src.at[there_x, there_y], dst.at[group]

    copies = []
    for i, device in enumerate(others):
        a, b = view(device)
        copies.append(pltpu.make_async_remote_copy(src_ref=a, dst_ref=b, send_sem=send.at[i], recv_sem=recv.at[i], device_id=device, device_id_type=MESH))
    a, b = view((replica, group))
    own = pltpu.make_async_copy(a, b, local)
    for copy in copies:
        copy.start()
    own.start()
    for copy in copies:
        copy.wait()
    own.wait()


def turn(entries, forth, collective):
    any_space = pl.BlockSpec(memory_space=pl.ANY)
    tail = entries.shape[-2:]
    lead = (2, 2) if forth else (4,)
    return pl.pallas_call(
        functools.partial(turn_kernel, forth),
        in_specs=[any_space],
        out_specs=any_space,
        out_shape=jax.ShapeDtypeStruct(lead + tail, entries.dtype),
        scratch_shapes=[pltpu.SemaphoreType.DMA((3,)), pltpu.SemaphoreType.DMA((3,)), pltpu.SemaphoreType.DMA],
        compiler_params=pltpu.CompilerParams(collective_id=collective, has_side_effects=True),
        name="turn_out" if forth else "turn_back",
    )(entries)


def quad_gather(entries):
    by_core = moved(entries, FLIP_CORE)
    by_z = moved(entries, FLIP_Z)
    by_both = moved(by_z, FLIP_CORE)
    return jnp.stack([entries, by_core, by_z, by_both])


def quad_scatter(parts):
    arrived = moved(jnp.stack([parts[1], parts[3]]), FLIP_CORE)
    own = wide(parts[0]) + wide(arrived[0])
    sent = low(wide(parts[2]) + wide(arrived[1]))
    return own + wide(moved(sent, FLIP_Z))


def line_sum(part, z):
    inner = low(wide(part) + wide(moved(part, INWARD)))
    total = low(wide(inner) + wide(moved(inner, MIDDLE)))
    outer = moved(total, OUTWARD)
    return jnp.where((z == 0) | (z == 3), outer, total)


def core_scatter(part, core):
    own = at(part, core)
    given = at(part, 1 - core)
    return low(wide(own) + wide(moved(given, FLIP_CORE)))


def head_columns(shard, half, axis):
    first = [lax.slice_in_dim(shard, 1600 * k + 768 * half, 1600 * k + 768 * half + 832, axis=axis) for k in range(3)]
    pad = [(0, 0)] * shard.ndim
    pad[axis] = (0, 64)
    return jnp.concatenate([jnp.pad(part, pad) for part in first], axis=axis)


def on_device(
    inputs,
    segments,
    cotangent,
    project_in,
    project_out,
    expand_weight,
    reduce_weight,
    query_bias,
    value_bias,
    project_bias,
    expand_bias,
    reduce_bias,
    first_gain,
    first_shift,
    second_gain,
    second_shift,
):
    replica, group, z, core, y, x = place()
    quad = lax.rem(replica, 4)
    width = 1600
    rows = 512

    vec = jnp.concatenate(
        [query_bias, value_bias, project_bias, reduce_bias, first_gain, first_shift, second_gain, second_shift, expand_bias]
    )[None]
    halves = jnp.stack([head_columns(project_in, 0, 1), head_columns(project_in, 1, 1)])
    x_seq, w_half, vecs, segs, cots = first_exchange(
        inputs, halves, vec, segments[:, None, :], cotangent.reshape(rows, width)
    )
    vecs = wide(vecs[:, 0, :])
    names = [vecs[:, 400 * k : 400 * k + 400].reshape(width) for k in range(8)]
    bias_query, bias_value, bias_project, bias_reduce, gain_first, shift_first, gain_second, shift_second = names
    bias_expand = lax.dynamic_slice_in_dim(vecs[:, 3200:], 400 * quad, 400, 1).reshape(width)
    segs = segs.reshape(1024)

    quarter_reduce = lax.dynamic_slice_in_dim(reduce_weight, 400 * quad, 400, 0)
    quarter_expand = lax.dynamic_slice_in_dim(expand_weight.reshape(400, 4, width), 400 * quad, 400, 2).reshape(400, width)
    after, out_shard, feed_shard = lax.optimization_barrier(
        (x_seq, project_out, jnp.stack([quarter_reduce, quarter_expand]))
    )
    x_seq = after
    full_out = lax.all_gather(out_shard, "group", axis=0, tiled=True)
    feed = lax.all_gather(feed_shard, "group", axis=0)
    reduce_part = feed[:, 0].reshape(width, width)
    expand_part = feed[:, 1].reshape(width, width)

    flat_seq = wide(x_seq.reshape(1024, width))
    normed = low(layer_norm(flat_seq, gain_first, shift_first))
    w_half = w_half.reshape(width, 2688)
    pad64 = jnp.zeros((64,), jnp.float32)
    bias_q = lax.dynamic_slice_in_dim(bias_query, 768 * y, 832, 0)
    bias_v = lax.dynamic_slice_in_dim(bias_value, 768 * y, 832, 0)
    bias_mix = jnp.concatenate([bias_q, pad64, jnp.zeros((896,), jnp.float32), bias_v, pad64])
    mixture = low(product(normed, w_half) + bias_mix)
    segc = segs[:, None]
    segr = segs[None]
    attended, lse = heads(mixture, segc, segr)
    att_tokens = turn(attended.reshape(4, 256, 896), True, 1)
    att_tokens = jnp.concatenate([att_tokens[:, 0].reshape(rows, 896), att_tokens[:, 1].reshape(rows, 896)], axis=1)

    zero_rows = jnp.zeros((64, width), jnp.bfloat16)
    out_pad = jnp.concatenate([full_out[:832], zero_rows, zero_rows, full_out[832:], zero_rows])
    flat_input = wide(inputs.reshape(rows, width))
    middle = flat_input + product(att_tokens, out_pad) + bias_project
    center = middle - jnp.mean(middle, axis=-1, keepdims=True)
    scale = lax.rsqrt(jnp.mean(center * center, axis=-1, keepdims=True) + epsilon)
    unit = center * scale
    second = low(unit * gain_second + shift_second)

    second_all = quad_gather(second).reshape(4 * rows, width)
    cot_all = cots.reshape(4 * rows, width)
    expanded = product(second_all, expand_part) + bias_expand
    activated, gelu_back = jax.vjp(lambda entry: jax.nn.gelu(entry, approximate=True), expanded)
    activated = low(activated)
    grad_expanded = low(gelu_back(product_back(cot_all, reduce_part))[0])
    grad_second = quad_scatter(low(product_back(grad_expanded, expand_part)).reshape(4, rows, width))

    q = grad_second * gain_second
    grad_middle = wide(cotangent.reshape(rows, width)) + scale * (
        q - jnp.mean(q, axis=-1, keepdims=True) - unit * jnp.mean(q * unit, axis=-1, keepdims=True)
    )
    second_gain_grad = jnp.sum(grad_second * unit, axis=0)
    second_shift_grad = jnp.sum(grad_second, axis=0)
    grad_middle_low = low(grad_middle)
    grad_att = low(product_back(grad_middle_low, out_pad))
    grad_att = jnp.stack([grad_att[:, :896].reshape(2, 256, 896), grad_att[:, 896:].reshape(2, 256, 896)], axis=1)
    grad_heads = turn(grad_att, False, 2).reshape(1024, 896)
    dq, dk, dv = heads_back(mixture, grad_heads, attended, lse, segc, segr)
    grad_mix = jnp.concatenate([dq, dk, dv], axis=1)
    grad_normed = product_back(grad_mix, w_half)

    result_part = low(product(activated, reduce_part)).reshape(4, rows, width)
    reduce_grad = low(weight_term(activated, cot_all)).reshape(4, 400, width)
    expand_grad = low(weight_term(second_all, grad_expanded)).reshape(4, 400, width)
    share_reduce = lax.psum_scatter(reduce_grad, "group", scatter_dimension=0, tiled=False)
    share_expand = lax.psum_scatter(expand_grad, "group", scatter_dimension=0, tiled=False)
    sum_reduce = low(wide(share_reduce) + wide(moved(share_reduce, FLIP_PAIR)))
    sum_expand = low(wide(share_expand) + wide(moved(share_expand, FLIP_PAIR)))
    all_reduce = quad_gather(sum_reduce)
    all_expand = quad_gather(sum_expand)
    total_reduce = wide(jnp.concatenate([at(all_reduce, quad ^ k) for k in range(4)]))
    total_expand = wide(
        jnp.stack([at(all_expand, quad ^ k).reshape(400, 4, 400) for k in range(4)], axis=2).reshape(400, 6400)
    )
    result = quad_scatter(result_part) + middle + bias_reduce
    outputs = low(result).reshape(2, 256, width)

    parts = low(grad_normed).reshape(4, 256, width)
    over = moved(at(parts, group ^ 3), FLIP_Y)
    given = low(wide(at(parts, group ^ 1)) + wide(over))
    cross = moved(given, FLIP_X)
    own = wide(at(parts, group)) + wide(moved(at(parts, group ^ 2), FLIP_Y))
    grad_tokens = jnp.where(x == 0, jnp.stack([own, wide(cross)]), jnp.stack([wide(cross), own])).reshape(rows, width)
    center1 = flat_input - jnp.mean(flat_input, axis=-1, keepdims=True)
    scale1 = lax.rsqrt(jnp.mean(center1 * center1, axis=-1, keepdims=True) + epsilon)
    unit1 = center1 * scale1
    q1 = grad_tokens * gain_first
    input_grad = grad_middle + scale1 * (
        q1 - jnp.mean(q1, axis=-1, keepdims=True) - unit1 * jnp.mean(q1 * unit1, axis=-1, keepdims=True)
    )
    first_gain_grad = jnp.sum(grad_tokens * unit1, axis=0)
    first_shift_grad = jnp.sum(grad_tokens, axis=0)

    out_grad = low(weight_term(att_tokens, grad_middle_low))
    out_grad = jnp.concatenate([out_grad[:832], out_grad[960:1728]]).reshape(4, 2, 200, width)
    in_grad = low(weight_term(normed, grad_mix)).reshape(4, 2, 200, 2688)
    out_core = core_scatter(jnp.swapaxes(out_grad, 0, 1), core)
    in_core = core_scatter(jnp.swapaxes(in_grad, 0, 1), core)
    out_share = lax.psum_scatter(out_core, "group", scatter_dimension=0, tiled=False)
    in_rows = in_core.reshape(2, 2, 200, 2688)
    in_x = low(wide(lax.dynamic_index_in_dim(in_rows, x, 1, False)) + wide(moved(lax.dynamic_index_in_dim(in_rows, 1 - x, 1, False), FLIP_X)))
    in_mine = at(in_x, y)
    in_other = moved(at(in_x, 1 - y), FLIP_Y)
    low_half = jnp.where(y == 0, in_mine, in_other).reshape(200, 3, 896)
    high_half = jnp.where(y == 0, in_other, in_mine).reshape(200, 3, 896)
    in_share = jnp.concatenate([low_half[:, :, :832], high_half[:, :, 64:832]], axis=2).reshape(200, 4800)
    out_total = line_sum(out_share, z)
    in_total = line_sum(in_share, z)
    out_there = moved(out_total, FLIP_CORE)
    in_there = moved(in_total, FLIP_CORE)
    total_out = wide(jnp.where(core == 0, jnp.concatenate([out_total, out_there]), jnp.concatenate([out_there, out_total])))
    total_in = wide(jnp.where(core == 0, jnp.concatenate([in_total, in_there]), jnp.concatenate([in_there, in_total])))

    def spread(columns):
        lower = jnp.concatenate([columns[:832], jnp.zeros((768,), jnp.float32)])
        upper = jnp.concatenate([jnp.zeros((832,), jnp.float32), columns[64:832]])
        return jnp.where(y == 0, lower, upper)

    expand_bias_part = column_sum(grad_expanded).reshape(4, 400)
    expand_bias_wide = lax.dynamic_update_slice_in_dim(jnp.zeros((4, width), jnp.float32), expand_bias_part, 400 * quad, 1)
    vectors = jnp.concatenate(
        [
            spread(column_sum(dq)).reshape(4, 400),
            spread(column_sum(dv)).reshape(4, 400),
            column_sum(grad_middle_low).reshape(4, 400),
            column_sum(cotangent.reshape(rows, width)).reshape(4, 400),
            first_gain_grad.reshape(4, 400),
            first_shift_grad.reshape(4, 400),
            second_gain_grad.reshape(4, 400),
            second_shift_grad.reshape(4, 400),
            expand_bias_wide,
        ],
        axis=1,
    )
    vectors = at(lax.psum(vectors, ("replica", "group")), group)
    pieces = [vectors[400 * k : 400 * k + 400] for k in range(8)]
    return (
        outputs,
        input_grad.reshape(2, 256, width),
        total_in,
        total_out,
        total_expand,
        total_reduce,
        pieces[0],
        pieces[1],
        pieces[2],
        vectors[3200:],
        pieces[3],
        pieces[4],
        pieces[5],
        pieces[6],
        pieces[7],
    )


def solution(mesh):
    placed = (
        P("replica", "group", None),
        P("replica", "group"),
        P("replica", "group", None),
        P("group", None),
        P("group", None),
        P("group", None),
        P("group", None),
        P("group"),
        P("group"),
        P("group"),
        P("group"),
        P("group"),
        P("group"),
        P("group"),
        P("group"),
        P("group"),
    )
    return jax.shard_map(
        on_device if dict(mesh.shape) == {"replica": 8, "group": 4} else on_device_any,
        mesh=mesh,
        in_specs=placed,
        out_specs=(
            P("replica", "group", None),
            P("replica", "group", None),
            P("group", None),
            P("group", None),
            P("group", None),
            P("group", None),
            P("group"),
            P("group"),
            P("group"),
            P("group"),
            P("group"),
            P("group"),
            P("group"),
            P("group"),
            P("group"),
        ),
        check_vma=False,
    )
```

```python
import functools
import math

import jax
import jax.numpy as jnp
from jax import lax
from jax.sharding import PartitionSpec as P

from jax.experimental import pallas as pl
from jax.experimental.pallas import tpu as pltpu

HEADS = 25
HEAD_DIM = 64


epsilon = 1e-05
very_low = -1e30


def carried_in(part, axis, combine, identity):
    place = lax.axis_index(axis)
    gathered = lax.all_gather(part, axis)
    state = jnp.zeros_like(part) + jnp.asarray(identity, part.dtype)

    def one(hop, state):
        return combine(state, lax.dynamic_index_in_dim(gathered, hop, 0, False))

    return lax.fori_loop(0, place, one, state)


def layer_norm(entries, gain, shift):
    center = entries - jnp.mean(entries, axis=-1, keepdims=True)
    spread = jnp.mean(center * center, axis=-1, keepdims=True)
    return center * lax.rsqrt(spread + epsilon) * gain + shift


def product(left, right):
    return jnp.dot(left, right, preferred_element_type=jnp.float32)


def product_back(left, right):
    return lax.dot_general(
        left, right, (((1,), (1,)), ((), ())), preferred_element_type=jnp.float32
    )


def weight_term(left, right):
    return lax.dot_general(
        left, right, (((0,), (0,)), ((), ())), preferred_element_type=jnp.float32
    )


def column_sum(entries):
    return jnp.sum(entries.astype(jnp.float32), axis=0)


def block_scores(queries, key_block, offset, query_pos, doc_start):
    block_count = key_block.shape[0]
    key_count = key_block.shape[2]
    scaling = 1.0 / math.sqrt(HEAD_DIM)
    scores = (
        jnp.einsum("schd,pskhd->shcpk", queries, key_block, preferred_element_type=jnp.float32)
        * scaling
    )
    key_pos = (offset + jnp.arange(block_count, dtype=jnp.int32))[:, None] * key_count + jnp.arange(
        key_count, dtype=jnp.int32
    )[None, :]
    allowed = (key_pos[None, None] <= query_pos[None, :, None, None]) & (
        key_pos[None, None] >= doc_start[:, :, None, None]
    )
    allowed = allowed[:, None]
    return (jnp.where(allowed, scores, very_low), allowed)


def attend(running, key_block, value_block, offset, queries, query_pos, doc_start):
    largest, denominator, summed = running
    masked, allowed = block_scores(queries, key_block, offset, query_pos, doc_start)
    fresh = jnp.maximum(largest, jnp.max(masked, axis=(3, 4)))
    shares = jnp.where(allowed, jnp.exp(masked - fresh[..., None, None]), 0.0)
    rescale = jnp.exp(largest - fresh)
    denominator = denominator * rescale + jnp.sum(shares, axis=(3, 4))
    added = jnp.einsum(
        "shcpk,pskhd->schd",
        shares.astype(jnp.bfloat16),
        value_block,
        preferred_element_type=jnp.float32,
    )
    summed = summed * jnp.transpose(rescale, (0, 2, 1))[..., None] + added
    return (fresh, denominator, summed)


def attend_back(
    grad_query,
    key_block,
    value_block,
    offset,
    queries,
    query_pos,
    doc_start,
    log_total,
    grad_low,
    row_dot,
):
    masked, allowed = block_scores(queries, key_block, offset, query_pos, doc_start)
    shares = jnp.where(allowed, jnp.exp(masked - log_total[..., None, None]), 0.0)
    grad_value = jnp.einsum(
        "shcpk,schd->pskhd",
        shares.astype(jnp.bfloat16),
        grad_low,
        preferred_element_type=jnp.float32,
    )
    grad_share = jnp.einsum(
        "schd,pskhd->shcpk", grad_low, value_block, preferred_element_type=jnp.float32
    )
    grad_score = (shares * (grad_share - row_dot[..., None, None])).astype(jnp.bfloat16)
    grad_query = grad_query + jnp.einsum(
        "shcpk,pskhd->schd", grad_score, key_block, preferred_element_type=jnp.float32
    )
    grad_key = jnp.einsum(
        "shcpk,schd->pskhd", grad_score, queries, preferred_element_type=jnp.float32
    )
    return (grad_query, (grad_key, grad_value))


def on_device_any(
    inputs,
    segments,
    cotangent,
    project_in,
    project_out,
    expand_weight,
    reduce_weight,
    query_bias,
    value_bias,
    project_bias,
    expand_bias,
    reduce_bias,
    first_gain,
    first_shift,
    second_gain,
    second_shift,
):
    seq_here, local_len, width = inputs.shape
    groups = lax.axis_size("group")
    total_rows = seq_here * local_len
    head_shape = (seq_here, local_len, HEADS, HEAD_DIM)
    shards = (
        project_in,
        project_out,
        expand_weight,
        reduce_weight,
        query_bias,
        value_bias,
        project_bias,
        expand_bias,
        reduce_bias,
        first_gain,
        first_shift,
        second_gain,
        second_shift,
    )
    whole = (
        lax.all_gather(shards[0], "group", axis=0, tiled=True),
        lax.all_gather(shards[1], "group", axis=0, tiled=True),
        lax.all_gather(shards[2], "group", axis=0, tiled=True),
        lax.all_gather(shards[3], "group", axis=0, tiled=True),
        lax.all_gather(shards[4], "group", axis=0, tiled=True),
        lax.all_gather(shards[5], "group", axis=0, tiled=True),
        lax.all_gather(shards[6], "group", axis=0, tiled=True),
        lax.all_gather(shards[7], "group", axis=0, tiled=True),
        lax.all_gather(shards[8], "group", axis=0, tiled=True),
        lax.all_gather(shards[9], "group", axis=0, tiled=True),
        lax.all_gather(shards[10], "group", axis=0, tiled=True),
        lax.all_gather(shards[11], "group", axis=0, tiled=True),
        lax.all_gather(shards[12], "group", axis=0, tiled=True),
    )
    (
        full_in,
        full_out,
        full_expand,
        full_reduce,
        bias_query,
        bias_value,
        bias_project,
        bias_expand,
        bias_reduce,
        gain_first,
        shift_first,
        gain_second,
        shift_second,
    ) = whole
    group_rank = lax.axis_index("group")
    query_pos = group_rank * local_len + jnp.arange(local_len, dtype=jnp.int32)
    positions = jnp.broadcast_to(query_pos[None, :], (seq_here, local_len))
    end_marks = jnp.where(segments == positions, positions + 1, 0)
    before = carried_in(
        jnp.max(end_marks, axis=1), "group", jnp.maximum, jnp.zeros((seq_here,), jnp.int32)
    )
    inside = lax.cummax(end_marks, axis=1)
    inside = jnp.concatenate([jnp.zeros((seq_here, 1), jnp.int32), inside[:, :-1]], axis=1)
    doc_start = jnp.maximum(before[:, None], inside)
    flat_input = inputs.reshape(total_rows, width).astype(jnp.float32)
    normed_low = layer_norm(
        flat_input, gain_first.astype(jnp.float32), shift_first.astype(jnp.float32)
    ).astype(jnp.bfloat16)
    mixture = product(normed_low, full_in)
    queries = (
        (mixture[:, :width] + bias_query.astype(jnp.float32))
        .astype(jnp.bfloat16)
        .reshape(head_shape)
    )
    key_rows = (
        mixture[:, width : 2 * width].astype(jnp.bfloat16).reshape(seq_here, local_len, width)
    )
    value_rows = (
        (mixture[:, 2 * width :] + bias_value.astype(jnp.float32))
        .astype(jnp.bfloat16)
        .reshape(seq_here, local_len, width)
    )
    initial = (
        jnp.full((seq_here, HEADS, local_len), very_low, jnp.float32),
        jnp.zeros((seq_here, HEADS, local_len), jnp.float32),
        jnp.zeros(head_shape, jnp.float32),
    )
    block_ids = jnp.arange(groups, dtype=jnp.int32)
    running = initial
    pieces = (
        lax.all_gather(key_rows[None], "group", axis=0, tiled=True),
        lax.all_gather(value_rows[None], "group", axis=0, tiled=True),
    )
    piece_count = pieces[0].shape[0]

    def one_piece(state, members):
        key_piece, value_piece, index = members
        updated = attend(
            state,
            key_piece.reshape((1,) + head_shape),
            value_piece.reshape((1,) + head_shape),
            index,
            queries,
            query_pos,
            doc_start,
        )
        return (updated, None)

    running, unused_steps = lax.scan(
        one_piece, running, (pieces[0], pieces[1], jnp.arange(piece_count, dtype=jnp.int32))
    )
    largest, denominator, summed = running
    attended = summed / jnp.transpose(denominator, (0, 2, 1))[..., None]
    log_total = largest + jnp.log(denominator)
    attended_low = attended.reshape(total_rows, width).astype(jnp.bfloat16)
    middle = flat_input + product(attended_low, full_out) + bias_project.astype(jnp.float32)
    second_low = layer_norm(
        middle, gain_second.astype(jnp.float32), shift_second.astype(jnp.float32)
    ).astype(jnp.bfloat16)
    expanded = product(second_low, full_expand) + bias_expand.astype(jnp.float32)
    activated_low = jax.nn.gelu(expanded, approximate=True).astype(jnp.bfloat16)
    result = middle + product(activated_low, full_reduce) + bias_reduce.astype(jnp.float32)
    outputs = result.astype(jnp.bfloat16).reshape(seq_here, local_len, width)
    whole_back = (
        lax.all_gather(shards[0], "group", axis=0, tiled=True),
        lax.all_gather(shards[1], "group", axis=0, tiled=True),
        lax.all_gather(shards[2], "group", axis=0, tiled=True),
        lax.all_gather(shards[3], "group", axis=0, tiled=True),
        lax.all_gather(shards[4], "group", axis=0, tiled=True),
        lax.all_gather(shards[5], "group", axis=0, tiled=True),
        lax.all_gather(shards[6], "group", axis=0, tiled=True),
        lax.all_gather(shards[7], "group", axis=0, tiled=True),
        lax.all_gather(shards[8], "group", axis=0, tiled=True),
        lax.all_gather(shards[9], "group", axis=0, tiled=True),
        lax.all_gather(shards[10], "group", axis=0, tiled=True),
        lax.all_gather(shards[11], "group", axis=0, tiled=True),
        lax.all_gather(shards[12], "group", axis=0, tiled=True),
    )
    keys_back = (
        lax.all_gather(key_rows[None], "group", axis=0, tiled=True),
        lax.all_gather(value_rows[None], "group", axis=0, tiled=True),
    )
    (
        back_in,
        back_out,
        back_expand,
        back_reduce,
        unused_query,
        unused_value,
        unused_project,
        unused_expand,
        unused_reduce,
        back_gain_first,
        back_shift_first,
        back_gain_second,
        back_shift_second,
    ) = whole_back
    grad_rows = cotangent.reshape(total_rows, width).astype(jnp.float32)
    grad_result_low = cotangent.reshape(total_rows, width)
    reduce_bias_grad = column_sum(grad_result_low)
    grad_activated = product_back(grad_result_low, back_reduce)
    unused_gelu, gelu_back = jax.vjp(lambda entry: jax.nn.gelu(entry, approximate=True), expanded)
    grad_expanded_low = gelu_back(grad_activated)[0].astype(jnp.bfloat16)
    expand_bias_grad = column_sum(grad_expanded_low)
    grad_second = product_back(grad_expanded_low, back_expand)
    unused_second, second_back = jax.vjp(
        layer_norm,
        middle,
        back_gain_second.astype(jnp.float32),
        back_shift_second.astype(jnp.float32),
    )
    grad_middle, second_gain_grad, second_shift_grad = second_back(grad_second)
    grad_middle = grad_middle + grad_rows
    reduce_weight_grad = weight_term(activated_low, grad_result_low)
    expand_weight_grad = weight_term(second_low, grad_expanded_low)
    feed_parts = (
        lax.psum_scatter(
            expand_weight_grad.astype(jnp.bfloat16), "group", scatter_dimension=0, tiled=True
        ).astype(jnp.float32),
        lax.psum_scatter(
            reduce_weight_grad.astype(jnp.bfloat16), "group", scatter_dimension=0, tiled=True
        ).astype(jnp.float32),
        lax.psum_scatter(
            expand_bias_grad.astype(jnp.bfloat16), "group", scatter_dimension=0, tiled=True
        ).astype(jnp.float32),
        lax.psum_scatter(
            reduce_bias_grad.astype(jnp.bfloat16), "group", scatter_dimension=0, tiled=True
        ).astype(jnp.float32),
        lax.psum_scatter(
            second_gain_grad.astype(jnp.bfloat16), "group", scatter_dimension=0, tiled=True
        ).astype(jnp.float32),
        lax.psum_scatter(
            second_shift_grad.astype(jnp.bfloat16), "group", scatter_dimension=0, tiled=True
        ).astype(jnp.float32),
    )
    grad_middle_low = grad_middle.astype(jnp.bfloat16)
    project_bias_grad = column_sum(grad_middle_low)
    grad_attended_low = (
        product_back(grad_middle_low, back_out).astype(jnp.bfloat16).reshape(head_shape)
    )
    row_dot = jnp.einsum("schd,schd->shc", grad_attended_low.astype(jnp.float32), attended)

    def back_step(grad_query, members):
        key_piece, value_piece, offset = members
        return attend_back(
            grad_query,
            key_piece.reshape((1,) + head_shape),
            value_piece.reshape((1,) + head_shape),
            offset,
            queries,
            query_pos,
            doc_start,
            log_total,
            grad_attended_low,
            row_dot,
        )

    grad_query, terms = lax.scan(
        back_step, jnp.zeros(head_shape, jnp.float32), (keys_back[0], keys_back[1], block_ids)
    )
    key_terms = terms[0].reshape(groups, seq_here, local_len, width)
    value_terms = terms[1].reshape(groups, seq_here, local_len, width)
    key_grad, value_grad = (
        lax.psum_scatter(
            key_terms.astype(jnp.bfloat16), "group", scatter_dimension=0, tiled=True
        ).astype(jnp.float32),
        lax.psum_scatter(
            value_terms.astype(jnp.bfloat16), "group", scatter_dimension=0, tiled=True
        ).astype(jnp.float32),
    )
    scaling = 1.0 / math.sqrt(HEAD_DIM)
    grad_query_low = (grad_query * scaling).reshape(total_rows, width).astype(jnp.bfloat16)
    grad_key_low = (key_grad * scaling).reshape(total_rows, width).astype(jnp.bfloat16)
    grad_value_low = value_grad.reshape(total_rows, width).astype(jnp.bfloat16)
    query_bias_grad = column_sum(grad_query_low)
    value_bias_grad = column_sum(grad_value_low)
    grad_mixture_low = jnp.concatenate([grad_query_low, grad_key_low, grad_value_low], axis=1)
    grad_normed = product_back(grad_mixture_low, back_in)
    unused_first, first_back = jax.vjp(
        layer_norm,
        flat_input,
        back_gain_first.astype(jnp.float32),
        back_shift_first.astype(jnp.float32),
    )
    grad_entry, first_gain_grad, first_shift_grad = first_back(grad_normed)
    input_grad = (grad_entry + grad_middle).reshape(seq_here, local_len, width)
    project_weight_grad = weight_term(attended_low, grad_middle_low)
    in_weight_grad = weight_term(normed_low, grad_mixture_low)
    mixer_parts = (
        lax.psum_scatter(
            in_weight_grad.astype(jnp.bfloat16), "group", scatter_dimension=0, tiled=True
        ).astype(jnp.float32),
        lax.psum_scatter(
            project_weight_grad.astype(jnp.bfloat16), "group", scatter_dimension=0, tiled=True
        ).astype(jnp.float32),
        lax.psum_scatter(
            query_bias_grad.astype(jnp.bfloat16), "group", scatter_dimension=0, tiled=True
        ).astype(jnp.float32),
        lax.psum_scatter(
            value_bias_grad.astype(jnp.bfloat16), "group", scatter_dimension=0, tiled=True
        ).astype(jnp.float32),
        lax.psum_scatter(
            project_bias_grad.astype(jnp.bfloat16), "group", scatter_dimension=0, tiled=True
        ).astype(jnp.float32),
        lax.psum_scatter(
            first_gain_grad.astype(jnp.bfloat16), "group", scatter_dimension=0, tiled=True
        ).astype(jnp.float32),
        lax.psum_scatter(
            first_shift_grad.astype(jnp.bfloat16), "group", scatter_dimension=0, tiled=True
        ).astype(jnp.float32),
    )
    share_in, share_out, share_expand, share_reduce = (
        mixer_parts[0],
        mixer_parts[1],
        feed_parts[0],
        feed_parts[1],
    )
    share_query, share_value, share_project = (mixer_parts[2], mixer_parts[3], mixer_parts[4])
    share_expand_bias, share_reduce_bias = (feed_parts[2], feed_parts[3])
    share_first_gain, share_first_shift = (mixer_parts[5], mixer_parts[6])
    share_second_gain, share_second_shift = (feed_parts[4], feed_parts[5])
    totals = (
        lax.psum(share_in.astype(jnp.bfloat16), "replica").astype(jnp.float32),
        lax.psum(share_out.astype(jnp.bfloat16), "replica").astype(jnp.float32),
        lax.psum(share_expand.astype(jnp.bfloat16), "replica").astype(jnp.float32),
        lax.psum(share_reduce.astype(jnp.bfloat16), "replica").astype(jnp.float32),
        lax.psum(share_query.astype(jnp.bfloat16), "replica").astype(jnp.float32),
        lax.psum(share_value.astype(jnp.bfloat16), "replica").astype(jnp.float32),
        lax.psum(share_project.astype(jnp.bfloat16), "replica").astype(jnp.float32),
        lax.psum(share_expand_bias.astype(jnp.bfloat16), "replica").astype(jnp.float32),
        lax.psum(share_reduce_bias.astype(jnp.bfloat16), "replica").astype(jnp.float32),
        lax.psum(share_first_gain.astype(jnp.bfloat16), "replica").astype(jnp.float32),
        lax.psum(share_first_shift.astype(jnp.bfloat16), "replica").astype(jnp.float32),
        lax.psum(share_second_gain.astype(jnp.bfloat16), "replica").astype(jnp.float32),
        lax.psum(share_second_shift.astype(jnp.bfloat16), "replica").astype(jnp.float32),
    )
    return (
        outputs,
        input_grad,
        totals[0],
        totals[1],
        totals[2],
        totals[3],
        totals[4],
        totals[5],
        totals[6],
        totals[7],
        totals[8],
        totals[9],
        totals[10],
        totals[11],
        totals[12],
    )


MESH = pl.DeviceIdType.MESH


def flipped(z=0, core=0, y=0, x=0):
    pairs = []
    for me in range(32):
        pairs.append((me, me ^ (8 * z + 4 * core + 2 * y + x)))
    return pairs


FLIP_X = flipped(x=1)
FLIP_Y = flipped(y=1)
FLIP_CORE = flipped(core=1)
FLIP_Z = flipped(z=1)
FLIP_PAIR = flipped(z=2)
INWARD = [(me, me + 8) for me in range(8)] + [(me, me - 8) for me in range(24, 32)]
MIDDLE = [(me, me + 8) for me in range(8, 16)] + [(me, me - 8) for me in range(16, 24)]
OUTWARD = [(me, me - 8) for me in range(8, 16)] + [(me, me + 8) for me in range(16, 24)]


def moved(entries, pairs):
    return lax.ppermute(entries, ("replica", "group"), pairs)


def low(entries):
    return entries.astype(jnp.bfloat16)


def wide(entries):
    return entries.astype(jnp.float32)


def at(entries, index):
    return lax.dynamic_index_in_dim(entries, index, 0, False)


def place():
    replica = lax.axis_index("replica")
    group = lax.axis_index("group")
    core = lax.rem(replica, 2)
    z = lax.div(replica, 2)
    return replica, group, z, core, lax.div(group, 2), lax.rem(group, 2)


def partners(replica, group):
    core = lax.rem(replica, 2)
    z = lax.rem(lax.div(replica, 2), 2)
    y = lax.div(group, 2)
    x = lax.rem(group, 2)
    by_x = (replica, group + 1 - 2 * x)
    by_y = (replica, group + 2 - 4 * y)
    by_both = (replica, group + 3 - 4 * y - 2 * x)
    by_core = (replica + 1 - 2 * core, group)
    by_z = (replica + 2 - 4 * z, group)
    return by_x, by_y, by_both, by_core, by_z


def greet(devices):
    barrier = pltpu.get_barrier_semaphore()
    for device in devices:
        pl.semaphore_signal(barrier, inc=1, device_id=device, device_id_type=MESH)
    pl.semaphore_wait(barrier, len(devices))


NT = (((1,), (1,)), ((), ()))

def dot_nt(a, b):
    return lax.dot_general(a, b, NT, preferred_element_type=jnp.float32)

def dot_nn(a, b):
    return jnp.dot(a, b, preferred_element_type=jnp.float32)

BLOCK = 256

def heads_kernel(q_ref, k_ref, v_ref, segc_ref, segr_ref, o_ref, lse_ref, ot_ref, vt_ref):
    tile = pl.program_id(0)
    length = q_ref.shape[0]
    blocks = length // BLOCK
    lane = lax.broadcasted_iota(jnp.int32, (1, 128), 1)
    ot_ref[...] = jnp.zeros_like(ot_ref)
    lse_ref[...] = jnp.zeros_like(lse_ref)
    vt_ref[...] = v_ref[...].T

    def head(h):
        k = jnp.where((lane >= 64 * h) & (lane < 64 * h + 64), k_ref[...], jnp.bfloat16(0))
        for i in range(blocks):
            low, high = i * BLOCK, (i + 1) * BLOCK
            q = q_ref[low:high, :] * jnp.bfloat16(0.125)
            s = dot_nt(k[:high], q)
            same = segc_ref[:high, :] == segr_ref[:, low:high]
            kpos = lax.broadcasted_iota(jnp.int32, (high, BLOCK), 0)
            qpos = lax.broadcasted_iota(jnp.int32, (high, BLOCK), 1) + low
            s = jnp.where(same & (kpos <= qpos), s, -1e30)
            m = jnp.max(s, axis=0, keepdims=True)
            p = jnp.exp(s - m)
            l = jnp.sum(p, axis=0, keepdims=True)
            ot = dot_nn(vt_ref[64 * h : 64 * h + 64, :high], p.astype(jnp.bfloat16))
            ot_ref[64 * h : 64 * h + 64, low:high] = ot / l
            lse_ref[0, h : h + 1, low:high] = m + jnp.log(l)

    head(0)

    @pl.when(tile < 6)
    def _():
        head(1)

    o_ref[...] = ot_ref[...].T.astype(jnp.bfloat16)


def heads(qkv, segc, segr):
    length = qkv.shape[0]
    spec = lambda off: pl.BlockSpec((length, 128), lambda t: (0, t + off))
    return pl.pallas_call(
        heads_kernel,
        grid=(7,),
        in_specs=[spec(0), spec(7), spec(14), pl.BlockSpec((length, 1), lambda t: (0, 0)), pl.BlockSpec((1, length), lambda t: (0, 0))],
        out_specs=[pl.BlockSpec((length, 128), lambda t: (0, t)), pl.BlockSpec((1, 8, length), lambda t: (t, 0, 0))],
        out_shape=[jax.ShapeDtypeStruct((length, 896), jnp.bfloat16), jax.ShapeDtypeStruct((7, 8, length), jnp.float32)],
        scratch_shapes=[pltpu.VMEM((128, length), jnp.float32), pltpu.VMEM((128, length), jnp.bfloat16)],
        compiler_params=pltpu.CompilerParams(vmem_limit_bytes=48 * 2**20),
        cost_estimate=pl.CostEstimate(flops=int(13 * 2 * 2 * length * length * 64 * 2), bytes_accessed=8 * length * 896, transcendentals=13 * length * length // 2),
        name="heads",
    )(qkv, qkv, qkv, segc, segr)


def heads_back_kernel(q_ref, k_ref, v_ref, do_ref, o_ref, lse_ref, segc_ref, segr_ref, share_ref, dq_ref, dk_ref, dv_ref, got_ref, dqt_ref, odt_ref, send, recv):
    tile = pl.program_id(0)
    by_pair = (lax.rem(lax.axis_index("replica") + 4, 8), lax.axis_index("group"))
    copy = pltpu.make_async_remote_copy(src_ref=share_ref, dst_ref=got_ref, send_sem=send, recv_sem=recv, device_id=by_pair, device_id_type=MESH)

    @pl.when(tile == 0)
    def _():
        greet([by_pair])
        copy.start()

    length = q_ref.shape[0]
    blocks = length // BLOCK
    lane = lax.broadcasted_iota(jnp.int32, (1, 128), 1)
    dqt_ref[...] = jnp.zeros_like(dqt_ref)
    odt_ref[...] = (do_ref[...].astype(jnp.float32) * o_ref[...].astype(jnp.float32)).T

    def head(h):
        mine = (lane >= 64 * h) & (lane < 64 * h + 64)
        dot_row = jnp.sum(odt_ref[64 * h : 64 * h + 64, :], axis=0, keepdims=True)
        for j in range(blocks):
            low, high = j * BLOCK, (j + 1) * BLOCK
            rest = length - low
            q = q_ref[low:, :] * jnp.bfloat16(0.125)
            do = do_ref[low:, :]
            k = jnp.where(mine, k_ref[low:high, :], jnp.bfloat16(0))
            v = jnp.where(mine, v_ref[low:high, :], jnp.bfloat16(0))
            s = dot_nt(k, q)
            same = segc_ref[low:high, :] == segr_ref[:, low:]
            kpos = lax.broadcasted_iota(jnp.int32, (BLOCK, rest), 0)
            qpos = lax.broadcasted_iota(jnp.int32, (BLOCK, rest), 1)
            p = jnp.where(same & (kpos <= qpos), jnp.exp(s - lse_ref[0, h : h + 1, low:]), 0.0)
            dp = dot_nt(v, do)
            ds = (p * (dp - dot_row[:, low:])).astype(jnp.bfloat16)
            dv = dot_nn(p.astype(jnp.bfloat16), do)
            dk = dot_nn(ds, q)
            if h == 0:
                dv_ref[low:high, :] = jnp.where(mine, dv, 0.0).astype(jnp.bfloat16)
                dk_ref[low:high, :] = jnp.where(mine, dk, 0.0).astype(jnp.bfloat16)
            else:
                dv_ref[low:high, :] = jnp.where(mine, dv.astype(jnp.bfloat16), dv_ref[low:high, :])
                dk_ref[low:high, :] = jnp.where(mine, dk.astype(jnp.bfloat16), dk_ref[low:high, :])
            dqt_ref[:, low:] += dot_nn(k.T, ds)

    head(0)

    @pl.when(tile < 6)
    def _():
        head(1)

    dq_ref[...] = (dqt_ref[...].T * 0.125).astype(jnp.bfloat16)

    @pl.when(tile == 6)
    def _():
        copy.wait()


def heads_back(qkv, grad, out, lse, segc, segr, share):
    length = qkv.shape[0]
    spec = lambda off: pl.BlockSpec((length, 128), lambda t: (0, t + off))
    one = pl.BlockSpec((length, 128), lambda t: (0, t))
    shape = jax.ShapeDtypeStruct((length, 896), jnp.bfloat16)
    return pl.pallas_call(
        heads_back_kernel,
        grid=(7,),
        in_specs=[spec(0), spec(7), spec(14), one, one, pl.BlockSpec((1, 8, length), lambda t: (t, 0, 0)), pl.BlockSpec((length, 1), lambda t: (0, 0)), pl.BlockSpec((1, length), lambda t: (0, 0)), pl.BlockSpec(memory_space=pl.ANY)],
        out_specs=[one, one, one, pl.BlockSpec(memory_space=pl.ANY)],
        out_shape=[shape, shape, shape, jax.ShapeDtypeStruct(share.shape, share.dtype)],
        scratch_shapes=[pltpu.VMEM((128, length), jnp.float32), pltpu.VMEM((128, length), jnp.float32), pltpu.SemaphoreType.DMA, pltpu.SemaphoreType.DMA],
        compiler_params=pltpu.CompilerParams(vmem_limit_bytes=48 * 2**20, collective_id=4, has_side_effects=True),
        cost_estimate=pl.CostEstimate(flops=int(13 * 5 * 2 * length * length * 64 * 2), bytes_accessed=16 * length * 896, transcendentals=13 * length * length // 2),
        name="heads_back",
    )(qkv, qkv, qkv, grad, out, lse, segc, segr, share)

ROWS = 256
PIECES = ((0, 512), (512, 1024), (1024, 1600))


def feed_kernel(near_ref, far_ref, cot_ref, expand_ref, reduce_ref, bias_ref, *refs):
    act_ref, back_ref, all_ref, part_ref, sum_ref, keep_ref = refs[-6:]
    step = pl.program_id(0)
    width = expand_ref.shape[0]
    second = jnp.where(step < 2, near_ref[:, :width], far_ref[:, :width])
    all_ref[...] = second
    cot = cot_ref[0]

    @pl.when(step == 0)
    def _():
        sum_ref[...] = jnp.zeros_like(sum_ref)

    for low_at, high_at in PIECES:
        u = jnp.dot(second, expand_ref[:, low_at:high_at], preferred_element_type=jnp.float32) + bias_ref[:, low_at:high_at]
        g = lax.dot_general(cot, reduce_ref[low_at:high_at, :], (((1,), (1,)), ((), ())), preferred_element_type=jnp.float32)
        root = 0.7978845608028654
        square = u * u
        t = jnp.tanh(root * u * (1.0 + 0.044715 * square))
        half = 0.5 * (1.0 + t)
        act_ref[:, low_at:high_at] = (u * half).astype(jnp.bfloat16)
        slope = half + (0.5 * root) * u * (1.0 - t * t) * (1.0 + (3.0 * 0.044715) * square)
        back = (g * slope).astype(jnp.bfloat16)
        back_ref[:, low_at:high_at] = back
        sum_ref[:, low_at:high_at] += jnp.sum(back.astype(jnp.float32).reshape(32, 8, high_at - low_at), axis=0)
    part_ref[:, width:] = jnp.zeros((ROWS, part_ref.shape[1] - width), jnp.bfloat16)
    part_ref[:, :width] = lax.dot_general(
        back_ref[...], expand_ref[...], (((1,), (1,)), ((), ())), preferred_element_type=jnp.float32
    ).astype(jnp.bfloat16)


def feed(near, far, cots, expand_part, reduce_part, bias, kept):
    full = near.shape[1]
    width = expand_part.shape[0]
    wide_rows = 4 * near.shape[0]
    shift = 0 if kept is None else 4
    whole = pl.BlockSpec((width, width), lambda i: (0, 0))
    row = lambda off: pl.BlockSpec((ROWS, width), lambda i: (i + off, 0))
    any_space = pl.BlockSpec(memory_space=pl.ANY)
    operands = [near, far, cots, expand_part, reduce_part, bias]
    specs = [
        pl.BlockSpec((ROWS, full), lambda i: (jnp.minimum(i, 1), 0)),
        pl.BlockSpec((ROWS, full), lambda i: (jnp.maximum(i - 2, 0), 0)),
        pl.BlockSpec((1, ROWS, width), lambda i: (shift // 2 + lax.div(i, 2), lax.rem(i, 2), 0)),
        whole,
        whole,
        pl.BlockSpec((1, width), lambda i: (0, 0)),
    ]
    aliases = {}
    if kept is not None:
        operands += list(kept)
        specs += [any_space] * 3
        aliases = {6: 0, 7: 1, 8: 2}
    big = jax.ShapeDtypeStruct((wide_rows, width), jnp.bfloat16)
    return pl.pallas_call(
        feed_kernel,
        grid=(4,),
        in_specs=specs,
        out_specs=[row(shift), row(shift), row(shift), pl.BlockSpec((ROWS, full), lambda i: (i, 0)), pl.BlockSpec((8, width), lambda i: (0, 0))],
        out_shape=[big, big, big, jax.ShapeDtypeStruct((4 * ROWS, full), jnp.bfloat16), jax.ShapeDtypeStruct((8, width), jnp.float32)],
        scratch_shapes=[pltpu.VMEM((8, 128), jnp.float32)],
        input_output_aliases=aliases,
        compiler_params=pltpu.CompilerParams(vmem_limit_bytes=56 * 2**20),
        cost_estimate=pl.CostEstimate(flops=6 * 4 * ROWS * width * width, bytes_accessed=2 * width * (2 * width + 24 * ROWS), transcendentals=4 * ROWS * width),
        name="feed",
    )(*operands)


def rows_kernel(a_ref, b_ref, o_ref):
    n = b_ref.shape[1]
    o_ref[:, n:] = jnp.zeros((o_ref.shape[0], o_ref.shape[1] - n), jnp.bfloat16)
    o_ref[:, :n] = jnp.dot(a_ref[...], b_ref[...], preferred_element_type=jnp.float32).astype(jnp.bfloat16)


def rows_times(a, b, name, block=512):
    m, k = a.shape
    n = b.shape[1]
    return pl.pallas_call(
        rows_kernel,
        grid=(m // block,),
        in_specs=[pl.BlockSpec((block, k), lambda i: (i, 0)), pl.BlockSpec((k, n), lambda i: (0, 0))],
        out_specs=pl.BlockSpec((block, n + 64), lambda i: (i, 0)),
        out_shape=jax.ShapeDtypeStruct((m, n + 64), jnp.bfloat16),
        compiler_params=pltpu.CompilerParams(vmem_limit_bytes=56 * 2**20),
        cost_estimate=pl.CostEstimate(flops=2 * m * k * n, bytes_accessed=2 * (m * k + k * n + m * n), transcendentals=0),
        name=name,
    )(a, b)


def first_exchange_kernel(inp, weights, vec, seg, cot, x_seq, w_full, vecs, segs, cots, send, recv, local, x_stage, w_stage, vec_stage, seg_stage, cot_stage):
    replica = lax.axis_index("replica")
    group = lax.axis_index("group")
    core = lax.rem(replica, 2)
    y = lax.div(group, 2)
    x = lax.rem(group, 2)
    by_x, by_y, by_both, by_core, by_z = partners(replica, group)
    greet((by_x, by_y, by_both, by_core, by_z))
    other_x = 1 - x
    other_y = 1 - y
    slot_x = group + 1 - 2 * x
    slot_y = group + 2 - 4 * y
    slot_both = group + 3 - 4 * y - 2 * x
    mine = pl.ds(pl.multiple_of(core * 192, 16), 208)
    shared = pl.ds(pl.multiple_of(core * 208, 16), 192)
    count = [0]

    def remote(src, dst, device):
        i = count[0]
        count[0] = i + 1
        copy = pltpu.make_async_remote_copy(src_ref=src, dst_ref=dst, send_sem=send.at[i], recv_sem=recv.at[i], device_id=device, device_id_type=MESH)
        copy.start()
        return copy

    small = [
        remote(vec, vecs.at[group], by_x),
        remote(vec, vecs.at[group], by_y),
        remote(vec, vecs.at[group], by_both),
        remote(seg.at[other_x], segs.at[group], by_x),
        remote(seg.at[x], segs.at[group], by_y),
        remote(seg.at[other_x], segs.at[group], by_both),
    ]
    x_block = remote(inp.at[other_x], x_seq.at[group], by_x)
    y_block = remote(inp.at[x], x_seq.at[group], by_y)
    w_x = remote(weights.at[y, mine], w_full.at[group, mine], by_x)
    w_y = remote(weights.at[other_y, mine], w_full.at[group, mine], by_y)
    cot_core = remote(cot, cots.at[1], by_core)
    cot_z = remote(cot, cots.at[2], by_z)
    staged = [
        (inp.at[x], x_stage, x_seq.at[group]),
        (weights.at[y], w_stage, w_full.at[group]),
        (vec, vec_stage, vecs.at[group]),
        (seg.at[x], seg_stage, segs.at[group]),
        (cot, cot_stage, cots.at[0]),
    ]
    loads = [pltpu.make_async_copy(here, stage, local.at[i]) for i, (here, stage, there) in enumerate(staged)]
    own = [pltpu.make_async_copy(stage, there, local.at[5 + i]) for i, (here, stage, there) in enumerate(staged)]
    for copy in loads:
        copy.start()
    for i, copy in enumerate(own):
        loads[i].wait()
        copy.start()
    x_block.wait_recv()
    y_more = remote(x_seq.at[slot_x], x_seq.at[slot_x], by_y)
    w_y.wait_recv()
    w_more = remote(w_full.at[slot_y, mine], w_full.at[slot_y, mine], by_x)
    w_y_core = remote(w_full.at[slot_y, shared], w_full.at[slot_y, shared], by_core)
    w_x.wait_recv()
    w_x_core = remote(w_full.at[slot_x, shared], w_full.at[slot_x, shared], by_core)
    cot_z.wait_recv()
    cot_more = remote(cots.at[2], cots.at[3], by_core)
    w_more.wait_recv()
    w_more_core = remote(w_full.at[slot_both, shared], w_full.at[slot_both, shared], by_core)
    for copy in small + [y_block, y_more, cot_core, cot_more, w_y_core, w_x_core, w_more_core]:
        copy.wait_recv()
    for copy in small + [x_block, y_block, y_more, w_x, w_y, w_more, cot_core, cot_z, cot_more, w_y_core, w_x_core, w_more_core]:
        copy.wait_send()
    for copy in own:
        copy.wait()


def first_exchange(inp, weights, vec, seg, cot):
    any_space = pl.BlockSpec(memory_space=pl.ANY)
    shape = jax.ShapeDtypeStruct
    return pl.pallas_call(
        first_exchange_kernel,
        in_specs=[any_space] * 5,
        out_specs=[any_space] * 5,
        out_shape=[
            shape((4,) + inp.shape[1:], inp.dtype),
            shape((4,) + weights.shape[1:], weights.dtype),
            shape((4,) + vec.shape, vec.dtype),
            shape((4,) + seg.shape[1:], seg.dtype),
            shape((4,) + cot.shape, cot.dtype),
        ],
        scratch_shapes=[
            pltpu.SemaphoreType.DMA((18,)),
            pltpu.SemaphoreType.DMA((18,)),
            pltpu.SemaphoreType.DMA((10,)),
            pltpu.VMEM(inp.shape[1:], inp.dtype),
            pltpu.VMEM(weights.shape[1:], weights.dtype),
            pltpu.VMEM(vec.shape, vec.dtype),
            pltpu.VMEM(seg.shape[1:], seg.dtype),
            pltpu.VMEM(cot.shape, cot.dtype),
        ],
        compiler_params=pltpu.CompilerParams(collective_id=0, has_side_effects=True, vmem_limit_bytes=32 * 2**20),
        name="first_exchange",
    )(inp, weights, vec, seg, cot)


def turn_kernel(forth, src, dst, send, recv, local, stage):
    replica = lax.axis_index("replica")
    group = lax.axis_index("group")
    y = lax.div(group, 2)
    x = lax.rem(group, 2)
    by_x, by_y, by_both, by_core, by_z = partners(replica, group)
    others = (by_both, by_x, by_y)
    greet(others)

    def view(device):
        there = device[1]
        there_y = lax.div(there, 2)
        there_x = lax.rem(there, 2)
        if forth:
            return src.at[there], dst.at[x, y]
        return src.at[there_x, there_y], dst.at[group]

    copies = []
    for i, device in enumerate(others):
        a, b = view(device)
        copies.append(pltpu.make_async_remote_copy(src_ref=a, dst_ref=b, send_sem=send.at[i], recv_sem=recv.at[i], device_id=device, device_id_type=MESH))
    a, b = view((replica, group))
    for copy in copies:
        copy.start()
    load = pltpu.make_async_copy(a, stage, local.at[0])
    own = pltpu.make_async_copy(stage, b, local.at[1])
    load.start()
    load.wait()
    own.start()
    for copy in copies:
        copy.wait()
    own.wait()


def turn(entries, forth, collective):
    any_space = pl.BlockSpec(memory_space=pl.ANY)
    tail = entries.shape[-2:]
    lead = (2, 2) if forth else (4,)
    return pl.pallas_call(
        functools.partial(turn_kernel, forth),
        in_specs=[any_space],
        out_specs=any_space,
        out_shape=jax.ShapeDtypeStruct(lead + tail, entries.dtype),
        scratch_shapes=[pltpu.SemaphoreType.DMA((3,)), pltpu.SemaphoreType.DMA((3,)), pltpu.SemaphoreType.DMA((2,)), pltpu.VMEM(tail, entries.dtype)],
        compiler_params=pltpu.CompilerParams(collective_id=collective, has_side_effects=True),
        cost_estimate=pl.CostEstimate(flops=0, bytes_accessed=60 * 2**20, transcendentals=0),
        name="turn_out" if forth else "turn_back",
    )(entries)


def head_columns(shard, half, axis):
    first = [lax.slice_in_dim(shard, 1600 * k + 768 * half, 1600 * k + 768 * half + 832, axis=axis) for k in range(3)]
    pad = [(0, 0)] * shard.ndim
    pad[axis] = (0, 64)
    return jnp.concatenate([jnp.pad(part, pad) for part in first], axis=axis)


def padded(entries):
    return jnp.pad(entries, [(0, 0)] * (entries.ndim - 1) + [(0, 64)])


def joined(first, other):
    lane = lax.broadcasted_iota(jnp.int32, (1, 128), 1)
    middle = jnp.where(lane < 64, first[..., 768:896], other[..., 0:128])
    return jnp.concatenate([first[..., :768], middle, other[..., 128:]], axis=-1)


def hold(entries, *until):
    return lax.optimization_barrier((entries,) + until)[0]


def group_scatter_start(parts, group):
    cuts = [part.shape[1] // 32 * 16 + (16 if part.shape[1] // 16 % 2 else 0) for part in parts]
    block = lambda k: [at(part, group ^ k) for part in parts]
    own, by_x, by_y, by_both = block(0), block(1), block(2), block(3)
    upper = lambda entries: [entry[:cut] for entry, cut in zip(entries, cuts)]
    lower = lambda entries: [entry[cut:] for entry, cut in zip(entries, cuts)]
    got_x = moved(jnp.concatenate(upper(by_x) + upper(by_both)), FLIP_X)
    got_y = moved(jnp.concatenate(lower(by_y) + lower(by_both)), FLIP_Y)
    return (cuts, [part.shape[1] for part in parts]), upper(own), lower(own), upper(by_y), lower(by_x), got_x, got_y


def group_scatter_pass(state, until):
    cuts, own_upper, own_lower, far_upper, far_lower, got_x, got_y = state
    got_x, got_y = hold((got_x, got_y), until)
    size_x = got_x.shape[0] // 2
    size_y = got_y.shape[0] // 2
    upper = wide(jnp.concatenate(own_upper)) + wide(got_x[:size_x])
    lower = wide(jnp.concatenate(own_lower)) + wide(got_y[:size_y])
    pass_y = low(wide(jnp.concatenate(far_upper)) + wide(got_x[size_x:]))
    pass_x = low(wide(jnp.concatenate(far_lower)) + wide(got_y[size_y:]))
    return cuts, upper, lower, moved(pass_y, FLIP_Y), moved(pass_x, FLIP_X)


def group_scatter_end(state, until):
    (cuts, sizes), upper, lower, got_y, got_x = state
    got_y, got_x = hold((got_y, got_x), until)
    upper = low(upper + wide(got_y))
    lower = low(lower + wide(got_x))
    shares = []
    top = bottom = 0
    for cut, size in zip(cuts, sizes):
        shares.append((upper[top : top + cut], lower[bottom : bottom + size - cut]))
        top += cut
        bottom += size - cut
    return shares


def sum_kernel(grad, out_share, gn, vec, shares, total, tokens, vec_total, quads, vec_got, vec_own, vec_core, vec_z, c_buf, x_buf, y_buf, line_buf, line_mid, part, inner, gn_y, send, recv, local):
    replica = lax.axis_index("replica")
    group = lax.axis_index("group")
    core = lax.rem(replica, 2)
    quad = lax.rem(replica, 4)
    quad_z = lax.rem(quad + 2, 4)
    z = lax.div(replica, 2)
    y = lax.div(group, 2)
    x = lax.rem(group, 2)
    by_x, by_y, by_both, by_core, by_z = partners(replica, group)
    outer = (z == 0) | (z == 3)
    by_line = (jnp.where(z == 0, replica + 2, jnp.where(z == 3, replica - 2, jnp.where(z == 1, replica - 2, replica + 2))), group)
    by_middle = (jnp.where(z == 1, replica + 2, replica - 2), group)
    lines_z = [(lax.rem(replica + 2 * k, 8), group) for k in (1, 2, 3)]
    greet([by_x, by_y, by_both, by_core] + lines_z)
    count = [0]
    locals_ = [0]

    def remote(src, dst, device):
        i = count[0]
        count[0] = i + 1
        return pltpu.make_async_remote_copy(src_ref=src, dst_ref=dst, send_sem=send.at[i], recv_sem=recv.at[i], device_id=device, device_id_type=MESH)

    def here(src, dst):
        i = locals_[0]
        locals_[0] = i + 1
        copy = pltpu.make_async_copy(src, dst, local.at[i])
        copy.start()
        return copy

    mine = pl.multiple_of(192 * core, 16)
    theirs = pl.multiple_of(192 * (1 - core), 16)
    other_x = 1 - x
    other_y = 1 - y
    sends = []
    kept = []

    def go(copy):
        copy.start()
        sends.append(copy)
        return copy

    def add(a, b):
        return (a.astype(jnp.float32) + b.astype(jnp.float32)).astype(jnp.bfloat16)

    c_copies = []
    loads = []
    for k in range(3):
        lanes = pl.ds(896 * k, 896)
        c_copies.append([go(remote(grad.at[r, pl.ds(theirs, 208), lanes], c_buf.at[k, r], by_core)) for r in range(4)])
        loads.append(here(grad.at[:, pl.ds(mine, 208), lanes], part.at[k]))
    vec_group = [go(remote(vec.at[device[1]], vec_got.at[group], device)) for device in (by_x, by_y, by_both)]
    share_load = here(out_share, total.at[3, pl.ds(mine, 208)])
    pieces = [(k, pl.ds(208 * m, 208 - 16 * m)) for k in range(2) for m in range(2)]
    quad_copies = []
    for k, rows in pieces:
        kept.append(here(shares.at[k, rows], quads.at[k, quad, rows]))
        over = go(remote(shares.at[k, rows], quads.at[k, quad, rows], by_z))
        quad_copies.append((over, go(remote(shares.at[k, rows], quads.at[k, quad, rows], by_core))))
    far = 2 * other_y
    near = 2 * y
    gn_pass = go(remote(gn.at[far + other_x], gn_y.at[0], by_y))
    gn_keep = go(remote(gn.at[far + x], gn_y.at[1], by_y))
    x_copies = []
    for k in range(3):
        loads[k].wait()
        for r in range(4):
            c_copies[k][r].wait_recv()
        for r in range(4):
            part[k, r] = add(part[k, r], c_buf[k, r])
        x_copies.append([go(remote(part.at[k, 2 * row + other_x], x_buf.at[k, row], by_x)) for row in range(2)])

    def line(k, rows, merge):
        i = count[0]
        count[0] = i + 3
        into = pltpu.make_async_remote_copy(src_ref=total.at[k, rows], dst_ref=line_buf.at[k, merge], send_sem=send.at[i], recv_sem=recv.at[i], device_id=by_line, device_id_type=MESH)
        middle = pltpu.make_async_remote_copy(src_ref=inner.at[k, merge], dst_ref=line_mid.at[k, merge], send_sem=send.at[i + 1], recv_sem=recv.at[i + 1], device_id=by_middle, device_id_type=MESH)
        back = pltpu.make_async_remote_copy(src_ref=total.at[k, rows], dst_ref=line_buf.at[k, merge], send_sem=send.at[i + 2], recv_sem=recv.at[i + 2], device_id=by_line, device_id_type=MESH)

        @pl.when(outer)
        def _():
            into.start()

        return rows, merge, into, middle, back

    def line_second(k):
        for rows, merge, into, middle, back in lines[k]:
            @pl.when(jnp.logical_not(outer))
            def _():
                into.wait_recv()
                inner[k, merge] = add(total[k, rows], line_buf[k, merge])
                middle.start()

    def line_third(k):
        for rows, merge, into, middle, back in lines[k]:
            @pl.when(jnp.logical_not(outer))
            def _():
                middle.wait_recv()
                total[k, rows] = add(inner[k, merge], line_mid[k, merge])
                back.start()

    def line_fourth(k):
        for rows, merge, into, middle, back in lines[k]:
            @pl.when(outer)
            def _():
                into.wait_send()
                back.wait_recv()
                total[k, rows] = line_buf[k, merge]

            @pl.when(jnp.logical_not(outer))
            def _():
                middle.wait_send()
                back.wait_send()

    def quad_pass(i):
        k, rows = pieces[i]
        quad_copies[i][0].wait_recv()
        return go(remote(quads.at[k, quad_z, rows], quads.at[k, quad_z, rows], by_core))

    lane = lax.broadcasted_iota(jnp.int32, (1, 128), 1)
    share_load.wait()
    halves = [(pl.ds(mine + 112 * m, 112 - 16 * m), pl.ds(112 * m, 112 - 16 * m)) for m in range(2)]
    lines = {}
    lines[3] = [line(3, rows, merge) for rows, merge in halves]
    gn_pass.wait_recv()
    gn_y[0] = add(gn_y[0], gn[near + other_x])
    gn_cross = remote(gn_y.at[0], tokens.at[x], by_x)
    y_copies = []
    for k in range(3):
        for row in range(2):
            x_copies[k][row].wait_recv()
        for row in range(2):
            part[k, 2 * row + x] = add(part[k, 2 * row + x], x_buf[k, row])
        y_copies.append(go(remote(part.at[k, 2 * other_y + x], y_buf.at[k], by_y)))
        if k == 0:
            for copy in vec_group:
                copy.wait_recv()
            vec_got[group] = vec[group]
            vec_own[...] = (vec_got[0] + vec_got[1]) + (vec_got[2] + vec_got[3])
            vec_pass = go(remote(vec_own, vec_core, by_core))
            line_second(3)
        if k == 1:
            vec_pass.wait_recv()
            vec_z[z] = vec_own[...] + vec_core[...]
            vec_line = [go(remote(vec_z.at[z], vec_z.at[z], device)) for device in lines_z]
        if k == 2:
            go(gn_cross)
        if k > 0:
            arrive(y_copies, part, y_buf, total, lane, k - 1, near + x, y, mine)
            lines[k - 1] = [line(k - 1, rows, merge) for rows, merge in halves]
            if k == 1:
                line_third(3)
            else:
                line_second(0)
    gn_keep.wait_recv()
    tokens[x] = add(gn_y[1], gn[near + x])
    arrive(y_copies, part, y_buf, total, lane, 2, near + x, y, mine)
    lines[2] = [line(2, rows, merge) for rows, merge in halves]
    passes = [quad_pass(0), quad_pass(1)]
    line_second(1)
    line_second(2)
    passes += [quad_pass(2), quad_pass(3)]
    line_third(0)
    line_third(1)
    line_third(2)
    for copy in vec_line:
        copy.wait_recv()
    vec_total[...] = (vec_z[0] + vec_z[1]) + (vec_z[2] + vec_z[3])
    last = []
    for k in (3, 0, 1, 2):
        line_fourth(k)
        rows = pl.ds(pl.multiple_of(208 * core, 16), 192)
        last.append(go(remote(total.at[k, rows], total.at[k, rows], by_core)))
    for copy in last + passes + [copies[1] for copies in quad_copies]:
        copy.wait_recv()
    gn_cross.wait_recv()
    for copy in kept:
        copy.wait()
    for copy in sends:
        copy.wait_send()


def arrive(y_copies, part, y_buf, full, lane, k, index, y, mine):
    y_copies[k].wait_recv()
    here = part[k, index]
    there = y_buf[k]
    first = jnp.where(y == 0, here, there)
    other = jnp.where(y == 0, there, here)
    rows = pl.ds(mine, 208)
    full[k, rows, 0:768] = first[:, 0:768]
    full[k, rows, 768:896] = jnp.where(lane < 64, first[:, 768:896], other[:, 0:128])
    full[k, rows, 896:1664] = other[:, 128:896]


def sum_grads(grad, out_share, gn, vec, shares):
    any_space = pl.BlockSpec(memory_space=pl.ANY)
    vmem = pl.BlockSpec(memory_space=pltpu.VMEM)
    shape = jax.ShapeDtypeStruct
    kind = jnp.bfloat16
    buf = lambda *dims: pltpu.VMEM(dims, kind)
    return pl.pallas_call(
        sum_kernel,
        in_specs=[any_space, any_space, vmem, vmem, vmem],
        out_specs=[vmem, vmem, vmem, any_space],
        out_shape=[
            shape((4, 400, 1664), kind),
            shape((2,) + gn.shape[1:], kind),
            shape(vec.shape[1:], vec.dtype),
            shape((2, 4) + shares.shape[1:], kind),
        ],
        scratch_shapes=[
            pltpu.VMEM(vec.shape, vec.dtype),
            pltpu.VMEM(vec.shape[1:], vec.dtype),
            pltpu.VMEM(vec.shape[1:], vec.dtype),
            pltpu.VMEM(vec.shape, vec.dtype),
            buf(3, 4, 208, 896),
            buf(3, 2, 208, 896),
            buf(3, 208, 896),
            buf(4, 208, 1664),
            buf(4, 208, 1664),
            buf(3, 4, 208, 896),
            buf(4, 208, 1664),
            buf(2, 256, gn.shape[2]),
            pltpu.SemaphoreType.DMA((88,)),
            pltpu.SemaphoreType.DMA((88,)),
            pltpu.SemaphoreType.DMA((8,)),
        ],
        compiler_params=pltpu.CompilerParams(collective_id=3, has_side_effects=True, vmem_limit_bytes=58 * 2**20),
        name="sum_grads",
    )(grad, out_share, gn, vec, shares)


def finish_feed_kernel(quads_ref, out_reduce, out_expand):
    for k in range(4):
        out_reduce[k] = quads_ref[0, k].astype(jnp.float32)
    for k in range(4):
        piece = quads_ref[1, k].astype(jnp.float32)
        for r in range(4):
            out_expand[:, 1600 * r + 400 * k : 1600 * r + 400 * k + 400] = piece[:, 400 * r : 400 * r + 400]


def finish_feed(quads):
    rows, width = quads.shape[2:]
    step = 80
    out = pl.pallas_call(
        finish_feed_kernel,
        grid=(rows // step,),
        in_specs=[pl.BlockSpec((2, 4, step, width), lambda i: (0, 0, i, 0))],
        out_specs=[pl.BlockSpec((4, step, width), lambda i: (0, i, 0)), pl.BlockSpec((step, 4 * width), lambda i: (i, 0))],
        out_shape=[jax.ShapeDtypeStruct((4, rows, width), jnp.float32), jax.ShapeDtypeStruct((rows, 4 * width), jnp.float32)],
        compiler_params=pltpu.CompilerParams(vmem_limit_bytes=48 * 2**20),
        name="finish_feed",
    )(quads)
    return out[0].reshape(4 * rows, width), out[1]


def finish_mixer_kernel(total_ref, in_ref, out_ref):
    for k in range(3):
        in_ref[:, 1600 * k : 1600 * k + 1600] = total_ref[k, :, :1600].astype(jnp.float32)
    out_ref[...] = total_ref[3, :, :1600].astype(jnp.float32)


def finish_mixer(total):
    rows = total.shape[1]
    step = 80
    return pl.pallas_call(
        finish_mixer_kernel,
        grid=(rows // step,),
        in_specs=[pl.BlockSpec((4, step, total.shape[2]), lambda i: (0, i, 0))],
        out_specs=[pl.BlockSpec((step, 4800), lambda i: (i, 0)), pl.BlockSpec((step, 1600), lambda i: (i, 0))],
        out_shape=[jax.ShapeDtypeStruct((rows, 4800), jnp.float32), jax.ShapeDtypeStruct((rows, 1600), jnp.float32)],
        compiler_params=pltpu.CompilerParams(vmem_limit_bytes=48 * 2**20),
        name="finish_mixer",
    )(total)


def on_device(
    inputs,
    segments,
    cotangent,
    project_in,
    project_out,
    expand_weight,
    reduce_weight,
    query_bias,
    value_bias,
    project_bias,
    expand_bias,
    reduce_bias,
    first_gain,
    first_shift,
    second_gain,
    second_shift,
):
    replica, group, z, core, y, x = place()
    quad = lax.rem(replica, 4)
    width = 1600
    rows = 512

    vec = jnp.concatenate(
        [
            jnp.stack([query_bias, value_bias, project_bias, reduce_bias, first_gain, first_shift, second_gain, second_shift]),
            expand_bias.reshape(4, 400),
            jnp.zeros((4, 400), jnp.bfloat16),
        ]
    )
    halves = jnp.stack([head_columns(project_in, 0, 1), head_columns(project_in, 1, 1)])
    x_seq, w_half, vecs, segs, cots = first_exchange(
        inputs, halves, vec, segments[:, None, :], cotangent.reshape(rows, width)
    )
    vecs = wide(vecs)
    names = [vecs[:, k].reshape(width) for k in range(8)]
    bias_query, bias_value, bias_project, bias_reduce, gain_first, shift_first, gain_second, shift_second = names
    bias_expand = lax.dynamic_index_in_dim(vecs, 8 + quad, 1, False).reshape(width)
    segs = segs.reshape(1024)

    x_seq, out_shard, reduce_shard, expand_shard = lax.optimization_barrier(
        (x_seq, project_out, reduce_weight, expand_weight)
    )
    quarter_reduce = lax.dynamic_slice_in_dim(reduce_shard, 400 * quad, 400, 0)
    quarter_expand = jnp.concatenate(
        [lax.dynamic_slice_in_dim(expand_shard, 1600 * k + 400 * quad, 400, 1) for k in range(4)], axis=1
    )
    full_out = lax.all_gather(out_shard, "group", axis=0, tiled=True)
    expand_part = lax.all_gather(quarter_expand, "group", axis=0, tiled=True)
    reduce_part = lax.all_gather(quarter_reduce, "group", axis=0, tiled=True)

    flat_seq = wide(x_seq.reshape(1024, width))
    normed = low(layer_norm(flat_seq, gain_first, shift_first))
    w_half = w_half.reshape(width, 2688)
    pad64 = jnp.zeros((64,), jnp.float32)
    bias_q = lax.dynamic_slice_in_dim(bias_query, 768 * y, 832, 0)
    bias_v = lax.dynamic_slice_in_dim(bias_value, 768 * y, 832, 0)
    bias_mix = jnp.concatenate([bias_q, pad64, jnp.zeros((896,), jnp.float32), bias_v, pad64])
    mixture = low(product(normed, w_half) + bias_mix)
    segc = segs[:, None]
    segr = segs[None]
    attended, lse = heads(mixture, segc, segr)
    att_tokens = turn(attended.reshape(4, 256, 896), True, 1)
    att_tokens = joined(att_tokens[:, 0].reshape(rows, 896), att_tokens[:, 1].reshape(rows, 896))[:, :width]

    flat_input = wide(inputs.reshape(rows, width))
    middle = flat_input + product(att_tokens, full_out) + bias_project
    center = middle - jnp.mean(middle, axis=-1, keepdims=True)
    scale = lax.rsqrt(jnp.mean(center * center, axis=-1, keepdims=True) + epsilon)
    unit = center * scale
    second = padded(low(unit * gain_second + shift_second))

    second_core = moved(second, FLIP_CORE)
    second_z = moved(second, FLIP_Z)
    second_both = moved(second_z, FLIP_CORE)
    near = feed(second, second_core, cots, expand_part, reduce_part, bias_expand[None], None)
    far = feed(second_z, second_both, cots, expand_part, reduce_part, bias_expand[None], near[:3])
    activated, grad_expanded, second_all = far[:3]
    cot_all = cots.reshape(4 * rows, width)
    part_far = far[3].reshape(2, rows, 1664)
    part_near = near[3].reshape(2, rows, 1664)
    passed = low(wide(part_far[0]) + wide(moved(part_far[1], FLIP_CORE)))
    own_part = wide(part_near[0]) + wide(moved(part_near[1], FLIP_CORE))
    over_part = moved(passed, FLIP_Z)
    reduce_grad = low(weight_term(activated, cot_all)).reshape(4, 400, width)
    scatter_reduce = group_scatter_start([reduce_grad], group)
    expand_grad = low(weight_term(second_all, hold(grad_expanded, reduce_grad))).reshape(4, 400, width)
    scatter_reduce = group_scatter_pass(scatter_reduce, expand_grad)
    result_part = rows_times(hold(activated, expand_grad), reduce_part, "out_rows").reshape(4, rows, 1664)
    result_core = moved(jnp.stack([result_part[1], result_part[3]]), FLIP_CORE)
    grad_second = (own_part + wide(hold(over_part, result_part)))[:, :width]

    q = grad_second * gain_second
    grad_middle = wide(cotangent.reshape(rows, width)) + scale * (
        q - jnp.mean(q, axis=-1, keepdims=True) - unit * jnp.mean(q * unit, axis=-1, keepdims=True)
    )
    second_gain_grad = jnp.sum(grad_second * unit, axis=0)
    second_shift_grad = jnp.sum(grad_second, axis=0)
    grad_middle_low = low(grad_middle)
    result_own = wide(result_part[0]) + wide(result_core[0])
    result_over = moved(low(wide(result_part[2]) + wide(result_core[1])), FLIP_Z)
    share_reduce, = group_scatter_end(scatter_reduce, grad_middle_low)
    pair_lower = moved(share_reduce[1], FLIP_PAIR)
    out_grad = low(weight_term(att_tokens, grad_middle_low)).reshape(4, 400, width)
    out_mine = lax.dynamic_slice_in_dim(out_grad, 192 * core, 208, 1)
    out_given = lax.dynamic_slice_in_dim(out_grad, 192 * (1 - core), 208, 1)
    out_core = low(wide(out_mine) + wide(moved(out_given, FLIP_CORE)))
    scatter_expand = group_scatter_start([expand_grad, out_core], group)
    grad_att = padded(low(product_back(grad_middle_low, full_out))).reshape(2, 256, 1664)
    lane = lax.broadcasted_iota(jnp.int32, (896,), 0)
    grad_att = jnp.stack(
        [jnp.where(lane < 832, grad_att[..., :896], 0), jnp.where(lane >= 64, grad_att[..., 768:], 0)], axis=1
    )
    outputs = low((result_own + wide(hold(result_over, grad_att)))[:, :width] + middle + bias_reduce).reshape(2, 256, width)
    grad_heads = turn(grad_att, False, 2).reshape(1024, 896)
    scatter_expand = group_scatter_pass(scatter_expand, grad_heads)
    dq, dk, dv, pair_upper = heads_back(mixture, grad_heads, attended, lse, segc, segr, share_reduce[0])
    sum_reduce_upper = low(wide(share_reduce[0]) + wide(pair_upper))
    sum_reduce_lower = low(wide(share_reduce[1]) + wide(hold(pair_lower, dq)))
    share_expand, share_out = group_scatter_end(scatter_expand, dq)
    pair_upper = moved(share_expand[0], FLIP_PAIR)
    pair_lower = moved(share_expand[1], FLIP_PAIR)
    grad_mix = jnp.concatenate([dq, dk, dv], axis=1)
    grad_normed = product_back(hold(grad_mix, sum_reduce_lower), w_half)
    sum_expand_upper = low(wide(share_expand[0]) + wide(hold(pair_upper, grad_normed)))
    out_share = padded(jnp.concatenate(share_out))
    flat_center = flat_seq - jnp.mean(flat_seq, axis=-1, keepdims=True)
    flat_unit = flat_center * lax.rsqrt(jnp.mean(flat_center * flat_center, axis=-1, keepdims=True) + epsilon)
    first_gain_grad = jnp.sum(grad_normed * flat_unit, axis=0)
    first_shift_grad = jnp.sum(grad_normed, axis=0)
    in_grad = low(weight_term(normed, grad_mix)).reshape(4, 400, 2688)
    def spread(columns):
        lower = jnp.concatenate([columns[:832], jnp.zeros((768,), jnp.float32)])
        upper = jnp.concatenate([jnp.zeros((832,), jnp.float32), columns[64:832]])
        return jnp.where(y == 0, lower, upper)

    expand_bias_part = jnp.sum(near[4] + far[4], axis=0).reshape(4, 400)
    expand_bias_wide = lax.dynamic_update_slice_in_dim(jnp.zeros((4, width), jnp.float32), expand_bias_part, 400 * quad, 1)
    vectors = jnp.concatenate(
        [
            spread(column_sum(dq)).reshape(4, 400),
            spread(column_sum(dv)).reshape(4, 400),
            column_sum(grad_middle_low).reshape(4, 400),
            column_sum(cotangent.reshape(rows, width)).reshape(4, 400),
            first_gain_grad.reshape(4, 400),
            first_shift_grad.reshape(4, 400),
            second_gain_grad.reshape(4, 400),
            second_shift_grad.reshape(4, 400),
            expand_bias_wide,
        ],
        axis=1,
    )
    vectors = jnp.pad(vectors, ((0, 0), (0, 320))).reshape(4, 40, 128)
    sum_expand_lower = low(wide(share_expand[1]) + wide(hold(pair_lower, in_grad)))
    shares = jnp.concatenate([sum_reduce_upper, sum_reduce_lower, sum_expand_upper, sum_expand_lower]).reshape(2, 400, width)
    grad_total, grad_tokens, vec_total, quads = sum_grads(in_grad, out_share, padded(low(grad_normed)).reshape(4, 256, 1664), vectors, shares)
    vec_total = vec_total.reshape(5120)
    pieces = [vec_total[400 * k : 400 * k + 400] for k in range(8)]
    total_reduce, total_expand = finish_feed(quads)
    total_in, total_out = finish_mixer(grad_total)
    grad_tokens = wide(grad_tokens[..., :width]).reshape(rows, width)
    center1 = flat_input - jnp.mean(flat_input, axis=-1, keepdims=True)
    scale1 = lax.rsqrt(jnp.mean(center1 * center1, axis=-1, keepdims=True) + epsilon)
    unit1 = center1 * scale1
    q1 = grad_tokens * gain_first
    input_grad = grad_middle + scale1 * (
        q1 - jnp.mean(q1, axis=-1, keepdims=True) - unit1 * jnp.mean(q1 * unit1, axis=-1, keepdims=True)
    )
    return (
        outputs,
        input_grad.reshape(2, 256, width),
        total_in,
        total_out,
        total_expand,
        total_reduce,
        pieces[0],
        pieces[1],
        pieces[2],
        vec_total[3200:4800],
        pieces[3],
        pieces[4],
        pieces[5],
        pieces[6],
        pieces[7],
    )


def solution(mesh):
    placed = (
        P("replica", "group", None),
        P("replica", "group"),
        P("replica", "group", None),
        P("group", None),
        P("group", None),
        P("group", None),
        P("group", None),
        P("group"),
        P("group"),
        P("group"),
        P("group"),
        P("group"),
        P("group"),
        P("group"),
        P("group"),
        P("group"),
    )
    return jax.shard_map(
        on_device if dict(mesh.shape) == {"replica": 8, "group": 4} else on_device_any,
        mesh=mesh,
        in_specs=placed,
        out_specs=(
            P("replica", "group", None),
            P("replica", "group", None),
            P("group", None),
            P("group", None),
            P("group", None),
            P("group", None),
            P("group"),
            P("group"),
            P("group"),
            P("group"),
            P("group"),
            P("group"),
            P("group"),
            P("group"),
            P("group"),
        ),
        check_vma=False,
    )
```

```python
import functools
import math

import jax
import jax.numpy as jnp
from jax import lax
from jax.sharding import PartitionSpec as P

from jax.experimental import pallas as pl
from jax.experimental.pallas import tpu as pltpu

HEADS = 25
HEAD_DIM = 64


epsilon = 1e-05
very_low = -1e30


def carried_in(part, axis, combine, identity):
    place = lax.axis_index(axis)
    gathered = lax.all_gather(part, axis)
    state = jnp.zeros_like(part) + jnp.asarray(identity, part.dtype)

    def one(hop, state):
        return combine(state, lax.dynamic_index_in_dim(gathered, hop, 0, False))

    return lax.fori_loop(0, place, one, state)


def layer_norm(entries, gain, shift):
    center = entries - jnp.mean(entries, axis=-1, keepdims=True)
    spread = jnp.mean(center * center, axis=-1, keepdims=True)
    return center * lax.rsqrt(spread + epsilon) * gain + shift


def product(left, right):
    return jnp.dot(left, right, preferred_element_type=jnp.float32)


def product_back(left, right):
    return lax.dot_general(
        left, right, (((1,), (1,)), ((), ())), preferred_element_type=jnp.float32
    )


def weight_term(left, right):
    return lax.dot_general(
        left, right, (((0,), (0,)), ((), ())), preferred_element_type=jnp.float32
    )


def column_sum(entries):
    return jnp.sum(entries.astype(jnp.float32), axis=0)


def block_scores(queries, key_block, offset, query_pos, doc_start):
    block_count = key_block.shape[0]
    key_count = key_block.shape[2]
    scaling = 1.0 / math.sqrt(HEAD_DIM)
    scores = (
        jnp.einsum("schd,pskhd->shcpk", queries, key_block, preferred_element_type=jnp.float32)
        * scaling
    )
    key_pos = (offset + jnp.arange(block_count, dtype=jnp.int32))[:, None] * key_count + jnp.arange(
        key_count, dtype=jnp.int32
    )[None, :]
    allowed = (key_pos[None, None] <= query_pos[None, :, None, None]) & (
        key_pos[None, None] >= doc_start[:, :, None, None]
    )
    allowed = allowed[:, None]
    return (jnp.where(allowed, scores, very_low), allowed)


def attend(running, key_block, value_block, offset, queries, query_pos, doc_start):
    largest, denominator, summed = running
    masked, allowed = block_scores(queries, key_block, offset, query_pos, doc_start)
    fresh = jnp.maximum(largest, jnp.max(masked, axis=(3, 4)))
    shares = jnp.where(allowed, jnp.exp(masked - fresh[..., None, None]), 0.0)
    rescale = jnp.exp(largest - fresh)
    denominator = denominator * rescale + jnp.sum(shares, axis=(3, 4))
    added = jnp.einsum(
        "shcpk,pskhd->schd",
        shares.astype(jnp.bfloat16),
        value_block,
        preferred_element_type=jnp.float32,
    )
    summed = summed * jnp.transpose(rescale, (0, 2, 1))[..., None] + added
    return (fresh, denominator, summed)


def attend_back(
    grad_query,
    key_block,
    value_block,
    offset,
    queries,
    query_pos,
    doc_start,
    log_total,
    grad_low,
    row_dot,
):
    masked, allowed = block_scores(queries, key_block, offset, query_pos, doc_start)
    shares = jnp.where(allowed, jnp.exp(masked - log_total[..., None, None]), 0.0)
    grad_value = jnp.einsum(
        "shcpk,schd->pskhd",
        shares.astype(jnp.bfloat16),
        grad_low,
        preferred_element_type=jnp.float32,
    )
    grad_share = jnp.einsum(
        "schd,pskhd->shcpk", grad_low, value_block, preferred_element_type=jnp.float32
    )
    grad_score = (shares * (grad_share - row_dot[..., None, None])).astype(jnp.bfloat16)
    grad_query = grad_query + jnp.einsum(
        "shcpk,pskhd->schd", grad_score, key_block, preferred_element_type=jnp.float32
    )
    grad_key = jnp.einsum(
        "shcpk,schd->pskhd", grad_score, queries, preferred_element_type=jnp.float32
    )
    return (grad_query, (grad_key, grad_value))


def on_device_any(
    inputs,
    segments,
    cotangent,
    project_in,
    project_out,
    expand_weight,
    reduce_weight,
    query_bias,
    value_bias,
    project_bias,
    expand_bias,
    reduce_bias,
    first_gain,
    first_shift,
    second_gain,
    second_shift,
):
    seq_here, local_len, width = inputs.shape
    groups = lax.axis_size("group")
    total_rows = seq_here * local_len
    head_shape = (seq_here, local_len, HEADS, HEAD_DIM)
    shards = (
        project_in,
        project_out,
        expand_weight,
        reduce_weight,
        query_bias,
        value_bias,
        project_bias,
        expand_bias,
        reduce_bias,
        first_gain,
        first_shift,
        second_gain,
        second_shift,
    )
    whole = (
        lax.all_gather(shards[0], "group", axis=0, tiled=True),
        lax.all_gather(shards[1], "group", axis=0, tiled=True),
        lax.all_gather(shards[2], "group", axis=0, tiled=True),
        lax.all_gather(shards[3], "group", axis=0, tiled=True),
        lax.all_gather(shards[4], "group", axis=0, tiled=True),
        lax.all_gather(shards[5], "group", axis=0, tiled=True),
        lax.all_gather(shards[6], "group", axis=0, tiled=True),
        lax.all_gather(shards[7], "group", axis=0, tiled=True),
        lax.all_gather(shards[8], "group", axis=0, tiled=True),
        lax.all_gather(shards[9], "group", axis=0, tiled=True),
        lax.all_gather(shards[10], "group", axis=0, tiled=True),
        lax.all_gather(shards[11], "group", axis=0, tiled=True),
        lax.all_gather(shards[12], "group", axis=0, tiled=True),
    )
    (
        full_in,
        full_out,
        full_expand,
        full_reduce,
        bias_query,
        bias_value,
        bias_project,
        bias_expand,
        bias_reduce,
        gain_first,
        shift_first,
        gain_second,
        shift_second,
    ) = whole
    group_rank = lax.axis_index("group")
    query_pos = group_rank * local_len + jnp.arange(local_len, dtype=jnp.int32)
    positions = jnp.broadcast_to(query_pos[None, :], (seq_here, local_len))
    end_marks = jnp.where(segments == positions, positions + 1, 0)
    before = carried_in(
        jnp.max(end_marks, axis=1), "group", jnp.maximum, jnp.zeros((seq_here,), jnp.int32)
    )
    inside = lax.cummax(end_marks, axis=1)
    inside = jnp.concatenate([jnp.zeros((seq_here, 1), jnp.int32), inside[:, :-1]], axis=1)
    doc_start = jnp.maximum(before[:, None], inside)
    flat_input = inputs.reshape(total_rows, width).astype(jnp.float32)
    normed_low = layer_norm(
        flat_input, gain_first.astype(jnp.float32), shift_first.astype(jnp.float32)
    ).astype(jnp.bfloat16)
    mixture = product(normed_low, full_in)
    queries = (
        (mixture[:, :width] + bias_query.astype(jnp.float32))
        .astype(jnp.bfloat16)
        .reshape(head_shape)
    )
    key_rows = (
        mixture[:, width : 2 * width].astype(jnp.bfloat16).reshape(seq_here, local_len, width)
    )
    value_rows = (
        (mixture[:, 2 * width :] + bias_value.astype(jnp.float32))
        .astype(jnp.bfloat16)
        .reshape(seq_here, local_len, width)
    )
    initial = (
        jnp.full((seq_here, HEADS, local_len), very_low, jnp.float32),
        jnp.zeros((seq_here, HEADS, local_len), jnp.float32),
        jnp.zeros(head_shape, jnp.float32),
    )
    block_ids = jnp.arange(groups, dtype=jnp.int32)
    running = initial
    pieces = (
        lax.all_gather(key_rows[None], "group", axis=0, tiled=True),
        lax.all_gather(value_rows[None], "group", axis=0, tiled=True),
    )
    piece_count = pieces[0].shape[0]

    def one_piece(state, members):
        key_piece, value_piece, index = members
        updated = attend(
            state,
            key_piece.reshape((1,) + head_shape),
            value_piece.reshape((1,) + head_shape),
            index,
            queries,
            query_pos,
            doc_start,
        )
        return (updated, None)

    running, unused_steps = lax.scan(
        one_piece, running, (pieces[0], pieces[1], jnp.arange(piece_count, dtype=jnp.int32))
    )
    largest, denominator, summed = running
    attended = summed / jnp.transpose(denominator, (0, 2, 1))[..., None]
    log_total = largest + jnp.log(denominator)
    attended_low = attended.reshape(total_rows, width).astype(jnp.bfloat16)
    middle = flat_input + product(attended_low, full_out) + bias_project.astype(jnp.float32)
    second_low = layer_norm(
        middle, gain_second.astype(jnp.float32), shift_second.astype(jnp.float32)
    ).astype(jnp.bfloat16)
    expanded = product(second_low, full_expand) + bias_expand.astype(jnp.float32)
    activated_low = jax.nn.gelu(expanded, approximate=True).astype(jnp.bfloat16)
    result = middle + product(activated_low, full_reduce) + bias_reduce.astype(jnp.float32)
    outputs = result.astype(jnp.bfloat16).reshape(seq_here, local_len, width)
    whole_back = (
        lax.all_gather(shards[0], "group", axis=0, tiled=True),
        lax.all_gather(shards[1], "group", axis=0, tiled=True),
        lax.all_gather(shards[2], "group", axis=0, tiled=True),
        lax.all_gather(shards[3], "group", axis=0, tiled=True),
        lax.all_gather(shards[4], "group", axis=0, tiled=True),
        lax.all_gather(shards[5], "group", axis=0, tiled=True),
        lax.all_gather(shards[6], "group", axis=0, tiled=True),
        lax.all_gather(shards[7], "group", axis=0, tiled=True),
        lax.all_gather(shards[8], "group", axis=0, tiled=True),
        lax.all_gather(shards[9], "group", axis=0, tiled=True),
        lax.all_gather(shards[10], "group", axis=0, tiled=True),
        lax.all_gather(shards[11], "group", axis=0, tiled=True),
        lax.all_gather(shards[12], "group", axis=0, tiled=True),
    )
    keys_back = (
        lax.all_gather(key_rows[None], "group", axis=0, tiled=True),
        lax.all_gather(value_rows[None], "group", axis=0, tiled=True),
    )
    (
        back_in,
        back_out,
        back_expand,
        back_reduce,
        unused_query,
        unused_value,
        unused_project,
        unused_expand,
        unused_reduce,
        back_gain_first,
        back_shift_first,
        back_gain_second,
        back_shift_second,
    ) = whole_back
    grad_rows = cotangent.reshape(total_rows, width).astype(jnp.float32)
    grad_result_low = cotangent.reshape(total_rows, width)
    reduce_bias_grad = column_sum(grad_result_low)
    grad_activated = product_back(grad_result_low, back_reduce)
    unused_gelu, gelu_back = jax.vjp(lambda entry: jax.nn.gelu(entry, approximate=True), expanded)
    grad_expanded_low = gelu_back(grad_activated)[0].astype(jnp.bfloat16)
    expand_bias_grad = column_sum(grad_expanded_low)
    grad_second = product_back(grad_expanded_low, back_expand)
    unused_second, second_back = jax.vjp(
        layer_norm,
        middle,
        back_gain_second.astype(jnp.float32),
        back_shift_second.astype(jnp.float32),
    )
    grad_middle, second_gain_grad, second_shift_grad = second_back(grad_second)
    grad_middle = grad_middle + grad_rows
    reduce_weight_grad = weight_term(activated_low, grad_result_low)
    expand_weight_grad = weight_term(second_low, grad_expanded_low)
    feed_parts = (
        lax.psum_scatter(
            expand_weight_grad.astype(jnp.bfloat16), "group", scatter_dimension=0, tiled=True
        ).astype(jnp.float32),
        lax.psum_scatter(
            reduce_weight_grad.astype(jnp.bfloat16), "group", scatter_dimension=0, tiled=True
        ).astype(jnp.float32),
        lax.psum_scatter(
            expand_bias_grad.astype(jnp.bfloat16), "group", scatter_dimension=0, tiled=True
        ).astype(jnp.float32),
        lax.psum_scatter(
            reduce_bias_grad.astype(jnp.bfloat16), "group", scatter_dimension=0, tiled=True
        ).astype(jnp.float32),
        lax.psum_scatter(
            second_gain_grad.astype(jnp.bfloat16), "group", scatter_dimension=0, tiled=True
        ).astype(jnp.float32),
        lax.psum_scatter(
            second_shift_grad.astype(jnp.bfloat16), "group", scatter_dimension=0, tiled=True
        ).astype(jnp.float32),
    )
    grad_middle_low = grad_middle.astype(jnp.bfloat16)
    project_bias_grad = column_sum(grad_middle_low)
    grad_attended_low = (
        product_back(grad_middle_low, back_out).astype(jnp.bfloat16).reshape(head_shape)
    )
    row_dot = jnp.einsum("schd,schd->shc", grad_attended_low.astype(jnp.float32), attended)

    def back_step(grad_query, members):
        key_piece, value_piece, offset = members
        return attend_back(
            grad_query,
            key_piece.reshape((1,) + head_shape),
            value_piece.reshape((1,) + head_shape),
            offset,
            queries,
            query_pos,
            doc_start,
            log_total,
            grad_attended_low,
            row_dot,
        )

    grad_query, terms = lax.scan(
        back_step, jnp.zeros(head_shape, jnp.float32), (keys_back[0], keys_back[1], block_ids)
    )
    key_terms = terms[0].reshape(groups, seq_here, local_len, width)
    value_terms = terms[1].reshape(groups, seq_here, local_len, width)
    key_grad, value_grad = (
        lax.psum_scatter(
            key_terms.astype(jnp.bfloat16), "group", scatter_dimension=0, tiled=True
        ).astype(jnp.float32),
        lax.psum_scatter(
            value_terms.astype(jnp.bfloat16), "group", scatter_dimension=0, tiled=True
        ).astype(jnp.float32),
    )
    scaling = 1.0 / math.sqrt(HEAD_DIM)
    grad_query_low = (grad_query * scaling).reshape(total_rows, width).astype(jnp.bfloat16)
    grad_key_low = (key_grad * scaling).reshape(total_rows, width).astype(jnp.bfloat16)
    grad_value_low = value_grad.reshape(total_rows, width).astype(jnp.bfloat16)
    query_bias_grad = column_sum(grad_query_low)
    value_bias_grad = column_sum(grad_value_low)
    grad_mixture_low = jnp.concatenate([grad_query_low, grad_key_low, grad_value_low], axis=1)
    grad_normed = product_back(grad_mixture_low, back_in)
    unused_first, first_back = jax.vjp(
        layer_norm,
        flat_input,
        back_gain_first.astype(jnp.float32),
        back_shift_first.astype(jnp.float32),
    )
    grad_entry, first_gain_grad, first_shift_grad = first_back(grad_normed)
    input_grad = (grad_entry + grad_middle).reshape(seq_here, local_len, width)
    project_weight_grad = weight_term(attended_low, grad_middle_low)
    in_weight_grad = weight_term(normed_low, grad_mixture_low)
    mixer_parts = (
        lax.psum_scatter(
            in_weight_grad.astype(jnp.bfloat16), "group", scatter_dimension=0, tiled=True
        ).astype(jnp.float32),
        lax.psum_scatter(
            project_weight_grad.astype(jnp.bfloat16), "group", scatter_dimension=0, tiled=True
        ).astype(jnp.float32),
        lax.psum_scatter(
            query_bias_grad.astype(jnp.bfloat16), "group", scatter_dimension=0, tiled=True
        ).astype(jnp.float32),
        lax.psum_scatter(
            value_bias_grad.astype(jnp.bfloat16), "group", scatter_dimension=0, tiled=True
        ).astype(jnp.float32),
        lax.psum_scatter(
            project_bias_grad.astype(jnp.bfloat16), "group", scatter_dimension=0, tiled=True
        ).astype(jnp.float32),
        lax.psum_scatter(
            first_gain_grad.astype(jnp.bfloat16), "group", scatter_dimension=0, tiled=True
        ).astype(jnp.float32),
        lax.psum_scatter(
            first_shift_grad.astype(jnp.bfloat16), "group", scatter_dimension=0, tiled=True
        ).astype(jnp.float32),
    )
    share_in, share_out, share_expand, share_reduce = (
        mixer_parts[0],
        mixer_parts[1],
        feed_parts[0],
        feed_parts[1],
    )
    share_query, share_value, share_project = (mixer_parts[2], mixer_parts[3], mixer_parts[4])
    share_expand_bias, share_reduce_bias = (feed_parts[2], feed_parts[3])
    share_first_gain, share_first_shift = (mixer_parts[5], mixer_parts[6])
    share_second_gain, share_second_shift = (feed_parts[4], feed_parts[5])
    totals = (
        lax.psum(share_in.astype(jnp.bfloat16), "replica").astype(jnp.float32),
        lax.psum(share_out.astype(jnp.bfloat16), "replica").astype(jnp.float32),
        lax.psum(share_expand.astype(jnp.bfloat16), "replica").astype(jnp.float32),
        lax.psum(share_reduce.astype(jnp.bfloat16), "replica").astype(jnp.float32),
        lax.psum(share_query.astype(jnp.bfloat16), "replica").astype(jnp.float32),
        lax.psum(share_value.astype(jnp.bfloat16), "replica").astype(jnp.float32),
        lax.psum(share_project.astype(jnp.bfloat16), "replica").astype(jnp.float32),
        lax.psum(share_expand_bias.astype(jnp.bfloat16), "replica").astype(jnp.float32),
        lax.psum(share_reduce_bias.astype(jnp.bfloat16), "replica").astype(jnp.float32),
        lax.psum(share_first_gain.astype(jnp.bfloat16), "replica").astype(jnp.float32),
        lax.psum(share_first_shift.astype(jnp.bfloat16), "replica").astype(jnp.float32),
        lax.psum(share_second_gain.astype(jnp.bfloat16), "replica").astype(jnp.float32),
        lax.psum(share_second_shift.astype(jnp.bfloat16), "replica").astype(jnp.float32),
    )
    return (
        outputs,
        input_grad,
        totals[0],
        totals[1],
        totals[2],
        totals[3],
        totals[4],
        totals[5],
        totals[6],
        totals[7],
        totals[8],
        totals[9],
        totals[10],
        totals[11],
        totals[12],
    )


MESH = pl.DeviceIdType.MESH


def flipped(z=0, core=0, y=0, x=0):
    pairs = []
    for me in range(32):
        pairs.append((me, me ^ (8 * z + 4 * core + 2 * y + x)))
    return pairs


FLIP_X = flipped(x=1)
FLIP_Y = flipped(y=1)
FLIP_CORE = flipped(core=1)
FLIP_Z = flipped(z=1)
FLIP_PAIR = flipped(z=2)
INWARD = [(me, me + 8) for me in range(8)] + [(me, me - 8) for me in range(24, 32)]
MIDDLE = [(me, me + 8) for me in range(8, 16)] + [(me, me - 8) for me in range(16, 24)]
OUTWARD = [(me, me - 8) for me in range(8, 16)] + [(me, me + 8) for me in range(16, 24)]


def moved(entries, pairs):
    return lax.ppermute(entries, ("replica", "group"), pairs)


def low(entries):
    return entries.astype(jnp.bfloat16)


def wide(entries):
    return entries.astype(jnp.float32)


def at(entries, index):
    return lax.dynamic_index_in_dim(entries, index, 0, False)


def place():
    replica = lax.axis_index("replica")
    group = lax.axis_index("group")
    core = lax.rem(replica, 2)
    z = lax.div(replica, 2)
    return replica, group, z, core, lax.div(group, 2), lax.rem(group, 2)


def partners(replica, group):
    core = lax.rem(replica, 2)
    z = lax.rem(lax.div(replica, 2), 2)
    y = lax.div(group, 2)
    x = lax.rem(group, 2)
    by_x = (replica, group + 1 - 2 * x)
    by_y = (replica, group + 2 - 4 * y)
    by_both = (replica, group + 3 - 4 * y - 2 * x)
    by_core = (replica + 1 - 2 * core, group)
    by_z = (replica + 2 - 4 * z, group)
    return by_x, by_y, by_both, by_core, by_z


def greet(devices):
    barrier = pltpu.get_barrier_semaphore()
    for device in devices:
        pl.semaphore_signal(barrier, inc=1, device_id=device, device_id_type=MESH)
    pl.semaphore_wait(barrier, len(devices))


NT = (((1,), (1,)), ((), ()))

def dot_nt(a, b):
    return lax.dot_general(a, b, NT, preferred_element_type=jnp.float32)

def dot_nn(a, b):
    return jnp.dot(a, b, preferred_element_type=jnp.float32)

BLOCK = 256

def heads_kernel(q_ref, k_ref, v_ref, segc_ref, segr_ref, o_ref, lse_ref, ot_ref, vt_ref):
    tile = pl.program_id(0)
    length = q_ref.shape[0]
    blocks = length // BLOCK
    lane = lax.broadcasted_iota(jnp.int32, (1, 128), 1)
    ot_ref[...] = jnp.zeros_like(ot_ref)
    lse_ref[...] = jnp.zeros_like(lse_ref)
    vt_ref[...] = v_ref[...].T

    def head(h):
        k = jnp.where((lane >= 64 * h) & (lane < 64 * h + 64), k_ref[...], jnp.bfloat16(0))
        for i in range(blocks):
            low, high = i * BLOCK, (i + 1) * BLOCK
            q = q_ref[low:high, :] * jnp.bfloat16(0.125)
            s = dot_nt(k[:high], q)
            same = segc_ref[:high, :] == segr_ref[:, low:high]
            kpos = lax.broadcasted_iota(jnp.int32, (high, BLOCK), 0)
            qpos = lax.broadcasted_iota(jnp.int32, (high, BLOCK), 1) + low
            s = jnp.where(same & (kpos <= qpos), s, -1e30)
            m = jnp.max(s, axis=0, keepdims=True)
            p = jnp.exp(s - m)
            l = jnp.sum(p, axis=0, keepdims=True)
            ot = dot_nn(vt_ref[64 * h : 64 * h + 64, :high], p.astype(jnp.bfloat16))
            ot_ref[64 * h : 64 * h + 64, low:high] = ot / l
            lse_ref[0, h : h + 1, low:high] = m + jnp.log(l)

    head(0)

    @pl.when(tile < 6)
    def _():
        head(1)

    o_ref[...] = ot_ref[...].T.astype(jnp.bfloat16)


def heads(qkv, segc, segr):
    length = qkv.shape[0]
    spec = lambda off: pl.BlockSpec((length, 128), lambda t: (0, t + off))
    return pl.pallas_call(
        heads_kernel,
        grid=(7,),
        in_specs=[spec(0), spec(7), spec(14), pl.BlockSpec((length, 1), lambda t: (0, 0)), pl.BlockSpec((1, length), lambda t: (0, 0))],
        out_specs=[pl.BlockSpec((length, 128), lambda t: (0, t)), pl.BlockSpec((1, 8, length), lambda t: (t, 0, 0))],
        out_shape=[jax.ShapeDtypeStruct((length, 896), jnp.bfloat16), jax.ShapeDtypeStruct((7, 8, length), jnp.float32)],
        scratch_shapes=[pltpu.VMEM((128, length), jnp.float32), pltpu.VMEM((128, length), jnp.bfloat16)],
        compiler_params=pltpu.CompilerParams(vmem_limit_bytes=48 * 2**20),
        cost_estimate=pl.CostEstimate(flops=int(13 * 2 * 2 * length * length * 64 * 2), bytes_accessed=8 * length * 896, transcendentals=13 * length * length // 2),
        name="heads",
    )(qkv, qkv, qkv, segc, segr)


def heads_back_kernel(q_ref, k_ref, v_ref, do_ref, o_ref, lse_ref, segc_ref, segr_ref, share_ref, dq_ref, dk_ref, dv_ref, got_ref, dqt_ref, odt_ref, send, recv):
    tile = pl.program_id(0)
    by_pair = (lax.rem(lax.axis_index("replica") + 4, 8), lax.axis_index("group"))
    copy = pltpu.make_async_remote_copy(src_ref=share_ref, dst_ref=got_ref, send_sem=send, recv_sem=recv, device_id=by_pair, device_id_type=MESH)

    @pl.when(tile == 0)
    def _():
        greet([by_pair])
        copy.start()

    length = q_ref.shape[0]
    blocks = length // BLOCK
    lane = lax.broadcasted_iota(jnp.int32, (1, 128), 1)
    dqt_ref[...] = jnp.zeros_like(dqt_ref)
    odt_ref[...] = (do_ref[...].astype(jnp.float32) * o_ref[...].astype(jnp.float32)).T

    def head(h):
        mine = (lane >= 64 * h) & (lane < 64 * h + 64)
        dot_row = jnp.sum(odt_ref[64 * h : 64 * h + 64, :], axis=0, keepdims=True)
        for j in range(blocks):
            low, high = j * BLOCK, (j + 1) * BLOCK
            rest = length - low
            q = q_ref[low:, :] * jnp.bfloat16(0.125)
            do = do_ref[low:, :]
            k = jnp.where(mine, k_ref[low:high, :], jnp.bfloat16(0))
            v = jnp.where(mine, v_ref[low:high, :], jnp.bfloat16(0))
            s = dot_nt(k, q)
            same = segc_ref[low:high, :] == segr_ref[:, low:]
            kpos = lax.broadcasted_iota(jnp.int32, (BLOCK, rest), 0)
            qpos = lax.broadcasted_iota(jnp.int32, (BLOCK, rest), 1)
            p = jnp.where(same & (kpos <= qpos), jnp.exp(s - lse_ref[0, h : h + 1, low:]), 0.0)
            dp = dot_nt(v, do)
            ds = (p * (dp - dot_row[:, low:])).astype(jnp.bfloat16)
            dv = dot_nn(p.astype(jnp.bfloat16), do)
            dk = dot_nn(ds, q)
            if h == 0:
                dv_ref[low:high, :] = jnp.where(mine, dv, 0.0).astype(jnp.bfloat16)
                dk_ref[low:high, :] = jnp.where(mine, dk, 0.0).astype(jnp.bfloat16)
            else:
                dv_ref[low:high, :] = jnp.where(mine, dv.astype(jnp.bfloat16), dv_ref[low:high, :])
                dk_ref[low:high, :] = jnp.where(mine, dk.astype(jnp.bfloat16), dk_ref[low:high, :])
            dqt_ref[:, low:] += dot_nn(k.T, ds)

    head(0)

    @pl.when(tile < 6)
    def _():
        head(1)

    dq_ref[...] = (dqt_ref[...].T * 0.125).astype(jnp.bfloat16)

    @pl.when(tile == 6)
    def _():
        copy.wait()


def heads_back(qkv, grad, out, lse, segc, segr, share):
    length = qkv.shape[0]
    spec = lambda off: pl.BlockSpec((length, 128), lambda t: (0, t + off))
    one = pl.BlockSpec((length, 128), lambda t: (0, t))
    shape = jax.ShapeDtypeStruct((length, 896), jnp.bfloat16)
    return pl.pallas_call(
        heads_back_kernel,
        grid=(7,),
        in_specs=[spec(0), spec(7), spec(14), one, one, pl.BlockSpec((1, 8, length), lambda t: (t, 0, 0)), pl.BlockSpec((length, 1), lambda t: (0, 0)), pl.BlockSpec((1, length), lambda t: (0, 0)), pl.BlockSpec(memory_space=pl.ANY)],
        out_specs=[one, one, one, pl.BlockSpec(memory_space=pl.ANY)],
        out_shape=[shape, shape, shape, jax.ShapeDtypeStruct(share.shape, share.dtype)],
        scratch_shapes=[pltpu.VMEM((128, length), jnp.float32), pltpu.VMEM((128, length), jnp.float32), pltpu.SemaphoreType.DMA, pltpu.SemaphoreType.DMA],
        compiler_params=pltpu.CompilerParams(vmem_limit_bytes=48 * 2**20, collective_id=4, has_side_effects=True),
        cost_estimate=pl.CostEstimate(flops=int(13 * 5 * 2 * length * length * 64 * 2), bytes_accessed=16 * length * 896, transcendentals=13 * length * length // 2),
        name="heads_back",
    )(qkv, qkv, qkv, grad, out, lse, segc, segr, share)

def first_exchange_kernel(inp, weights, vec, seg, cot, x_seq, w_full, vecs, segs, cots, send, recv, local, x_stage, w_stage, vec_stage, seg_stage, cot_stage):
    replica = lax.axis_index("replica")
    group = lax.axis_index("group")
    core = lax.rem(replica, 2)
    y = lax.div(group, 2)
    x = lax.rem(group, 2)
    by_x, by_y, by_both, by_core, by_z = partners(replica, group)
    greet((by_x, by_y, by_both, by_core, by_z))
    other_x = 1 - x
    other_y = 1 - y
    slot_x = group + 1 - 2 * x
    slot_y = group + 2 - 4 * y
    slot_both = group + 3 - 4 * y - 2 * x
    mine = pl.ds(pl.multiple_of(core * 192, 16), 208)
    shared = pl.ds(pl.multiple_of(core * 208, 16), 192)
    count = [0]

    def remote(src, dst, device):
        i = count[0]
        count[0] = i + 1
        copy = pltpu.make_async_remote_copy(src_ref=src, dst_ref=dst, send_sem=send.at[i], recv_sem=recv.at[i], device_id=device, device_id_type=MESH)
        copy.start()
        return copy

    small = [
        remote(vec, vecs.at[group], by_x),
        remote(vec, vecs.at[group], by_y),
        remote(vec, vecs.at[group], by_both),
        remote(seg.at[other_x], segs.at[group], by_x),
        remote(seg.at[x], segs.at[group], by_y),
        remote(seg.at[other_x], segs.at[group], by_both),
    ]
    x_block = remote(inp.at[other_x], x_seq.at[group], by_x)
    y_block = remote(inp.at[x], x_seq.at[group], by_y)
    w_x = remote(weights.at[y, mine], w_full.at[group, mine], by_x)
    w_y = remote(weights.at[other_y, mine], w_full.at[group, mine], by_y)
    cot_core = remote(cot, cots.at[1], by_core)
    cot_z = remote(cot, cots.at[2], by_z)
    staged = [
        (inp.at[x], x_stage, x_seq.at[group]),
        (weights.at[y], w_stage, w_full.at[group]),
        (vec, vec_stage, vecs.at[group]),
        (seg.at[x], seg_stage, segs.at[group]),
        (cot, cot_stage, cots.at[0]),
    ]
    loads = [pltpu.make_async_copy(here, stage, local.at[i]) for i, (here, stage, there) in enumerate(staged)]
    own = [pltpu.make_async_copy(stage, there, local.at[5 + i]) for i, (here, stage, there) in enumerate(staged)]
    for copy in loads:
        copy.start()
    for i, copy in enumerate(own):
        loads[i].wait()
        copy.start()
    x_block.wait_recv()
    y_more = remote(x_seq.at[slot_x], x_seq.at[slot_x], by_y)
    w_y.wait_recv()
    w_more = remote(w_full.at[slot_y, mine], w_full.at[slot_y, mine], by_x)
    w_y_core = remote(w_full.at[slot_y, shared], w_full.at[slot_y, shared], by_core)
    w_x.wait_recv()
    w_x_core = remote(w_full.at[slot_x, shared], w_full.at[slot_x, shared], by_core)
    cot_z.wait_recv()
    cot_more = remote(cots.at[2], cots.at[3], by_core)
    w_more.wait_recv()
    w_more_core = remote(w_full.at[slot_both, shared], w_full.at[slot_both, shared], by_core)
    for copy in small + [y_block, y_more, cot_core, cot_more, w_y_core, w_x_core, w_more_core]:
        copy.wait_recv()
    for copy in small + [x_block, y_block, y_more, w_x, w_y, w_more, cot_core, cot_z, cot_more, w_y_core, w_x_core, w_more_core]:
        copy.wait_send()
    for copy in own:
        copy.wait()


def first_exchange(inp, weights, vec, seg, cot):
    any_space = pl.BlockSpec(memory_space=pl.ANY)
    shape = jax.ShapeDtypeStruct
    return pl.pallas_call(
        first_exchange_kernel,
        in_specs=[any_space] * 5,
        out_specs=[any_space] * 5,
        out_shape=[
            shape((4,) + inp.shape[1:], inp.dtype),
            shape((4,) + weights.shape[1:], weights.dtype),
            shape((4,) + vec.shape, vec.dtype),
            shape((4,) + seg.shape[1:], seg.dtype),
            shape((4,) + cot.shape, cot.dtype),
        ],
        scratch_shapes=[
            pltpu.SemaphoreType.DMA((18,)),
            pltpu.SemaphoreType.DMA((18,)),
            pltpu.SemaphoreType.DMA((10,)),
            pltpu.VMEM(inp.shape[1:], inp.dtype),
            pltpu.VMEM(weights.shape[1:], weights.dtype),
            pltpu.VMEM(vec.shape, vec.dtype),
            pltpu.VMEM(seg.shape[1:], seg.dtype),
            pltpu.VMEM(cot.shape, cot.dtype),
        ],
        compiler_params=pltpu.CompilerParams(collective_id=0, has_side_effects=True, vmem_limit_bytes=32 * 2**20),
        name="first_exchange",
    )(inp, weights, vec, seg, cot)


def turn_kernel(forth, src, dst, send, recv, local, stage):
    replica = lax.axis_index("replica")
    group = lax.axis_index("group")
    y = lax.div(group, 2)
    x = lax.rem(group, 2)
    by_x, by_y, by_both, by_core, by_z = partners(replica, group)
    others = (by_both, by_x, by_y)
    greet(others)

    def view(device):
        there = device[1]
        there_y = lax.div(there, 2)
        there_x = lax.rem(there, 2)
        if forth:
            return src.at[there], dst.at[x, y]
        return src.at[there_x, there_y], dst.at[group]

    copies = []
    for i, device in enumerate(others):
        a, b = view(device)
        copies.append(pltpu.make_async_remote_copy(src_ref=a, dst_ref=b, send_sem=send.at[i], recv_sem=recv.at[i], device_id=device, device_id_type=MESH))
    a, b = view((replica, group))
    for copy in copies:
        copy.start()
    load = pltpu.make_async_copy(a, stage, local.at[0])
    own = pltpu.make_async_copy(stage, b, local.at[1])
    load.start()
    load.wait()
    own.start()
    for copy in copies:
        copy.wait()
    own.wait()


def turn(entries, forth, collective):
    any_space = pl.BlockSpec(memory_space=pl.ANY)
    tail = entries.shape[-2:]
    lead = (2, 2) if forth else (4,)
    return pl.pallas_call(
        functools.partial(turn_kernel, forth),
        in_specs=[any_space],
        out_specs=any_space,
        out_shape=jax.ShapeDtypeStruct(lead + tail, entries.dtype),
        scratch_shapes=[pltpu.SemaphoreType.DMA((3,)), pltpu.SemaphoreType.DMA((3,)), pltpu.SemaphoreType.DMA((2,)), pltpu.VMEM(tail, entries.dtype)],
        compiler_params=pltpu.CompilerParams(collective_id=collective, has_side_effects=True),
        cost_estimate=pl.CostEstimate(flops=0, bytes_accessed=60 * 2**20, transcendentals=0),
        name="turn_out" if forth else "turn_back",
    )(entries)


def head_columns(shard, half, axis):
    first = [lax.slice_in_dim(shard, 1600 * k + 768 * half, 1600 * k + 768 * half + 832, axis=axis) for k in range(3)]
    pad = [(0, 0)] * shard.ndim
    pad[axis] = (0, 64)
    return jnp.concatenate([jnp.pad(part, pad) for part in first], axis=axis)


def padded(entries):
    return jnp.pad(entries, [(0, 0)] * (entries.ndim - 1) + [(0, 64)])


def joined(first, other):
    lane = lax.broadcasted_iota(jnp.int32, (1, 128), 1)
    middle = jnp.where(lane < 64, first[..., 768:896], other[..., 0:128])
    return jnp.concatenate([first[..., :768], middle, other[..., 128:]], axis=-1)


def hold(entries, *until):
    return lax.optimization_barrier((entries,) + until)[0]


def group_scatter_start(parts, group):
    cuts = [part.shape[1] // 32 * 16 + (16 if part.shape[1] // 16 % 2 else 0) for part in parts]
    block = lambda k: [at(part, group ^ k) for part in parts]
    own, by_x, by_y, by_both = block(0), block(1), block(2), block(3)
    upper = lambda entries: [entry[:cut] for entry, cut in zip(entries, cuts)]
    lower = lambda entries: [entry[cut:] for entry, cut in zip(entries, cuts)]
    got_x = moved(jnp.concatenate(upper(by_x) + upper(by_both)), FLIP_X)
    got_y = moved(jnp.concatenate(lower(by_y) + lower(by_both)), FLIP_Y)
    return (cuts, [part.shape[1] for part in parts]), upper(own), lower(own), upper(by_y), lower(by_x), got_x, got_y


def group_scatter_pass(state, until):
    cuts, own_upper, own_lower, far_upper, far_lower, got_x, got_y = state
    got_x, got_y = hold((got_x, got_y), until)
    size_x = got_x.shape[0] // 2
    size_y = got_y.shape[0] // 2
    upper = wide(jnp.concatenate(own_upper)) + wide(got_x[:size_x])
    lower = wide(jnp.concatenate(own_lower)) + wide(got_y[:size_y])
    pass_y = low(wide(jnp.concatenate(far_upper)) + wide(got_x[size_x:]))
    pass_x = low(wide(jnp.concatenate(far_lower)) + wide(got_y[size_y:]))
    return cuts, upper, lower, moved(pass_y, FLIP_Y), moved(pass_x, FLIP_X)


def group_scatter_end(state, until):
    (cuts, sizes), upper, lower, got_y, got_x = state
    got_y, got_x = hold((got_y, got_x), until)
    upper = low(upper + wide(got_y))
    lower = low(lower + wide(got_x))
    shares = []
    top = bottom = 0
    for cut, size in zip(cuts, sizes):
        shares.append((upper[top : top + cut], lower[bottom : bottom + size - cut]))
        top += cut
        bottom += size - cut
    return shares


def sum_kernel(grad, out_share, gn, vec, shares, total, tokens, vec_total, quads, vec_got, vec_own, vec_core, vec_z, c_buf, x_buf, y_buf, line_buf, line_mid, part, inner, gn_y, send, recv, local):
    replica = lax.axis_index("replica")
    group = lax.axis_index("group")
    core = lax.rem(replica, 2)
    quad = lax.rem(replica, 4)
    quad_z = lax.rem(quad + 2, 4)
    z = lax.div(replica, 2)
    y = lax.div(group, 2)
    x = lax.rem(group, 2)
    by_x, by_y, by_both, by_core, by_z = partners(replica, group)
    outer = (z == 0) | (z == 3)
    by_line = (jnp.where(z == 0, replica + 2, jnp.where(z == 3, replica - 2, jnp.where(z == 1, replica - 2, replica + 2))), group)
    by_middle = (jnp.where(z == 1, replica + 2, replica - 2), group)
    lines_z = [(lax.rem(replica + 2 * k, 8), group) for k in (1, 2, 3)]
    greet([by_x, by_y, by_both, by_core] + lines_z)
    count = [0]
    locals_ = [0]

    def remote(src, dst, device):
        i = count[0]
        count[0] = i + 1
        return pltpu.make_async_remote_copy(src_ref=src, dst_ref=dst, send_sem=send.at[i], recv_sem=recv.at[i], device_id=device, device_id_type=MESH)

    def here(src, dst):
        i = locals_[0]
        locals_[0] = i + 1
        copy = pltpu.make_async_copy(src, dst, local.at[i])
        copy.start()
        return copy

    mine = pl.multiple_of(192 * core, 16)
    theirs = pl.multiple_of(192 * (1 - core), 16)
    other_x = 1 - x
    other_y = 1 - y
    sends = []
    kept = []

    def go(copy):
        copy.start()
        sends.append(copy)
        return copy

    def add(a, b):
        return (a.astype(jnp.float32) + b.astype(jnp.float32)).astype(jnp.bfloat16)

    c_copies = []
    loads = []
    for k in range(3):
        lanes = pl.ds(896 * k, 896)
        c_copies.append([go(remote(grad.at[r, pl.ds(theirs, 208), lanes], c_buf.at[k, r], by_core)) for r in range(4)])
        loads.append(here(grad.at[:, pl.ds(mine, 208), lanes], part.at[k]))
    vec_group = [go(remote(vec.at[device[1]], vec_got.at[group], device)) for device in (by_x, by_y, by_both)]
    share_load = here(out_share, total.at[3, pl.ds(mine, 208)])
    pieces = [(k, pl.ds(208 * m, 208 - 16 * m)) for k in range(2) for m in range(2)]
    quad_copies = []
    for k, rows in pieces:
        kept.append(here(shares.at[k, rows], quads.at[k, quad, rows]))
        over = go(remote(shares.at[k, rows], quads.at[k, quad, rows], by_z))
        quad_copies.append((over, go(remote(shares.at[k, rows], quads.at[k, quad, rows], by_core))))
    far = 2 * other_y
    near = 2 * y
    gn_pass = go(remote(gn.at[far + other_x], gn_y.at[0], by_y))
    gn_keep = go(remote(gn.at[far + x], gn_y.at[1], by_y))
    x_copies = []
    for k in range(3):
        loads[k].wait()
        for r in range(4):
            c_copies[k][r].wait_recv()
        for r in range(4):
            part[k, r] = add(part[k, r], c_buf[k, r])
        x_copies.append([go(remote(part.at[k, 2 * row + other_x], x_buf.at[k, row], by_x)) for row in range(2)])

    def line(k, rows, merge):
        i = count[0]
        count[0] = i + 3
        into = pltpu.make_async_remote_copy(src_ref=total.at[k, rows], dst_ref=line_buf.at[k, merge], send_sem=send.at[i], recv_sem=recv.at[i], device_id=by_line, device_id_type=MESH)
        middle = pltpu.make_async_remote_copy(src_ref=inner.at[k, merge], dst_ref=line_mid.at[k, merge], send_sem=send.at[i + 1], recv_sem=recv.at[i + 1], device_id=by_middle, device_id_type=MESH)
        back = pltpu.make_async_remote_copy(src_ref=total.at[k, rows], dst_ref=line_buf.at[k, merge], send_sem=send.at[i + 2], recv_sem=recv.at[i + 2], device_id=by_line, device_id_type=MESH)

        @pl.when(outer)
        def _():
            into.start()

        return rows, merge, into, middle, back

    def line_second(k):
        for rows, merge, into, middle, back in lines[k]:
            @pl.when(jnp.logical_not(outer))
            def _():
                into.wait_recv()
                inner[k, merge] = add(total[k, rows], line_buf[k, merge])
                middle.start()

    def line_third(k):
        for rows, merge, into, middle, back in lines[k]:
            @pl.when(jnp.logical_not(outer))
            def _():
                middle.wait_recv()
                total[k, rows] = add(inner[k, merge], line_mid[k, merge])
                back.start()

    def line_fourth(k):
        for rows, merge, into, middle, back in lines[k]:
            @pl.when(outer)
            def _():
                into.wait_send()
                back.wait_recv()
                total[k, rows] = line_buf[k, merge]

            @pl.when(jnp.logical_not(outer))
            def _():
                middle.wait_send()
                back.wait_send()

    def quad_pass(i):
        k, rows = pieces[i]
        quad_copies[i][0].wait_recv()
        return go(remote(quads.at[k, quad_z, rows], quads.at[k, quad_z, rows], by_core))

    lane = lax.broadcasted_iota(jnp.int32, (1, 128), 1)
    share_load.wait()
    halves = [(pl.ds(mine + 112 * m, 112 - 16 * m), pl.ds(112 * m, 112 - 16 * m)) for m in range(2)]
    lines = {}
    lines[3] = [line(3, rows, merge) for rows, merge in halves]
    gn_pass.wait_recv()
    gn_y[0] = add(gn_y[0], gn[near + other_x])
    gn_cross = remote(gn_y.at[0], tokens.at[x], by_x)
    y_copies = []
    for k in range(3):
        for row in range(2):
            x_copies[k][row].wait_recv()
        for row in range(2):
            part[k, 2 * row + x] = add(part[k, 2 * row + x], x_buf[k, row])
        y_copies.append(go(remote(part.at[k, 2 * other_y + x], y_buf.at[k], by_y)))
        if k == 0:
            for copy in vec_group:
                copy.wait_recv()
            vec_got[group] = vec[group]
            vec_own[...] = (vec_got[0] + vec_got[1]) + (vec_got[2] + vec_got[3])
            vec_pass = go(remote(vec_own, vec_core, by_core))
            line_second(3)
        if k == 1:
            vec_pass.wait_recv()
            vec_z[z] = vec_own[...] + vec_core[...]
            vec_line = [go(remote(vec_z.at[z], vec_z.at[z], device)) for device in lines_z]
        if k == 2:
            go(gn_cross)
        if k > 0:
            arrive(y_copies, part, y_buf, total, lane, k - 1, near + x, y, mine)
            lines[k - 1] = [line(k - 1, rows, merge) for rows, merge in halves]
            if k == 1:
                line_third(3)
            else:
                line_second(0)
    gn_keep.wait_recv()
    tokens[x] = add(gn_y[1], gn[near + x])
    arrive(y_copies, part, y_buf, total, lane, 2, near + x, y, mine)
    lines[2] = [line(2, rows, merge) for rows, merge in halves]
    passes = [quad_pass(0), quad_pass(1)]
    line_second(1)
    line_second(2)
    passes += [quad_pass(2), quad_pass(3)]
    line_third(0)
    line_third(1)
    line_third(2)
    for copy in vec_line:
        copy.wait_recv()
    vec_total[...] = (vec_z[0] + vec_z[1]) + (vec_z[2] + vec_z[3])
    last = []
    for k in (3, 0, 1, 2):
        line_fourth(k)
        rows = pl.ds(pl.multiple_of(208 * core, 16), 192)
        last.append(go(remote(total.at[k, rows], total.at[k, rows], by_core)))
    for copy in last + passes + [copies[1] for copies in quad_copies]:
        copy.wait_recv()
    gn_cross.wait_recv()
    for copy in kept:
        copy.wait()
    for copy in sends:
        copy.wait_send()


def arrive(y_copies, part, y_buf, full, lane, k, index, y, mine):
    y_copies[k].wait_recv()
    here = part[k, index]
    there = y_buf[k]
    first = jnp.where(y == 0, here, there)
    other = jnp.where(y == 0, there, here)
    rows = pl.ds(mine, 208)
    full[k, rows, 0:768] = first[:, 0:768]
    full[k, rows, 768:896] = jnp.where(lane < 64, first[:, 768:896], other[:, 0:128])
    full[k, rows, 896:1664] = other[:, 128:896]


def sum_grads(grad, out_share, gn, vec, shares):
    any_space = pl.BlockSpec(memory_space=pl.ANY)
    vmem = pl.BlockSpec(memory_space=pltpu.VMEM)
    shape = jax.ShapeDtypeStruct
    kind = jnp.bfloat16
    buf = lambda *dims: pltpu.VMEM(dims, kind)
    return pl.pallas_call(
        sum_kernel,
        in_specs=[any_space, any_space, vmem, vmem, vmem],
        out_specs=[vmem, vmem, vmem, any_space],
        out_shape=[
            shape((4, 400, 1664), kind),
            shape((2,) + gn.shape[1:], kind),
            shape(vec.shape[1:], vec.dtype),
            shape((2, 4) + shares.shape[1:], kind),
        ],
        scratch_shapes=[
            pltpu.VMEM(vec.shape, vec.dtype),
            pltpu.VMEM(vec.shape[1:], vec.dtype),
            pltpu.VMEM(vec.shape[1:], vec.dtype),
            pltpu.VMEM(vec.shape, vec.dtype),
            buf(3, 4, 208, 896),
            buf(3, 2, 208, 896),
            buf(3, 208, 896),
            buf(4, 208, 1664),
            buf(4, 208, 1664),
            buf(3, 4, 208, 896),
            buf(4, 208, 1664),
            buf(2, 256, gn.shape[2]),
            pltpu.SemaphoreType.DMA((88,)),
            pltpu.SemaphoreType.DMA((88,)),
            pltpu.SemaphoreType.DMA((8,)),
        ],
        compiler_params=pltpu.CompilerParams(collective_id=3, has_side_effects=True, vmem_limit_bytes=58 * 2**20),
        name="sum_grads",
    )(grad, out_share, gn, vec, shares)


def finish_feed_kernel(quads_ref, out_reduce, out_expand):
    for k in range(4):
        out_reduce[k] = quads_ref[0, k].astype(jnp.float32)
    for k in range(4):
        piece = quads_ref[1, k].astype(jnp.float32)
        for r in range(4):
            out_expand[:, 1600 * r + 400 * k : 1600 * r + 400 * k + 400] = piece[:, 400 * r : 400 * r + 400]


def finish_feed(quads):
    rows, width = quads.shape[2:]
    step = 80
    out = pl.pallas_call(
        finish_feed_kernel,
        grid=(rows // step,),
        in_specs=[pl.BlockSpec((2, 4, step, width), lambda i: (0, 0, i, 0))],
        out_specs=[pl.BlockSpec((4, step, width), lambda i: (0, i, 0)), pl.BlockSpec((step, 4 * width), lambda i: (i, 0))],
        out_shape=[jax.ShapeDtypeStruct((4, rows, width), jnp.float32), jax.ShapeDtypeStruct((rows, 4 * width), jnp.float32)],
        compiler_params=pltpu.CompilerParams(vmem_limit_bytes=48 * 2**20),
        name="finish_feed",
    )(quads)
    return out[0].reshape(4 * rows, width), out[1]


def finish_mixer_kernel(total_ref, in_ref, out_ref):
    for k in range(3):
        in_ref[:, 1600 * k : 1600 * k + 1600] = total_ref[k, :, :1600].astype(jnp.float32)
    out_ref[...] = total_ref[3, :, :1600].astype(jnp.float32)


def finish_mixer(total):
    rows = total.shape[1]
    step = 80
    return pl.pallas_call(
        finish_mixer_kernel,
        grid=(rows // step,),
        in_specs=[pl.BlockSpec((4, step, total.shape[2]), lambda i: (0, i, 0))],
        out_specs=[pl.BlockSpec((step, 4800), lambda i: (i, 0)), pl.BlockSpec((step, 1600), lambda i: (i, 0))],
        out_shape=[jax.ShapeDtypeStruct((rows, 4800), jnp.float32), jax.ShapeDtypeStruct((rows, 1600), jnp.float32)],
        compiler_params=pltpu.CompilerParams(vmem_limit_bytes=48 * 2**20),
        name="finish_mixer",
    )(total)


PIECES = ((0, 512), (512, 1024), (1024, 1600))
HALF = 208


class Wires:
    def __init__(self, send, recv, local):
        self.send, self.recv, self.local = send, recv, local
        self.remotes = self.locals = 0
        self.sent = []
        self.kept = []

    def make(self, src, dst, device):
        i = self.remotes
        self.remotes = i + 1
        return pltpu.make_async_remote_copy(src_ref=src, dst_ref=dst, send_sem=self.send.at[i], recv_sem=self.recv.at[i], device_id=device, device_id_type=MESH)

    def go(self, src, dst, device):
        copy = self.make(src, dst, device)
        copy.start()
        self.sent.append(copy)
        return copy

    def here(self, src, dst):
        i = self.locals
        self.locals = i + 1
        copy = pltpu.make_async_copy(src, dst, self.local.at[i])
        copy.start()
        return copy

    def keep(self, src, dst):
        self.kept.append(self.here(src, dst))

    def finish(self):
        for copy in self.sent:
            copy.wait_send()
        for copy in self.kept:
            copy.wait()


def rows16(start, size):
    return pl.ds(pl.multiple_of(start, 16), size)


def dot_tn(a, b):
    return lax.dot_general(a, b, (((0,), (0,)), ((), ())), preferred_element_type=jnp.float32)


def add_low(a, b):
    return (a.astype(jnp.float32) + b.astype(jnp.float32)).astype(jnp.bfloat16)


def weight_sum(a, b, out):
    width = out.shape[0]
    whole = width // 256

    def chunk(j, carry):
        lanes = pl.ds(pl.multiple_of(256 * j, 256), 256)
        out[lanes, :] = dot_tn(a[:, lanes], b[...]).astype(jnp.bfloat16)
        return carry

    lax.fori_loop(0, whole, chunk, 0)
    if width > 256 * whole:
        out[256 * whole :, :] = dot_tn(a[:, 256 * whole : width], b[...]).astype(jnp.bfloat16)


def feed_all_kernel(second, cots, expand_part, reduce_shard, bias, act_out, back_out, second_out, reduce_out, gs_out, own_out, pass_out, sum_out, wexp, wred, s, c, a, b, gs, got_core, got_z, rg, got_x, got_y, send, recv, local):
    replica = lax.axis_index("replica")
    group = lax.axis_index("group")
    quad = lax.rem(replica, 4)
    y = lax.div(group, 2)
    x = lax.rem(group, 2)
    by_x, by_y, by_both, by_core, by_z = partners(replica, group)
    slot_x, slot_y, slot_both = by_x[1], by_y[1], by_both[1]
    wires = Wires(send, recv, local)
    greet([by_x, by_y, by_core, by_z])
    width = wexp.shape[0]
    block = lambda rel: pl.ds(512 * rel, 512)
    sec_core = wires.go(second, s.at[block(1)], by_core)
    sec_z = wires.go(second, s.at[block(2)], by_z)
    quarter = reduce_shard.at[rows16(400 * quad, 400)]
    spot = lambda rank: rows16(400 * rank, 400)
    red_x = wires.go(quarter, wred.at[spot(group)], by_x)
    red_y = wires.go(quarter, wred.at[spot(group)], by_y)
    load_s = wires.here(second, s.at[block(0)])
    load_e = wires.here(expand_part, wexp)
    load_r = wires.here(quarter, wred.at[spot(group)])
    load_c = wires.here(cots, c)
    sum_out[...] = jnp.zeros_like(sum_out)
    root = 0.7978845608028654

    def gelu(u):
        square = u * u
        t = jnp.tanh(root * u * (1.0 + 0.044715 * square))
        half = 0.5 * (1.0 + t)
        slope = half + (0.5 * root) * u * (1.0 - t * t) * (1.0 + (3.0 * 0.044715) * square)
        return u * half, slope

    def steps(rel, body):
        def one(i, carry):
            body(pl.ds(pl.multiple_of(512 * rel + 256 * i, 256), 256))
            return carry

        lax.fori_loop(0, 2, one, 0)

    def keep_back(rows, low_at, high_at, back):
        back = back.astype(jnp.bfloat16)
        b[rows, low_at:high_at] = back
        sum_out[:, low_at:high_at] += jnp.sum(back.astype(jnp.float32).reshape(32, 8, high_at - low_at), axis=0)

    def up_only(rows):
        entries = s[rows, :width]
        for low_at, high_at in PIECES:
            act, slope = gelu(dot_nn(entries, wexp[:, low_at:high_at]) + bias[:, low_at:high_at])
            a[rows, low_at:high_at] = act.astype(jnp.bfloat16)
            b[rows, low_at:high_at] = slope.astype(jnp.bfloat16)

    def finish_rows(rows):
        gs[rows, width:] = jnp.zeros((256, gs.shape[1] - width), jnp.bfloat16)
        gs[rows, :width] = dot_nt(b[rows, :], wexp[...]).astype(jnp.bfloat16)

    def back_only(rows):
        cot = c[rows, :]
        for low_at, high_at in PIECES:
            keep_back(rows, low_at, high_at, dot_nt(cot, wred[low_at:high_at, :]) * b[rows, low_at:high_at].astype(jnp.float32))
        finish_rows(rows)

    def both(rows):
        entries = s[rows, :width]
        cot = c[rows, :]
        for low_at, high_at in PIECES:
            act, slope = gelu(dot_nn(entries, wexp[:, low_at:high_at]) + bias[:, low_at:high_at])
            a[rows, low_at:high_at] = act.astype(jnp.bfloat16)
            keep_back(rows, low_at, high_at, dot_nt(cot, wred[low_at:high_at, :]) * slope)
        finish_rows(rows)

    load_s.wait()
    load_e.wait()
    steps(0, up_only)
    sec_core.wait_recv()
    steps(1, up_only)
    red_x.wait_recv()
    more_y = wires.go(wred.at[rows16(400 * slot_x, HALF)], wred.at[rows16(400 * slot_x, HALF)], by_y)
    red_y.wait_recv()
    more_x = wires.go(wred.at[rows16(400 * slot_y + HALF, 400 - HALF)], wred.at[rows16(400 * slot_y + HALF, 400 - HALF)], by_x)
    sec_z.wait_recv()
    sec_both = wires.go(s.at[block(2)], s.at[block(3)], by_core)
    load_r.wait()
    load_c.wait()
    more_x.wait_recv()
    more_y.wait_recv()
    wires.keep(wred, reduce_out)
    sec_both.wait_recv()
    wires.keep(s, second_out)
    steps(3, both)
    gs_both = wires.go(gs.at[block(3)], got_core.at[1], by_core)
    steps(2, both)
    gs_both.wait_recv()
    gs[block(2), :] = add_low(gs[block(2), :], got_core[1])
    gs_z = wires.go(gs.at[block(2)], got_z, by_z)
    wires.keep(a, act_out)
    weight_sum(a, c, rg)
    x_copies = [wires.go(rg.at[rows16(400 * slot, HALF)], got_x.at[i], by_x) for i, slot in enumerate((slot_x, slot_both))]
    y_copies = [wires.go(rg.at[rows16(400 * slot + HALF, 400 - HALF)], got_y.at[i], by_y) for i, slot in enumerate((slot_y, slot_both))]
    steps(1, back_only)
    gs_core = wires.go(gs.at[block(1)], got_core.at[0], by_core)
    steps(0, back_only)
    wires.keep(b, back_out)
    gs_core.wait_recv()
    gs_z.wait_recv()
    gs_out[...] = gs[block(0), :width].astype(jnp.float32) + got_core[0, :, :width].astype(jnp.float32) + got_z[:, :width].astype(jnp.float32)
    for copy in x_copies + y_copies:
        copy.wait_recv()
    own_out[:HALF] = add_low(rg[rows16(400 * group, HALF), :], got_x[0])
    own_out[HALF:] = add_low(rg[rows16(400 * group + HALF, 400 - HALF), :], got_y[0])
    pass_out[:HALF] = add_low(rg[rows16(400 * slot_y, HALF), :], got_x[1])
    pass_out[HALF:] = add_low(rg[rows16(400 * slot_x + HALF, 400 - HALF), :], got_y[1])
    wires.finish()


def feed_all(second, cots, expand_part, reduce_shard, bias):
    any_space = pl.BlockSpec(memory_space=pl.ANY)
    vmem = pl.BlockSpec(memory_space=pltpu.VMEM)
    shape = jax.ShapeDtypeStruct
    kind = jnp.bfloat16
    rows, full = second.shape
    width = expand_part.shape[0]
    buf = lambda *dims: pltpu.VMEM(dims, kind)
    return pl.pallas_call(
        feed_all_kernel,
        in_specs=[any_space] * 4 + [vmem],
        out_specs=[any_space] * 4 + [vmem] * 4,
        out_shape=[
            shape((4 * rows, width), kind),
            shape((4 * rows, width), kind),
            shape((4 * rows, full), kind),
            shape((width, width), kind),
            shape((rows, width), jnp.float32),
            shape((400, width), kind),
            shape((400, width), kind),
            shape((8, width), jnp.float32),
        ],
        scratch_shapes=[
            buf(width, width),
            buf(width, width),
            buf(4 * rows, full),
            buf(4 * rows, width),
            buf(4 * rows, width),
            buf(4 * rows, width),
            buf(4 * rows, full),
            buf(2, rows, full),
            buf(rows, full),
            buf(width, width),
            buf(2, HALF, width),
            buf(2, 400 - HALF, width),
            pltpu.SemaphoreType.DMA((16,)),
            pltpu.SemaphoreType.DMA((16,)),
            pltpu.SemaphoreType.DMA((8,)),
        ],
        compiler_params=pltpu.CompilerParams(collective_id=5, has_side_effects=True, vmem_limit_bytes=63 * 2**20),
        cost_estimate=pl.CostEstimate(flops=10**11, bytes_accessed=2**26, transcendentals=0),
        name="feed_all",
    )(second, cots, expand_part, reduce_shard, bias)


def turn_more_kernel(grad_att, back, second, act, wred_in, pass_in, own_in, heads_out, expand_out, result_out, share_out, stage, b, s, a, wred, rg, result, got_core, got_z, got, send, recv, local):
    replica = lax.axis_index("replica")
    group = lax.axis_index("group")
    y = lax.div(group, 2)
    x = lax.rem(group, 2)
    by_x, by_y, by_both, by_core, by_z = partners(replica, group)
    wires = Wires(send, recv, local)
    greet([by_x, by_y, by_both, by_core, by_z])
    width = wred.shape[0]
    block = lambda rel: pl.ds(512 * rel, 512)
    turns = []
    for device in (by_both, by_x, by_y):
        there = device[1]
        turns.append(wires.go(grad_att.at[lax.rem(there, 2), lax.div(there, 2)], heads_out.at[group], device))
    pass_y = wires.go(pass_in.at[pl.ds(0, HALF)], got.at[pl.ds(0, HALF)], by_y)
    pass_x = wires.go(pass_in.at[pl.ds(HALF, 400 - HALF)], got.at[pl.ds(HALF, 400 - HALF)], by_x)
    load_a = wires.here(act, a)
    load_w = wires.here(wred_in, wred)
    load_own = wires.here(grad_att.at[x, y], stage)
    load_s = wires.here(second, s)
    load_b = wires.here(back, b)
    load_own.wait()
    wires.keep(stage, heads_out.at[group])
    load_a.wait()
    load_w.wait()

    def rows_out(rel):
        def one(i, carry):
            rows = pl.ds(pl.multiple_of(512 * rel + 256 * i, 256), 256)
            result[rows, :] = dot_nn(a[rows, :], wred[...]).astype(jnp.bfloat16)
            return carry

        lax.fori_loop(0, 2, one, 0)

    rows_out(3)
    to_both = wires.go(result.at[block(3)], got_core.at[1], by_core)
    rows_out(2)
    to_both.wait_recv()
    result[block(2), :] = add_low(result[block(2), :], got_core[1])
    to_z = wires.go(result.at[block(2)], got_z, by_z)
    rows_out(1)
    to_core = wires.go(result.at[block(1)], got_core.at[0], by_core)
    rows_out(0)
    load_s.wait()
    load_b.wait()
    weight_sum(s, b, rg)
    wires.keep(rg, expand_out)
    pass_y.wait_recv()
    pass_x.wait_recv()
    share_out[...] = add_low(own_in[...], got[...])
    to_core.wait_recv()
    to_z.wait_recv()
    result_out[...] = result[block(0), :].astype(jnp.float32) + got_core[0].astype(jnp.float32) + got_z[...].astype(jnp.float32)
    for copy in turns:
        copy.wait_recv()
    wires.finish()


def turn_more(grad_att, back, second, act, wred, passed, own):
    any_space = pl.BlockSpec(memory_space=pl.ANY)
    vmem = pl.BlockSpec(memory_space=pltpu.VMEM)
    shape = jax.ShapeDtypeStruct
    kind = jnp.bfloat16
    width = wred.shape[0]
    rows = act.shape[0] // 4
    buf = lambda *dims: pltpu.VMEM(dims, kind)
    return pl.pallas_call(
        turn_more_kernel,
        in_specs=[any_space] * 5 + [any_space, vmem],
        out_specs=[any_space, any_space, vmem, vmem],
        out_shape=[
            shape((4,) + grad_att.shape[2:], kind),
            shape((width, width), kind),
            shape((rows, width), jnp.float32),
            shape((400, width), kind),
        ],
        scratch_shapes=[
            buf(*grad_att.shape[2:]),
            buf(4 * rows, width),
            buf(*second.shape),
            buf(4 * rows, width),
            buf(width, width),
            buf(width, width),
            buf(4 * rows, width),
            buf(2, rows, width),
            buf(rows, width),
            buf(400, width),
            pltpu.SemaphoreType.DMA((10,)),
            pltpu.SemaphoreType.DMA((10,)),
            pltpu.SemaphoreType.DMA((8,)),
        ],
        compiler_params=pltpu.CompilerParams(collective_id=2, has_side_effects=True, vmem_limit_bytes=60 * 2**20),
        cost_estimate=pl.CostEstimate(flops=3 * 10**10, bytes_accessed=2**26, transcendentals=0),
        name="turn_more",
    )(grad_att, back, second, act, wred, passed, own)


def on_device(
    inputs,
    segments,
    cotangent,
    project_in,
    project_out,
    expand_weight,
    reduce_weight,
    query_bias,
    value_bias,
    project_bias,
    expand_bias,
    reduce_bias,
    first_gain,
    first_shift,
    second_gain,
    second_shift,
):
    replica, group, z, core, y, x = place()
    quad = lax.rem(replica, 4)
    width = 1600
    rows = 512

    vec = jnp.concatenate(
        [
            jnp.stack([query_bias, value_bias, project_bias, reduce_bias, first_gain, first_shift, second_gain, second_shift]),
            expand_bias.reshape(4, 400),
            jnp.zeros((4, 400), jnp.bfloat16),
        ]
    )
    halves = jnp.stack([head_columns(project_in, 0, 1), head_columns(project_in, 1, 1)])
    x_seq, w_half, vecs, segs, cots = first_exchange(
        inputs, halves, vec, segments[:, None, :], cotangent.reshape(rows, width)
    )
    vecs = wide(vecs)
    names = [vecs[:, k].reshape(width) for k in range(8)]
    bias_query, bias_value, bias_project, bias_reduce, gain_first, shift_first, gain_second, shift_second = names
    bias_expand = lax.dynamic_index_in_dim(vecs, 8 + quad, 1, False).reshape(width)
    segs = segs.reshape(1024)

    x_seq, out_shard, reduce_shard, expand_shard = lax.optimization_barrier(
        (x_seq, project_out, reduce_weight, expand_weight)
    )
    quarter_expand = jnp.concatenate(
        [lax.dynamic_slice_in_dim(expand_shard, 1600 * k + 400 * quad, 400, 1) for k in range(4)], axis=1
    )
    full_out = lax.all_gather(out_shard, "group", axis=0, tiled=True)
    expand_part = lax.all_gather(quarter_expand, "group", axis=0, tiled=True)

    flat_seq = wide(x_seq.reshape(1024, width))
    normed = low(layer_norm(flat_seq, gain_first, shift_first))
    w_half = w_half.reshape(width, 2688)
    pad64 = jnp.zeros((64,), jnp.float32)
    bias_q = lax.dynamic_slice_in_dim(bias_query, 768 * y, 832, 0)
    bias_v = lax.dynamic_slice_in_dim(bias_value, 768 * y, 832, 0)
    bias_mix = jnp.concatenate([bias_q, pad64, jnp.zeros((896,), jnp.float32), bias_v, pad64])
    mixture = low(product(normed, w_half) + bias_mix)
    segc = segs[:, None]
    segr = segs[None]
    attended, lse = heads(mixture, segc, segr)
    att_tokens = turn(attended.reshape(4, 256, 896), True, 1)
    att_tokens = joined(att_tokens[:, 0].reshape(rows, 896), att_tokens[:, 1].reshape(rows, 896))[:, :width]

    flat_input = wide(inputs.reshape(rows, width))
    middle = flat_input + product(att_tokens, full_out) + bias_project
    center = middle - jnp.mean(middle, axis=-1, keepdims=True)
    scale = lax.rsqrt(jnp.mean(center * center, axis=-1, keepdims=True) + epsilon)
    unit = center * scale
    second = padded(low(unit * gain_second + shift_second))

    activated, grad_expanded, second_all, reduce_part, grad_second, own_reduce, pass_reduce, expand_sums = feed_all(
        second, cots.reshape(4 * rows, width), expand_part, reduce_shard, bias_expand[None]
    )

    q = grad_second * gain_second
    grad_middle = wide(cotangent.reshape(rows, width)) + scale * (
        q - jnp.mean(q, axis=-1, keepdims=True) - unit * jnp.mean(q * unit, axis=-1, keepdims=True)
    )
    second_gain_grad = jnp.sum(grad_second * unit, axis=0)
    second_shift_grad = jnp.sum(grad_second, axis=0)
    grad_middle_low = low(grad_middle)
    out_grad = low(weight_term(att_tokens, grad_middle_low)).reshape(4, 400, width)
    out_mine = lax.dynamic_slice_in_dim(out_grad, 192 * core, 208, 1)
    out_given = lax.dynamic_slice_in_dim(out_grad, 192 * (1 - core), 208, 1)
    out_core = low(wide(out_mine) + wide(moved(out_given, FLIP_CORE)))
    out_share = lax.psum_scatter(out_core, "group", scatter_dimension=0, tiled=False)
    grad_att = padded(low(product_back(grad_middle_low, full_out))).reshape(2, 256, 1664)
    lane = lax.broadcasted_iota(jnp.int32, (896,), 0)
    grad_att = jnp.stack(
        [jnp.where(lane < 832, grad_att[..., :896], 0), jnp.where(lane >= 64, grad_att[..., 768:], 0)], axis=1
    )
    grad_heads, expand_grad, result, share_reduce = turn_more(
        grad_att, grad_expanded, second_all, activated, reduce_part, pass_reduce, own_reduce
    )
    outputs = low(result + middle + bias_reduce).reshape(2, 256, width)
    scatter_expand = group_scatter_start([expand_grad.reshape(4, 400, width)], group)
    dq, dk, dv, pair_upper = heads_back(mixture, grad_heads.reshape(1024, 896), attended, lse, segc, segr, share_reduce[:HALF])
    scatter_expand = group_scatter_pass(scatter_expand, dq)
    sum_reduce_upper = low(wide(share_reduce[:HALF]) + wide(pair_upper))
    pair_lower = moved(share_reduce[HALF:], FLIP_PAIR)
    sum_reduce_lower = low(wide(share_reduce[HALF:]) + wide(hold(pair_lower, dq)))
    share_expand, = group_scatter_end(scatter_expand, dq)
    pair_upper = moved(share_expand[0], FLIP_PAIR)
    pair_lower = moved(share_expand[1], FLIP_PAIR)
    grad_mix = jnp.concatenate([dq, dk, dv], axis=1)
    grad_normed = product_back(hold(grad_mix, sum_reduce_lower), w_half)
    sum_expand_upper = low(wide(share_expand[0]) + wide(hold(pair_upper, grad_normed)))
    out_share = padded(out_share)
    flat_center = flat_seq - jnp.mean(flat_seq, axis=-1, keepdims=True)
    flat_unit = flat_center * lax.rsqrt(jnp.mean(flat_center * flat_center, axis=-1, keepdims=True) + epsilon)
    first_gain_grad = jnp.sum(grad_normed * flat_unit, axis=0)
    first_shift_grad = jnp.sum(grad_normed, axis=0)
    in_grad = low(weight_term(normed, grad_mix)).reshape(4, 400, 2688)
    def spread(columns):
        lower = jnp.concatenate([columns[:832], jnp.zeros((768,), jnp.float32)])
        upper = jnp.concatenate([jnp.zeros((832,), jnp.float32), columns[64:832]])
        return jnp.where(y == 0, lower, upper)

    expand_bias_part = jnp.sum(expand_sums, axis=0).reshape(4, 400)
    expand_bias_wide = lax.dynamic_update_slice_in_dim(jnp.zeros((4, width), jnp.float32), expand_bias_part, 400 * quad, 1)
    vectors = jnp.concatenate(
        [
            spread(column_sum(dq)).reshape(4, 400),
            spread(column_sum(dv)).reshape(4, 400),
            column_sum(grad_middle_low).reshape(4, 400),
            column_sum(cotangent.reshape(rows, width)).reshape(4, 400),
            first_gain_grad.reshape(4, 400),
            first_shift_grad.reshape(4, 400),
            second_gain_grad.reshape(4, 400),
            second_shift_grad.reshape(4, 400),
            expand_bias_wide,
        ],
        axis=1,
    )
    vectors = jnp.pad(vectors, ((0, 0), (0, 320))).reshape(4, 40, 128)
    sum_expand_lower = low(wide(share_expand[1]) + wide(hold(pair_lower, in_grad)))
    shares = jnp.concatenate([sum_reduce_upper, sum_reduce_lower, sum_expand_upper, sum_expand_lower]).reshape(2, 400, width)
    grad_total, grad_tokens, vec_total, quads = sum_grads(in_grad, out_share, padded(low(grad_normed)).reshape(4, 256, 1664), vectors, shares)
    vec_total = vec_total.reshape(5120)
    pieces = [vec_total[400 * k : 400 * k + 400] for k in range(8)]
    total_reduce, total_expand = finish_feed(quads)
    total_in, total_out = finish_mixer(grad_total)
    grad_tokens = wide(grad_tokens[..., :width]).reshape(rows, width)
    center1 = flat_input - jnp.mean(flat_input, axis=-1, keepdims=True)
    scale1 = lax.rsqrt(jnp.mean(center1 * center1, axis=-1, keepdims=True) + epsilon)
    unit1 = center1 * scale1
    q1 = grad_tokens * gain_first
    input_grad = grad_middle + scale1 * (
        q1 - jnp.mean(q1, axis=-1, keepdims=True) - unit1 * jnp.mean(q1 * unit1, axis=-1, keepdims=True)
    )
    return (
        outputs,
        input_grad.reshape(2, 256, width),
        total_in,
        total_out,
        total_expand,
        total_reduce,
        pieces[0],
        pieces[1],
        pieces[2],
        vec_total[3200:4800],
        pieces[3],
        pieces[4],
        pieces[5],
        pieces[6],
        pieces[7],
    )


def solution(mesh):
    placed = (
        P("replica", "group", None),
        P("replica", "group"),
        P("replica", "group", None),
        P("group", None),
        P("group", None),
        P("group", None),
        P("group", None),
        P("group"),
        P("group"),
        P("group"),
        P("group"),
        P("group"),
        P("group"),
        P("group"),
        P("group"),
        P("group"),
    )
    return jax.shard_map(
        on_device if dict(mesh.shape) == {"replica": 8, "group": 4} else on_device_any,
        mesh=mesh,
        in_specs=placed,
        out_specs=(
            P("replica", "group", None),
            P("replica", "group", None),
            P("group", None),
            P("group", None),
            P("group", None),
            P("group", None),
            P("group"),
            P("group"),
            P("group"),
            P("group"),
            P("group"),
            P("group"),
            P("group"),
            P("group"),
            P("group"),
        ),
        check_vma=False,
    )
```

```python
import functools
import math

import jax
import jax.numpy as jnp
from jax import lax
from jax.sharding import PartitionSpec as P

from jax.experimental import pallas as pl
from jax.experimental.pallas import tpu as pltpu

HEADS = 25
HEAD_DIM = 64


epsilon = 1e-05
very_low = -1e30


def carried_in(part, axis, combine, identity):
    place = lax.axis_index(axis)
    gathered = lax.all_gather(part, axis)
    state = jnp.zeros_like(part) + jnp.asarray(identity, part.dtype)

    def one(hop, state):
        return combine(state, lax.dynamic_index_in_dim(gathered, hop, 0, False))

    return lax.fori_loop(0, place, one, state)


def layer_norm(entries, gain, shift):
    center = entries - jnp.mean(entries, axis=-1, keepdims=True)
    spread = jnp.mean(center * center, axis=-1, keepdims=True)
    return center * lax.rsqrt(spread + epsilon) * gain + shift


def product(left, right):
    return jnp.dot(left, right, preferred_element_type=jnp.float32)


def product_back(left, right):
    return lax.dot_general(
        left, right, (((1,), (1,)), ((), ())), preferred_element_type=jnp.float32
    )


def weight_term(left, right):
    return lax.dot_general(
        left, right, (((0,), (0,)), ((), ())), preferred_element_type=jnp.float32
    )


def column_sum(entries):
    return jnp.sum(entries.astype(jnp.float32), axis=0)


def block_scores(queries, key_block, offset, query_pos, doc_start):
    block_count = key_block.shape[0]
    key_count = key_block.shape[2]
    scaling = 1.0 / math.sqrt(HEAD_DIM)
    scores = (
        jnp.einsum("schd,pskhd->shcpk", queries, key_block, preferred_element_type=jnp.float32)
        * scaling
    )
    key_pos = (offset + jnp.arange(block_count, dtype=jnp.int32))[:, None] * key_count + jnp.arange(
        key_count, dtype=jnp.int32
    )[None, :]
    allowed = (key_pos[None, None] <= query_pos[None, :, None, None]) & (
        key_pos[None, None] >= doc_start[:, :, None, None]
    )
    allowed = allowed[:, None]
    return (jnp.where(allowed, scores, very_low), allowed)


def attend(running, key_block, value_block, offset, queries, query_pos, doc_start):
    largest, denominator, summed = running
    masked, allowed = block_scores(queries, key_block, offset, query_pos, doc_start)
    fresh = jnp.maximum(largest, jnp.max(masked, axis=(3, 4)))
    shares = jnp.where(allowed, jnp.exp(masked - fresh[..., None, None]), 0.0)
    rescale = jnp.exp(largest - fresh)
    denominator = denominator * rescale + jnp.sum(shares, axis=(3, 4))
    added = jnp.einsum(
        "shcpk,pskhd->schd",
        shares.astype(jnp.bfloat16),
        value_block,
        preferred_element_type=jnp.float32,
    )
    summed = summed * jnp.transpose(rescale, (0, 2, 1))[..., None] + added
    return (fresh, denominator, summed)


def attend_back(
    grad_query,
    key_block,
    value_block,
    offset,
    queries,
    query_pos,
    doc_start,
    log_total,
    grad_low,
    row_dot,
):
    masked, allowed = block_scores(queries, key_block, offset, query_pos, doc_start)
    shares = jnp.where(allowed, jnp.exp(masked - log_total[..., None, None]), 0.0)
    grad_value = jnp.einsum(
        "shcpk,schd->pskhd",
        shares.astype(jnp.bfloat16),
        grad_low,
        preferred_element_type=jnp.float32,
    )
    grad_share = jnp.einsum(
        "schd,pskhd->shcpk", grad_low, value_block, preferred_element_type=jnp.float32
    )
    grad_score = (shares * (grad_share - row_dot[..., None, None])).astype(jnp.bfloat16)
    grad_query = grad_query + jnp.einsum(
        "shcpk,pskhd->schd", grad_score, key_block, preferred_element_type=jnp.float32
    )
    grad_key = jnp.einsum(
        "shcpk,schd->pskhd", grad_score, queries, preferred_element_type=jnp.float32
    )
    return (grad_query, (grad_key, grad_value))


def on_device_any(
    inputs,
    segments,
    cotangent,
    project_in,
    project_out,
    expand_weight,
    reduce_weight,
    query_bias,
    value_bias,
    project_bias,
    expand_bias,
    reduce_bias,
    first_gain,
    first_shift,
    second_gain,
    second_shift,
):
    seq_here, local_len, width = inputs.shape
    groups = lax.axis_size("group")
    total_rows = seq_here * local_len
    head_shape = (seq_here, local_len, HEADS, HEAD_DIM)
    shards = (
        project_in,
        project_out,
        expand_weight,
        reduce_weight,
        query_bias,
        value_bias,
        project_bias,
        expand_bias,
        reduce_bias,
        first_gain,
        first_shift,
        second_gain,
        second_shift,
    )
    whole = (
        lax.all_gather(shards[0], "group", axis=0, tiled=True),
        lax.all_gather(shards[1], "group", axis=0, tiled=True),
        lax.all_gather(shards[2], "group", axis=0, tiled=True),
        lax.all_gather(shards[3], "group", axis=0, tiled=True),
        lax.all_gather(shards[4], "group", axis=0, tiled=True),
        lax.all_gather(shards[5], "group", axis=0, tiled=True),
        lax.all_gather(shards[6], "group", axis=0, tiled=True),
        lax.all_gather(shards[7], "group", axis=0, tiled=True),
        lax.all_gather(shards[8], "group", axis=0, tiled=True),
        lax.all_gather(shards[9], "group", axis=0, tiled=True),
        lax.all_gather(shards[10], "group", axis=0, tiled=True),
        lax.all_gather(shards[11], "group", axis=0, tiled=True),
        lax.all_gather(shards[12], "group", axis=0, tiled=True),
    )
    (
        full_in,
        full_out,
        full_expand,
        full_reduce,
        bias_query,
        bias_value,
        bias_project,
        bias_expand,
        bias_reduce,
        gain_first,
        shift_first,
        gain_second,
        shift_second,
    ) = whole
    group_rank = lax.axis_index("group")
    query_pos = group_rank * local_len + jnp.arange(local_len, dtype=jnp.int32)
    positions = jnp.broadcast_to(query_pos[None, :], (seq_here, local_len))
    end_marks = jnp.where(segments == positions, positions + 1, 0)
    before = carried_in(
        jnp.max(end_marks, axis=1), "group", jnp.maximum, jnp.zeros((seq_here,), jnp.int32)
    )
    inside = lax.cummax(end_marks, axis=1)
    inside = jnp.concatenate([jnp.zeros((seq_here, 1), jnp.int32), inside[:, :-1]], axis=1)
    doc_start = jnp.maximum(before[:, None], inside)
    flat_input = inputs.reshape(total_rows, width).astype(jnp.float32)
    normed_low = layer_norm(
        flat_input, gain_first.astype(jnp.float32), shift_first.astype(jnp.float32)
    ).astype(jnp.bfloat16)
    mixture = product(normed_low, full_in)
    queries = (
        (mixture[:, :width] + bias_query.astype(jnp.float32))
        .astype(jnp.bfloat16)
        .reshape(head_shape)
    )
    key_rows = (
        mixture[:, width : 2 * width].astype(jnp.bfloat16).reshape(seq_here, local_len, width)
    )
    value_rows = (
        (mixture[:, 2 * width :] + bias_value.astype(jnp.float32))
        .astype(jnp.bfloat16)
        .reshape(seq_here, local_len, width)
    )
    initial = (
        jnp.full((seq_here, HEADS, local_len), very_low, jnp.float32),
        jnp.zeros((seq_here, HEADS, local_len), jnp.float32),
        jnp.zeros(head_shape, jnp.float32),
    )
    block_ids = jnp.arange(groups, dtype=jnp.int32)
    running = initial
    pieces = (
        lax.all_gather(key_rows[None], "group", axis=0, tiled=True),
        lax.all_gather(value_rows[None], "group", axis=0, tiled=True),
    )
    piece_count = pieces[0].shape[0]

    def one_piece(state, members):
        key_piece, value_piece, index = members
        updated = attend(
            state,
            key_piece.reshape((1,) + head_shape),
            value_piece.reshape((1,) + head_shape),
            index,
            queries,
            query_pos,
            doc_start,
        )
        return (updated, None)

    running, unused_steps = lax.scan(
        one_piece, running, (pieces[0], pieces[1], jnp.arange(piece_count, dtype=jnp.int32))
    )
    largest, denominator, summed = running
    attended = summed / jnp.transpose(denominator, (0, 2, 1))[..., None]
    log_total = largest + jnp.log(denominator)
    attended_low = attended.reshape(total_rows, width).astype(jnp.bfloat16)
    middle = flat_input + product(attended_low, full_out) + bias_project.astype(jnp.float32)
    second_low = layer_norm(
        middle, gain_second.astype(jnp.float32), shift_second.astype(jnp.float32)
    ).astype(jnp.bfloat16)
    expanded = product(second_low, full_expand) + bias_expand.astype(jnp.float32)
    activated_low = jax.nn.gelu(expanded, approximate=True).astype(jnp.bfloat16)
    result = middle + product(activated_low, full_reduce) + bias_reduce.astype(jnp.float32)
    outputs = result.astype(jnp.bfloat16).reshape(seq_here, local_len, width)
    whole_back = (
        lax.all_gather(shards[0], "group", axis=0, tiled=True),
        lax.all_gather(shards[1], "group", axis=0, tiled=True),
        lax.all_gather(shards[2], "group", axis=0, tiled=True),
        lax.all_gather(shards[3], "group", axis=0, tiled=True),
        lax.all_gather(shards[4], "group", axis=0, tiled=True),
        lax.all_gather(shards[5], "group", axis=0, tiled=True),
        lax.all_gather(shards[6], "group", axis=0, tiled=True),
        lax.all_gather(shards[7], "group", axis=0, tiled=True),
        lax.all_gather(shards[8], "group", axis=0, tiled=True),
        lax.all_gather(shards[9], "group", axis=0, tiled=True),
        lax.all_gather(shards[10], "group", axis=0, tiled=True),
        lax.all_gather(shards[11], "group", axis=0, tiled=True),
        lax.all_gather(shards[12], "group", axis=0, tiled=True),
    )
    keys_back = (
        lax.all_gather(key_rows[None], "group", axis=0, tiled=True),
        lax.all_gather(value_rows[None], "group", axis=0, tiled=True),
    )
    (
        back_in,
        back_out,
        back_expand,
        back_reduce,
        unused_query,
        unused_value,
        unused_project,
        unused_expand,
        unused_reduce,
        back_gain_first,
        back_shift_first,
        back_gain_second,
        back_shift_second,
    ) = whole_back
    grad_rows = cotangent.reshape(total_rows, width).astype(jnp.float32)
    grad_result_low = cotangent.reshape(total_rows, width)
    reduce_bias_grad = column_sum(grad_result_low)
    grad_activated = product_back(grad_result_low, back_reduce)
    unused_gelu, gelu_back = jax.vjp(lambda entry: jax.nn.gelu(entry, approximate=True), expanded)
    grad_expanded_low = gelu_back(grad_activated)[0].astype(jnp.bfloat16)
    expand_bias_grad = column_sum(grad_expanded_low)
    grad_second = product_back(grad_expanded_low, back_expand)
    unused_second, second_back = jax.vjp(
        layer_norm,
        middle,
        back_gain_second.astype(jnp.float32),
        back_shift_second.astype(jnp.float32),
    )
    grad_middle, second_gain_grad, second_shift_grad = second_back(grad_second)
    grad_middle = grad_middle + grad_rows
    reduce_weight_grad = weight_term(activated_low, grad_result_low)
    expand_weight_grad = weight_term(second_low, grad_expanded_low)
    feed_parts = (
        lax.psum_scatter(
            expand_weight_grad.astype(jnp.bfloat16), "group", scatter_dimension=0, tiled=True
        ).astype(jnp.float32),
        lax.psum_scatter(
            reduce_weight_grad.astype(jnp.bfloat16), "group", scatter_dimension=0, tiled=True
        ).astype(jnp.float32),
        lax.psum_scatter(
            expand_bias_grad.astype(jnp.bfloat16), "group", scatter_dimension=0, tiled=True
        ).astype(jnp.float32),
        lax.psum_scatter(
            reduce_bias_grad.astype(jnp.bfloat16), "group", scatter_dimension=0, tiled=True
        ).astype(jnp.float32),
        lax.psum_scatter(
            second_gain_grad.astype(jnp.bfloat16), "group", scatter_dimension=0, tiled=True
        ).astype(jnp.float32),
        lax.psum_scatter(
            second_shift_grad.astype(jnp.bfloat16), "group", scatter_dimension=0, tiled=True
        ).astype(jnp.float32),
    )
    grad_middle_low = grad_middle.astype(jnp.bfloat16)
    project_bias_grad = column_sum(grad_middle_low)
    grad_attended_low = (
        product_back(grad_middle_low, back_out).astype(jnp.bfloat16).reshape(head_shape)
    )
    row_dot = jnp.einsum("schd,schd->shc", grad_attended_low.astype(jnp.float32), attended)

    def back_step(grad_query, members):
        key_piece, value_piece, offset = members
        return attend_back(
            grad_query,
            key_piece.reshape((1,) + head_shape),
            value_piece.reshape((1,) + head_shape),
            offset,
            queries,
            query_pos,
            doc_start,
            log_total,
            grad_attended_low,
            row_dot,
        )

    grad_query, terms = lax.scan(
        back_step, jnp.zeros(head_shape, jnp.float32), (keys_back[0], keys_back[1], block_ids)
    )
    key_terms = terms[0].reshape(groups, seq_here, local_len, width)
    value_terms = terms[1].reshape(groups, seq_here, local_len, width)
    key_grad, value_grad = (
        lax.psum_scatter(
            key_terms.astype(jnp.bfloat16), "group", scatter_dimension=0, tiled=True
        ).astype(jnp.float32),
        lax.psum_scatter(
            value_terms.astype(jnp.bfloat16), "group", scatter_dimension=0, tiled=True
        ).astype(jnp.float32),
    )
    scaling = 1.0 / math.sqrt(HEAD_DIM)
    grad_query_low = (grad_query * scaling).reshape(total_rows, width).astype(jnp.bfloat16)
    grad_key_low = (key_grad * scaling).reshape(total_rows, width).astype(jnp.bfloat16)
    grad_value_low = value_grad.reshape(total_rows, width).astype(jnp.bfloat16)
    query_bias_grad = column_sum(grad_query_low)
    value_bias_grad = column_sum(grad_value_low)
    grad_mixture_low = jnp.concatenate([grad_query_low, grad_key_low, grad_value_low], axis=1)
    grad_normed = product_back(grad_mixture_low, back_in)
    unused_first, first_back = jax.vjp(
        layer_norm,
        flat_input,
        back_gain_first.astype(jnp.float32),
        back_shift_first.astype(jnp.float32),
    )
    grad_entry, first_gain_grad, first_shift_grad = first_back(grad_normed)
    input_grad = (grad_entry + grad_middle).reshape(seq_here, local_len, width)
    project_weight_grad = weight_term(attended_low, grad_middle_low)
    in_weight_grad = weight_term(normed_low, grad_mixture_low)
    mixer_parts = (
        lax.psum_scatter(
            in_weight_grad.astype(jnp.bfloat16), "group", scatter_dimension=0, tiled=True
        ).astype(jnp.float32),
        lax.psum_scatter(
            project_weight_grad.astype(jnp.bfloat16), "group", scatter_dimension=0, tiled=True
        ).astype(jnp.float32),
        lax.psum_scatter(
            query_bias_grad.astype(jnp.bfloat16), "group", scatter_dimension=0, tiled=True
        ).astype(jnp.float32),
        lax.psum_scatter(
            value_bias_grad.astype(jnp.bfloat16), "group", scatter_dimension=0, tiled=True
        ).astype(jnp.float32),
        lax.psum_scatter(
            project_bias_grad.astype(jnp.bfloat16), "group", scatter_dimension=0, tiled=True
        ).astype(jnp.float32),
        lax.psum_scatter(
            first_gain_grad.astype(jnp.bfloat16), "group", scatter_dimension=0, tiled=True
        ).astype(jnp.float32),
        lax.psum_scatter(
            first_shift_grad.astype(jnp.bfloat16), "group", scatter_dimension=0, tiled=True
        ).astype(jnp.float32),
    )
    share_in, share_out, share_expand, share_reduce = (
        mixer_parts[0],
        mixer_parts[1],
        feed_parts[0],
        feed_parts[1],
    )
    share_query, share_value, share_project = (mixer_parts[2], mixer_parts[3], mixer_parts[4])
    share_expand_bias, share_reduce_bias = (feed_parts[2], feed_parts[3])
    share_first_gain, share_first_shift = (mixer_parts[5], mixer_parts[6])
    share_second_gain, share_second_shift = (feed_parts[4], feed_parts[5])
    totals = (
        lax.psum(share_in.astype(jnp.bfloat16), "replica").astype(jnp.float32),
        lax.psum(share_out.astype(jnp.bfloat16), "replica").astype(jnp.float32),
        lax.psum(share_expand.astype(jnp.bfloat16), "replica").astype(jnp.float32),
        lax.psum(share_reduce.astype(jnp.bfloat16), "replica").astype(jnp.float32),
        lax.psum(share_query.astype(jnp.bfloat16), "replica").astype(jnp.float32),
        lax.psum(share_value.astype(jnp.bfloat16), "replica").astype(jnp.float32),
        lax.psum(share_project.astype(jnp.bfloat16), "replica").astype(jnp.float32),
        lax.psum(share_expand_bias.astype(jnp.bfloat16), "replica").astype(jnp.float32),
        lax.psum(share_reduce_bias.astype(jnp.bfloat16), "replica").astype(jnp.float32),
        lax.psum(share_first_gain.astype(jnp.bfloat16), "replica").astype(jnp.float32),
        lax.psum(share_first_shift.astype(jnp.bfloat16), "replica").astype(jnp.float32),
        lax.psum(share_second_gain.astype(jnp.bfloat16), "replica").astype(jnp.float32),
        lax.psum(share_second_shift.astype(jnp.bfloat16), "replica").astype(jnp.float32),
    )
    return (
        outputs,
        input_grad,
        totals[0],
        totals[1],
        totals[2],
        totals[3],
        totals[4],
        totals[5],
        totals[6],
        totals[7],
        totals[8],
        totals[9],
        totals[10],
        totals[11],
        totals[12],
    )


MESH = pl.DeviceIdType.MESH


def flipped(z=0, core=0, y=0, x=0):
    pairs = []
    for me in range(32):
        pairs.append((me, me ^ (8 * z + 4 * core + 2 * y + x)))
    return pairs


FLIP_X = flipped(x=1)
FLIP_Y = flipped(y=1)
FLIP_CORE = flipped(core=1)
FLIP_Z = flipped(z=1)
FLIP_PAIR = flipped(z=2)
INWARD = [(me, me + 8) for me in range(8)] + [(me, me - 8) for me in range(24, 32)]
MIDDLE = [(me, me + 8) for me in range(8, 16)] + [(me, me - 8) for me in range(16, 24)]
OUTWARD = [(me, me - 8) for me in range(8, 16)] + [(me, me + 8) for me in range(16, 24)]


def moved(entries, pairs):
    return lax.ppermute(entries, ("replica", "group"), pairs)


def low(entries):
    return entries.astype(jnp.bfloat16)


def wide(entries):
    return entries.astype(jnp.float32)


def at(entries, index):
    return lax.dynamic_index_in_dim(entries, index, 0, False)


def place():
    replica = lax.axis_index("replica")
    group = lax.axis_index("group")
    core = lax.rem(replica, 2)
    z = lax.div(replica, 2)
    return replica, group, z, core, lax.div(group, 2), lax.rem(group, 2)


def partners(replica, group):
    core = lax.rem(replica, 2)
    z = lax.rem(lax.div(replica, 2), 2)
    y = lax.div(group, 2)
    x = lax.rem(group, 2)
    by_x = (replica, group + 1 - 2 * x)
    by_y = (replica, group + 2 - 4 * y)
    by_both = (replica, group + 3 - 4 * y - 2 * x)
    by_core = (replica + 1 - 2 * core, group)
    by_z = (replica + 2 - 4 * z, group)
    return by_x, by_y, by_both, by_core, by_z


def greet(devices):
    barrier = pltpu.get_barrier_semaphore()
    for device in devices:
        pl.semaphore_signal(barrier, inc=1, device_id=device, device_id_type=MESH)
    pl.semaphore_wait(barrier, len(devices))


def first_exchange_kernel(inp, weights, vec, seg, cot, x_seq, w_full, vecs, segs, cots, send, recv, local, x_stage, w_stage, vec_stage, seg_stage, cot_stage):
    replica = lax.axis_index("replica")
    group = lax.axis_index("group")
    core = lax.rem(replica, 2)
    y = lax.div(group, 2)
    x = lax.rem(group, 2)
    by_x, by_y, by_both, by_core, by_z = partners(replica, group)
    greet((by_x, by_y, by_both, by_core, by_z))
    other_x = 1 - x
    other_y = 1 - y
    slot_x = group + 1 - 2 * x
    slot_y = group + 2 - 4 * y
    slot_both = group + 3 - 4 * y - 2 * x
    mine = pl.ds(pl.multiple_of(core * 192, 16), 208)
    shared = pl.ds(pl.multiple_of(core * 208, 16), 192)
    count = [0]

    def remote(src, dst, device):
        i = count[0]
        count[0] = i + 1
        copy = pltpu.make_async_remote_copy(src_ref=src, dst_ref=dst, send_sem=send.at[i], recv_sem=recv.at[i], device_id=device, device_id_type=MESH)
        copy.start()
        return copy

    small = [
        remote(vec, vecs.at[group], by_x),
        remote(vec, vecs.at[group], by_y),
        remote(vec, vecs.at[group], by_both),
        remote(seg.at[other_x], segs.at[group], by_x),
        remote(seg.at[x], segs.at[group], by_y),
        remote(seg.at[other_x], segs.at[group], by_both),
    ]
    x_block = remote(inp.at[other_x], x_seq.at[group], by_x)
    y_block = remote(inp.at[x], x_seq.at[group], by_y)
    w_x = remote(weights.at[y, mine], w_full.at[group, mine], by_x)
    w_y = remote(weights.at[other_y, mine], w_full.at[group, mine], by_y)
    cot_core = remote(cot, cots.at[1], by_core)
    cot_z = remote(cot, cots.at[2], by_z)
    staged = [
        (inp.at[x], x_stage, x_seq.at[group]),
        (weights.at[y], w_stage, w_full.at[group]),
        (vec, vec_stage, vecs.at[group]),
        (seg.at[x], seg_stage, segs.at[group]),
        (cot, cot_stage, cots.at[0]),
    ]
    loads = [pltpu.make_async_copy(here, stage, local.at[i]) for i, (here, stage, there) in enumerate(staged)]
    own = [pltpu.make_async_copy(stage, there, local.at[5 + i]) for i, (here, stage, there) in enumerate(staged)]
    for copy in loads:
        copy.start()
    for i, copy in enumerate(own):
        loads[i].wait()
        copy.start()
    x_block.wait_recv()
    y_more = remote(x_seq.at[slot_x], x_seq.at[slot_x], by_y)
    w_y.wait_recv()
    w_more = remote(w_full.at[slot_y, mine], w_full.at[slot_y, mine], by_x)
    w_y_core = remote(w_full.at[slot_y, shared], w_full.at[slot_y, shared], by_core)
    w_x.wait_recv()
    w_x_core = remote(w_full.at[slot_x, shared], w_full.at[slot_x, shared], by_core)
    cot_z.wait_recv()
    cot_more = remote(cots.at[2], cots.at[3], by_core)
    w_more.wait_recv()
    w_more_core = remote(w_full.at[slot_both, shared], w_full.at[slot_both, shared], by_core)
    for copy in small + [y_block, y_more, cot_core, cot_more, w_y_core, w_x_core, w_more_core]:
        copy.wait_recv()
    for copy in small + [x_block, y_block, y_more, w_x, w_y, w_more, cot_core, cot_z, cot_more, w_y_core, w_x_core, w_more_core]:
        copy.wait_send()
    for copy in own:
        copy.wait()


def first_exchange(inp, weights, vec, seg, cot):
    any_space = pl.BlockSpec(memory_space=pl.ANY)
    shape = jax.ShapeDtypeStruct
    return pl.pallas_call(
        first_exchange_kernel,
        in_specs=[any_space] * 5,
        out_specs=[any_space] * 5,
        out_shape=[
            shape((4,) + inp.shape[1:], inp.dtype),
            shape((4,) + weights.shape[1:], weights.dtype),
            shape((4,) + vec.shape, vec.dtype),
            shape((4,) + seg.shape[1:], seg.dtype),
            shape((4,) + cot.shape, cot.dtype),
        ],
        scratch_shapes=[
            pltpu.SemaphoreType.DMA((18,)),
            pltpu.SemaphoreType.DMA((18,)),
            pltpu.SemaphoreType.DMA((10,)),
            pltpu.VMEM(inp.shape[1:], inp.dtype),
            pltpu.VMEM(weights.shape[1:], weights.dtype),
            pltpu.VMEM(vec.shape, vec.dtype),
            pltpu.VMEM(seg.shape[1:], seg.dtype),
            pltpu.VMEM(cot.shape, cot.dtype),
        ],
        compiler_params=pltpu.CompilerParams(collective_id=0, has_side_effects=True, vmem_limit_bytes=32 * 2**20),
        name="first_exchange",
    )(inp, weights, vec, seg, cot)


def turn_kernel(forth, src, dst, send, recv, local, stage):
    replica = lax.axis_index("replica")
    group = lax.axis_index("group")
    y = lax.div(group, 2)
    x = lax.rem(group, 2)
    by_x, by_y, by_both, by_core, by_z = partners(replica, group)
    others = (by_both, by_x, by_y)
    greet(others)

    def view(device):
        there = device[1]
        there_y = lax.div(there, 2)
        there_x = lax.rem(there, 2)
        if forth:
            return src.at[there], dst.at[x, y]
        return src.at[there_x, there_y], dst.at[group]

    copies = []
    for i, device in enumerate(others):
        a, b = view(device)
        copies.append(pltpu.make_async_remote_copy(src_ref=a, dst_ref=b, send_sem=send.at[i], recv_sem=recv.at[i], device_id=device, device_id_type=MESH))
    a, b = view((replica, group))
    for copy in copies:
        copy.start()
    load = pltpu.make_async_copy(a, stage, local.at[0])
    own = pltpu.make_async_copy(stage, b, local.at[1])
    load.start()
    load.wait()
    own.start()
    for copy in copies:
        copy.wait()
    own.wait()


def turn(entries, forth, collective):
    any_space = pl.BlockSpec(memory_space=pl.ANY)
    tail = entries.shape[-2:]
    lead = (2, 2) if forth else (4,)
    return pl.pallas_call(
        functools.partial(turn_kernel, forth),
        in_specs=[any_space],
        out_specs=any_space,
        out_shape=jax.ShapeDtypeStruct(lead + tail, entries.dtype),
        scratch_shapes=[pltpu.SemaphoreType.DMA((3,)), pltpu.SemaphoreType.DMA((3,)), pltpu.SemaphoreType.DMA((2,)), pltpu.VMEM(tail, entries.dtype)],
        compiler_params=pltpu.CompilerParams(collective_id=collective, has_side_effects=True),
        cost_estimate=pl.CostEstimate(flops=0, bytes_accessed=60 * 2**20, transcendentals=0),
        name="turn_out" if forth else "turn_back",
    )(entries)


def head_columns(shard, half, axis):
    first = [lax.slice_in_dim(shard, 1600 * k + 768 * half, 1600 * k + 768 * half + 832, axis=axis) for k in range(3)]
    pad = [(0, 0)] * shard.ndim
    pad[axis] = (0, 64)
    return jnp.concatenate([jnp.pad(part, pad) for part in first], axis=axis)


def padded(entries):
    return jnp.pad(entries, [(0, 0)] * (entries.ndim - 1) + [(0, 64)])


def joined(first, other):
    lane = lax.broadcasted_iota(jnp.int32, (1, 128), 1)
    middle = jnp.where(lane < 64, first[..., 768:896], other[..., 0:128])
    return jnp.concatenate([first[..., :768], middle, other[..., 128:]], axis=-1)


def hold(entries, *until):
    return lax.optimization_barrier((entries,) + until)[0]


def finish_feed_kernel(quads_ref, out_expand):
    for k in range(4):
        piece = quads_ref[k].astype(jnp.float32)
        for r in range(4):
            out_expand[:, 1600 * r + 400 * k : 1600 * r + 400 * k + 400] = piece[:, 400 * r : 400 * r + 400]


def finish_feed(quads):
    rows, width = quads.shape[1:]
    step = 80
    return pl.pallas_call(
        finish_feed_kernel,
        grid=(rows // step,),
        in_specs=[pl.BlockSpec((4, step, width), lambda i: (0, i, 0))],
        out_specs=pl.BlockSpec((step, 4 * width), lambda i: (i, 0)),
        out_shape=jax.ShapeDtypeStruct((rows, 4 * width), jnp.float32),
        compiler_params=pltpu.CompilerParams(vmem_limit_bytes=48 * 2**20),
        name="finish_feed",
    )(quads)


def finish_mixer_kernel(total_ref, in_ref, out_ref):
    for k in range(3):
        in_ref[:, 1600 * k : 1600 * k + 1600] = total_ref[k, :, :1600].astype(jnp.float32)
    out_ref[...] = total_ref[3, :, :1600].astype(jnp.float32)


def finish_mixer(total):
    rows = total.shape[1]
    step = 80
    return pl.pallas_call(
        finish_mixer_kernel,
        grid=(rows // step,),
        in_specs=[pl.BlockSpec((4, step, total.shape[2]), lambda i: (0, i, 0))],
        out_specs=[pl.BlockSpec((step, 4800), lambda i: (i, 0)), pl.BlockSpec((step, 1600), lambda i: (i, 0))],
        out_shape=[jax.ShapeDtypeStruct((rows, 4800), jnp.float32), jax.ShapeDtypeStruct((rows, 1600), jnp.float32)],
        compiler_params=pltpu.CompilerParams(vmem_limit_bytes=48 * 2**20),
        name="finish_mixer",
    )(total)


PIECES = ((0, 512), (512, 1024), (1024, 1600))
HALF = 208


class Wires:
    def __init__(self, send, recv, local):
        self.send, self.recv, self.local = send, recv, local
        self.remotes = self.locals = 0
        self.sent = []
        self.kept = []

    def make(self, src, dst, device):
        i = self.remotes
        self.remotes = i + 1
        return pltpu.make_async_remote_copy(src_ref=src, dst_ref=dst, send_sem=self.send.at[i], recv_sem=self.recv.at[i], device_id=device, device_id_type=MESH)

    def go(self, src, dst, device):
        copy = self.make(src, dst, device)
        copy.start()
        self.sent.append(copy)
        return copy

    def here(self, src, dst):
        i = self.locals
        self.locals = i + 1
        copy = pltpu.make_async_copy(src, dst, self.local.at[i])
        copy.start()
        return copy

    def keep(self, src, dst):
        self.kept.append(self.here(src, dst))

    def drain(self, copies):
        for copy in copies:
            copy.wait_send()
        self.sent = [copy for copy in self.sent if all(copy is not done for done in copies)]

    def finish(self):
        for copy in self.sent:
            copy.wait_send()
        for copy in self.kept:
            copy.wait()


def rows16(start, size):
    return pl.ds(pl.multiple_of(start, 16), size)


def dot_tn(a, b):
    return lax.dot_general(a, b, (((0,), (0,)), ((), ())), preferred_element_type=jnp.float32)


def add_low(a, b):
    return (a.astype(jnp.float32) + b.astype(jnp.float32)).astype(jnp.bfloat16)


def weight_sum(a, b, out):
    width = out.shape[0]
    whole = width // 256

    def chunk(j, carry):
        lanes = pl.ds(pl.multiple_of(256 * j, 256), 256)
        out[lanes, :] = dot_tn(a[:, lanes], b[...]).astype(jnp.bfloat16)
        return carry

    lax.fori_loop(0, whole, chunk, 0)
    if width > 256 * whole:
        out[256 * whole :, :] = dot_tn(a[:, 256 * whole : width], b[...]).astype(jnp.bfloat16)


NT = (((1,), (1,)), ((), ()))

def dot_nt(a, b):
    return lax.dot_general(a, b, NT, preferred_element_type=jnp.float32)

def dot_nn(a, b):
    return jnp.dot(a, b, preferred_element_type=jnp.float32)

BLOCK = 256

def heads_kernel(q_ref, k_ref, v_ref, segc_ref, segr_ref, o_ref, lse_ref, ot_ref, vt_ref):
    tile = pl.program_id(0)
    length = q_ref.shape[0]
    blocks = length // BLOCK
    lane = lax.broadcasted_iota(jnp.int32, (1, 128), 1)
    ot_ref[...] = jnp.zeros_like(ot_ref)
    lse_ref[...] = jnp.zeros_like(lse_ref)
    vt_ref[...] = v_ref[...].T

    def head(h):
        k = jnp.where((lane >= 64 * h) & (lane < 64 * h + 64), k_ref[...], jnp.bfloat16(0))
        for i in range(blocks):
            low, high = i * BLOCK, (i + 1) * BLOCK
            q = q_ref[low:high, :] * jnp.bfloat16(0.125)
            s = dot_nt(k[:high], q)
            same = segc_ref[:high, :] == segr_ref[:, low:high]
            kpos = lax.broadcasted_iota(jnp.int32, (high, BLOCK), 0)
            qpos = lax.broadcasted_iota(jnp.int32, (high, BLOCK), 1) + low
            s = jnp.where(same & (kpos <= qpos), s, -1e30)
            m = jnp.max(s, axis=0, keepdims=True)
            p = jnp.exp(s - m)
            l = jnp.sum(p, axis=0, keepdims=True)
            ot = dot_nn(vt_ref[64 * h : 64 * h + 64, :high], p.astype(jnp.bfloat16))
            ot_ref[64 * h : 64 * h + 64, low:high] = ot / l
            lse_ref[0, h : h + 1, low:high] = m + jnp.log(l)

    head(0)

    @pl.when(tile < 6)
    def _():
        head(1)

    o_ref[...] = ot_ref[...].T.astype(jnp.bfloat16)


def heads(qkv, segc, segr):
    length = qkv.shape[0]
    spec = lambda off: pl.BlockSpec((length, 128), lambda t: (0, t + off))
    return pl.pallas_call(
        heads_kernel,
        grid=(7,),
        in_specs=[spec(0), spec(7), spec(14), pl.BlockSpec((length, 1), lambda t: (0, 0)), pl.BlockSpec((1, length), lambda t: (0, 0))],
        out_specs=[pl.BlockSpec((length, 128), lambda t: (0, t)), pl.BlockSpec((1, 8, length), lambda t: (t, 0, 0))],
        out_shape=[jax.ShapeDtypeStruct((length, 896), jnp.bfloat16), jax.ShapeDtypeStruct((7, 8, length), jnp.float32)],
        scratch_shapes=[pltpu.VMEM((128, length), jnp.float32), pltpu.VMEM((128, length), jnp.bfloat16)],
        compiler_params=pltpu.CompilerParams(vmem_limit_bytes=48 * 2**20),
        cost_estimate=pl.CostEstimate(flops=int(13 * 2 * 2 * length * length * 64 * 2), bytes_accessed=8 * length * 896, transcendentals=13 * length * length // 2),
        name="heads",
    )(qkv, qkv, qkv, segc, segr)


def heads_back_kernel(q_ref, k_ref, v_ref, do_ref, o_ref, lse_ref, segc_ref, segr_ref, normed_ref, share_ref, expand_ref, dq_ref, dk_ref, dv_ref, sums_ref, grad_ref, share_out, quads, dqt_ref, odt_ref, pair, own, share_own, passed, got_x, got_y, got, send, recv, local):
    tile = pl.program_id(0)
    replica = lax.axis_index("replica")
    group = lax.axis_index("group")
    quad = lax.rem(replica, 4)
    quad_z = lax.rem(quad + 2, 4)
    by_x, by_y, by_both, by_core, by_z = partners(replica, group)
    by_pair = (lax.rem(replica + 4, 8), group)
    slot_x, slot_y, slot_both = by_x[1], by_y[1], by_both[1]
    wires = Wires(send, recv, local)
    pieces = [pl.ds(0, HALF), pl.ds(HALF, 400 - HALF)]
    pairs = [wires.make(share_ref.at[rows], pair.at[rows], by_pair) for rows in pieces]
    x_copies = [wires.make(expand_ref.at[rows16(400 * slot, HALF)], got_x.at[i], by_x) for i, slot in enumerate((slot_x, slot_both))]
    y_copies = [wires.make(expand_ref.at[rows16(400 * slot + HALF, 400 - HALF)], got_y.at[i], by_y) for i, slot in enumerate((slot_y, slot_both))]
    loads = [
        pltpu.make_async_copy(expand_ref.at[rows16(400 * group, 400)], own, local.at[0]),
        pltpu.make_async_copy(expand_ref.at[rows16(400 * slot_y, HALF)], passed.at[pieces[0]], local.at[1]),
        pltpu.make_async_copy(expand_ref.at[rows16(400 * slot_x + HALF, 400 - HALF)], passed.at[pieces[1]], local.at[2]),
        pltpu.make_async_copy(share_ref, share_own, local.at[3]),
    ]
    keeps = [pltpu.make_async_copy(pair.at[rows], quads.at[quad, rows], local.at[4 + i]) for i, rows in enumerate(pieces)]
    pass_y = wires.make(passed.at[pieces[0]], got.at[pieces[0]], by_y)
    pass_x = wires.make(passed.at[pieces[1]], got.at[pieces[1]], by_x)
    overs = [wires.make(pair.at[rows], quads.at[quad, rows], by_z) for rows in pieces]
    cores = [wires.make(pair.at[rows], quads.at[quad, rows], by_core) for rows in pieces]
    passes = [wires.make(quads.at[quad_z, rows], quads.at[quad_z, rows], by_core) for rows in pieces]

    def spread(i):
        pairs[i].wait()
        rows = pieces[i]
        pair[rows, :] = add_low(pair[rows, :], share_own[rows, :])
        keeps[i].start()
        overs[i].start()
        cores[i].start()

    @pl.when(tile == 0)
    def _():
        greet([by_pair, by_x, by_y, by_core, by_z])
        for copy in [pairs[0]] + x_copies + y_copies + loads:
            copy.start()

    @pl.when(tile == 4)
    def _():
        for copy in loads:
            copy.wait()
        spread(0)
        pairs[1].start()

    length = q_ref.shape[0]
    blocks = length // BLOCK
    lane = lax.broadcasted_iota(jnp.int32, (1, 128), 1)
    dqt_ref[...] = jnp.zeros_like(dqt_ref)
    odt_ref[...] = (do_ref[...].astype(jnp.float32) * o_ref[...].astype(jnp.float32)).T

    def head(h):
        mine = (lane >= 64 * h) & (lane < 64 * h + 64)
        dot_row = jnp.sum(odt_ref[64 * h : 64 * h + 64, :], axis=0, keepdims=True)
        for j in range(blocks):
            low, high = j * BLOCK, (j + 1) * BLOCK
            rest = length - low
            q = q_ref[low:, :] * jnp.bfloat16(0.125)
            do = do_ref[low:, :]
            k = jnp.where(mine, k_ref[low:high, :], jnp.bfloat16(0))
            v = jnp.where(mine, v_ref[low:high, :], jnp.bfloat16(0))
            s = dot_nt(k, q)
            same = segc_ref[low:high, :] == segr_ref[:, low:]
            kpos = lax.broadcasted_iota(jnp.int32, (BLOCK, rest), 0)
            qpos = lax.broadcasted_iota(jnp.int32, (BLOCK, rest), 1)
            p = jnp.where(same & (kpos <= qpos), jnp.exp(s - lse_ref[0, h : h + 1, low:]), 0.0)
            dp = dot_nt(v, do)
            ds = (p * (dp - dot_row[:, low:])).astype(jnp.bfloat16)
            dv = dot_nn(p.astype(jnp.bfloat16), do)
            dk = dot_nn(ds, q)
            if h == 0:
                dv_ref[low:high, :] = jnp.where(mine, dv, 0.0).astype(jnp.bfloat16)
                dk_ref[low:high, :] = jnp.where(mine, dk, 0.0).astype(jnp.bfloat16)
            else:
                dv_ref[low:high, :] = jnp.where(mine, dv.astype(jnp.bfloat16), dv_ref[low:high, :])
                dk_ref[low:high, :] = jnp.where(mine, dk.astype(jnp.bfloat16), dk_ref[low:high, :])
            dqt_ref[:, low:] += dot_nn(k.T, ds)

    head(0)

    @pl.when(tile < 6)
    def _():
        head(1)

    dq_ref[...] = (dqt_ref[...].T * 0.125).astype(jnp.bfloat16)

    row = lax.broadcasted_iota(jnp.int32, (8, 128), 0)
    sum_q = jnp.sum(dq_ref[...].astype(jnp.float32), axis=0, keepdims=True)
    sum_v = jnp.sum(dv_ref[...].astype(jnp.float32), axis=0, keepdims=True)
    sums_ref[...] = jnp.where(row == 0, sum_q, jnp.where(row == 1, sum_v, 0.0))

    for i, part_ref in enumerate((dq_ref, dk_ref, dv_ref)):
        grad_ref[i] = dot_tn(normed_ref[...], part_ref[...]).astype(jnp.bfloat16)

    @pl.when(tile == 6)
    def _():
        for copy in x_copies + y_copies:
            copy.wait()
        passed[:HALF] = add_low(passed[:HALF], got_x[1])
        passed[HALF:] = add_low(passed[HALF:], got_y[1])
        pass_y.start()
        pass_x.start()
        own[:HALF] = add_low(own[:HALF], got_x[0])
        own[HALF:] = add_low(own[HALF:], got_y[0])
        overs[0].wait_recv()
        passes[0].start()
        spread(1)
        pass_y.wait()
        pass_x.wait()
        share_out[...] = add_low(own[...], got[...])
        overs[1].wait_recv()
        passes[1].start()
        for copy in cores + passes + keeps:
            copy.wait()
        for copy in overs:
            copy.wait_send()


def heads_back(qkv, grad, out, lse, segc, segr, normed, share, expand):
    length = qkv.shape[0]
    width = share.shape[1]
    buf = lambda *dims: pltpu.VMEM(dims, jnp.bfloat16)
    still = lambda *dims: pl.BlockSpec(dims, lambda t: (0,) * len(dims))
    spec = lambda off: pl.BlockSpec((length, 128), lambda t: (0, t + off))
    one = pl.BlockSpec((length, 128), lambda t: (0, t))
    shape = jax.ShapeDtypeStruct((length, 896), jnp.bfloat16)
    return pl.pallas_call(
        heads_back_kernel,
        grid=(7,),
        in_specs=[spec(0), spec(7), spec(14), one, one, pl.BlockSpec((1, 8, length), lambda t: (t, 0, 0)), pl.BlockSpec((length, 1), lambda t: (0, 0)), pl.BlockSpec((1, length), lambda t: (0, 0)), still(*normed.shape), pl.BlockSpec(memory_space=pl.ANY), pl.BlockSpec(memory_space=pl.ANY)],
        out_specs=[one, one, one, pl.BlockSpec((8, 128), lambda t: (0, t)), pl.BlockSpec((3, width, 128), lambda t: (0, 0, t)), still(*share.shape), pl.BlockSpec(memory_space=pl.ANY)],
        out_shape=[
            shape,
            shape,
            shape,
            jax.ShapeDtypeStruct((8, 896), jnp.float32),
            jax.ShapeDtypeStruct((3, width, 896), jnp.bfloat16),
            jax.ShapeDtypeStruct(share.shape, share.dtype),
            jax.ShapeDtypeStruct((4,) + share.shape, share.dtype),
        ],
        scratch_shapes=[pltpu.VMEM((128, length), jnp.float32), pltpu.VMEM((128, length), jnp.float32), buf(400, width), buf(400, width), buf(400, width), buf(400, width), buf(2, HALF, width), buf(2, 400 - HALF, width), buf(400, width), pltpu.SemaphoreType.DMA((14,)), pltpu.SemaphoreType.DMA((14,)), pltpu.SemaphoreType.DMA((6,))],
        compiler_params=pltpu.CompilerParams(vmem_limit_bytes=56 * 2**20, collective_id=4, has_side_effects=True),
        cost_estimate=pl.CostEstimate(flops=int(13 * 5 * 2 * length * length * 64 * 2), bytes_accessed=16 * length * 896, transcendentals=13 * length * length // 2),
        name="heads_back",
    )(qkv, qkv, qkv, grad, out, lse, segc, segr, normed, share, expand)

def feed_all_kernel(second, cots, expand_part, reduce_shard, bias, act_out, back_out, second_out, reduce_out, gs_out, own_out, pass_out, sum_out, wexp, wred, s, c, a, b, gs, got_core, got_z, rg, got_x, got_y, send, recv, local):
    replica = lax.axis_index("replica")
    group = lax.axis_index("group")
    quad = lax.rem(replica, 4)
    y = lax.div(group, 2)
    x = lax.rem(group, 2)
    by_x, by_y, by_both, by_core, by_z = partners(replica, group)
    slot_x, slot_y, slot_both = by_x[1], by_y[1], by_both[1]
    wires = Wires(send, recv, local)
    greet([by_x, by_y, by_core, by_z])
    width = wexp.shape[0]
    block = lambda rel: pl.ds(512 * rel, 512)
    sec_core = wires.go(second, s.at[block(1)], by_core)
    sec_z = wires.go(second, s.at[block(2)], by_z)
    quarter = reduce_shard.at[rows16(400 * quad, 400)]
    spot = lambda rank: rows16(400 * rank, 400)
    red_x = wires.go(quarter, wred.at[spot(group)], by_x)
    red_y = wires.go(quarter, wred.at[spot(group)], by_y)
    load_s = wires.here(second, s.at[block(0)])
    load_e = wires.here(expand_part, wexp)
    load_r = wires.here(quarter, wred.at[spot(group)])
    load_c = wires.here(cots, c)
    sum_out[...] = jnp.zeros_like(sum_out)
    root = 0.7978845608028654

    def gelu(u):
        square = u * u
        t = jnp.tanh(root * u * (1.0 + 0.044715 * square))
        half = 0.5 * (1.0 + t)
        slope = half + (0.5 * root) * u * (1.0 - t * t) * (1.0 + (3.0 * 0.044715) * square)
        return u * half, slope

    def steps(rel, body):
        def one(i, carry):
            body(pl.ds(pl.multiple_of(512 * rel + 256 * i, 256), 256))
            return carry

        lax.fori_loop(0, 2, one, 0)

    def keep_back(rows, low_at, high_at, back):
        back = back.astype(jnp.bfloat16)
        b[rows, low_at:high_at] = back
        sum_out[:, low_at:high_at] += jnp.sum(back.astype(jnp.float32).reshape(32, 8, high_at - low_at), axis=0)

    def up_only(rows):
        entries = s[rows, :width]
        for low_at, high_at in PIECES:
            act, slope = gelu(dot_nn(entries, wexp[:, low_at:high_at]) + bias[:, low_at:high_at])
            a[rows, low_at:high_at] = act.astype(jnp.bfloat16)
            b[rows, low_at:high_at] = slope.astype(jnp.bfloat16)

    def finish_rows(rows):
        gs[rows, width:] = jnp.zeros((256, gs.shape[1] - width), jnp.bfloat16)
        gs[rows, :width] = dot_nt(b[rows, :], wexp[...]).astype(jnp.bfloat16)

    def back_only(rows):
        cot = c[rows, :]
        for low_at, high_at in PIECES:
            keep_back(rows, low_at, high_at, dot_nt(cot, wred[low_at:high_at, :]) * b[rows, low_at:high_at].astype(jnp.float32))
        finish_rows(rows)

    def both(rows):
        entries = s[rows, :width]
        cot = c[rows, :]
        for low_at, high_at in PIECES:
            act, slope = gelu(dot_nn(entries, wexp[:, low_at:high_at]) + bias[:, low_at:high_at])
            a[rows, low_at:high_at] = act.astype(jnp.bfloat16)
            keep_back(rows, low_at, high_at, dot_nt(cot, wred[low_at:high_at, :]) * slope)
        finish_rows(rows)

    load_s.wait()
    load_e.wait()
    steps(0, up_only)
    sec_core.wait_recv()
    steps(1, up_only)
    red_x.wait_recv()
    more_y = wires.go(wred.at[rows16(400 * slot_x, HALF)], wred.at[rows16(400 * slot_x, HALF)], by_y)
    red_y.wait_recv()
    more_x = wires.go(wred.at[rows16(400 * slot_y + HALF, 400 - HALF)], wred.at[rows16(400 * slot_y + HALF, 400 - HALF)], by_x)
    sec_z.wait_recv()
    sec_both = wires.go(s.at[block(2)], s.at[block(3)], by_core)
    load_r.wait()
    load_c.wait()
    more_x.wait_recv()
    more_y.wait_recv()
    wires.keep(wred, reduce_out)
    sec_both.wait_recv()
    wires.keep(s, second_out)
    steps(3, both)
    gs_both = wires.go(gs.at[block(3)], got_core.at[1], by_core)
    steps(2, both)
    gs_both.wait_recv()
    gs[block(2), :] = add_low(gs[block(2), :], got_core[1])
    gs_z = wires.go(gs.at[block(2)], got_z, by_z)
    wires.keep(a, act_out)
    weight_sum(a, c, rg)
    x_copies = [wires.go(rg.at[rows16(400 * slot, HALF)], got_x.at[i], by_x) for i, slot in enumerate((slot_x, slot_both))]
    y_copies = [wires.go(rg.at[rows16(400 * slot + HALF, 400 - HALF)], got_y.at[i], by_y) for i, slot in enumerate((slot_y, slot_both))]
    steps(1, back_only)
    gs_core = wires.go(gs.at[block(1)], got_core.at[0], by_core)
    steps(0, back_only)
    wires.keep(b, back_out)
    gs_core.wait_recv()
    gs_z.wait_recv()
    gs_out[...] = gs[block(0), :width].astype(jnp.float32) + got_core[0, :, :width].astype(jnp.float32) + got_z[:, :width].astype(jnp.float32)
    for copy in x_copies + y_copies:
        copy.wait_recv()
    own_out[:HALF] = add_low(rg[rows16(400 * group, HALF), :], got_x[0])
    own_out[HALF:] = add_low(rg[rows16(400 * group + HALF, 400 - HALF), :], got_y[0])
    pass_out[:HALF] = add_low(rg[rows16(400 * slot_y, HALF), :], got_x[1])
    pass_out[HALF:] = add_low(rg[rows16(400 * slot_x + HALF, 400 - HALF), :], got_y[1])
    wires.finish()


def feed_all(second, cots, expand_part, reduce_shard, bias):
    any_space = pl.BlockSpec(memory_space=pl.ANY)
    vmem = pl.BlockSpec(memory_space=pltpu.VMEM)
    shape = jax.ShapeDtypeStruct
    kind = jnp.bfloat16
    rows, full = second.shape
    width = expand_part.shape[0]
    buf = lambda *dims: pltpu.VMEM(dims, kind)
    return pl.pallas_call(
        feed_all_kernel,
        in_specs=[any_space] * 4 + [vmem],
        out_specs=[any_space] * 4 + [vmem] * 4,
        out_shape=[
            shape((4 * rows, width), kind),
            shape((4 * rows, width), kind),
            shape((4 * rows, full), kind),
            shape((width, width), kind),
            shape((rows, width), jnp.float32),
            shape((400, width), kind),
            shape((400, width), kind),
            shape((8, width), jnp.float32),
        ],
        scratch_shapes=[
            buf(width, width),
            buf(width, width),
            buf(4 * rows, full),
            buf(4 * rows, width),
            buf(4 * rows, width),
            buf(4 * rows, width),
            buf(4 * rows, full),
            buf(2, rows, full),
            buf(rows, full),
            buf(width, width),
            buf(2, HALF, width),
            buf(2, 400 - HALF, width),
            pltpu.SemaphoreType.DMA((16,)),
            pltpu.SemaphoreType.DMA((16,)),
            pltpu.SemaphoreType.DMA((8,)),
        ],
        compiler_params=pltpu.CompilerParams(collective_id=5, has_side_effects=True, vmem_limit_bytes=63 * 2**20),
        cost_estimate=pl.CostEstimate(flops=10**11, bytes_accessed=2**26, transcendentals=0),
        name="feed_all",
    )(second, cots, expand_part, reduce_shard, bias)


def turn_more_kernel(grad_att, back, second, act, wred_in, pass_in, att_in, grad_in, own_in, heads_out, expand_out, result_out, share_out, core_out, att, grad, got_rows, stage, b, s, a, wred, rg, result, got_core, got_z, got, send, recv, local):
    replica = lax.axis_index("replica")
    group = lax.axis_index("group")
    y = lax.div(group, 2)
    x = lax.rem(group, 2)
    by_x, by_y, by_both, by_core, by_z = partners(replica, group)
    wires = Wires(send, recv, local)
    greet([by_x, by_y, by_both, by_core, by_z])
    width = wred.shape[0]
    block = lambda rel: pl.ds(512 * rel, 512)
    turns = []
    for device in (by_both, by_x, by_y):
        there = device[1]
        turns.append(wires.go(grad_att.at[lax.rem(there, 2), lax.div(there, 2)], heads_out.at[group], device))
    pass_y = wires.go(pass_in.at[pl.ds(0, HALF)], got.at[pl.ds(0, HALF)], by_y)
    pass_x = wires.go(pass_in.at[pl.ds(HALF, 400 - HALF)], got.at[pl.ds(HALF, 400 - HALF)], by_x)
    load_a = wires.here(act, a)
    load_w = wires.here(wred_in, wred)
    load_own = wires.here(grad_att.at[x, y], stage)
    load_s = wires.here(second, s)
    load_b = wires.here(back, b)
    load_att = wires.here(att_in, att)
    load_grad = wires.here(grad_in, grad)
    load_own.wait()
    wires.keep(stage, heads_out.at[group])
    load_a.wait()
    load_w.wait()

    def rows_out(rel):
        def one(i, carry):
            rows = pl.ds(pl.multiple_of(512 * rel + 256 * i, 256), 256)
            result[rows, :] = dot_nn(a[rows, :], wred[...]).astype(jnp.bfloat16)
            return carry

        lax.fori_loop(0, 2, one, 0)

    rows_out(3)
    to_both = wires.go(result.at[block(3)], got_core.at[1], by_core)
    rows_out(2)
    to_both.wait_recv()
    result[block(2), :] = add_low(result[block(2), :], got_core[1])
    to_z = wires.go(result.at[block(2)], got_z, by_z)
    rows_out(1)
    to_core = wires.go(result.at[block(1)], got_core.at[0], by_core)
    rows_out(0)
    load_att.wait()
    load_grad.wait()
    weight_sum(att, grad, wred)
    core = lax.rem(replica, 2)
    out_core = [wires.go(wred.at[rows16(400 * r + 192 * (1 - core), 208)], got_rows.at[r], by_core) for r in range(4)]
    load_s.wait()
    load_b.wait()
    weight_sum(s, b, rg)
    wires.keep(rg, expand_out)
    for r in range(4):
        out_core[r].wait_recv()
        core_out[r] = add_low(wred[rows16(400 * r + 192 * core, 208), :], got_rows[r])
    pass_y.wait_recv()
    pass_x.wait_recv()
    share_out[...] = add_low(own_in[...], got[...])
    to_core.wait_recv()
    to_z.wait_recv()
    result_out[...] = result[block(0), :].astype(jnp.float32) + got_core[0].astype(jnp.float32) + got_z[...].astype(jnp.float32)
    for copy in turns:
        copy.wait_recv()
    wires.finish()


def turn_more(grad_att, back, second, act, wred, passed, att, grad, own):
    any_space = pl.BlockSpec(memory_space=pl.ANY)
    vmem = pl.BlockSpec(memory_space=pltpu.VMEM)
    shape = jax.ShapeDtypeStruct
    kind = jnp.bfloat16
    width = wred.shape[0]
    rows = act.shape[0] // 4
    buf = lambda *dims: pltpu.VMEM(dims, kind)
    return pl.pallas_call(
        turn_more_kernel,
        in_specs=[any_space] * 8 + [vmem],
        out_specs=[any_space, any_space, vmem, vmem, vmem],
        out_shape=[
            shape((4,) + grad_att.shape[2:], kind),
            shape((width, width), kind),
            shape((rows, width), jnp.float32),
            shape((400, width), kind),
            shape((4, 208, width), kind),
        ],
        scratch_shapes=[
            buf(rows, width),
            buf(rows, width),
            buf(4, 208, width),
            buf(*grad_att.shape[2:]),
            buf(4 * rows, width),
            buf(*second.shape),
            buf(4 * rows, width),
            buf(width, width),
            buf(width, width),
            buf(4 * rows, width),
            buf(2, rows, width),
            buf(rows, width),
            buf(400, width),
            pltpu.SemaphoreType.DMA((14,)),
            pltpu.SemaphoreType.DMA((14,)),
            pltpu.SemaphoreType.DMA((10,)),
        ],
        compiler_params=pltpu.CompilerParams(collective_id=2, has_side_effects=True, vmem_limit_bytes=62 * 2**20),
        cost_estimate=pl.CostEstimate(flops=3 * 10**10, bytes_accessed=2**26, transcendentals=0),
        name="turn_more",
    )(grad_att, back, second, act, wred, passed, att, grad, own)


def arrive(here, there, total, lane, k, y, mine):
    first = jnp.where(y == 0, here, there)
    other = jnp.where(y == 0, there, here)
    rows = pl.ds(mine, 208)
    total[k, rows, 0:768] = first[:, 0:768]
    total[k, rows, 768:896] = jnp.where(lane < 64, first[:, 768:896], other[:, 0:128])
    total[k, rows, 896:1664] = other[:, 128:896]


def last_kernel(dq, dk, dv, grad_in, w_in, share_in, share_expand, vec, gm_in, inp_in, gain, total, grad_out, vec_total, wide_total, quads, d, w, part, c_buf, x_buf, y_buf, line_buf, line_mid, gn, gn_y, gn_cross, inp, pair_buf, vec_got, vec_own, vec_core, vec_z, more_got, more_core, more_z, send, recv, local):
    replica = lax.axis_index("replica")
    group = lax.axis_index("group")
    core = lax.rem(replica, 2)
    quad = lax.rem(replica, 4)
    quad_z = lax.rem(quad + 2, 4)
    z = lax.div(replica, 2)
    y = lax.div(group, 2)
    x = lax.rem(group, 2)
    by_x, by_y, by_both, by_core, by_z = partners(replica, group)
    outer = (z == 0) | (z == 3)
    inner = jnp.logical_not(outer)
    by_line = (jnp.where(z == 0, replica + 2, jnp.where(z == 3, replica - 2, jnp.where(z == 1, replica - 2, replica + 2))), group)
    by_middle = (jnp.where(z == 1, replica + 2, replica - 2), group)
    lines_z = [(lax.rem(replica + 2 * k, 8), group) for k in (1, 2, 3)]
    by_pair = lines_z[1]
    wires = Wires(send, recv, local)
    greet([by_x, by_y, by_both, by_core] + lines_z)
    mine = pl.multiple_of(192 * core, 16)
    theirs = pl.multiple_of(192 * (1 - core), 16)
    other_x = 1 - x
    other_y = 1 - y
    far = 2 * other_y
    near = 2 * y
    width = w.shape[0]
    lane = lax.broadcasted_iota(jnp.int32, (1, 128), 1)
    halves = [(pl.ds(mine + 112 * m, 112 - 16 * m), pl.ds(112 * m, 112 - 16 * m)) for m in range(2)]
    pieces = [pl.ds(0, 208), pl.ds(208, 192)]

    pairs = [wires.go(share_expand.at[rows], pair_buf.at[rows], by_pair) for rows in pieces]
    c_copies = []
    part_loads = []
    for k in range(3):
        c_copies.append([wires.go(grad_in.at[k, rows16(400 * r + theirs, 208)], c_buf.at[k, r], by_core) for r in range(4)])
        part_loads.append([wires.here(grad_in.at[k, pl.ds(400 * r + mine, 208)], part.at[k, r]) for r in range(4)])
    loads = [wires.here(part, d.at[k]) for k, part in enumerate((dq, dk, dv))]
    load_w = wires.here(w_in, w)
    load_share = wires.here(share_in, total.at[3, pl.ds(mine, 208)])
    vec_group = [wires.go(vec.at[device[1]], vec_got.at[group], device) for device in (by_x, by_y, by_both)]

    def spread(value, rows):
        wires.keep(value, quads.at[quad, rows])
        over = wires.go(value, quads.at[quad, rows], by_z)
        return over, wires.go(value, quads.at[quad, rows], by_core)

    def spread_on(over, rows):
        over.wait_recv()
        return wires.go(quads.at[quad_z, rows], quads.at[quad_z, rows], by_core)

    load_gm = wires.here(gm_in, grad_out)
    load_inp = wires.here(inp_in, inp)

    def line(k):
        states = []
        for rows, merge in halves:
            into = wires.make(total.at[k, rows], line_buf.at[k, merge], by_line)
            middle = wires.make(total.at[k, rows], line_mid.at[k, merge], by_middle)
            back = wires.make(total.at[k, rows], line_buf.at[k, merge], by_line)

            @pl.when(outer)
            def _():
                into.start()

            states.append((rows, merge, into, middle, back))
        lines[k] = states

    def line_second(k):
        for rows, merge, into, middle, back in lines[k]:
            @pl.when(inner)
            def _():
                into.wait_recv()
                total[k, rows] = add_low(total[k, rows], line_buf[k, merge])
                middle.start()

    def line_third(k):
        for rows, merge, into, middle, back in lines[k]:
            @pl.when(inner)
            def _():
                middle.wait_recv()
                middle.wait_send()
                total[k, rows] = add_low(total[k, rows], line_mid[k, merge])
                back.start()

    def line_fourth(k):
        for rows, merge, into, middle, back in lines[k]:
            @pl.when(outer)
            def _():
                into.wait_send()
                back.wait_recv()
                total[k, rows] = line_buf[k, merge]

            @pl.when(inner)
            def _():
                back.wait_send()

    lines = {}
    x_copies = {}
    y_copies = {}

    def core_sum(k):
        for r in range(4):
            part_loads[k][r].wait()
            c_copies[k][r].wait_recv()
            c_buf[k, r] = add_low(c_buf[k, r], part[k, r])

    def x_start(k):
        x_copies[k] = [wires.go(c_buf.at[k, 2 * row + other_x], x_buf.at[k, i], by_x) for i, row in enumerate((other_y, y))]

    def x_sum(k):
        x_copies[k][0].wait_recv()
        c_buf[k, far + x] = add_low(c_buf[k, far + x], x_buf[k, 0])
        y_copies[k] = wires.go(c_buf.at[k, far + x], y_buf.at[k], by_y)
        x_copies[k][1].wait_recv()
        c_buf[k, near + x] = add_low(c_buf[k, near + x], x_buf[k, 1])

    def y_done(k):
        y_copies[k].wait_recv()
        arrive(c_buf[k, near + x], y_buf[k], total, lane, k, y, mine)
        line(k)

    def normed_grad(b):
        rows = pl.ds(pl.multiple_of(256 * b, 256), 256)
        value = dot_nt(d[0, rows, :], w[:, 0:896]) + dot_nt(d[1, rows, :], w[:, 896:1792]) + dot_nt(d[2, rows, :], w[:, 1792:2688])
        gn[b] = value.astype(jnp.bfloat16)

    core_sum(0)
    x_start(0)
    core_sum(1)
    core_sum(2)
    load_share.wait()
    line(3)
    for copy in loads + [load_w]:
        copy.wait()
    normed_grad(far + other_x)
    y_pass = wires.go(gn.at[far + other_x], gn_y.at[0], by_y)
    normed_grad(near + other_x)
    wires.drain(x_copies[0])
    x_start(1)
    x_sum(0)
    line_second(3)
    normed_grad(far + x)
    for copy in vec_group:
        copy.wait_recv()
    vec_got[group] = vec[group]
    vec_own[...] = (vec_got[0] + vec_got[1]) + (vec_got[2] + vec_got[3])
    vec_pass = wires.go(vec_own, vec_core, by_core)
    y_done(0)
    wires.drain(x_copies[1])
    x_start(2)
    x_sum(1)
    y_keep = wires.go(gn.at[far + x], gn_y.at[1], by_y)
    normed_grad(near + x)
    line_third(3)
    y_done(1)
    line_second(0)
    y_pass.wait_recv()
    gn_y[0] = add_low(gn_y[0], gn[near + other_x])
    vec_pass.wait_recv()
    vec_z[z] = vec_own[...] + vec_core[...]
    vec_line = [wires.go(vec_z.at[z], vec_z.at[z], device) for device in lines_z]
    wires.drain(x_copies[2])
    cross = wires.go(gn_y.at[0], gn_cross, by_x)
    x_sum(2)
    spread_expand = []
    for i, rows in enumerate(pieces):
        pairs[i].wait_recv()
        pair_buf[rows, :] = add_low(pair_buf[rows, :], share_expand[rows, :])
        spread_expand.append(spread(pair_buf.at[rows], rows))
    y_done(2)
    line_third(0)
    line_second(1)

    y_keep.wait_recv()
    load_gm.wait()
    load_inp.wait()

    def norm_back(seq, grad):
        entries = inp[seq].astype(jnp.float32)
        center = entries - jnp.mean(entries, axis=-1, keepdims=True)
        scale = lax.rsqrt(jnp.mean(center * center, axis=-1, keepdims=True) + epsilon)
        unit = center * scale
        q = grad * gain[...]
        grad_out[seq] += scale * (q - jnp.mean(q, axis=-1, keepdims=True) - unit * jnp.mean(q * unit, axis=-1, keepdims=True))
        return jnp.sum(grad * unit, axis=0, keepdims=True), jnp.sum(grad, axis=0, keepdims=True)

    own_gain, own_shift = norm_back(x, gn_y[1].astype(jnp.float32) + gn[near + x].astype(jnp.float32))
    line_second(2)
    line_third(1)
    cross.wait_recv()
    cross_gain, cross_shift = norm_back(other_x, gn_cross[...].astype(jnp.float32))
    more_got[group] = jnp.zeros(more_got.shape[1:], jnp.float32)
    more_got[group, 0:1, 0:width] = own_gain + cross_gain
    more_got[group, 1:2, 0:width] = own_shift + cross_shift
    more_group = [wires.go(more_got.at[group], more_got.at[group], device) for device in (by_x, by_y, by_both)]
    for copy in more_group:
        copy.wait_recv()
    more_z[z] = (more_got[0] + more_got[1]) + (more_got[2] + more_got[3])
    more_pass = wires.go(more_z.at[z], more_core, by_core)
    line_third(2)
    more_pass.wait_recv()
    wires.drain([more_pass])
    more_z[z] = more_z[z] + more_core[...]
    more_line = [wires.go(more_z.at[z], more_z.at[z], device) for device in lines_z]
    for copy in vec_line:
        copy.wait_recv()
    vec_total[...] = (vec_z[0] + vec_z[1]) + (vec_z[2] + vec_z[3])
    passes = [spread_on(spread_expand[i][0], rows) for i, rows in enumerate(pieces)]
    last = []
    for k in (3, 0, 1, 2):
        line_fourth(k)
        rows = pl.ds(pl.multiple_of(208 * core, 16), 192)
        last.append(wires.go(total.at[k, rows], total.at[k, rows], by_core))
    for copy in more_line:
        copy.wait_recv()
    wide_total[...] = (more_z[0] + more_z[1]) + (more_z[2] + more_z[3])
    for copy in last + passes + [both for over, both in spread_expand]:
        copy.wait_recv()
    wires.finish()


def last_sums(dq, dk, dv, in_grad, w_half, out_share, share_expand, vec, grad_middle, inputs, gain):
    any_space = pl.BlockSpec(memory_space=pl.ANY)
    vmem = pl.BlockSpec(memory_space=pltpu.VMEM)
    shape = jax.ShapeDtypeStruct
    kind = jnp.bfloat16
    width = w_half.shape[0]
    buf = lambda *dims: pltpu.VMEM(dims, kind)
    flat = lambda *dims: pltpu.VMEM(dims, jnp.float32)
    return pl.pallas_call(
        last_kernel,
        in_specs=[any_space] * 6 + [vmem, vmem, any_space, any_space, vmem],
        out_specs=[vmem, vmem, vmem, vmem, any_space],
        out_shape=[
            shape((4, 400, 1664), kind),
            shape(grad_middle.shape, jnp.float32),
            shape(vec.shape[1:], vec.dtype),
            shape((8, 1664), jnp.float32),
            shape((4,) + share_expand.shape, kind),
        ],
        scratch_shapes=[
            buf(3, 1024, 896),
            buf(*w_half.shape),
            buf(3, 4, 208, 896),
            buf(3, 4, 208, 896),
            buf(3, 2, 208, 896),
            buf(3, 208, 896),
            buf(4, 208, 1664),
            buf(4, 208, 1664),
            buf(4, 256, width),
            buf(2, 256, width),
            buf(256, width),
            buf(*inputs.shape),
            buf(*share_expand.shape),
            flat(*vec.shape),
            flat(*vec.shape[1:]),
            flat(*vec.shape[1:]),
            flat(*vec.shape),
            flat(4, 8, 1664),
            flat(8, 1664),
            flat(4, 8, 1664),
            pltpu.SemaphoreType.DMA((88,)),
            pltpu.SemaphoreType.DMA((88,)),
            pltpu.SemaphoreType.DMA((24,)),
        ],
        compiler_params=pltpu.CompilerParams(collective_id=3, has_side_effects=True, vmem_limit_bytes=63 * 2**20),
        cost_estimate=pl.CostEstimate(flops=10**11, bytes_accessed=2**26, transcendentals=0),
        name="last_sums",
    )(dq, dk, dv, in_grad, w_half, out_share, share_expand, vec, grad_middle, inputs, gain)


def on_device(
    inputs,
    segments,
    cotangent,
    project_in,
    project_out,
    expand_weight,
    reduce_weight,
    query_bias,
    value_bias,
    project_bias,
    expand_bias,
    reduce_bias,
    first_gain,
    first_shift,
    second_gain,
    second_shift,
):
    replica, group, z, core, y, x = place()
    quad = lax.rem(replica, 4)
    width = 1600
    rows = 512

    vec = jnp.concatenate(
        [
            jnp.stack([query_bias, value_bias, project_bias, reduce_bias, first_gain, first_shift, second_gain, second_shift]),
            expand_bias.reshape(4, 400),
            jnp.zeros((4, 400), jnp.bfloat16),
        ]
    )
    halves = jnp.stack([head_columns(project_in, 0, 1), head_columns(project_in, 1, 1)])
    x_seq, w_half, vecs, segs, cots = first_exchange(
        inputs, halves, vec, segments[:, None, :], cotangent.reshape(rows, width)
    )
    vecs = wide(vecs)
    names = [vecs[:, k].reshape(width) for k in range(8)]
    bias_query, bias_value, bias_project, bias_reduce, gain_first, shift_first, gain_second, shift_second = names
    bias_expand = lax.dynamic_index_in_dim(vecs, 8 + quad, 1, False).reshape(width)
    segs = segs.reshape(1024)

    x_seq, out_shard, reduce_shard, expand_shard = lax.optimization_barrier(
        (x_seq, project_out, reduce_weight, expand_weight)
    )
    quarter_expand = jnp.concatenate(
        [lax.dynamic_slice_in_dim(expand_shard, 1600 * k + 400 * quad, 400, 1) for k in range(4)], axis=1
    )
    full_out = lax.all_gather(out_shard, "group", axis=0, tiled=True)
    expand_part = lax.all_gather(quarter_expand, "group", axis=0, tiled=True)

    flat_seq = wide(x_seq.reshape(1024, width))
    normed = low(layer_norm(flat_seq, gain_first, shift_first))
    w_half = w_half.reshape(width, 2688)
    pad64 = jnp.zeros((64,), jnp.float32)
    bias_q = lax.dynamic_slice_in_dim(bias_query, 768 * y, 832, 0)
    bias_v = lax.dynamic_slice_in_dim(bias_value, 768 * y, 832, 0)
    bias_mix = jnp.concatenate([bias_q, pad64, jnp.zeros((896,), jnp.float32), bias_v, pad64])
    mixture = low(product(normed, w_half) + bias_mix)
    segc = segs[:, None]
    segr = segs[None]
    attended, lse = heads(mixture, segc, segr)
    att_tokens = turn(attended.reshape(4, 256, 896), True, 1)
    att_tokens = joined(att_tokens[:, 0].reshape(rows, 896), att_tokens[:, 1].reshape(rows, 896))[:, :width]

    flat_input = wide(inputs.reshape(rows, width))
    middle = flat_input + product(att_tokens, full_out) + bias_project
    center = middle - jnp.mean(middle, axis=-1, keepdims=True)
    scale = lax.rsqrt(jnp.mean(center * center, axis=-1, keepdims=True) + epsilon)
    unit = center * scale
    second = padded(low(unit * gain_second + shift_second))

    activated, grad_expanded, second_all, reduce_part, grad_second, own_reduce, pass_reduce, expand_sums = feed_all(
        second, cots.reshape(4 * rows, width), expand_part, reduce_shard, bias_expand[None]
    )

    q = grad_second * gain_second
    grad_middle = wide(cotangent.reshape(rows, width)) + scale * (
        q - jnp.mean(q, axis=-1, keepdims=True) - unit * jnp.mean(q * unit, axis=-1, keepdims=True)
    )
    second_gain_grad = jnp.sum(grad_second * unit, axis=0)
    second_shift_grad = jnp.sum(grad_second, axis=0)
    grad_middle_low = low(grad_middle)
    grad_att = padded(low(product_back(grad_middle_low, full_out))).reshape(2, 256, 1664)
    lane = lax.broadcasted_iota(jnp.int32, (896,), 0)
    grad_att = jnp.stack(
        [jnp.where(lane < 832, grad_att[..., :896], 0), jnp.where(lane >= 64, grad_att[..., 768:], 0)], axis=1
    )
    grad_heads, expand_grad, result, share_reduce, out_core = turn_more(
        grad_att, grad_expanded, second_all, activated, reduce_part, pass_reduce, att_tokens, grad_middle_low, own_reduce
    )
    out_share = padded(lax.psum_scatter(out_core, "group", scatter_dimension=0, tiled=False))
    outputs = low(result + middle + bias_reduce).reshape(2, 256, width)
    dq, dk, dv, bias_sums, in_grad, share_expand, quads_reduce = heads_back(
        mixture, grad_heads.reshape(1024, 896), attended, lse, segc, segr, normed, share_reduce, expand_grad
    )

    def spread(columns):
        lower = jnp.concatenate([columns[:832], jnp.zeros((768,), jnp.float32)])
        upper = jnp.concatenate([jnp.zeros((832,), jnp.float32), columns[64:832]])
        return jnp.where(y == 0, lower, upper)

    expand_bias_part = jnp.sum(expand_sums, axis=0).reshape(4, 400)
    expand_bias_wide = lax.dynamic_update_slice_in_dim(jnp.zeros((4, width), jnp.float32), expand_bias_part, 400 * quad, 1)
    vectors = jnp.concatenate(
        [
            spread(bias_sums[0]).reshape(4, 400),
            spread(bias_sums[1]).reshape(4, 400),
            column_sum(grad_middle_low).reshape(4, 400),
            column_sum(cotangent.reshape(rows, width)).reshape(4, 400),
            second_gain_grad.reshape(4, 400),
            second_shift_grad.reshape(4, 400),
            expand_bias_wide,
        ],
        axis=1,
    )
    vectors = jnp.pad(vectors, ((0, 0), (0, 96))).reshape(4, 32, 128)
    grad_total, input_grad, vec_total, wide_total, quads_expand = last_sums(
        dq, dk, dv, in_grad, w_half, out_share, share_expand, vectors, grad_middle.reshape(2, 256, width), inputs, gain_first[None]
    )
    vec_total = vec_total.reshape(4096)
    pieces = [vec_total[400 * k : 400 * k + 400] for k in range(6)]
    first_sums = lax.dynamic_index_in_dim(wide_total[:2, :width].reshape(2, 4, 400), group, 1, False)
    total_reduce = wide(quads_reduce.reshape(width, width))
    total_expand = finish_feed(quads_expand)
    total_in, total_out = finish_mixer(grad_total)
    return (
        outputs,
        input_grad,
        total_in,
        total_out,
        total_expand,
        total_reduce,
        pieces[0],
        pieces[1],
        pieces[2],
        vec_total[2400:4000],
        pieces[3],
        first_sums[0],
        first_sums[1],
        pieces[4],
        pieces[5],
    )


def solution(mesh):
    placed = (
        P("replica", "group", None),
        P("replica", "group"),
        P("replica", "group", None),
        P("group", None),
        P("group", None),
        P("group", None),
        P("group", None),
        P("group"),
        P("group"),
        P("group"),
        P("group"),
        P("group"),
        P("group"),
        P("group"),
        P("group"),
        P("group"),
    )
    return jax.shard_map(
        on_device if dict(mesh.shape) == {"replica": 8, "group": 4} else on_device_any,
        mesh=mesh,
        in_specs=placed,
        out_specs=(
            P("replica", "group", None),
            P("replica", "group", None),
            P("group", None),
            P("group", None),
            P("group", None),
            P("group", None),
            P("group"),
            P("group"),
            P("group"),
            P("group"),
            P("group"),
            P("group"),
            P("group"),
            P("group"),
            P("group"),
        ),
        check_vma=False,
    )
```

```python
import functools
import math

import jax
import jax.numpy as jnp
from jax import lax
from jax.sharding import PartitionSpec as P

from jax.experimental import pallas as pl
from jax.experimental.pallas import tpu as pltpu

HEADS = 25
HEAD_DIM = 64


epsilon = 1e-05
very_low = -1e30


def carried_in(part, axis, combine, identity):
    place = lax.axis_index(axis)
    gathered = lax.all_gather(part, axis)
    state = jnp.zeros_like(part) + jnp.asarray(identity, part.dtype)

    def one(hop, state):
        return combine(state, lax.dynamic_index_in_dim(gathered, hop, 0, False))

    return lax.fori_loop(0, place, one, state)


def layer_norm(entries, gain, shift):
    center = entries - jnp.mean(entries, axis=-1, keepdims=True)
    spread = jnp.mean(center * center, axis=-1, keepdims=True)
    return center * lax.rsqrt(spread + epsilon) * gain + shift


def product(left, right):
    return jnp.dot(left, right, preferred_element_type=jnp.float32)


def product_back(left, right):
    return lax.dot_general(
        left, right, (((1,), (1,)), ((), ())), preferred_element_type=jnp.float32
    )


def weight_term(left, right):
    return lax.dot_general(
        left, right, (((0,), (0,)), ((), ())), preferred_element_type=jnp.float32
    )


def column_sum(entries):
    return jnp.sum(entries.astype(jnp.float32), axis=0)


def block_scores(queries, key_block, offset, query_pos, doc_start):
    block_count = key_block.shape[0]
    key_count = key_block.shape[2]
    scaling = 1.0 / math.sqrt(HEAD_DIM)
    scores = (
        jnp.einsum("schd,pskhd->shcpk", queries, key_block, preferred_element_type=jnp.float32)
        * scaling
    )
    key_pos = (offset + jnp.arange(block_count, dtype=jnp.int32))[:, None] * key_count + jnp.arange(
        key_count, dtype=jnp.int32
    )[None, :]
    allowed = (key_pos[None, None] <= query_pos[None, :, None, None]) & (
        key_pos[None, None] >= doc_start[:, :, None, None]
    )
    allowed = allowed[:, None]
    return (jnp.where(allowed, scores, very_low), allowed)


def attend(running, key_block, value_block, offset, queries, query_pos, doc_start):
    largest, denominator, summed = running
    masked, allowed = block_scores(queries, key_block, offset, query_pos, doc_start)
    fresh = jnp.maximum(largest, jnp.max(masked, axis=(3, 4)))
    shares = jnp.where(allowed, jnp.exp(masked - fresh[..., None, None]), 0.0)
    rescale = jnp.exp(largest - fresh)
    denominator = denominator * rescale + jnp.sum(shares, axis=(3, 4))
    added = jnp.einsum(
        "shcpk,pskhd->schd",
        shares.astype(jnp.bfloat16),
        value_block,
        preferred_element_type=jnp.float32,
    )
    summed = summed * jnp.transpose(rescale, (0, 2, 1))[..., None] + added
    return (fresh, denominator, summed)


def attend_back(
    grad_query,
    key_block,
    value_block,
    offset,
    queries,
    query_pos,
    doc_start,
    log_total,
    grad_low,
    row_dot,
):
    masked, allowed = block_scores(queries, key_block, offset, query_pos, doc_start)
    shares = jnp.where(allowed, jnp.exp(masked - log_total[..., None, None]), 0.0)
    grad_value = jnp.einsum(
        "shcpk,schd->pskhd",
        shares.astype(jnp.bfloat16),
        grad_low,
        preferred_element_type=jnp.float32,
    )
    grad_share = jnp.einsum(
        "schd,pskhd->shcpk", grad_low, value_block, preferred_element_type=jnp.float32
    )
    grad_score = (shares * (grad_share - row_dot[..., None, None])).astype(jnp.bfloat16)
    grad_query = grad_query + jnp.einsum(
        "shcpk,pskhd->schd", grad_score, key_block, preferred_element_type=jnp.float32
    )
    grad_key = jnp.einsum(
        "shcpk,schd->pskhd", grad_score, queries, preferred_element_type=jnp.float32
    )
    return (grad_query, (grad_key, grad_value))


def on_device_any(
    inputs,
    segments,
    cotangent,
    project_in,
    project_out,
    expand_weight,
    reduce_weight,
    query_bias,
    value_bias,
    project_bias,
    expand_bias,
    reduce_bias,
    first_gain,
    first_shift,
    second_gain,
    second_shift,
):
    seq_here, local_len, width = inputs.shape
    groups = lax.axis_size("group")
    total_rows = seq_here * local_len
    head_shape = (seq_here, local_len, HEADS, HEAD_DIM)
    shards = (
        project_in,
        project_out,
        expand_weight,
        reduce_weight,
        query_bias,
        value_bias,
        project_bias,
        expand_bias,
        reduce_bias,
        first_gain,
        first_shift,
        second_gain,
        second_shift,
    )
    whole = (
        lax.all_gather(shards[0], "group", axis=0, tiled=True),
        lax.all_gather(shards[1], "group", axis=0, tiled=True),
        lax.all_gather(shards[2], "group", axis=0, tiled=True),
        lax.all_gather(shards[3], "group", axis=0, tiled=True),
        lax.all_gather(shards[4], "group", axis=0, tiled=True),
        lax.all_gather(shards[5], "group", axis=0, tiled=True),
        lax.all_gather(shards[6], "group", axis=0, tiled=True),
        lax.all_gather(shards[7], "group", axis=0, tiled=True),
        lax.all_gather(shards[8], "group", axis=0, tiled=True),
        lax.all_gather(shards[9], "group", axis=0, tiled=True),
        lax.all_gather(shards[10], "group", axis=0, tiled=True),
        lax.all_gather(shards[11], "group", axis=0, tiled=True),
        lax.all_gather(shards[12], "group", axis=0, tiled=True),
    )
    (
        full_in,
        full_out,
        full_expand,
        full_reduce,
        bias_query,
        bias_value,
        bias_project,
        bias_expand,
        bias_reduce,
        gain_first,
        shift_first,
        gain_second,
        shift_second,
    ) = whole
    group_rank = lax.axis_index("group")
    query_pos = group_rank * local_len + jnp.arange(local_len, dtype=jnp.int32)
    positions = jnp.broadcast_to(query_pos[None, :], (seq_here, local_len))
    end_marks = jnp.where(segments == positions, positions + 1, 0)
    before = carried_in(
        jnp.max(end_marks, axis=1), "group", jnp.maximum, jnp.zeros((seq_here,), jnp.int32)
    )
    inside = lax.cummax(end_marks, axis=1)
    inside = jnp.concatenate([jnp.zeros((seq_here, 1), jnp.int32), inside[:, :-1]], axis=1)
    doc_start = jnp.maximum(before[:, None], inside)
    flat_input = inputs.reshape(total_rows, width).astype(jnp.float32)
    normed_low = layer_norm(
        flat_input, gain_first.astype(jnp.float32), shift_first.astype(jnp.float32)
    ).astype(jnp.bfloat16)
    mixture = product(normed_low, full_in)
    queries = (
        (mixture[:, :width] + bias_query.astype(jnp.float32))
        .astype(jnp.bfloat16)
        .reshape(head_shape)
    )
    key_rows = (
        mixture[:, width : 2 * width].astype(jnp.bfloat16).reshape(seq_here, local_len, width)
    )
    value_rows = (
        (mixture[:, 2 * width :] + bias_value.astype(jnp.float32))
        .astype(jnp.bfloat16)
        .reshape(seq_here, local_len, width)
    )
    initial = (
        jnp.full((seq_here, HEADS, local_len), very_low, jnp.float32),
        jnp.zeros((seq_here, HEADS, local_len), jnp.float32),
        jnp.zeros(head_shape, jnp.float32),
    )
    block_ids = jnp.arange(groups, dtype=jnp.int32)
    running = initial
    pieces = (
        lax.all_gather(key_rows[None], "group", axis=0, tiled=True),
        lax.all_gather(value_rows[None], "group", axis=0, tiled=True),
    )
    piece_count = pieces[0].shape[0]

    def one_piece(state, members):
        key_piece, value_piece, index = members
        updated = attend(
            state,
            key_piece.reshape((1,) + head_shape),
            value_piece.reshape((1,) + head_shape),
            index,
            queries,
            query_pos,
            doc_start,
        )
        return (updated, None)

    running, unused_steps = lax.scan(
        one_piece, running, (pieces[0], pieces[1], jnp.arange(piece_count, dtype=jnp.int32))
    )
    largest, denominator, summed = running
    attended = summed / jnp.transpose(denominator, (0, 2, 1))[..., None]
    log_total = largest + jnp.log(denominator)
    attended_low = attended.reshape(total_rows, width).astype(jnp.bfloat16)
    middle = flat_input + product(attended_low, full_out) + bias_project.astype(jnp.float32)
    second_low = layer_norm(
        middle, gain_second.astype(jnp.float32), shift_second.astype(jnp.float32)
    ).astype(jnp.bfloat16)
    expanded = product(second_low, full_expand) + bias_expand.astype(jnp.float32)
    activated_low = jax.nn.gelu(expanded, approximate=True).astype(jnp.bfloat16)
    result = middle + product(activated_low, full_reduce) + bias_reduce.astype(jnp.float32)
    outputs = result.astype(jnp.bfloat16).reshape(seq_here, local_len, width)
    whole_back = (
        lax.all_gather(shards[0], "group", axis=0, tiled=True),
        lax.all_gather(shards[1], "group", axis=0, tiled=True),
        lax.all_gather(shards[2], "group", axis=0, tiled=True),
        lax.all_gather(shards[3], "group", axis=0, tiled=True),
        lax.all_gather(shards[4], "group", axis=0, tiled=True),
        lax.all_gather(shards[5], "group", axis=0, tiled=True),
        lax.all_gather(shards[6], "group", axis=0, tiled=True),
        lax.all_gather(shards[7], "group", axis=0, tiled=True),
        lax.all_gather(shards[8], "group", axis=0, tiled=True),
        lax.all_gather(shards[9], "group", axis=0, tiled=True),
        lax.all_gather(shards[10], "group", axis=0, tiled=True),
        lax.all_gather(shards[11], "group", axis=0, tiled=True),
        lax.all_gather(shards[12], "group", axis=0, tiled=True),
    )
    keys_back = (
        lax.all_gather(key_rows[None], "group", axis=0, tiled=True),
        lax.all_gather(value_rows[None], "group", axis=0, tiled=True),
    )
    (
        back_in,
        back_out,
        back_expand,
        back_reduce,
        unused_query,
        unused_value,
        unused_project,
        unused_expand,
        unused_reduce,
        back_gain_first,
        back_shift_first,
        back_gain_second,
        back_shift_second,
    ) = whole_back
    grad_rows = cotangent.reshape(total_rows, width).astype(jnp.float32)
    grad_result_low = cotangent.reshape(total_rows, width)
    reduce_bias_grad = column_sum(grad_result_low)
    grad_activated = product_back(grad_result_low, back_reduce)
    unused_gelu, gelu_back = jax.vjp(lambda entry: jax.nn.gelu(entry, approximate=True), expanded)
    grad_expanded_low = gelu_back(grad_activated)[0].astype(jnp.bfloat16)
    expand_bias_grad = column_sum(grad_expanded_low)
    grad_second = product_back(grad_expanded_low, back_expand)
    unused_second, second_back = jax.vjp(
        layer_norm,
        middle,
        back_gain_second.astype(jnp.float32),
        back_shift_second.astype(jnp.float32),
    )
    grad_middle, second_gain_grad, second_shift_grad = second_back(grad_second)
    grad_middle = grad_middle + grad_rows
    reduce_weight_grad = weight_term(activated_low, grad_result_low)
    expand_weight_grad = weight_term(second_low, grad_expanded_low)
    feed_parts = (
        lax.psum_scatter(
            expand_weight_grad.astype(jnp.bfloat16), "group", scatter_dimension=0, tiled=True
        ).astype(jnp.float32),
        lax.psum_scatter(
            reduce_weight_grad.astype(jnp.bfloat16), "group", scatter_dimension=0, tiled=True
        ).astype(jnp.float32),
        lax.psum_scatter(
            expand_bias_grad.astype(jnp.bfloat16), "group", scatter_dimension=0, tiled=True
        ).astype(jnp.float32),
        lax.psum_scatter(
            reduce_bias_grad.astype(jnp.bfloat16), "group", scatter_dimension=0, tiled=True
        ).astype(jnp.float32),
        lax.psum_scatter(
            second_gain_grad.astype(jnp.bfloat16), "group", scatter_dimension=0, tiled=True
        ).astype(jnp.float32),
        lax.psum_scatter(
            second_shift_grad.astype(jnp.bfloat16), "group", scatter_dimension=0, tiled=True
        ).astype(jnp.float32),
    )
    grad_middle_low = grad_middle.astype(jnp.bfloat16)
    project_bias_grad = column_sum(grad_middle_low)
    grad_attended_low = (
        product_back(grad_middle_low, back_out).astype(jnp.bfloat16).reshape(head_shape)
    )
    row_dot = jnp.einsum("schd,schd->shc", grad_attended_low.astype(jnp.float32), attended)

    def back_step(grad_query, members):
        key_piece, value_piece, offset = members
        return attend_back(
            grad_query,
            key_piece.reshape((1,) + head_shape),
            value_piece.reshape((1,) + head_shape),
            offset,
            queries,
            query_pos,
            doc_start,
            log_total,
            grad_attended_low,
            row_dot,
        )

    grad_query, terms = lax.scan(
        back_step, jnp.zeros(head_shape, jnp.float32), (keys_back[0], keys_back[1], block_ids)
    )
    key_terms = terms[0].reshape(groups, seq_here, local_len, width)
    value_terms = terms[1].reshape(groups, seq_here, local_len, width)
    key_grad, value_grad = (
        lax.psum_scatter(
            key_terms.astype(jnp.bfloat16), "group", scatter_dimension=0, tiled=True
        ).astype(jnp.float32),
        lax.psum_scatter(
            value_terms.astype(jnp.bfloat16), "group", scatter_dimension=0, tiled=True
        ).astype(jnp.float32),
    )
    scaling = 1.0 / math.sqrt(HEAD_DIM)
    grad_query_low = (grad_query * scaling).reshape(total_rows, width).astype(jnp.bfloat16)
    grad_key_low = (key_grad * scaling).reshape(total_rows, width).astype(jnp.bfloat16)
    grad_value_low = value_grad.reshape(total_rows, width).astype(jnp.bfloat16)
    query_bias_grad = column_sum(grad_query_low)
    value_bias_grad = column_sum(grad_value_low)
    grad_mixture_low = jnp.concatenate([grad_query_low, grad_key_low, grad_value_low], axis=1)
    grad_normed = product_back(grad_mixture_low, back_in)
    unused_first, first_back = jax.vjp(
        layer_norm,
        flat_input,
        back_gain_first.astype(jnp.float32),
        back_shift_first.astype(jnp.float32),
    )
    grad_entry, first_gain_grad, first_shift_grad = first_back(grad_normed)
    input_grad = (grad_entry + grad_middle).reshape(seq_here, local_len, width)
    project_weight_grad = weight_term(attended_low, grad_middle_low)
    in_weight_grad = weight_term(normed_low, grad_mixture_low)
    mixer_parts = (
        lax.psum_scatter(
            in_weight_grad.astype(jnp.bfloat16), "group", scatter_dimension=0, tiled=True
        ).astype(jnp.float32),
        lax.psum_scatter(
            project_weight_grad.astype(jnp.bfloat16), "group", scatter_dimension=0, tiled=True
        ).astype(jnp.float32),
        lax.psum_scatter(
            query_bias_grad.astype(jnp.bfloat16), "group", scatter_dimension=0, tiled=True
        ).astype(jnp.float32),
        lax.psum_scatter(
            value_bias_grad.astype(jnp.bfloat16), "group", scatter_dimension=0, tiled=True
        ).astype(jnp.float32),
        lax.psum_scatter(
            project_bias_grad.astype(jnp.bfloat16), "group", scatter_dimension=0, tiled=True
        ).astype(jnp.float32),
        lax.psum_scatter(
            first_gain_grad.astype(jnp.bfloat16), "group", scatter_dimension=0, tiled=True
        ).astype(jnp.float32),
        lax.psum_scatter(
            first_shift_grad.astype(jnp.bfloat16), "group", scatter_dimension=0, tiled=True
        ).astype(jnp.float32),
    )
    share_in, share_out, share_expand, share_reduce = (
        mixer_parts[0],
        mixer_parts[1],
        feed_parts[0],
        feed_parts[1],
    )
    share_query, share_value, share_project = (mixer_parts[2], mixer_parts[3], mixer_parts[4])
    share_expand_bias, share_reduce_bias = (feed_parts[2], feed_parts[3])
    share_first_gain, share_first_shift = (mixer_parts[5], mixer_parts[6])
    share_second_gain, share_second_shift = (feed_parts[4], feed_parts[5])
    totals = (
        lax.psum(share_in.astype(jnp.bfloat16), "replica").astype(jnp.float32),
        lax.psum(share_out.astype(jnp.bfloat16), "replica").astype(jnp.float32),
        lax.psum(share_expand.astype(jnp.bfloat16), "replica").astype(jnp.float32),
        lax.psum(share_reduce.astype(jnp.bfloat16), "replica").astype(jnp.float32),
        lax.psum(share_query.astype(jnp.bfloat16), "replica").astype(jnp.float32),
        lax.psum(share_value.astype(jnp.bfloat16), "replica").astype(jnp.float32),
        lax.psum(share_project.astype(jnp.bfloat16), "replica").astype(jnp.float32),
        lax.psum(share_expand_bias.astype(jnp.bfloat16), "replica").astype(jnp.float32),
        lax.psum(share_reduce_bias.astype(jnp.bfloat16), "replica").astype(jnp.float32),
        lax.psum(share_first_gain.astype(jnp.bfloat16), "replica").astype(jnp.float32),
        lax.psum(share_first_shift.astype(jnp.bfloat16), "replica").astype(jnp.float32),
        lax.psum(share_second_gain.astype(jnp.bfloat16), "replica").astype(jnp.float32),
        lax.psum(share_second_shift.astype(jnp.bfloat16), "replica").astype(jnp.float32),
    )
    return (
        outputs,
        input_grad,
        totals[0],
        totals[1],
        totals[2],
        totals[3],
        totals[4],
        totals[5],
        totals[6],
        totals[7],
        totals[8],
        totals[9],
        totals[10],
        totals[11],
        totals[12],
    )


MESH = pl.DeviceIdType.MESH


def flipped(z=0, core=0, y=0, x=0):
    pairs = []
    for me in range(32):
        pairs.append((me, me ^ (8 * z + 4 * core + 2 * y + x)))
    return pairs


FLIP_X = flipped(x=1)
FLIP_Y = flipped(y=1)
FLIP_CORE = flipped(core=1)
FLIP_Z = flipped(z=1)
FLIP_PAIR = flipped(z=2)
INWARD = [(me, me + 8) for me in range(8)] + [(me, me - 8) for me in range(24, 32)]
MIDDLE = [(me, me + 8) for me in range(8, 16)] + [(me, me - 8) for me in range(16, 24)]
OUTWARD = [(me, me - 8) for me in range(8, 16)] + [(me, me + 8) for me in range(16, 24)]


def moved(entries, pairs):
    return lax.ppermute(entries, ("replica", "group"), pairs)


def low(entries):
    return entries.astype(jnp.bfloat16)


def wide(entries):
    return entries.astype(jnp.float32)


def at(entries, index):
    return lax.dynamic_index_in_dim(entries, index, 0, False)


def place():
    replica = lax.axis_index("replica")
    group = lax.axis_index("group")
    core = lax.rem(replica, 2)
    z = lax.div(replica, 2)
    return replica, group, z, core, lax.div(group, 2), lax.rem(group, 2)


def partners(replica, group):
    core = lax.rem(replica, 2)
    z = lax.rem(lax.div(replica, 2), 2)
    y = lax.div(group, 2)
    x = lax.rem(group, 2)
    by_x = (replica, group + 1 - 2 * x)
    by_y = (replica, group + 2 - 4 * y)
    by_both = (replica, group + 3 - 4 * y - 2 * x)
    by_core = (replica + 1 - 2 * core, group)
    by_z = (replica + 2 - 4 * z, group)
    return by_x, by_y, by_both, by_core, by_z


def greet(devices):
    barrier = pltpu.get_barrier_semaphore()
    for device in devices:
        pl.semaphore_signal(barrier, inc=1, device_id=device, device_id_type=MESH)
    pl.semaphore_wait(barrier, len(devices))


def first_exchange_kernel(inp, weights, vec, seg, x_seq, w_full, vecs, segs, raw, halves, x_stage, vec_stage, seg_stage, send, recv, local):
    replica = lax.axis_index("replica")
    group = lax.axis_index("group")
    core = lax.rem(replica, 2)
    level = lax.rem(lax.div(replica, 2), 2)
    y = lax.div(group, 2)
    x = lax.rem(group, 2)
    by_x, by_y, by_both, by_core, by_z = partners(replica, group)
    slot_x, slot_y, slot_both = by_x[1], by_y[1], by_both[1]
    other_x = 1 - x
    other_y = 1 - y
    wires = Wires(send, recv, local)
    load_raw = wires.here(weights, raw)
    greet((by_x, by_y, by_both, by_core, by_z))
    small = [wires.go(vec, vecs.at[group], device) for device in (by_x, by_y, by_both)]
    small += [wires.go(seg.at[pick], segs.at[group], device) for pick, device in ((other_x, by_x), (x, by_y), (other_x, by_both))]
    loads = [wires.here(here, there) for here, there in ((inp.at[x], x_stage), (vec, vec_stage), (seg.at[x], seg_stage))]
    load_raw.wait()
    for half in range(2):
        for k in range(3):
            first = 1600 * k + 768 * half
            halves[half, :, 896 * k : 896 * k + 832] = raw[:, first : first + 832]
            halves[half, :, 896 * k + 832 : 896 * k + 896] = jnp.zeros((halves.shape[1], 64), halves.dtype)

    part = 2 * level + core
    mine = rows16(96 * part, 112)
    to_core = rows16(96 * part + 16 * core, 96)
    to_z = rows16(96 * part + 16 * level, 96)
    passed = rows16(96 * (part + 2 - 4 * level) + 16 * (1 - level), 96)
    w_x = wires.go(halves.at[y, mine], w_full.at[group, mine], by_x)
    w_y = wires.go(halves.at[other_y, mine], w_full.at[group, mine], by_y)
    wires.keep(halves.at[y], w_full.at[group])
    for load, here, there in zip(loads, (x_stage, vec_stage, seg_stage), (x_seq, vecs, segs)):
        load.wait()
        wires.keep(here, there.at[group])
    shares = []
    over_z = []

    def share(slot):
        shares.append(wires.go(w_full.at[slot, to_core], w_full.at[slot, to_core], by_core))
        over_z.append((slot, wires.go(w_full.at[slot, to_z], w_full.at[slot, to_z], by_z)))

    wires.drain([w_x, w_y])
    x_block = wires.go(inp.at[other_x], x_seq.at[group], by_x)
    y_block = wires.go(inp.at[x], x_seq.at[group], by_y)
    w_y.wait_recv()
    share(slot_y)
    w_x.wait_recv()
    share(slot_x)
    wires.drain([x_block])
    w_more = wires.go(w_full.at[slot_y, mine], w_full.at[slot_y, mine], by_x)
    x_block.wait_recv()
    y_more = wires.go(x_seq.at[slot_x], x_seq.at[slot_x], by_y)
    w_more.wait_recv()
    share(slot_both)
    for slot, copy in over_z:
        copy.wait_recv()
        shares.append(wires.go(w_full.at[slot, passed], w_full.at[slot, passed], by_core))
    for copy in small + shares + [y_block, y_more]:
        copy.wait_recv()
    wires.finish()


def first_exchange(inp, weights, vec, seg):
    any_space = pl.BlockSpec(memory_space=pl.ANY)
    shape = jax.ShapeDtypeStruct
    rows = weights.shape[0]
    return pl.pallas_call(
        first_exchange_kernel,
        in_specs=[any_space] * 4,
        out_specs=[any_space] * 4,
        out_shape=[
            shape((4,) + inp.shape[1:], inp.dtype),
            shape((4, rows, 2688), weights.dtype),
            shape((4,) + vec.shape, vec.dtype),
            shape((4,) + seg.shape[1:], seg.dtype),
        ],
        scratch_shapes=[
            pltpu.VMEM(weights.shape, weights.dtype),
            pltpu.VMEM((2, rows, 2688), weights.dtype),
            pltpu.VMEM(inp.shape[1:], inp.dtype),
            pltpu.VMEM(vec.shape, vec.dtype),
            pltpu.VMEM(seg.shape[1:], seg.dtype),
            pltpu.SemaphoreType.DMA((24,)),
            pltpu.SemaphoreType.DMA((24,)),
            pltpu.SemaphoreType.DMA((8,)),
        ],
        compiler_params=pltpu.CompilerParams(collective_id=0, has_side_effects=True, vmem_limit_bytes=40 * 2**20),
        name="first_exchange",
    )(inp, weights, vec, seg)


def turn_middle_kernel(src, out_in, inp_in, rows_ref, att_out, middle_out, second_out, att, w, inp, send, recv, local):
    replica = lax.axis_index("replica")
    group = lax.axis_index("group")
    y = lax.div(group, 2)
    x = lax.rem(group, 2)
    by_x, by_y, by_both, by_core, by_z = partners(replica, group)
    others = (by_both, by_x, by_y)
    wires = Wires(send, recv, local)
    greet(others)
    copies = [wires.go(src.at[device[1]], att.at[x, y], device) for device in others]
    own = wires.here(src.at[group], att.at[x, y])
    load_w = wires.here(out_in, w)
    load_inp = wires.here(inp_in, inp)
    width = w.shape[0]
    lane = lax.broadcasted_iota(jnp.int32, (1, 128), 1)
    for copy in (own, load_w, load_inp):
        copy.wait()
    for copy in copies:
        copy.wait_recv()
    for seq in range(2):
        rows = pl.ds(256 * seq, 256)
        att_out[rows, 0:768] = att[seq, 0, :, 0:768]
        att_out[rows, 768:896] = jnp.where(lane < 64, att[seq, 0, :, 768:896], att[seq, 1, :, 0:128])
        att_out[rows, 896:width] = att[seq, 1, :, 128 : width - 768]
        middle = inp[seq].astype(jnp.float32) + dot_nn(att_out[rows, :], w[...]) + rows_ref[2:3, :width]
        middle_out[rows, :] = middle
        center = middle - jnp.mean(middle, axis=-1, keepdims=True)
        spread = jnp.mean(center * center, axis=-1, keepdims=True)
        second = center * lax.rsqrt(spread + epsilon) * rows_ref[6:7, :width] + rows_ref[7:8, :width]
        second_out[rows, :width] = second.astype(jnp.bfloat16)
        second_out[rows, width:] = jnp.zeros((256, second_out.shape[1] - width), jnp.bfloat16)
    wires.finish()


def turn_middle(entries, full_out, inputs, rows):
    any_space = pl.BlockSpec(memory_space=pl.ANY)
    vmem = pl.BlockSpec(memory_space=pltpu.VMEM)
    shape = jax.ShapeDtypeStruct
    width = full_out.shape[0]
    return pl.pallas_call(
        turn_middle_kernel,
        in_specs=[any_space, any_space, any_space, vmem],
        out_specs=[vmem, vmem, vmem],
        out_shape=[shape((512, width), jnp.bfloat16), shape((512, width), jnp.float32), shape((512, width + 64), jnp.bfloat16)],
        scratch_shapes=[
            pltpu.VMEM((2, 2) + entries.shape[1:], jnp.bfloat16),
            pltpu.VMEM(full_out.shape, jnp.bfloat16),
            pltpu.VMEM(inputs.shape, jnp.bfloat16),
            pltpu.SemaphoreType.DMA((3,)),
            pltpu.SemaphoreType.DMA((3,)),
            pltpu.SemaphoreType.DMA((3,)),
        ],
        compiler_params=pltpu.CompilerParams(collective_id=1, has_side_effects=True, vmem_limit_bytes=40 * 2**20),
        cost_estimate=pl.CostEstimate(flops=0, bytes_accessed=60 * 2**20, transcendentals=0),
        name="turn_middle",
    )(entries, full_out, inputs, rows)


def padded(entries):
    return jnp.pad(entries, [(0, 0)] * (entries.ndim - 1) + [(0, 64)])


def joined(first, other):
    lane = lax.broadcasted_iota(jnp.int32, (1, 128), 1)
    middle = jnp.where(lane < 64, first[..., 768:896], other[..., 0:128])
    return jnp.concatenate([first[..., :768], middle, other[..., 128:]], axis=-1)


def hold(entries, *until):
    return lax.optimization_barrier((entries,) + until)[0]


def finish_feed_kernel(quads_ref, out_expand):
    for k in range(4):
        piece = quads_ref[k].astype(jnp.float32)
        for r in range(4):
            out_expand[:, 1600 * r + 400 * k : 1600 * r + 400 * k + 400] = piece[:, 400 * r : 400 * r + 400]


def finish_feed(quads):
    rows, width = quads.shape[1:]
    step = 80
    return pl.pallas_call(
        finish_feed_kernel,
        grid=(rows // step,),
        in_specs=[pl.BlockSpec((4, step, width), lambda i: (0, i, 0))],
        out_specs=pl.BlockSpec((step, 4 * width), lambda i: (i, 0)),
        out_shape=jax.ShapeDtypeStruct((rows, 4 * width), jnp.float32),
        compiler_params=pltpu.CompilerParams(vmem_limit_bytes=48 * 2**20),
        name="finish_feed",
    )(quads)


def finish_mixer_kernel(total_ref, in_ref, out_ref):
    for k in range(3):
        in_ref[:, 1600 * k : 1600 * k + 1600] = total_ref[k, :, :1600].astype(jnp.float32)
    out_ref[...] = total_ref[3, :, :1600].astype(jnp.float32)


def finish_mixer(total):
    rows = total.shape[1]
    step = 80
    return pl.pallas_call(
        finish_mixer_kernel,
        grid=(rows // step,),
        in_specs=[pl.BlockSpec((4, step, total.shape[2]), lambda i: (0, i, 0))],
        out_specs=[pl.BlockSpec((step, 4800), lambda i: (i, 0)), pl.BlockSpec((step, 1600), lambda i: (i, 0))],
        out_shape=[jax.ShapeDtypeStruct((rows, 4800), jnp.float32), jax.ShapeDtypeStruct((rows, 1600), jnp.float32)],
        compiler_params=pltpu.CompilerParams(vmem_limit_bytes=48 * 2**20),
        name="finish_mixer",
    )(total)


PIECES = ((0, 512), (512, 1024), (1024, 1600))
HALF = 208


class Wires:
    def __init__(self, send, recv, local):
        self.send, self.recv, self.local = send, recv, local
        self.remotes = self.locals = 0
        self.sent = []
        self.kept = []

    def make(self, src, dst, device):
        i = self.remotes
        self.remotes = i + 1
        return pltpu.make_async_remote_copy(src_ref=src, dst_ref=dst, send_sem=self.send.at[i], recv_sem=self.recv.at[i], device_id=device, device_id_type=MESH)

    def go(self, src, dst, device):
        copy = self.make(src, dst, device)
        copy.start()
        self.sent.append(copy)
        return copy

    def here(self, src, dst):
        i = self.locals
        self.locals = i + 1
        copy = pltpu.make_async_copy(src, dst, self.local.at[i])
        copy.start()
        return copy

    def keep(self, src, dst):
        self.kept.append(self.here(src, dst))

    def drain(self, copies):
        for copy in copies:
            copy.wait_send()
        self.sent = [copy for copy in self.sent if all(copy is not done for done in copies)]

    def finish(self):
        for copy in self.sent:
            copy.wait_send()
        for copy in self.kept:
            copy.wait()


def rows16(start, size):
    return pl.ds(pl.multiple_of(start, 16), size)


def dot_tn(a, b):
    return lax.dot_general(a, b, (((0,), (0,)), ((), ())), preferred_element_type=jnp.float32)


def add_low(a, b):
    return (a.astype(jnp.float32) + b.astype(jnp.float32)).astype(jnp.bfloat16)


def weight_sum(a, b, out):
    width = out.shape[0]
    whole = width // 256

    def chunk(j, carry):
        lanes = pl.ds(pl.multiple_of(256 * j, 256), 256)
        out[lanes, :] = dot_tn(a[:, lanes], b[:, : out.shape[1]]).astype(jnp.bfloat16)
        return carry

    lax.fori_loop(0, whole, chunk, 0)
    if width > 256 * whole:
        out[256 * whole :, :] = dot_tn(a[:, 256 * whole : width], b[:, : out.shape[1]]).astype(jnp.bfloat16)


NT = (((1,), (1,)), ((), ()))

def dot_nt(a, b):
    return lax.dot_general(a, b, NT, preferred_element_type=jnp.float32)

def dot_nn(a, b):
    return jnp.dot(a, b, preferred_element_type=jnp.float32)

BLOCK = 256

def mix_heads_kernel(x_seq, w_in, rows_ref, segc_ref, segr_ref, out_shard, expand_shard, cot, mix, normed, unit_out, o_ref, lse_ref, full_out, full_expand, cots, x_buf, w, stage_out, stage_expand, ot_ref, vt_ref, send, recv, local):
    replica = lax.axis_index("replica")
    group = lax.axis_index("group")
    core = lax.rem(replica, 2)
    y = lax.div(group, 2)
    x = lax.rem(group, 2)
    by_x, by_y, by_both, by_core, by_z = partners(replica, group)
    slot_x, slot_y, slot_both = by_x[1], by_y[1], by_both[1]
    wires = Wires(send, recv, local)
    greet([by_x, by_y, by_core, by_z])
    start = 192 * core
    mine = rows16(start, 208)
    shared = rows16(208 * core, 192)
    out_x = wires.go(out_shard.at[mine], full_out.at[group, mine], by_x)
    out_y = wires.go(out_shard.at[mine], full_out.at[group, mine], by_y)
    expand_x = wires.go(expand_shard, full_expand.at[group], by_x)
    expand_y = wires.go(expand_shard, full_expand.at[group], by_y)
    cot_core = wires.go(cot, cots.at[0], by_core)
    cot_z = wires.go(cot, cots.at[1], by_z)
    load_x = wires.here(x_seq, x_buf)
    load_w = wires.here(w_in, w)
    load_out = wires.here(out_shard, stage_out)
    load_expand = wires.here(expand_shard, stage_expand)
    length = mix.shape[0]
    blocks = length // BLOCK
    lane = lax.broadcasted_iota(jnp.int32, (1, 128), 1)
    lse_ref[...] = jnp.zeros_like(lse_ref)
    half_lanes = pl.ds(pl.multiple_of(768 * y, 128), 896)
    load_x.wait()
    load_w.wait()

    def mix_rows(i, carry):
        rows = pl.ds(pl.multiple_of(256 * i, 256), 256)
        width = x_buf.shape[1]
        entries = x_buf[rows, :].astype(jnp.float32)
        center = entries - jnp.mean(entries, axis=-1, keepdims=True)
        spread = jnp.mean(center * center, axis=-1, keepdims=True)
        unit = center * lax.rsqrt(spread + epsilon)
        unit_out[rows, :] = unit.astype(jnp.bfloat16)
        low_rows = (unit * rows_ref[4:5, :width] + rows_ref[5:6, :width]).astype(jnp.bfloat16)
        normed[rows, :] = low_rows
        mix[rows, 0:896] = (dot_nn(low_rows, w[:, 0:896]) + rows_ref[0:1, half_lanes]).astype(jnp.bfloat16)
        mix[rows, 896:1792] = dot_nn(low_rows, w[:, 896:1792]).astype(jnp.bfloat16)
        mix[rows, 1792:2688] = (dot_nn(low_rows, w[:, 1792:2688]) + rows_ref[1:2, half_lanes]).astype(jnp.bfloat16)
        return carry

    lax.fori_loop(0, 4, mix_rows, 0)
    load_out.wait()
    wires.keep(stage_out, full_out.at[group])
    load_expand.wait()
    wires.keep(stage_expand, full_expand.at[group])
    upper = rows16(start, 112)
    lower = rows16(start + 112, 96)
    top = pl.ds(0, HALF)
    bottom = pl.ds(HALF, 400 - HALF)
    more = [wires.make(full_out.at[slot_x, upper], full_out.at[slot_x, upper], by_y), wires.make(full_out.at[slot_y, lower], full_out.at[slot_y, lower], by_x)]
    cores = [wires.make(full_out.at[slot, shared], full_out.at[slot, shared], by_core) for slot in (slot_x, slot_y)]
    expand_more = [wires.make(full_expand.at[slot_x, top], full_expand.at[slot_x, top], by_y), wires.make(full_expand.at[slot_y, bottom], full_expand.at[slot_y, bottom], by_x)]
    cot_both = wires.make(cots.at[1], cots.at[2], by_core)

    def tile_heads(tile, carry):
        at_lanes = lambda off: pl.ds(pl.multiple_of(128 * tile + off, 128), 128)
        ot_ref[...] = jnp.zeros_like(ot_ref)
        vt_ref[...] = mix[:, at_lanes(1792)].T

        def head(h):
            k = jnp.where((lane >= 64 * h) & (lane < 64 * h + 64), mix[:, at_lanes(896)], jnp.bfloat16(0))
            for i in range(blocks):
                low_at, high_at = i * BLOCK, (i + 1) * BLOCK
                q = mix[low_at:high_at, at_lanes(0)] * jnp.bfloat16(0.125)
                s = dot_nt(k[:high_at], q)
                same = segc_ref[:high_at, :] == segr_ref[:, low_at:high_at]
                kpos = lax.broadcasted_iota(jnp.int32, (high_at, BLOCK), 0)
                qpos = lax.broadcasted_iota(jnp.int32, (high_at, BLOCK), 1) + low_at
                s = jnp.where(same & (kpos <= qpos), s, -1e30)
                m = jnp.max(s, axis=0, keepdims=True)
                p = jnp.exp(s - m)
                l = jnp.sum(p, axis=0, keepdims=True)
                ot = dot_nn(vt_ref[64 * h : 64 * h + 64, :high_at], p.astype(jnp.bfloat16))
                ot_ref[64 * h : 64 * h + 64, low_at:high_at] = ot / l
                lse_ref[tile, h : h + 1, low_at:high_at] = m + jnp.log(l)

        head(0)

        @pl.when(tile < 6)
        def _():
            head(1)

        @pl.when(tile == 2)
        def _():
            out_x.wait_recv()
            out_y.wait_recv()
            for copy in more + cores:
                copy.start()

        @pl.when(tile == 4)
        def _():
            expand_x.wait_recv()
            expand_y.wait_recv()
            for copy in expand_more:
                copy.start()

        o_ref[:, at_lanes(0)] = ot_ref[...].T.astype(jnp.bfloat16)
        return carry

    lax.fori_loop(0, 7, tile_heads, 0)
    cot_z.wait_recv()
    cot_both.start()
    for copy in more:
        copy.wait_recv()
    last = wires.go(full_out.at[slot_both, shared], full_out.at[slot_both, shared], by_core)
    for copy in expand_more + cores + [cot_core, cot_both, last]:
        copy.wait_recv()
    for copy in more + cores + expand_more + [cot_both]:
        copy.wait_send()
    wires.finish()


def mix_heads(x_seq, w_in, rows, segc, segr, out_shard, expand_shard, cot):
    any_space = pl.BlockSpec(memory_space=pl.ANY)
    vmem = pl.BlockSpec(memory_space=pltpu.VMEM)
    shape = jax.ShapeDtypeStruct
    kind = jnp.bfloat16
    length = x_seq.shape[0]
    buf = lambda *dims: pltpu.VMEM(dims, kind)
    return pl.pallas_call(
        mix_heads_kernel,
        in_specs=[any_space, any_space, vmem, vmem, vmem, any_space, any_space, any_space],
        out_specs=[vmem] * 5 + [any_space] * 3,
        out_shape=[
            shape((length, 2688), kind),
            shape(x_seq.shape, kind),
            shape(x_seq.shape, kind),
            shape((length, 896), kind),
            shape((7, 8, length), jnp.float32),
            shape((4,) + out_shard.shape, kind),
            shape((4,) + expand_shard.shape, kind),
            shape((3,) + cot.shape, kind),
        ],
        scratch_shapes=[
            buf(*x_seq.shape),
            buf(*w_in.shape),
            buf(*out_shard.shape),
            buf(*expand_shard.shape),
            pltpu.VMEM((128, length), jnp.float32),
            buf(128, length),
            pltpu.SemaphoreType.DMA((16,)),
            pltpu.SemaphoreType.DMA((16,)),
            pltpu.SemaphoreType.DMA((8,)),
        ],
        compiler_params=pltpu.CompilerParams(collective_id=6, has_side_effects=True, vmem_limit_bytes=56 * 2**20),
        cost_estimate=pl.CostEstimate(flops=5 * 10**10, bytes_accessed=2**26, transcendentals=0),
        name="mix_heads",
    )(x_seq, w_in, rows, segc, segr, out_shard, expand_shard, cot)


def heads_back_kernel(q_ref, k_ref, v_ref, do_ref, o_ref, lse_ref, segc_ref, segr_ref, normed_ref, share_ref, first_ref, own_ref, pass_ref, dq_ref, dk_ref, dv_ref, sums_ref, grad_ref, share_out, first_out, quads, dqt_ref, odt_ref, pair, own, share_own, got, pair_next, normed_t, send, recv, local):
    tile = pl.program_id(0)
    replica = lax.axis_index("replica")
    group = lax.axis_index("group")
    quad = lax.rem(replica, 4)
    quad_z = lax.rem(quad + 2, 4)
    by_x, by_y, by_both, by_core, by_z = partners(replica, group)
    by_pair = (lax.rem(replica + 4, 8), group)
    wires = Wires(send, recv, local)
    pieces = [pl.ds(0, HALF), pl.ds(HALF, 400 - HALF)]
    pass_y = wires.make(pass_ref.at[pieces[0]], got.at[pieces[0]], by_y)
    pass_x = wires.make(pass_ref.at[pieces[1]], got.at[pieces[1]], by_x)
    pair_lower = wires.make(share_ref.at[pieces[1]], pair.at[pieces[1]], by_pair)
    pair_upper = wires.make(own.at[pieces[0]], pair_next, by_pair)
    loads = [
        pltpu.make_async_copy(first_ref, pair.at[pieces[0]], local.at[0]),
        pltpu.make_async_copy(own_ref, own, local.at[1]),
        pltpu.make_async_copy(share_ref, share_own, local.at[2]),
    ]
    keeps = [pltpu.make_async_copy(pair.at[rows], quads.at[quad, rows], local.at[3 + i]) for i, rows in enumerate(pieces)]
    overs = [wires.make(pair.at[rows], quads.at[quad, rows], by_z) for rows in pieces]
    cores = [wires.make(pair.at[rows], quads.at[quad, rows], by_core) for rows in pieces]
    passes = [wires.make(quads.at[quad_z, rows], quads.at[quad_z, rows], by_core) for rows in pieces]

    def spread(i):
        keeps[i].start()
        overs[i].start()
        cores[i].start()

    @pl.when(tile == 0)
    def _():
        greet([by_pair, by_x, by_y, by_core, by_z])
        for copy in [pass_y, pass_x, pair_lower] + loads:
            copy.start()
        normed_t[...] = normed_ref[...].T

    @pl.when(tile == 1)
    def _():
        for copy in loads:
            copy.wait()
        spread(0)

    @pl.when(tile == 2)
    def _():
        pass_y.wait()
        pass_x.wait()
        own[...] = add_low(own[...], got[...])

    @pl.when(tile == 4)
    def _():
        pair_lower.wait()
        pair_upper.start()
        pair[HALF:, :] = add_low(pair[HALF:, :], share_own[HALF:, :])
        spread(1)
        overs[0].wait_recv()
        passes[0].start()

    length = q_ref.shape[0]
    blocks = length // BLOCK
    lane = lax.broadcasted_iota(jnp.int32, (1, 128), 1)
    dqt_ref[...] = jnp.zeros_like(dqt_ref)
    odt_ref[...] = (do_ref[...].astype(jnp.float32) * o_ref[...].astype(jnp.float32)).T

    def head(h):
        mine = (lane >= 64 * h) & (lane < 64 * h + 64)
        dot_row = jnp.sum(odt_ref[64 * h : 64 * h + 64, :], axis=0, keepdims=True)
        for j in range(blocks):
            low, high = j * BLOCK, (j + 1) * BLOCK
            rest = length - low
            q = q_ref[low:, :] * jnp.bfloat16(0.125)
            do = do_ref[low:, :]
            k = jnp.where(mine, k_ref[low:high, :], jnp.bfloat16(0))
            v = jnp.where(mine, v_ref[low:high, :], jnp.bfloat16(0))
            s = dot_nt(k, q)
            same = segc_ref[low:high, :] == segr_ref[:, low:]
            kpos = lax.broadcasted_iota(jnp.int32, (BLOCK, rest), 0)
            qpos = lax.broadcasted_iota(jnp.int32, (BLOCK, rest), 1)
            p = jnp.where(same & (kpos <= qpos), jnp.exp(s - lse_ref[0, h : h + 1, low:]), 0.0)
            dp = dot_nt(v, do)
            ds = (p * (dp - dot_row[:, low:])).astype(jnp.bfloat16)
            dv = dot_nn(p.astype(jnp.bfloat16), do)
            dk = dot_nn(ds, q)
            if h == 0:
                dv_ref[low:high, :] = jnp.where(mine, dv, 0.0).astype(jnp.bfloat16)
                dk_ref[low:high, :] = jnp.where(mine, dk, 0.0).astype(jnp.bfloat16)
            else:
                dv_ref[low:high, :] = jnp.where(mine, dv.astype(jnp.bfloat16), dv_ref[low:high, :])
                dk_ref[low:high, :] = jnp.where(mine, dk.astype(jnp.bfloat16), dk_ref[low:high, :])
            dqt_ref[:, low:] += dot_nn(k.T, ds)

    head(0)

    @pl.when(tile < 6)
    def _():
        head(1)

    dq_ref[...] = (dqt_ref[...].T * 0.125).astype(jnp.bfloat16)

    row = lax.broadcasted_iota(jnp.int32, (8, 128), 0)
    sum_q = jnp.sum(dq_ref[...].astype(jnp.float32), axis=0, keepdims=True)
    sum_v = jnp.sum(dv_ref[...].astype(jnp.float32), axis=0, keepdims=True)
    sums_ref[...] = jnp.where(row == 0, sum_q, jnp.where(row == 1, sum_v, 0.0))

    grads = jnp.concatenate([dq_ref[...], dk_ref[...], dv_ref[...]], axis=1)
    weights = dot_nn(normed_t[...], grads).astype(jnp.bfloat16)
    for i in range(3):
        grad_ref[i] = weights[:, 128 * i : 128 * i + 128]

    @pl.when(tile == 6)
    def _():
        overs[1].wait_recv()
        passes[1].start()
        share_out[...] = own[...]
        pair_upper.wait()
        first_out[...] = add_low(own[:HALF, :], pair_next[...])
        for copy in cores + passes + keeps:
            copy.wait()
        for copy in overs:
            copy.wait_send()


def heads_back(qkv, grad, out, lse, segc, segr, normed, share, first, own, passed):
    length = qkv.shape[0]
    width = share.shape[1]
    buf = lambda *dims: pltpu.VMEM(dims, jnp.bfloat16)
    still = lambda *dims: pl.BlockSpec(dims, lambda t: (0,) * len(dims))
    spec = lambda off: pl.BlockSpec((length, 128), lambda t: (0, t + off))
    one = pl.BlockSpec((length, 128), lambda t: (0, t))
    shape = jax.ShapeDtypeStruct((length, 896), jnp.bfloat16)
    return pl.pallas_call(
        heads_back_kernel,
        grid=(7,),
        in_specs=[spec(0), spec(7), spec(14), one, one, pl.BlockSpec((1, 8, length), lambda t: (t, 0, 0)), pl.BlockSpec((length, 1), lambda t: (0, 0)), pl.BlockSpec((1, length), lambda t: (0, 0)), still(*normed.shape)] + [pl.BlockSpec(memory_space=pl.ANY)] * 4,
        out_specs=[one, one, one, pl.BlockSpec((8, 128), lambda t: (0, t)), pl.BlockSpec((3, width, 128), lambda t: (0, 0, t)), still(*share.shape), still(*first.shape), pl.BlockSpec(memory_space=pl.ANY)],
        out_shape=[
            shape,
            shape,
            shape,
            jax.ShapeDtypeStruct((8, 896), jnp.float32),
            jax.ShapeDtypeStruct((3, width, 896), jnp.bfloat16),
            jax.ShapeDtypeStruct(share.shape, share.dtype),
            jax.ShapeDtypeStruct(first.shape, share.dtype),
            jax.ShapeDtypeStruct((4,) + share.shape, share.dtype),
        ],
        scratch_shapes=[pltpu.VMEM((128, length), jnp.float32), pltpu.VMEM((128, length), jnp.float32), buf(400, width), buf(400, width), buf(400, width), buf(400, width), buf(HALF, width), buf(width, length), pltpu.SemaphoreType.DMA((10,)), pltpu.SemaphoreType.DMA((10,)), pltpu.SemaphoreType.DMA((5,))],
        compiler_params=pltpu.CompilerParams(vmem_limit_bytes=56 * 2**20, collective_id=4, has_side_effects=True),
        cost_estimate=pl.CostEstimate(flops=int(13 * 5 * 2 * length * length * 64 * 2), bytes_accessed=16 * length * 896, transcendentals=13 * length * length // 2),
        name="heads_back",
    )(qkv, qkv, qkv, grad, out, lse, segc, segr, normed, share, first, own, passed)

def feed_all_kernel(second, cot_in, cots, expand_part, reduce_shard, middle_in, out_in, bias, rows_ref, act_out, back_out, second_out, reduce_out, low_out, att_out, gs_out, own_out, pass_out, sum_out, norm_sums, wexp, wred, s, c, a, b, gs, got_core, got_z, rg, got_x, got_y, send, recv, local):
    replica = lax.axis_index("replica")
    group = lax.axis_index("group")
    quad = lax.rem(replica, 4)
    y = lax.div(group, 2)
    x = lax.rem(group, 2)
    by_x, by_y, by_both, by_core, by_z = partners(replica, group)
    slot_x, slot_y, slot_both = by_x[1], by_y[1], by_both[1]
    wires = Wires(send, recv, local)
    greet([by_x, by_y, by_core, by_z])
    width = wexp.shape[0]
    block = lambda rel: pl.ds(512 * rel, 512)
    sec_core = wires.go(second, s.at[block(1)], by_core)
    sec_z = wires.go(second, s.at[block(2)], by_z)
    quarter = reduce_shard.at[rows16(400 * quad, 400)]
    spot = lambda rank: rows16(400 * rank, 400)
    red_x = wires.go(quarter, wred.at[spot(group)], by_x)
    red_y = wires.go(quarter, wred.at[spot(group)], by_y)
    load_s = wires.here(second, s.at[block(0)])
    load_e = wires.here(expand_part, wexp)
    load_r = wires.here(quarter, wred.at[spot(group)])
    load_m = wires.here(middle_in, gs_out)
    load_c = [wires.here(cot_in, c.at[block(0)])] + [wires.here(cots.at[i], c.at[block(i + 1)]) for i in range(3)]
    sum_out[...] = jnp.zeros_like(sum_out)
    root = 0.7978845608028654

    def gelu(u):
        square = u * u
        t = jnp.tanh(root * u * (1.0 + 0.044715 * square))
        half = 0.5 * (1.0 + t)
        slope = half + (0.5 * root) * u * (1.0 - t * t) * (1.0 + (3.0 * 0.044715) * square)
        return u * half, slope

    def steps(rel, body):
        def one(i, carry):
            body(pl.ds(pl.multiple_of(512 * rel + 256 * i, 256), 256))
            return carry

        lax.fori_loop(0, 2, one, 0)

    def keep_back(rows, low_at, high_at, back):
        back = back.astype(jnp.bfloat16)
        b[rows, low_at:high_at] = back
        sum_out[:, low_at:high_at] += jnp.sum(back.astype(jnp.float32).reshape(32, 8, high_at - low_at), axis=0)

    def up_only(rows):
        entries = s[rows, :width]
        for low_at, high_at in PIECES:
            act, slope = gelu(dot_nn(entries, wexp[:, low_at:high_at]) + bias[:, low_at:high_at])
            a[rows, low_at:high_at] = act.astype(jnp.bfloat16)
            b[rows, low_at:high_at] = slope.astype(jnp.bfloat16)

    def finish_rows(rows):
        gs[rows, width:] = jnp.zeros((256, gs.shape[1] - width), jnp.bfloat16)
        gs[rows, :width] = dot_nt(b[rows, :], wexp[...]).astype(jnp.bfloat16)

    def back_only(rows):
        cot = c[rows, :]
        for low_at, high_at in PIECES:
            keep_back(rows, low_at, high_at, dot_nt(cot, wred[low_at:high_at, :]) * b[rows, low_at:high_at].astype(jnp.float32))
        finish_rows(rows)

    def both(rows):
        entries = s[rows, :width]
        cot = c[rows, :]
        for low_at, high_at in PIECES:
            act, slope = gelu(dot_nn(entries, wexp[:, low_at:high_at]) + bias[:, low_at:high_at])
            a[rows, low_at:high_at] = act.astype(jnp.bfloat16)
            keep_back(rows, low_at, high_at, dot_nt(cot, wred[low_at:high_at, :]) * slope)
        finish_rows(rows)

    load_s.wait()
    load_e.wait()
    steps(0, up_only)
    sec_core.wait_recv()
    steps(1, up_only)
    red_x.wait_recv()
    more_y = wires.go(wred.at[rows16(400 * slot_x, HALF)], wred.at[rows16(400 * slot_x, HALF)], by_y)
    red_y.wait_recv()
    more_x = wires.go(wred.at[rows16(400 * slot_y + HALF, 400 - HALF)], wred.at[rows16(400 * slot_y + HALF, 400 - HALF)], by_x)
    sec_z.wait_recv()
    sec_both = wires.go(s.at[block(2)], s.at[block(3)], by_core)
    load_r.wait()
    for copy in load_c:
        copy.wait()
    more_x.wait_recv()
    more_y.wait_recv()
    wires.keep(wred, reduce_out)
    sec_both.wait_recv()
    wires.keep(s, second_out)
    steps(3, both)
    gs_both = wires.go(gs.at[block(3)], got_core.at[1], by_core)
    steps(2, both)
    gs_both.wait_recv()
    gs[block(2), :] = add_low(gs[block(2), :], got_core[1])
    gs_z = wires.go(gs.at[block(2)], got_z, by_z)
    wires.keep(a, act_out)
    weight_sum(a, c, rg)
    x_copies = [wires.go(rg.at[rows16(400 * slot, HALF)], got_x.at[i], by_x) for i, slot in enumerate((slot_x, slot_both))]
    y_copies = [wires.go(rg.at[rows16(400 * slot + HALF, 400 - HALF)], got_y.at[i], by_y) for i, slot in enumerate((slot_y, slot_both))]
    steps(1, back_only)
    gs_core = wires.go(gs.at[block(1)], got_core.at[0], by_core)
    steps(0, back_only)
    wires.keep(b, back_out)
    load_w = wires.here(out_in, wexp)
    load_m.wait()
    gs_core.wait_recv()
    wires.drain([gs_both])
    gs_z.wait_recv()
    load_w.wait()
    norm_sums[...] = jnp.zeros_like(norm_sums)
    lanes = lax.broadcasted_iota(jnp.int32, (1, 128), 1)
    for seq in range(2):
        stage = got_core.at[1 - seq]

        def norm_back(j, carry):
            rows = pl.ds(pl.multiple_of(256 * seq + 128 * j, 128), 128)
            first = pl.ds(pl.multiple_of(128 * j, 128), 128)
            other = pl.ds(pl.multiple_of(256 + 128 * j, 128), 128)
            grad = gs[rows, :width].astype(jnp.float32) + got_core[0, rows, :width].astype(jnp.float32) + got_z[rows, :width].astype(jnp.float32)
            middle = gs_out[rows, :]
            center = middle - jnp.mean(middle, axis=-1, keepdims=True)
            scale = lax.rsqrt(jnp.mean(center * center, axis=-1, keepdims=True) + epsilon)
            unit = center * scale
            q = grad * rows_ref[6:7, :width]
            grad_middle = c[rows, :].astype(jnp.float32) + scale * (
                q - jnp.mean(q, axis=-1, keepdims=True) - unit * jnp.mean(q * unit, axis=-1, keepdims=True)
            )
            gs_out[rows, :] = grad_middle
            grad_low = grad_middle.astype(jnp.bfloat16)
            gs[rows, :width] = grad_low
            norm_sums[0:1, :] += jnp.sum(grad * unit, axis=0, keepdims=True)
            norm_sums[1:2, :] += jnp.sum(grad, axis=0, keepdims=True)
            norm_sums[2:3, :] += jnp.sum(grad_low.astype(jnp.float32), axis=0, keepdims=True)
            att = dot_nt(grad_low, wexp[...]).astype(jnp.bfloat16)
            stage[first, 0:768] = att[:, 0:768]
            stage[first, 768:896] = jnp.where(lanes < 64, att[:, 768:896], jnp.bfloat16(0))
            stage[other, 0:128] = jnp.where(lanes >= 64, att[:, 768:896], jnp.bfloat16(0))
            stage[other, 128 : width - 768] = att[:, 896:width]
            stage[other, width - 768 : 896] = jnp.zeros((128, 896 + 768 - width), jnp.bfloat16)
            return carry

        lax.fori_loop(0, 2, norm_back, 0)
        for half in range(2):
            wires.keep(stage.at[pl.ds(256 * half, 256), pl.ds(0, 896)], att_out.at[seq, half])
    wires.keep(gs.at[block(0)], low_out)
    for copy in x_copies + y_copies:
        copy.wait_recv()
    own_out[:HALF] = add_low(rg[rows16(400 * group, HALF), :], got_x[0])
    own_out[HALF:] = add_low(rg[rows16(400 * group + HALF, 400 - HALF), :], got_y[0])
    pass_out[:HALF] = add_low(rg[rows16(400 * slot_y, HALF), :], got_x[1])
    pass_out[HALF:] = add_low(rg[rows16(400 * slot_x + HALF, 400 - HALF), :], got_y[1])
    wires.finish()


def feed_all(second, cot, cots, expand_part, reduce_shard, middle, full_out, bias, rows_in):
    any_space = pl.BlockSpec(memory_space=pl.ANY)
    vmem = pl.BlockSpec(memory_space=pltpu.VMEM)
    shape = jax.ShapeDtypeStruct
    kind = jnp.bfloat16
    rows, full = second.shape
    width = expand_part.shape[0]
    buf = lambda *dims: pltpu.VMEM(dims, kind)
    return pl.pallas_call(
        feed_all_kernel,
        in_specs=[any_space] * 7 + [vmem, vmem],
        out_specs=[any_space] * 6 + [vmem] * 5,
        out_shape=[
            shape((4 * rows, width), kind),
            shape((4 * rows, width), kind),
            shape((4 * rows, full), kind),
            shape((width, width), kind),
            shape((rows, full), kind),
            shape((2, 2, 256, 896), kind),
            shape((rows, width), jnp.float32),
            shape((400, width), kind),
            shape((400, width), kind),
            shape((8, width), jnp.float32),
            shape((8, width), jnp.float32),
        ],
        scratch_shapes=[
            buf(width, width),
            buf(width, width),
            buf(4 * rows, full),
            buf(4 * rows, width),
            buf(4 * rows, width),
            buf(4 * rows, width),
            buf(4 * rows, full),
            buf(2, rows, full),
            buf(rows, full),
            buf(width, width),
            buf(2, HALF, width),
            buf(2, 400 - HALF, width),
            pltpu.SemaphoreType.DMA((16,)),
            pltpu.SemaphoreType.DMA((16,)),
            pltpu.SemaphoreType.DMA((20,)),
        ],
        compiler_params=pltpu.CompilerParams(collective_id=5, has_side_effects=True, vmem_limit_bytes=63 * 2**20),
        cost_estimate=pl.CostEstimate(flops=10**11, bytes_accessed=2**26, transcendentals=0),
        name="feed_all",
    )(second, cot, cots, expand_part, reduce_shard, middle, full_out, bias, rows_in)


def turn_more_kernel(grad_att, back, second, act, wred_in, pass_in, att_in, grad_in, own_in, heads_out, result_out, share_out, first_out, own_out, pass_out, core_out, att, grad, stage, b, s, a, wred, rg, result, got_core, got_z, got, got_x, got_y, pair, send, recv, local):
    replica = lax.axis_index("replica")
    group = lax.axis_index("group")
    core = lax.rem(replica, 2)
    y = lax.div(group, 2)
    x = lax.rem(group, 2)
    by_x, by_y, by_both, by_core, by_z = partners(replica, group)
    by_pair = (lax.rem(replica + 4, 8), group)
    slot_x, slot_y, slot_both = by_x[1], by_y[1], by_both[1]
    wires = Wires(send, recv, local)
    load_a = wires.here(act, a)
    load_w = wires.here(wred_in, wred)
    load_own = wires.here(grad_att.at[x, y], stage)
    load_s = wires.here(second, s)
    load_b = wires.here(back, b)
    load_att = wires.here(att_in, att)
    load_grad = wires.here(grad_in, grad)
    greet([by_x, by_y, by_both, by_core, by_z, by_pair])
    width = wred.shape[0]
    block = lambda rel: pl.ds(512 * rel, 512)
    pass_y = wires.go(pass_in.at[pl.ds(0, HALF)], got.at[pl.ds(0, HALF)], by_y)
    pass_x = wires.go(pass_in.at[pl.ds(HALF, 400 - HALF)], got.at[pl.ds(HALF, 400 - HALF)], by_x)
    load_a.wait()
    load_w.wait()

    def rows_out(rel):
        def one(i, carry):
            rows = pl.ds(pl.multiple_of(512 * rel + 256 * i, 256), 256)
            result[rows, :] = dot_nn(a[rows, :], wred[...]).astype(jnp.bfloat16)
            return carry

        lax.fori_loop(0, 2, one, 0)

    rows_out(3)
    to_both = wires.go(result.at[block(3)], got_core.at[1], by_core)
    rows_out(2)
    wires.drain([pass_y, pass_x])
    turns = []
    for device in (by_both, by_x, by_y):
        there = device[1]
        turns.append(wires.go(grad_att.at[lax.rem(there, 2), lax.div(there, 2)], heads_out.at[group], device))
    to_both.wait_recv()
    result[block(2), :] = add_low(result[block(2), :], got_core[1])
    to_z = wires.go(result.at[block(2)], got_z, by_z)
    pass_y.wait_recv()
    pass_x.wait_recv()
    share_out[...] = add_low(own_in[...], got[...])
    pair_upper = wires.go(share_out.at[pl.ds(0, HALF)], pair, by_pair)
    load_own.wait()
    wires.keep(stage, heads_out.at[group])
    load_s.wait()
    load_b.wait()
    weight_sum(s, b, rg)
    x_copies = [wires.go(rg.at[rows16(400 * slot, HALF)], got_x.at[i], by_x) for i, slot in enumerate((slot_x, slot_both))]
    y_copies = [wires.go(rg.at[rows16(400 * slot + HALF, 400 - HALF)], got_y.at[i], by_y) for i, slot in enumerate((slot_y, slot_both))]
    rows_out(1)
    to_core = wires.go(result.at[block(1)], got_core.at[0], by_core)
    rows_out(0)
    load_att.wait()
    load_grad.wait()
    weight_sum(att, grad, wred)
    out_core = [wires.go(wred.at[rows16(400 * r + 192 * (1 - core), 208)], core_out.at[r], by_core) for r in range(4)]
    for r in range(4):
        out_core[r].wait_recv()
        core_out[r] = add_low(wred[rows16(400 * r + 192 * core, 208), :], core_out[r])
    to_core.wait_recv()
    to_z.wait_recv()
    result_out[...] = result[block(0), :].astype(jnp.float32) + got_core[0].astype(jnp.float32) + got_z[...].astype(jnp.float32)
    pair_upper.wait_recv()
    first_out[...] = add_low(share_out[:HALF, :], pair[...])
    for copy in x_copies + y_copies:
        copy.wait_recv()
    own_out[:HALF] = add_low(rg[rows16(400 * group, HALF), :], got_x[0])
    own_out[HALF:] = add_low(rg[rows16(400 * group + HALF, 400 - HALF), :], got_y[0])
    pass_out[:HALF] = add_low(rg[rows16(400 * slot_y, HALF), :], got_x[1])
    pass_out[HALF:] = add_low(rg[rows16(400 * slot_x + HALF, 400 - HALF), :], got_y[1])
    for copy in turns:
        copy.wait_recv()
    wires.finish()


def turn_more(grad_att, back, second, act, wred, passed, att, grad, own):
    any_space = pl.BlockSpec(memory_space=pl.ANY)
    vmem = pl.BlockSpec(memory_space=pltpu.VMEM)
    shape = jax.ShapeDtypeStruct
    kind = jnp.bfloat16
    width = wred.shape[0]
    rows = act.shape[0] // 4
    buf = lambda *dims: pltpu.VMEM(dims, kind)
    return pl.pallas_call(
        turn_more_kernel,
        in_specs=[any_space] * 8 + [vmem],
        out_specs=[any_space] + [vmem] * 6,
        out_shape=[
            shape((4,) + grad_att.shape[2:], kind),
            shape((rows, width), jnp.float32),
            shape((400, width), kind),
            shape((HALF, width), kind),
            shape((400, width), kind),
            shape((400, width), kind),
            shape((4, 208, width), kind),
        ],
        scratch_shapes=[
            buf(rows, width),
            buf(*grad.shape),
            buf(*grad_att.shape[2:]),
            buf(4 * rows, width),
            buf(*second.shape),
            buf(4 * rows, width),
            buf(width, width),
            buf(width, width),
            buf(4 * rows, width),
            buf(2, rows, width),
            buf(rows, width),
            buf(400, width),
            buf(2, HALF, width),
            buf(2, 400 - HALF, width),
            buf(HALF, width),
            pltpu.SemaphoreType.DMA((18,)),
            pltpu.SemaphoreType.DMA((18,)),
            pltpu.SemaphoreType.DMA((10,)),
        ],
        compiler_params=pltpu.CompilerParams(collective_id=2, has_side_effects=True, vmem_limit_bytes=63 * 2**20),
        cost_estimate=pl.CostEstimate(flops=3 * 10**10, bytes_accessed=2**26, transcendentals=0),
        name="turn_more",
    )(grad_att, back, second, act, wred, passed, att, grad, own)


def arrive(here, there, total, lane, k, y, mine):
    first = jnp.where(y == 0, here, there)
    other = jnp.where(y == 0, there, here)
    rows = pl.ds(mine, 208)
    total[k, rows, 0:768] = first[:, 0:768]
    total[k, rows, 768:896] = jnp.where(lane < 64, first[:, 768:896], other[:, 0:128])
    total[k, rows, 896:1664] = other[:, 128:896]


def last_kernel(dq, dk, dv, grad_in, unit_in, w_in, share_in, share_expand, first_expand, vec, gm_in, inp_in, gain, total, grad_out, vec_total, wide_total, quads, d, unit_rows, w, part, c_buf, x_buf, y_buf, line_buf, line_mid, gn, gn_y, gn_cross, inp, pair_buf, vec_got, vec_own, vec_core, vec_z, more_got, more_core, more_z, send, recv, local):
    replica = lax.axis_index("replica")
    group = lax.axis_index("group")
    core = lax.rem(replica, 2)
    quad = lax.rem(replica, 4)
    quad_z = lax.rem(quad + 2, 4)
    z = lax.div(replica, 2)
    y = lax.div(group, 2)
    x = lax.rem(group, 2)
    by_x, by_y, by_both, by_core, by_z = partners(replica, group)
    outer = (z == 0) | (z == 3)
    inner = jnp.logical_not(outer)
    by_line = (jnp.where(z == 0, replica + 2, jnp.where(z == 3, replica - 2, jnp.where(z == 1, replica - 2, replica + 2))), group)
    by_middle = (jnp.where(z == 1, replica + 2, replica - 2), group)
    lines_z = [(lax.rem(replica + 2 * k, 8), group) for k in (1, 2, 3)]
    by_pair = lines_z[1]
    wires = Wires(send, recv, local)
    greet([by_x, by_y, by_both, by_core] + lines_z)
    mine = pl.multiple_of(192 * core, 16)
    theirs = pl.multiple_of(192 * (1 - core), 16)
    other_x = 1 - x
    other_y = 1 - y
    far = 2 * other_y
    near = 2 * y
    width = w.shape[0]
    lane = lax.broadcasted_iota(jnp.int32, (1, 128), 1)
    halves = [(pl.ds(mine + 112 * m, 112 - 16 * m), pl.ds(112 * m, 112 - 16 * m)) for m in range(2)]
    pieces = [pl.ds(0, 208), pl.ds(208, 192)]

    pair_lower = wires.go(share_expand.at[pieces[1]], pair_buf, by_pair)
    c_copies = []
    part_loads = []
    for k in range(3):
        c_copies.append([wires.go(grad_in.at[k, rows16(400 * r + theirs, 208)], c_buf.at[k, r], by_core) for r in range(4)])
        part_loads.append([wires.here(grad_in.at[k, pl.ds(400 * r + mine, 208)], part.at[k, r]) for r in range(4)])
    loads = [wires.here(part, d.at[k]) for k, part in enumerate((dq, dk, dv))]
    load_w = [wires.here(w_in, w), wires.here(unit_in, unit_rows)]
    load_share = wires.here(share_in, total.at[3, pl.ds(mine, 208)])
    vec_group = [wires.go(vec.at[device[1]], vec_got.at[group], device) for device in (by_x, by_y, by_both)]

    def spread(value, rows):
        wires.keep(value, quads.at[quad, rows])
        over = wires.go(value, quads.at[quad, rows], by_z)
        return over, wires.go(value, quads.at[quad, rows], by_core)

    def spread_on(over, rows):
        over.wait_recv()
        return wires.go(quads.at[quad_z, rows], quads.at[quad_z, rows], by_core)

    load_gm = wires.here(gm_in, grad_out)
    load_inp = wires.here(inp_in, inp)

    def line_start(k, m):
        rows, merge = halves[m]
        into = wires.make(total.at[k, rows], line_buf.at[k, merge], by_line)
        middle = wires.make(total.at[k, rows], line_mid.at[k, merge], by_middle)
        back = wires.make(total.at[k, rows], line_buf.at[k, merge], by_line)

        @pl.when(outer)
        def _():
            if m == 1:
                lines[k, 0][0].wait_send()
            into.start()

        lines[k, m] = into, middle, back

    def line_second(k, m):
        rows, merge = halves[m]
        into, middle, back = lines[k, m]

        @pl.when(inner)
        def _():
            into.wait_recv()
            total[k, rows] = add_low(total[k, rows], line_buf[k, merge])
            middle.start()

    def line_third(k, m):
        rows, merge = halves[m]
        into, middle, back = lines[k, m]

        @pl.when(inner)
        def _():
            middle.wait_recv()
            middle.wait_send()
            total[k, rows] = add_low(total[k, rows], line_mid[k, merge])
            back.start()

    def line_fourth(k, m):
        rows, merge = halves[m]
        into, middle, back = lines[k, m]

        @pl.when(outer)
        def _():
            if m == 1:
                into.wait_send()
            back.wait_recv()
            total[k, rows] = line_buf[k, merge]

        @pl.when(inner)
        def _():
            back.wait_send()

    lines = {}
    x_copies = {}
    y_copies = {}

    def core_sum(k):
        for r in range(4):
            part_loads[k][r].wait()
            c_copies[k][r].wait_recv()
            c_buf[k, r] = add_low(c_buf[k, r], part[k, r])

    def x_go(k, i):
        row = (other_y, y)[i]
        x_copies[k, i] = wires.go(c_buf.at[k, 2 * row + other_x], x_buf.at[k, i], by_x)

    def x_next(k, i, after):
        wires.drain([x_copies[k, i]])
        if after is not None:
            x_go(*after)
        x_copies[k, i].wait_recv()
        spot = (far, near)[i] + x
        c_buf[k, spot] = add_low(c_buf[k, spot], x_buf[k, i])
        if i == 0:
            y_copies[k] = wires.go(c_buf.at[k, spot], y_buf.at[k], by_y)

    def y_done(k):
        y_copies[k].wait_recv()
        arrive(c_buf[k, near + x], y_buf[k], total, lane, k, y, mine)
        line_start(k, 0)

    def normed_grad(b):
        rows = pl.ds(pl.multiple_of(256 * b, 256), 256)
        value = dot_nt(d[0, rows, :], w[:, 0:896]) + dot_nt(d[1, rows, :], w[:, 896:1792]) + dot_nt(d[2, rows, :], w[:, 1792:2688])
        gn[b] = value.astype(jnp.bfloat16)
        more_got[group, 0:1, 0:width] += jnp.sum(value * unit_rows[rows, :].astype(jnp.float32), axis=0, keepdims=True)
        more_got[group, 1:2, 0:width] += jnp.sum(value, axis=0, keepdims=True)

    spread_expand = [spread(first_expand, pieces[0])]
    core_sum(0)
    x_go(0, 0)
    x_go(0, 1)
    core_sum(1)
    core_sum(2)
    load_share.wait()
    line_start(3, 0)
    more_got[group] = jnp.zeros(more_got.shape[1:], jnp.float32)
    for copy in loads + load_w:
        copy.wait()
    normed_grad(far + other_x)
    y_pass = wires.go(gn.at[far + other_x], gn_y.at[0], by_y)
    normed_grad(near + other_x)
    x_next(0, 0, (1, 0))
    x_next(0, 1, (1, 1))
    line_start(3, 1)
    line_second(3, 0)
    normed_grad(far + x)
    y_done(0)
    normed_grad(near + x)
    more_group = [wires.go(more_got.at[group], more_got.at[group], device) for device in (by_x, by_y, by_both)]
    for copy in vec_group:
        copy.wait_recv()
    vec_got[group] = vec[group]
    vec_own[...] = (vec_got[0] + vec_got[1]) + (vec_got[2] + vec_got[3])
    vec_pass = wires.go(vec_own, vec_core, by_core)
    x_next(1, 0, (2, 0))
    line_start(0, 1)
    line_second(3, 1)
    y_pass.wait_recv()
    gn_y[0] = add_low(gn_y[0], gn[near + other_x])
    line_second(0, 0)
    x_next(1, 1, (2, 1))
    y_done(1)
    for copy in more_group:
        copy.wait_recv()
    more_z[z] = (more_got[0] + more_got[1]) + (more_got[2] + more_got[3])
    more_pass = wires.go(more_z.at[z], more_core, by_core)
    line_third(3, 0)
    line_second(0, 1)
    vec_pass.wait_recv()
    vec_z[z] = vec_own[...] + vec_core[...]
    vec_line = [wires.go(vec_z.at[z], vec_z.at[z], device) for device in lines_z]
    line_start(1, 1)
    x_next(2, 0, None)
    cross = wires.go(gn_y.at[0], gn_cross, by_x)
    y_keep = wires.go(gn.at[far + x], gn_y.at[1], by_y)
    line_second(1, 0)
    line_third(3, 1)
    x_next(2, 1, None)
    y_done(2)
    pair_lower.wait_recv()
    pair_buf[...] = add_low(pair_buf[...], share_expand[HALF:, :])
    spread_expand.append(spread(pair_buf, pieces[1]))
    line_third(0, 0)
    line_second(1, 1)
    line_start(2, 1)
    more_pass.wait_recv()
    wires.drain([more_pass])
    more_z[z] = more_z[z] + more_core[...]
    more_line = [wires.go(more_z.at[z], more_z.at[z], device) for device in lines_z]
    line_third(0, 1)
    line_second(2, 0)
    line_third(1, 0)
    passes = [spread_on(spread_expand[0][0], pieces[0])]
    line_second(2, 1)
    line_third(1, 1)

    load_gm.wait()
    load_inp.wait()

    def norm_back(seq, grad):
        entries = inp[seq].astype(jnp.float32)
        center = entries - jnp.mean(entries, axis=-1, keepdims=True)
        scale = lax.rsqrt(jnp.mean(center * center, axis=-1, keepdims=True) + epsilon)
        unit = center * scale
        q = grad * gain[...]
        grad_out[seq] += scale * (q - jnp.mean(q, axis=-1, keepdims=True) - unit * jnp.mean(q * unit, axis=-1, keepdims=True))

    y_keep.wait_recv()
    norm_back(x, gn_y[1].astype(jnp.float32) + gn[near + x].astype(jnp.float32))
    cross.wait_recv()
    norm_back(other_x, gn_cross[...].astype(jnp.float32))
    line_third(2, 0)
    line_third(2, 1)
    for copy in vec_line:
        copy.wait_recv()
    vec_total[...] = (vec_z[0] + vec_z[1]) + (vec_z[2] + vec_z[3])
    passes.append(spread_on(spread_expand[1][0], pieces[1]))
    last = []
    for k in (3, 0, 1, 2):
        line_fourth(k, 0)
        line_fourth(k, 1)
        rows = pl.ds(pl.multiple_of(208 * core, 16), 192)
        last.append(wires.go(total.at[k, rows], total.at[k, rows], by_core))
    for copy in more_line:
        copy.wait_recv()
    wide_total[...] = (more_z[0] + more_z[1]) + (more_z[2] + more_z[3])
    for copy in last + passes + [both for over, both in spread_expand]:
        copy.wait_recv()
    wires.finish()


def last_sums(dq, dk, dv, in_grad, unit, w_half, out_share, share_expand, first_expand, vec, grad_middle, inputs, gain):
    any_space = pl.BlockSpec(memory_space=pl.ANY)
    vmem = pl.BlockSpec(memory_space=pltpu.VMEM)
    shape = jax.ShapeDtypeStruct
    kind = jnp.bfloat16
    width = w_half.shape[0]
    buf = lambda *dims: pltpu.VMEM(dims, kind)
    flat = lambda *dims: pltpu.VMEM(dims, jnp.float32)
    return pl.pallas_call(
        last_kernel,
        in_specs=[any_space] * 7 + [vmem, vmem, vmem, any_space, any_space, vmem],
        out_specs=[vmem, vmem, vmem, vmem, any_space],
        out_shape=[
            shape((4, 400, 1664), kind),
            shape(grad_middle.shape, jnp.float32),
            shape(vec.shape[1:], vec.dtype),
            shape((8, 1664), jnp.float32),
            shape((4,) + share_expand.shape, kind),
        ],
        scratch_shapes=[
            buf(3, 1024, 896),
            buf(*unit.shape),
            buf(*w_half.shape),
            buf(3, 4, 208, 896),
            buf(3, 4, 208, 896),
            buf(3, 2, 208, 896),
            buf(3, 208, 896),
            buf(4, 208, 1664),
            buf(4, 208, 1664),
            buf(4, 256, width),
            buf(2, 256, width),
            buf(256, width),
            buf(*inputs.shape),
            buf(400 - HALF, width),
            flat(*vec.shape),
            flat(*vec.shape[1:]),
            flat(*vec.shape[1:]),
            flat(*vec.shape),
            flat(4, 8, 1664),
            flat(8, 1664),
            flat(4, 8, 1664),
            pltpu.SemaphoreType.DMA((88,)),
            pltpu.SemaphoreType.DMA((88,)),
            pltpu.SemaphoreType.DMA((24,)),
        ],
        compiler_params=pltpu.CompilerParams(collective_id=3, has_side_effects=True, vmem_limit_bytes=63 * 2**20),
        cost_estimate=pl.CostEstimate(flops=10**11, bytes_accessed=2**26, transcendentals=0),
        name="last_sums",
    )(dq, dk, dv, in_grad, unit, w_half, out_share, share_expand, first_expand, vec, grad_middle, inputs, gain)


def on_device(
    inputs,
    segments,
    cotangent,
    project_in,
    project_out,
    expand_weight,
    reduce_weight,
    query_bias,
    value_bias,
    project_bias,
    expand_bias,
    reduce_bias,
    first_gain,
    first_shift,
    second_gain,
    second_shift,
):
    replica, group, z, core, y, x = place()
    quad = lax.rem(replica, 4)
    width = 1600
    rows = 512

    vec = jnp.concatenate(
        [
            jnp.stack([query_bias, value_bias, project_bias, reduce_bias, first_gain, first_shift, second_gain, second_shift]),
            expand_bias.reshape(4, 400),
            jnp.zeros((4, 400), jnp.bfloat16),
        ]
    )
    x_seq, w_half, vecs, segs = first_exchange(inputs, project_in, vec, segments[:, None, :])
    row_vectors = padded(jnp.swapaxes(wide(vecs), 0, 1).reshape(16, width))
    bias_reduce = row_vectors[3:4, :width]
    bias_expand = lax.dynamic_index_in_dim(wide(vecs), 8 + quad, 1, False).reshape(1, width)
    segs = segs.reshape(1024)

    expand_shard = hold(expand_weight, x_seq)
    quarter_expand = jnp.concatenate(
        [lax.dynamic_slice_in_dim(expand_shard, 1600 * k + 400 * quad, 400, 1) for k in range(4)], axis=1
    )
    w_half = w_half.reshape(width, 2688)
    segc = segs[:, None]
    segr = segs[None]
    own_cot = cotangent.reshape(rows, width)
    mixture, normed, unit_seq, attended, lse, full_out, expand_part, cots = mix_heads(
        x_seq.reshape(1024, width), w_half, row_vectors, segc, segr, project_out, quarter_expand, own_cot
    )
    full_out = full_out.reshape(width, width)
    att_tokens, middle, second = turn_middle(attended.reshape(4, 256, 896), full_out, inputs, row_vectors)
    (
        activated,
        grad_expanded,
        second_all,
        reduce_part,
        grad_middle_low,
        grad_att,
        grad_middle,
        own_reduce,
        pass_reduce,
        expand_sums,
        norm_sums,
    ) = feed_all(
        second, own_cot, cots, expand_part.reshape(width, width), reduce_weight, middle, full_out, bias_expand, row_vectors
    )

    grad_heads, result, share_reduce, first_reduce, own_expand, pass_expand, out_core = turn_more(
        grad_att, grad_expanded, second_all, activated, reduce_part, pass_reduce, att_tokens, grad_middle_low, own_reduce
    )
    out_share = padded(lax.psum_scatter(out_core, "group", scatter_dimension=0, tiled=False))
    outputs = low(result + middle + bias_reduce).reshape(2, 256, width)
    dq, dk, dv, bias_sums, in_grad, share_expand, first_expand, quads_reduce = heads_back(
        mixture, grad_heads.reshape(1024, 896), attended, lse, segc, segr, normed, share_reduce, first_reduce, own_expand, pass_expand
    )

    def spread(columns):
        lower = jnp.concatenate([columns[:832], jnp.zeros((768,), jnp.float32)])
        upper = jnp.concatenate([jnp.zeros((832,), jnp.float32), columns[64:832]])
        return jnp.where(y == 0, lower, upper)

    expand_bias_part = jnp.sum(expand_sums, axis=0).reshape(4, 400)
    expand_bias_wide = lax.dynamic_update_slice_in_dim(jnp.zeros((4, width), jnp.float32), expand_bias_part, 400 * quad, 1)
    vectors = jnp.concatenate(
        [
            spread(bias_sums[0]).reshape(4, 400),
            spread(bias_sums[1]).reshape(4, 400),
            norm_sums[2].reshape(4, 400),
            column_sum(cotangent.reshape(rows, width)).reshape(4, 400),
            norm_sums[0].reshape(4, 400),
            norm_sums[1].reshape(4, 400),
            expand_bias_wide,
        ],
        axis=1,
    )
    vectors = jnp.pad(vectors, ((0, 0), (0, 96))).reshape(4, 32, 128)
    grad_total, input_grad, vec_total, wide_total, quads_expand = last_sums(
        dq, dk, dv, in_grad, unit_seq, w_half, out_share, share_expand, first_expand, vectors, grad_middle.reshape(2, 256, width), inputs, row_vectors[4:5, :width]
    )
    vec_total = vec_total.reshape(4096)
    pieces = [vec_total[400 * k : 400 * k + 400] for k in range(6)]
    first_sums = lax.dynamic_index_in_dim(wide_total[:2, :width].reshape(2, 4, 400), group, 1, False)
    total_reduce = wide(quads_reduce.reshape(width, width))
    total_expand = finish_feed(quads_expand)
    total_in, total_out = finish_mixer(grad_total)
    return (
        outputs,
        input_grad,
        total_in,
        total_out,
        total_expand,
        total_reduce,
        pieces[0],
        pieces[1],
        pieces[2],
        vec_total[2400:4000],
        pieces[3],
        first_sums[0],
        first_sums[1],
        pieces[4],
        pieces[5],
    )


def solution(mesh):
    placed = (
        P("replica", "group", None),
        P("replica", "group"),
        P("replica", "group", None),
        P("group", None),
        P("group", None),
        P("group", None),
        P("group", None),
        P("group"),
        P("group"),
        P("group"),
        P("group"),
        P("group"),
        P("group"),
        P("group"),
        P("group"),
        P("group"),
    )
    return jax.shard_map(
        on_device if dict(mesh.shape) == {"replica": 8, "group": 4} else on_device_any,
        mesh=mesh,
        in_specs=placed,
        out_specs=(
            P("replica", "group", None),
            P("replica", "group", None),
            P("group", None),
            P("group", None),
            P("group", None),
            P("group", None),
            P("group"),
            P("group"),
            P("group"),
            P("group"),
            P("group"),
            P("group"),
            P("group"),
            P("group"),
            P("group"),
        ),
        check_vma=False,
    )
```

```python
import functools
import math

import jax
import jax.numpy as jnp
from jax import lax
from jax.sharding import PartitionSpec as P

from jax.experimental import pallas as pl
from jax.experimental.pallas import tpu as pltpu

HEADS = 25
HEAD_DIM = 64


epsilon = 1e-05
very_low = -1e30


def carried_in(part, axis, combine, identity):
    place = lax.axis_index(axis)
    gathered = lax.all_gather(part, axis)
    state = jnp.zeros_like(part) + jnp.asarray(identity, part.dtype)

    def one(hop, state):
        return combine(state, lax.dynamic_index_in_dim(gathered, hop, 0, False))

    return lax.fori_loop(0, place, one, state)


def layer_norm(entries, gain, shift):
    center = entries - jnp.mean(entries, axis=-1, keepdims=True)
    spread = jnp.mean(center * center, axis=-1, keepdims=True)
    return center * lax.rsqrt(spread + epsilon) * gain + shift


def product(left, right):
    return jnp.dot(left, right, preferred_element_type=jnp.float32)


def product_back(left, right):
    return lax.dot_general(
        left, right, (((1,), (1,)), ((), ())), preferred_element_type=jnp.float32
    )


def weight_term(left, right):
    return lax.dot_general(
        left, right, (((0,), (0,)), ((), ())), preferred_element_type=jnp.float32
    )


def column_sum(entries):
    return jnp.sum(entries.astype(jnp.float32), axis=0)


def block_scores(queries, key_block, offset, query_pos, doc_start):
    block_count = key_block.shape[0]
    key_count = key_block.shape[2]
    scaling = 1.0 / math.sqrt(HEAD_DIM)
    scores = (
        jnp.einsum("schd,pskhd->shcpk", queries, key_block, preferred_element_type=jnp.float32)
        * scaling
    )
    key_pos = (offset + jnp.arange(block_count, dtype=jnp.int32))[:, None] * key_count + jnp.arange(
        key_count, dtype=jnp.int32
    )[None, :]
    allowed = (key_pos[None, None] <= query_pos[None, :, None, None]) & (
        key_pos[None, None] >= doc_start[:, :, None, None]
    )
    allowed = allowed[:, None]
    return (jnp.where(allowed, scores, very_low), allowed)


def attend(running, key_block, value_block, offset, queries, query_pos, doc_start):
    largest, denominator, summed = running
    masked, allowed = block_scores(queries, key_block, offset, query_pos, doc_start)
    fresh = jnp.maximum(largest, jnp.max(masked, axis=(3, 4)))
    shares = jnp.where(allowed, jnp.exp(masked - fresh[..., None, None]), 0.0)
    rescale = jnp.exp(largest - fresh)
    denominator = denominator * rescale + jnp.sum(shares, axis=(3, 4))
    added = jnp.einsum(
        "shcpk,pskhd->schd",
        shares.astype(jnp.bfloat16),
        value_block,
        preferred_element_type=jnp.float32,
    )
    summed = summed * jnp.transpose(rescale, (0, 2, 1))[..., None] + added
    return (fresh, denominator, summed)


def attend_back(
    grad_query,
    key_block,
    value_block,
    offset,
    queries,
    query_pos,
    doc_start,
    log_total,
    grad_low,
    row_dot,
):
    masked, allowed = block_scores(queries, key_block, offset, query_pos, doc_start)
    shares = jnp.where(allowed, jnp.exp(masked - log_total[..., None, None]), 0.0)
    grad_value = jnp.einsum(
        "shcpk,schd->pskhd",
        shares.astype(jnp.bfloat16),
        grad_low,
        preferred_element_type=jnp.float32,
    )
    grad_share = jnp.einsum(
        "schd,pskhd->shcpk", grad_low, value_block, preferred_element_type=jnp.float32
    )
    grad_score = (shares * (grad_share - row_dot[..., None, None])).astype(jnp.bfloat16)
    grad_query = grad_query + jnp.einsum(
        "shcpk,pskhd->schd", grad_score, key_block, preferred_element_type=jnp.float32
    )
    grad_key = jnp.einsum(
        "shcpk,schd->pskhd", grad_score, queries, preferred_element_type=jnp.float32
    )
    return (grad_query, (grad_key, grad_value))


def on_device_any(
    inputs,
    segments,
    cotangent,
    project_in,
    project_out,
    expand_weight,
    reduce_weight,
    query_bias,
    value_bias,
    project_bias,
    expand_bias,
    reduce_bias,
    first_gain,
    first_shift,
    second_gain,
    second_shift,
):
    seq_here, local_len, width = inputs.shape
    groups = lax.axis_size("group")
    total_rows = seq_here * local_len
    head_shape = (seq_here, local_len, HEADS, HEAD_DIM)
    shards = (
        project_in,
        project_out,
        expand_weight,
        reduce_weight,
        query_bias,
        value_bias,
        project_bias,
        expand_bias,
        reduce_bias,
        first_gain,
        first_shift,
        second_gain,
        second_shift,
    )
    whole = (
        lax.all_gather(shards[0], "group", axis=0, tiled=True),
        lax.all_gather(shards[1], "group", axis=0, tiled=True),
        lax.all_gather(shards[2], "group", axis=0, tiled=True),
        lax.all_gather(shards[3], "group", axis=0, tiled=True),
        lax.all_gather(shards[4], "group", axis=0, tiled=True),
        lax.all_gather(shards[5], "group", axis=0, tiled=True),
        lax.all_gather(shards[6], "group", axis=0, tiled=True),
        lax.all_gather(shards[7], "group", axis=0, tiled=True),
        lax.all_gather(shards[8], "group", axis=0, tiled=True),
        lax.all_gather(shards[9], "group", axis=0, tiled=True),
        lax.all_gather(shards[10], "group", axis=0, tiled=True),
        lax.all_gather(shards[11], "group", axis=0, tiled=True),
        lax.all_gather(shards[12], "group", axis=0, tiled=True),
    )
    (
        full_in,
        full_out,
        full_expand,
        full_reduce,
        bias_query,
        bias_value,
        bias_project,
        bias_expand,
        bias_reduce,
        gain_first,
        shift_first,
        gain_second,
        shift_second,
    ) = whole
    group_rank = lax.axis_index("group")
    query_pos = group_rank * local_len + jnp.arange(local_len, dtype=jnp.int32)
    positions = jnp.broadcast_to(query_pos[None, :], (seq_here, local_len))
    end_marks = jnp.where(segments == positions, positions + 1, 0)
    before = carried_in(
        jnp.max(end_marks, axis=1), "group", jnp.maximum, jnp.zeros((seq_here,), jnp.int32)
    )
    inside = lax.cummax(end_marks, axis=1)
    inside = jnp.concatenate([jnp.zeros((seq_here, 1), jnp.int32), inside[:, :-1]], axis=1)
    doc_start = jnp.maximum(before[:, None], inside)
    flat_input = inputs.reshape(total_rows, width).astype(jnp.float32)
    normed_low = layer_norm(
        flat_input, gain_first.astype(jnp.float32), shift_first.astype(jnp.float32)
    ).astype(jnp.bfloat16)
    mixture = product(normed_low, full_in)
    queries = (
        (mixture[:, :width] + bias_query.astype(jnp.float32))
        .astype(jnp.bfloat16)
        .reshape(head_shape)
    )
    key_rows = (
        mixture[:, width : 2 * width].astype(jnp.bfloat16).reshape(seq_here, local_len, width)
    )
    value_rows = (
        (mixture[:, 2 * width :] + bias_value.astype(jnp.float32))
        .astype(jnp.bfloat16)
        .reshape(seq_here, local_len, width)
    )
    initial = (
        jnp.full((seq_here, HEADS, local_len), very_low, jnp.float32),
        jnp.zeros((seq_here, HEADS, local_len), jnp.float32),
        jnp.zeros(head_shape, jnp.float32),
    )
    block_ids = jnp.arange(groups, dtype=jnp.int32)
    running = initial
    pieces = (
        lax.all_gather(key_rows[None], "group", axis=0, tiled=True),
        lax.all_gather(value_rows[None], "group", axis=0, tiled=True),
    )
    piece_count = pieces[0].shape[0]

    def one_piece(state, members):
        key_piece, value_piece, index = members
        updated = attend(
            state,
            key_piece.reshape((1,) + head_shape),
            value_piece.reshape((1,) + head_shape),
            index,
            queries,
            query_pos,
            doc_start,
        )
        return (updated, None)

    running, unused_steps = lax.scan(
        one_piece, running, (pieces[0], pieces[1], jnp.arange(piece_count, dtype=jnp.int32))
    )
    largest, denominator, summed = running
    attended = summed / jnp.transpose(denominator, (0, 2, 1))[..., None]
    log_total = largest + jnp.log(denominator)
    attended_low = attended.reshape(total_rows, width).astype(jnp.bfloat16)
    middle = flat_input + product(attended_low, full_out) + bias_project.astype(jnp.float32)
    second_low = layer_norm(
        middle, gain_second.astype(jnp.float32), shift_second.astype(jnp.float32)
    ).astype(jnp.bfloat16)
    expanded = product(second_low, full_expand) + bias_expand.astype(jnp.float32)
    activated_low = jax.nn.gelu(expanded, approximate=True).astype(jnp.bfloat16)
    result = middle + product(activated_low, full_reduce) + bias_reduce.astype(jnp.float32)
    outputs = result.astype(jnp.bfloat16).reshape(seq_here, local_len, width)
    whole_back = (
        lax.all_gather(shards[0], "group", axis=0, tiled=True),
        lax.all_gather(shards[1], "group", axis=0, tiled=True),
        lax.all_gather(shards[2], "group", axis=0, tiled=True),
        lax.all_gather(shards[3], "group", axis=0, tiled=True),
        lax.all_gather(shards[4], "group", axis=0, tiled=True),
        lax.all_gather(shards[5], "group", axis=0, tiled=True),
        lax.all_gather(shards[6], "group", axis=0, tiled=True),
        lax.all_gather(shards[7], "group", axis=0, tiled=True),
        lax.all_gather(shards[8], "group", axis=0, tiled=True),
        lax.all_gather(shards[9], "group", axis=0, tiled=True),
        lax.all_gather(shards[10], "group", axis=0, tiled=True),
        lax.all_gather(shards[11], "group", axis=0, tiled=True),
        lax.all_gather(shards[12], "group", axis=0, tiled=True),
    )
    keys_back = (
        lax.all_gather(key_rows[None], "group", axis=0, tiled=True),
        lax.all_gather(value_rows[None], "group", axis=0, tiled=True),
    )
    (
        back_in,
        back_out,
        back_expand,
        back_reduce,
        unused_query,
        unused_value,
        unused_project,
        unused_expand,
        unused_reduce,
        back_gain_first,
        back_shift_first,
        back_gain_second,
        back_shift_second,
    ) = whole_back
    grad_rows = cotangent.reshape(total_rows, width).astype(jnp.float32)
    grad_result_low = cotangent.reshape(total_rows, width)
    reduce_bias_grad = column_sum(grad_result_low)
    grad_activated = product_back(grad_result_low, back_reduce)
    unused_gelu, gelu_back = jax.vjp(lambda entry: jax.nn.gelu(entry, approximate=True), expanded)
    grad_expanded_low = gelu_back(grad_activated)[0].astype(jnp.bfloat16)
    expand_bias_grad = column_sum(grad_expanded_low)
    grad_second = product_back(grad_expanded_low, back_expand)
    unused_second, second_back = jax.vjp(
        layer_norm,
        middle,
        back_gain_second.astype(jnp.float32),
        back_shift_second.astype(jnp.float32),
    )
    grad_middle, second_gain_grad, second_shift_grad = second_back(grad_second)
    grad_middle = grad_middle + grad_rows
    reduce_weight_grad = weight_term(activated_low, grad_result_low)
    expand_weight_grad = weight_term(second_low, grad_expanded_low)
    feed_parts = (
        lax.psum_scatter(
            expand_weight_grad.astype(jnp.bfloat16), "group", scatter_dimension=0, tiled=True
        ).astype(jnp.float32),
        lax.psum_scatter(
            reduce_weight_grad.astype(jnp.bfloat16), "group", scatter_dimension=0, tiled=True
        ).astype(jnp.float32),
        lax.psum_scatter(
            expand_bias_grad.astype(jnp.bfloat16), "group", scatter_dimension=0, tiled=True
        ).astype(jnp.float32),
        lax.psum_scatter(
            reduce_bias_grad.astype(jnp.bfloat16), "group", scatter_dimension=0, tiled=True
        ).astype(jnp.float32),
        lax.psum_scatter(
            second_gain_grad.astype(jnp.bfloat16), "group", scatter_dimension=0, tiled=True
        ).astype(jnp.float32),
        lax.psum_scatter(
            second_shift_grad.astype(jnp.bfloat16), "group", scatter_dimension=0, tiled=True
        ).astype(jnp.float32),
    )
    grad_middle_low = grad_middle.astype(jnp.bfloat16)
    project_bias_grad = column_sum(grad_middle_low)
    grad_attended_low = (
        product_back(grad_middle_low, back_out).astype(jnp.bfloat16).reshape(head_shape)
    )
    row_dot = jnp.einsum("schd,schd->shc", grad_attended_low.astype(jnp.float32), attended)

    def back_step(grad_query, members):
        key_piece, value_piece, offset = members
        return attend_back(
            grad_query,
            key_piece.reshape((1,) + head_shape),
            value_piece.reshape((1,) + head_shape),
            offset,
            queries,
            query_pos,
            doc_start,
            log_total,
            grad_attended_low,
            row_dot,
        )

    grad_query, terms = lax.scan(
        back_step, jnp.zeros(head_shape, jnp.float32), (keys_back[0], keys_back[1], block_ids)
    )
    key_terms = terms[0].reshape(groups, seq_here, local_len, width)
    value_terms = terms[1].reshape(groups, seq_here, local_len, width)
    key_grad, value_grad = (
        lax.psum_scatter(
            key_terms.astype(jnp.bfloat16), "group", scatter_dimension=0, tiled=True
        ).astype(jnp.float32),
        lax.psum_scatter(
            value_terms.astype(jnp.bfloat16), "group", scatter_dimension=0, tiled=True
        ).astype(jnp.float32),
    )
    scaling = 1.0 / math.sqrt(HEAD_DIM)
    grad_query_low = (grad_query * scaling).reshape(total_rows, width).astype(jnp.bfloat16)
    grad_key_low = (key_grad * scaling).reshape(total_rows, width).astype(jnp.bfloat16)
    grad_value_low = value_grad.reshape(total_rows, width).astype(jnp.bfloat16)
    query_bias_grad = column_sum(grad_query_low)
    value_bias_grad = column_sum(grad_value_low)
    grad_mixture_low = jnp.concatenate([grad_query_low, grad_key_low, grad_value_low], axis=1)
    grad_normed = product_back(grad_mixture_low, back_in)
    unused_first, first_back = jax.vjp(
        layer_norm,
        flat_input,
        back_gain_first.astype(jnp.float32),
        back_shift_first.astype(jnp.float32),
    )
    grad_entry, first_gain_grad, first_shift_grad = first_back(grad_normed)
    input_grad = (grad_entry + grad_middle).reshape(seq_here, local_len, width)
    project_weight_grad = weight_term(attended_low, grad_middle_low)
    in_weight_grad = weight_term(normed_low, grad_mixture_low)
    mixer_parts = (
        lax.psum_scatter(
            in_weight_grad.astype(jnp.bfloat16), "group", scatter_dimension=0, tiled=True
        ).astype(jnp.float32),
        lax.psum_scatter(
            project_weight_grad.astype(jnp.bfloat16), "group", scatter_dimension=0, tiled=True
        ).astype(jnp.float32),
        lax.psum_scatter(
            query_bias_grad.astype(jnp.bfloat16), "group", scatter_dimension=0, tiled=True
        ).astype(jnp.float32),
        lax.psum_scatter(
            value_bias_grad.astype(jnp.bfloat16), "group", scatter_dimension=0, tiled=True
        ).astype(jnp.float32),
        lax.psum_scatter(
            project_bias_grad.astype(jnp.bfloat16), "group", scatter_dimension=0, tiled=True
        ).astype(jnp.float32),
        lax.psum_scatter(
            first_gain_grad.astype(jnp.bfloat16), "group", scatter_dimension=0, tiled=True
        ).astype(jnp.float32),
        lax.psum_scatter(
            first_shift_grad.astype(jnp.bfloat16), "group", scatter_dimension=0, tiled=True
        ).astype(jnp.float32),
    )
    share_in, share_out, share_expand, share_reduce = (
        mixer_parts[0],
        mixer_parts[1],
        feed_parts[0],
        feed_parts[1],
    )
    share_query, share_value, share_project = (mixer_parts[2], mixer_parts[3], mixer_parts[4])
    share_expand_bias, share_reduce_bias = (feed_parts[2], feed_parts[3])
    share_first_gain, share_first_shift = (mixer_parts[5], mixer_parts[6])
    share_second_gain, share_second_shift = (feed_parts[4], feed_parts[5])
    totals = (
        lax.psum(share_in.astype(jnp.bfloat16), "replica").astype(jnp.float32),
        lax.psum(share_out.astype(jnp.bfloat16), "replica").astype(jnp.float32),
        lax.psum(share_expand.astype(jnp.bfloat16), "replica").astype(jnp.float32),
        lax.psum(share_reduce.astype(jnp.bfloat16), "replica").astype(jnp.float32),
        lax.psum(share_query.astype(jnp.bfloat16), "replica").astype(jnp.float32),
        lax.psum(share_value.astype(jnp.bfloat16), "replica").astype(jnp.float32),
        lax.psum(share_project.astype(jnp.bfloat16), "replica").astype(jnp.float32),
        lax.psum(share_expand_bias.astype(jnp.bfloat16), "replica").astype(jnp.float32),
        lax.psum(share_reduce_bias.astype(jnp.bfloat16), "replica").astype(jnp.float32),
        lax.psum(share_first_gain.astype(jnp.bfloat16), "replica").astype(jnp.float32),
        lax.psum(share_first_shift.astype(jnp.bfloat16), "replica").astype(jnp.float32),
        lax.psum(share_second_gain.astype(jnp.bfloat16), "replica").astype(jnp.float32),
        lax.psum(share_second_shift.astype(jnp.bfloat16), "replica").astype(jnp.float32),
    )
    return (
        outputs,
        input_grad,
        totals[0],
        totals[1],
        totals[2],
        totals[3],
        totals[4],
        totals[5],
        totals[6],
        totals[7],
        totals[8],
        totals[9],
        totals[10],
        totals[11],
        totals[12],
    )


MESH = pl.DeviceIdType.MESH


def flipped(z=0, core=0, y=0, x=0):
    pairs = []
    for me in range(32):
        pairs.append((me, me ^ (8 * z + 4 * core + 2 * y + x)))
    return pairs


FLIP_X = flipped(x=1)
FLIP_Y = flipped(y=1)
FLIP_CORE = flipped(core=1)
FLIP_Z = flipped(z=1)
FLIP_PAIR = flipped(z=2)
INWARD = [(me, me + 8) for me in range(8)] + [(me, me - 8) for me in range(24, 32)]
MIDDLE = [(me, me + 8) for me in range(8, 16)] + [(me, me - 8) for me in range(16, 24)]
OUTWARD = [(me, me - 8) for me in range(8, 16)] + [(me, me + 8) for me in range(16, 24)]


def moved(entries, pairs):
    return lax.ppermute(entries, ("replica", "group"), pairs)


def low(entries):
    return entries.astype(jnp.bfloat16)


def wide(entries):
    return entries.astype(jnp.float32)


def at(entries, index):
    return lax.dynamic_index_in_dim(entries, index, 0, False)


def place():
    replica = lax.axis_index("replica")
    group = lax.axis_index("group")
    core = lax.rem(replica, 2)
    z = lax.div(replica, 2)
    return replica, group, z, core, lax.div(group, 2), lax.rem(group, 2)


def partners(replica, group):
    core = lax.rem(replica, 2)
    z = lax.rem(lax.div(replica, 2), 2)
    y = lax.div(group, 2)
    x = lax.rem(group, 2)
    by_x = (replica, group + 1 - 2 * x)
    by_y = (replica, group + 2 - 4 * y)
    by_both = (replica, group + 3 - 4 * y - 2 * x)
    by_core = (replica + 1 - 2 * core, group)
    by_z = (replica + 2 - 4 * z, group)
    return by_x, by_y, by_both, by_core, by_z


def greet(devices):
    barrier = pltpu.get_barrier_semaphore()
    for device in devices:
        pl.semaphore_signal(barrier, inc=1, device_id=device, device_id_type=MESH)
    pl.semaphore_wait(barrier, len(devices))


def first_exchange_kernel(inp, weights, vec, seg, expand, x_seq, w_full, vecs, segs, quarter, wide_raw, raw, halves, x_stage, vec_stage, seg_stage, send, recv, local):
    replica = lax.axis_index("replica")
    group = lax.axis_index("group")
    core = lax.rem(replica, 2)
    level = lax.rem(lax.div(replica, 2), 2)
    y = lax.div(group, 2)
    x = lax.rem(group, 2)
    by_x, by_y, by_both, by_core, by_z = partners(replica, group)
    slot_x, slot_y, slot_both = by_x[1], by_y[1], by_both[1]
    other_x = 1 - x
    other_y = 1 - y
    wires = Wires(send, recv, local)
    load_raw = wires.here(weights, raw)
    load_wide = wires.here(expand, wide_raw)
    greet((by_x, by_y, by_both, by_core, by_z))
    small = [wires.go(vec, vecs.at[group], device) for device in (by_x, by_y, by_both)]
    small += [wires.go(seg.at[pick], segs.at[group], device) for pick, device in ((other_x, by_x), (x, by_y), (other_x, by_both))]
    loads = [wires.here(here, there) for here, there in ((inp.at[x], x_stage), (vec, vec_stage), (seg.at[x], seg_stage))]
    load_raw.wait()
    for half in range(2):
        for k in range(3):
            first = 1600 * k + 768 * half
            halves[half, :, 896 * k : 896 * k + 832] = raw[:, first : first + 832]
            halves[half, :, 896 * k + 832 : 896 * k + 896] = jnp.zeros((halves.shape[1], 64), halves.dtype)

    part = 2 * level + core
    mine = rows16(96 * part, 112)
    to_core = rows16(96 * part + 16 * core, 96)
    to_z = rows16(96 * part + 16 * level, 96)
    passed = rows16(96 * (part + 2 - 4 * level) + 16 * (1 - level), 96)
    w_x = wires.go(halves.at[y, mine], w_full.at[group, mine], by_x)
    w_y = wires.go(halves.at[other_y, mine], w_full.at[group, mine], by_y)
    wires.keep(halves.at[y], w_full.at[group])
    for load, here, there in zip(loads, (x_stage, vec_stage, seg_stage), (x_seq, vecs, segs)):
        load.wait()
        wires.keep(here, there.at[group])
    shares = []
    over_z = []

    def share(slot):
        shares.append(wires.go(w_full.at[slot, to_core], w_full.at[slot, to_core], by_core))
        over_z.append((slot, wires.go(w_full.at[slot, to_z], w_full.at[slot, to_z], by_z)))

    wires.drain([w_x, w_y])
    x_block = wires.go(inp.at[other_x], x_seq.at[group], by_x)
    y_block = wires.go(inp.at[x], x_seq.at[group], by_y)
    w_y.wait_recv()
    share(slot_y)
    w_x.wait_recv()
    share(slot_x)
    load_wide.wait()
    quad = lax.rem(replica, 4)
    for pick in range(4):

        @pl.when(quad == pick)
        def _():
            for k in range(4):
                first = 1600 * k + 400 * pick
                quarter[:, 400 * k : 400 * k + 400] = wide_raw[:, first : first + 400]

    wires.drain([x_block])
    w_more = wires.go(w_full.at[slot_y, mine], w_full.at[slot_y, mine], by_x)
    x_block.wait_recv()
    y_more = wires.go(x_seq.at[slot_x], x_seq.at[slot_x], by_y)
    w_more.wait_recv()
    share(slot_both)
    for slot, copy in over_z:
        copy.wait_recv()
        shares.append(wires.go(w_full.at[slot, passed], w_full.at[slot, passed], by_core))
    for copy in small + shares + [y_block, y_more]:
        copy.wait_recv()
    wires.finish()


def first_exchange(inp, weights, vec, seg, expand):
    any_space = pl.BlockSpec(memory_space=pl.ANY)
    shape = jax.ShapeDtypeStruct
    rows = weights.shape[0]
    return pl.pallas_call(
        first_exchange_kernel,
        in_specs=[any_space] * 5,
        out_specs=[any_space] * 4 + [pl.BlockSpec(memory_space=pltpu.VMEM)],
        out_shape=[
            shape((4,) + inp.shape[1:], inp.dtype),
            shape((4, rows, 2688), weights.dtype),
            shape((4,) + vec.shape, vec.dtype),
            shape((4,) + seg.shape[1:], seg.dtype),
            shape((rows, 1600), expand.dtype),
        ],
        scratch_shapes=[
            pltpu.VMEM(expand.shape, expand.dtype),
            pltpu.VMEM(weights.shape, weights.dtype),
            pltpu.VMEM((2, rows, 2688), weights.dtype),
            pltpu.VMEM(inp.shape[1:], inp.dtype),
            pltpu.VMEM(vec.shape, vec.dtype),
            pltpu.VMEM(seg.shape[1:], seg.dtype),
            pltpu.SemaphoreType.DMA((24,)),
            pltpu.SemaphoreType.DMA((24,)),
            pltpu.SemaphoreType.DMA((12,)),
        ],
        compiler_params=pltpu.CompilerParams(collective_id=0, has_side_effects=True, vmem_limit_bytes=40 * 2**20),
        name="first_exchange",
    )(inp, weights, vec, seg, expand)


def turn_middle_kernel(src, out_in, inp_in, rows_ref, att_out, middle_out, second_out, att, w, inp, send, recv, local):
    replica = lax.axis_index("replica")
    group = lax.axis_index("group")
    y = lax.div(group, 2)
    x = lax.rem(group, 2)
    by_x, by_y, by_both, by_core, by_z = partners(replica, group)
    others = (by_both, by_x, by_y)
    wires = Wires(send, recv, local)
    greet(others)
    copies = [wires.go(src.at[device[1]], att.at[x, y], device) for device in others]
    own = wires.here(src.at[group], att.at[x, y])
    load_w = wires.here(out_in, w)
    load_inp = wires.here(inp_in, inp)
    width = w.shape[0]
    lane = lax.broadcasted_iota(jnp.int32, (1, 128), 1)
    for copy in (own, load_w, load_inp):
        copy.wait()
    for copy in copies:
        copy.wait_recv()
    for seq in range(2):
        rows = pl.ds(256 * seq, 256)
        att_out[rows, 0:768] = att[seq, 0, :, 0:768]
        att_out[rows, 768:896] = jnp.where(lane < 64, att[seq, 0, :, 768:896], att[seq, 1, :, 0:128])
        att_out[rows, 896:width] = att[seq, 1, :, 128 : width - 768]
        middle = inp[seq].astype(jnp.float32) + dot_nn(att_out[rows, :], w[...]) + rows_ref[2:3, :width]
        middle_out[rows, :] = middle
        center = middle - jnp.mean(middle, axis=-1, keepdims=True)
        spread = jnp.mean(center * center, axis=-1, keepdims=True)
        second = center * lax.rsqrt(spread + epsilon) * rows_ref[6:7, :width] + rows_ref[7:8, :width]
        second_out[rows, :width] = second.astype(jnp.bfloat16)
        second_out[rows, width:] = jnp.zeros((256, second_out.shape[1] - width), jnp.bfloat16)
    wires.finish()


def turn_middle(entries, full_out, inputs, rows):
    any_space = pl.BlockSpec(memory_space=pl.ANY)
    vmem = pl.BlockSpec(memory_space=pltpu.VMEM)
    shape = jax.ShapeDtypeStruct
    width = full_out.shape[0]
    return pl.pallas_call(
        turn_middle_kernel,
        in_specs=[any_space, any_space, any_space, vmem],
        out_specs=[vmem, vmem, vmem],
        out_shape=[shape((512, width), jnp.bfloat16), shape((512, width), jnp.float32), shape((512, width + 64), jnp.bfloat16)],
        scratch_shapes=[
            pltpu.VMEM((2, 2) + entries.shape[1:], jnp.bfloat16),
            pltpu.VMEM(full_out.shape, jnp.bfloat16),
            pltpu.VMEM(inputs.shape, jnp.bfloat16),
            pltpu.SemaphoreType.DMA((3,)),
            pltpu.SemaphoreType.DMA((3,)),
            pltpu.SemaphoreType.DMA((3,)),
        ],
        compiler_params=pltpu.CompilerParams(collective_id=1, has_side_effects=True, vmem_limit_bytes=40 * 2**20),
        cost_estimate=pl.CostEstimate(flops=0, bytes_accessed=60 * 2**20, transcendentals=0),
        name="turn_middle",
    )(entries, full_out, inputs, rows)


def padded(entries):
    return jnp.pad(entries, [(0, 0)] * (entries.ndim - 1) + [(0, 64)])


def joined(first, other):
    lane = lax.broadcasted_iota(jnp.int32, (1, 128), 1)
    middle = jnp.where(lane < 64, first[..., 768:896], other[..., 0:128])
    return jnp.concatenate([first[..., :768], middle, other[..., 128:]], axis=-1)


def hold(entries, *until):
    return lax.optimization_barrier((entries,) + until)[0]


def finish_feed_kernel(quads_ref, out_expand):
    for k in range(4):
        piece = quads_ref[k].astype(jnp.float32)
        for r in range(4):
            out_expand[:, 1600 * r + 400 * k : 1600 * r + 400 * k + 400] = piece[:, 400 * r : 400 * r + 400]


def finish_feed(quads):
    rows, width = quads.shape[1:]
    step = 80
    return pl.pallas_call(
        finish_feed_kernel,
        grid=(rows // step,),
        in_specs=[pl.BlockSpec((4, step, width), lambda i: (0, i, 0))],
        out_specs=pl.BlockSpec((step, 4 * width), lambda i: (i, 0)),
        out_shape=jax.ShapeDtypeStruct((rows, 4 * width), jnp.float32),
        compiler_params=pltpu.CompilerParams(vmem_limit_bytes=48 * 2**20),
        name="finish_feed",
    )(quads)


def finish_mixer_kernel(total_ref, in_ref, out_ref):
    for k in range(3):
        in_ref[:, 1600 * k : 1600 * k + 1600] = total_ref[k, :, :1600].astype(jnp.float32)
    out_ref[...] = total_ref[3, :, :1600].astype(jnp.float32)


def finish_mixer(total):
    rows = total.shape[1]
    step = 80
    return pl.pallas_call(
        finish_mixer_kernel,
        grid=(rows // step,),
        in_specs=[pl.BlockSpec((4, step, total.shape[2]), lambda i: (0, i, 0))],
        out_specs=[pl.BlockSpec((step, 4800), lambda i: (i, 0)), pl.BlockSpec((step, 1600), lambda i: (i, 0))],
        out_shape=[jax.ShapeDtypeStruct((rows, 4800), jnp.float32), jax.ShapeDtypeStruct((rows, 1600), jnp.float32)],
        compiler_params=pltpu.CompilerParams(vmem_limit_bytes=48 * 2**20),
        name="finish_mixer",
    )(total)


PIECES = ((0, 512), (512, 1024), (1024, 1600))
HALF = 208


class Wires:
    def __init__(self, send, recv, local):
        self.send, self.recv, self.local = send, recv, local
        self.remotes = self.locals = 0
        self.sent = []
        self.kept = []

    def make(self, src, dst, device):
        i = self.remotes
        assert i < self.send.shape[0]
        self.remotes = i + 1
        return pltpu.make_async_remote_copy(src_ref=src, dst_ref=dst, send_sem=self.send.at[i], recv_sem=self.recv.at[i], device_id=device, device_id_type=MESH)

    def go(self, src, dst, device):
        copy = self.make(src, dst, device)
        copy.start()
        self.sent.append(copy)
        return copy

    def here(self, src, dst):
        i = self.locals
        assert i < self.local.shape[0]
        self.locals = i + 1
        copy = pltpu.make_async_copy(src, dst, self.local.at[i])
        copy.start()
        return copy

    def keep(self, src, dst):
        self.kept.append(self.here(src, dst))

    def drain(self, copies):
        for copy in copies:
            copy.wait_send()
        self.sent = [copy for copy in self.sent if all(copy is not done for done in copies)]

    def finish(self):
        for copy in self.sent:
            copy.wait_send()
        for copy in self.kept:
            copy.wait()


def rows16(start, size):
    return pl.ds(pl.multiple_of(start, 16), size)


def dot_tn(a, b):
    return lax.dot_general(a, b, (((0,), (0,)), ((), ())), preferred_element_type=jnp.float32)


def add_low(a, b):
    return (a.astype(jnp.float32) + b.astype(jnp.float32)).astype(jnp.bfloat16)


def weight_sum(a, b, out):
    width = out.shape[0]
    whole = width // 256

    def chunk(j, carry):
        lanes = pl.ds(pl.multiple_of(256 * j, 256), 256)
        out[lanes, :] = dot_tn(a[:, lanes], b[:, : out.shape[1]]).astype(jnp.bfloat16)
        return carry

    lax.fori_loop(0, whole, chunk, 0)
    if width > 256 * whole:
        out[256 * whole :, :] = dot_tn(a[:, 256 * whole : width], b[:, : out.shape[1]]).astype(jnp.bfloat16)


NT = (((1,), (1,)), ((), ()))

def dot_nt(a, b):
    return lax.dot_general(a, b, NT, preferred_element_type=jnp.float32)

def dot_nn(a, b):
    return jnp.dot(a, b, preferred_element_type=jnp.float32)

BLOCK = 256

def mix_heads_kernel(x_seq, w_in, rows_ref, segc_ref, segr_ref, out_shard, expand_shard, cot, mix, normed, unit_out, o_ref, lse_ref, full_out, full_expand, cots, x_buf, w, stage_out, stage_expand, ot_ref, vt_ref, send, recv, local):
    replica = lax.axis_index("replica")
    group = lax.axis_index("group")
    core = lax.rem(replica, 2)
    y = lax.div(group, 2)
    x = lax.rem(group, 2)
    by_x, by_y, by_both, by_core, by_z = partners(replica, group)
    slot_x, slot_y, slot_both = by_x[1], by_y[1], by_both[1]
    wires = Wires(send, recv, local)
    greet([by_x, by_y, by_core, by_z])
    level = lax.rem(lax.div(replica, 2), 2)
    part = 2 * level + core
    mine = rows16(96 * part, 112)
    to_core = rows16(96 * part + 16 * core, 96)
    to_z = rows16(96 * part + 16 * level, 96)
    passed = rows16(96 * (part + 2 - 4 * level) + 16 * (1 - level), 96)
    out_x = wires.go(out_shard.at[mine], full_out.at[group, mine], by_x)
    out_y = wires.go(out_shard.at[mine], full_out.at[group, mine], by_y)
    expand_x = wires.go(expand_shard, full_expand.at[group], by_x)
    expand_y = wires.go(expand_shard, full_expand.at[group], by_y)
    cot_core = wires.go(cot, cots.at[0], by_core)
    cot_z = wires.go(cot, cots.at[1], by_z)
    load_x = wires.here(x_seq, x_buf)
    load_w = wires.here(w_in, w)
    load_out = wires.here(out_shard, stage_out)
    load_expand = wires.here(expand_shard, stage_expand)
    length = mix.shape[0]
    blocks = length // BLOCK
    lane = lax.broadcasted_iota(jnp.int32, (1, 128), 1)
    lse_ref[...] = jnp.zeros_like(lse_ref)
    half_lanes = pl.ds(pl.multiple_of(768 * y, 128), 896)
    load_x.wait()
    load_w.wait()

    def mix_rows(i, carry):
        rows = pl.ds(pl.multiple_of(256 * i, 256), 256)
        width = x_buf.shape[1]
        entries = x_buf[rows, :].astype(jnp.float32)
        center = entries - jnp.mean(entries, axis=-1, keepdims=True)
        spread = jnp.mean(center * center, axis=-1, keepdims=True)
        unit = center * lax.rsqrt(spread + epsilon)
        unit_out[rows, :] = unit.astype(jnp.bfloat16)
        low_rows = (unit * rows_ref[4:5, :width] + rows_ref[5:6, :width]).astype(jnp.bfloat16)
        normed[rows, :] = low_rows
        mix[rows, 0:896] = (dot_nn(low_rows, w[:, 0:896]) + rows_ref[0:1, half_lanes]).astype(jnp.bfloat16)
        mix[rows, 896:1792] = dot_nn(low_rows, w[:, 896:1792]).astype(jnp.bfloat16)
        mix[rows, 1792:2688] = (dot_nn(low_rows, w[:, 1792:2688]) + rows_ref[1:2, half_lanes]).astype(jnp.bfloat16)
        return carry

    lax.fori_loop(0, 4, mix_rows, 0)
    load_out.wait()
    wires.keep(stage_out, full_out.at[group])
    load_expand.wait()
    wires.keep(stage_expand, full_expand.at[group])
    upper = rows16(96 * part, 64)
    lower = rows16(96 * part + 64, 48)
    top = pl.ds(0, HALF)
    bottom = pl.ds(HALF, 400 - HALF)
    spot = lambda slot, rows: full_out.at[slot, rows]
    more = [wires.make(spot(slot_x, upper), spot(slot_x, upper), by_y), wires.make(spot(slot_y, lower), spot(slot_y, lower), by_x)]
    slots = (slot_x, slot_y, slot_both)
    cores = [wires.make(spot(slot, to_core), spot(slot, to_core), by_core) for slot in slots]
    overs = [wires.make(spot(slot, to_z), spot(slot, to_z), by_z) for slot in slots]
    passes = [wires.make(spot(slot, passed), spot(slot, passed), by_core) for slot in slots]
    expand_more = [wires.make(full_expand.at[slot_x, top], full_expand.at[slot_x, top], by_y), wires.make(full_expand.at[slot_y, bottom], full_expand.at[slot_y, bottom], by_x)]
    cot_both = wires.make(cots.at[1], cots.at[2], by_core)

    def tile_heads(tile, carry):
        at_lanes = lambda off: pl.ds(pl.multiple_of(128 * tile + off, 128), 128)
        ot_ref[...] = jnp.zeros_like(ot_ref)
        vt_ref[...] = mix[:, at_lanes(1792)].T

        def head(h):
            k = jnp.where((lane >= 64 * h) & (lane < 64 * h + 64), mix[:, at_lanes(896)], jnp.bfloat16(0))
            for i in range(blocks):
                low_at, high_at = i * BLOCK, (i + 1) * BLOCK
                q = mix[low_at:high_at, at_lanes(0)] * jnp.bfloat16(0.125)
                s = dot_nt(k[:high_at], q)
                same = segc_ref[:high_at, :] == segr_ref[:, low_at:high_at]
                kpos = lax.broadcasted_iota(jnp.int32, (high_at, BLOCK), 0)
                qpos = lax.broadcasted_iota(jnp.int32, (high_at, BLOCK), 1) + low_at
                s = jnp.where(same & (kpos <= qpos), s, -1e30)
                m = jnp.max(s, axis=0, keepdims=True)
                p = jnp.exp(s - m)
                l = jnp.sum(p, axis=0, keepdims=True)
                ot = dot_nn(vt_ref[64 * h : 64 * h + 64, :high_at], p.astype(jnp.bfloat16))
                ot_ref[64 * h : 64 * h + 64, low_at:high_at] = ot / l
                lse_ref[tile, h : h + 1, low_at:high_at] = m + jnp.log(l)

        head(0)

        @pl.when(tile < 6)
        def _():
            head(1)

        @pl.when(tile == 2)
        def _():
            out_x.wait_recv()
            out_y.wait_recv()
            for copy in more + cores[:2] + overs[:2]:
                copy.start()

        @pl.when(tile == 4)
        def _():
            expand_x.wait_recv()
            expand_y.wait_recv()
            for copy in expand_more:
                copy.start()
            for copy in more:
                copy.wait_recv()
            cores[2].start()
            overs[2].start()

        o_ref[:, at_lanes(0)] = ot_ref[...].T.astype(jnp.bfloat16)
        return carry

    lax.fori_loop(0, 7, tile_heads, 0)
    cot_z.wait_recv()
    cot_both.start()
    for i in range(3):
        overs[i].wait_recv()
        passes[i].start()
    for copy in expand_more + cores + passes + [cot_core, cot_both]:
        copy.wait_recv()
    for copy in more + cores + overs + passes + expand_more + [cot_both]:
        copy.wait_send()
    wires.finish()


def mix_heads(x_seq, w_in, rows, segc, segr, out_shard, expand_shard, cot):
    any_space = pl.BlockSpec(memory_space=pl.ANY)
    vmem = pl.BlockSpec(memory_space=pltpu.VMEM)
    shape = jax.ShapeDtypeStruct
    kind = jnp.bfloat16
    length = x_seq.shape[0]
    buf = lambda *dims: pltpu.VMEM(dims, kind)
    return pl.pallas_call(
        mix_heads_kernel,
        in_specs=[any_space, any_space, vmem, vmem, vmem, any_space, any_space, any_space],
        out_specs=[vmem] * 5 + [any_space] * 3,
        out_shape=[
            shape((length, 2688), kind),
            shape(x_seq.shape, kind),
            shape(x_seq.shape, kind),
            shape((length, 896), kind),
            shape((7, 8, length), jnp.float32),
            shape((4,) + out_shard.shape, kind),
            shape((4,) + expand_shard.shape, kind),
            shape((3,) + cot.shape, kind),
        ],
        scratch_shapes=[
            buf(*x_seq.shape),
            buf(*w_in.shape),
            buf(*out_shard.shape),
            buf(*expand_shard.shape),
            pltpu.VMEM((128, length), jnp.float32),
            buf(128, length),
            pltpu.SemaphoreType.DMA((24,)),
            pltpu.SemaphoreType.DMA((24,)),
            pltpu.SemaphoreType.DMA((8,)),
        ],
        compiler_params=pltpu.CompilerParams(collective_id=6, has_side_effects=True, vmem_limit_bytes=56 * 2**20),
        cost_estimate=pl.CostEstimate(flops=5 * 10**10, bytes_accessed=2**26, transcendentals=0),
        name="mix_heads",
    )(x_seq, w_in, rows, segc, segr, out_shard, expand_shard, cot)


def heads_back_kernel(q_ref, k_ref, v_ref, do_ref, o_ref, lse_ref, segc_ref, segr_ref, normed_ref, share_ref, first_ref, own_ref, pass_ref, dq_ref, dk_ref, dv_ref, sums_ref, grad_ref, share_out, first_out, quads, dqt_ref, odt_ref, pair, own, share_own, got, pair_next, normed_t, send, recv, local):
    tile = pl.program_id(0)
    replica = lax.axis_index("replica")
    group = lax.axis_index("group")
    quad = lax.rem(replica, 4)
    quad_z = lax.rem(quad + 2, 4)
    by_x, by_y, by_both, by_core, by_z = partners(replica, group)
    by_pair = (lax.rem(replica + 4, 8), group)
    wires = Wires(send, recv, local)
    pieces = [pl.ds(0, HALF), pl.ds(HALF, 400 - HALF)]
    pass_y = wires.make(pass_ref.at[pieces[0]], got.at[pieces[0]], by_y)
    pass_x = wires.make(pass_ref.at[pieces[1]], got.at[pieces[1]], by_x)
    pair_lower = wires.make(share_ref.at[pieces[1]], pair.at[pieces[1]], by_pair)
    pair_upper = wires.make(own.at[pieces[0]], pair_next, by_pair)
    loads = [
        pltpu.make_async_copy(first_ref, pair.at[pieces[0]], local.at[0]),
        pltpu.make_async_copy(own_ref, own, local.at[1]),
        pltpu.make_async_copy(share_ref, share_own, local.at[2]),
    ]
    keeps = [pltpu.make_async_copy(pair.at[rows], quads.at[quad, rows], local.at[3 + i]) for i, rows in enumerate(pieces)]
    overs = [wires.make(pair.at[rows], quads.at[quad, rows], by_z) for rows in pieces]
    cores = [wires.make(pair.at[rows], quads.at[quad, rows], by_core) for rows in pieces]
    passes = [wires.make(quads.at[quad_z, rows], quads.at[quad_z, rows], by_core) for rows in pieces]

    def spread(i):
        keeps[i].start()
        overs[i].start()
        cores[i].start()

    @pl.when(tile == 0)
    def _():
        greet([by_pair, by_x, by_y, by_core, by_z])
        for copy in [pass_y, pass_x, pair_lower] + loads:
            copy.start()
        normed_t[...] = normed_ref[...].T

    @pl.when(tile == 1)
    def _():
        for copy in loads:
            copy.wait()
        spread(0)

    @pl.when(tile == 2)
    def _():
        pass_y.wait()
        pass_x.wait()
        own[...] = add_low(own[...], got[...])

    @pl.when(tile == 4)
    def _():
        pair_lower.wait()
        pair_upper.start()
        pair[HALF:, :] = add_low(pair[HALF:, :], share_own[HALF:, :])
        spread(1)
        overs[0].wait_recv()
        passes[0].start()

    length = q_ref.shape[0]
    blocks = length // BLOCK
    lane = lax.broadcasted_iota(jnp.int32, (1, 128), 1)
    dqt_ref[...] = jnp.zeros_like(dqt_ref)
    odt_ref[...] = (do_ref[...].astype(jnp.float32) * o_ref[...].astype(jnp.float32)).T

    def head(h):
        mine = (lane >= 64 * h) & (lane < 64 * h + 64)
        dot_row = jnp.sum(odt_ref[64 * h : 64 * h + 64, :], axis=0, keepdims=True)
        for j in range(blocks):
            low, high = j * BLOCK, (j + 1) * BLOCK
            rest = length - low
            q = q_ref[low:, :] * jnp.bfloat16(0.125)
            do = do_ref[low:, :]
            k = jnp.where(mine, k_ref[low:high, :], jnp.bfloat16(0))
            v = jnp.where(mine, v_ref[low:high, :], jnp.bfloat16(0))
            s = dot_nt(k, q)
            same = segc_ref[low:high, :] == segr_ref[:, low:]
            kpos = lax.broadcasted_iota(jnp.int32, (BLOCK, rest), 0)
            qpos = lax.broadcasted_iota(jnp.int32, (BLOCK, rest), 1)
            p = jnp.where(same & (kpos <= qpos), jnp.exp(s - lse_ref[0, h : h + 1, low:]), 0.0)
            dp = dot_nt(v, do)
            ds = (p * (dp - dot_row[:, low:])).astype(jnp.bfloat16)
            dv = dot_nn(p.astype(jnp.bfloat16), do)
            dk = dot_nn(ds, q)
            if h == 0:
                dv_ref[low:high, :] = jnp.where(mine, dv, 0.0).astype(jnp.bfloat16)
                dk_ref[low:high, :] = jnp.where(mine, dk, 0.0).astype(jnp.bfloat16)
            else:
                dv_ref[low:high, :] = jnp.where(mine, dv.astype(jnp.bfloat16), dv_ref[low:high, :])
                dk_ref[low:high, :] = jnp.where(mine, dk.astype(jnp.bfloat16), dk_ref[low:high, :])
            dqt_ref[:, low:] += dot_nn(k.T, ds)

    head(0)

    @pl.when(tile < 6)
    def _():
        head(1)

    dq_ref[...] = (dqt_ref[...].T * 0.125).astype(jnp.bfloat16)

    row = lax.broadcasted_iota(jnp.int32, (8, 128), 0)
    sum_q = jnp.sum(dq_ref[...].astype(jnp.float32), axis=0, keepdims=True)
    sum_v = jnp.sum(dv_ref[...].astype(jnp.float32), axis=0, keepdims=True)
    sums_ref[...] = jnp.where(row == 0, sum_q, jnp.where(row == 1, sum_v, 0.0))

    grads = jnp.concatenate([dq_ref[...], dk_ref[...], dv_ref[...]], axis=1)
    weights = dot_nn(normed_t[...], grads).astype(jnp.bfloat16)
    for i in range(3):
        grad_ref[i] = weights[:, 128 * i : 128 * i + 128]

    @pl.when(tile == 6)
    def _():
        overs[1].wait_recv()
        passes[1].start()
        share_out[...] = own[...]
        pair_upper.wait()
        first_out[...] = add_low(own[:HALF, :], pair_next[...])
        for copy in cores + passes + keeps:
            copy.wait()
        for copy in overs:
            copy.wait_send()


def heads_back(qkv, grad, out, lse, segc, segr, normed, share, first, own, passed):
    length = qkv.shape[0]
    width = share.shape[1]
    buf = lambda *dims: pltpu.VMEM(dims, jnp.bfloat16)
    still = lambda *dims: pl.BlockSpec(dims, lambda t: (0,) * len(dims))
    spec = lambda off: pl.BlockSpec((length, 128), lambda t: (0, t + off))
    one = pl.BlockSpec((length, 128), lambda t: (0, t))
    shape = jax.ShapeDtypeStruct((length, 896), jnp.bfloat16)
    return pl.pallas_call(
        heads_back_kernel,
        grid=(7,),
        in_specs=[spec(0), spec(7), spec(14), one, one, pl.BlockSpec((1, 8, length), lambda t: (t, 0, 0)), pl.BlockSpec((length, 1), lambda t: (0, 0)), pl.BlockSpec((1, length), lambda t: (0, 0)), still(*normed.shape)] + [pl.BlockSpec(memory_space=pl.ANY)] * 4,
        out_specs=[one, one, one, pl.BlockSpec((8, 128), lambda t: (0, t)), pl.BlockSpec((3, width, 128), lambda t: (0, 0, t)), still(*share.shape), still(*first.shape), pl.BlockSpec(memory_space=pl.ANY)],
        out_shape=[
            shape,
            shape,
            shape,
            jax.ShapeDtypeStruct((8, 896), jnp.float32),
            jax.ShapeDtypeStruct((3, width, 896), jnp.bfloat16),
            jax.ShapeDtypeStruct(share.shape, share.dtype),
            jax.ShapeDtypeStruct(first.shape, share.dtype),
            jax.ShapeDtypeStruct((4,) + share.shape, share.dtype),
        ],
        scratch_shapes=[pltpu.VMEM((128, length), jnp.float32), pltpu.VMEM((128, length), jnp.float32), buf(400, width), buf(400, width), buf(400, width), buf(400, width), buf(HALF, width), buf(width, length), pltpu.SemaphoreType.DMA((10,)), pltpu.SemaphoreType.DMA((10,)), pltpu.SemaphoreType.DMA((5,))],
        compiler_params=pltpu.CompilerParams(vmem_limit_bytes=56 * 2**20, collective_id=4, has_side_effects=True),
        cost_estimate=pl.CostEstimate(flops=int(13 * 5 * 2 * length * length * 64 * 2), bytes_accessed=16 * length * 896, transcendentals=13 * length * length // 2),
        name="heads_back",
    )(qkv, qkv, qkv, grad, out, lse, segc, segr, normed, share, first, own, passed)

def feed_all_kernel(second, cot_in, cots, expand_part, reduce_shard, middle_in, out_in, bias, rows_ref, act_out, back_out, second_out, reduce_out, low_out, att_out, gs_out, own_out, pass_out, sum_out, norm_sums, wexp, wred, s, c, a, b, gs, got_core, got_z, rg, got_x, got_y, send, recv, local):
    replica = lax.axis_index("replica")
    group = lax.axis_index("group")
    quad = lax.rem(replica, 4)
    y = lax.div(group, 2)
    x = lax.rem(group, 2)
    by_x, by_y, by_both, by_core, by_z = partners(replica, group)
    slot_x, slot_y, slot_both = by_x[1], by_y[1], by_both[1]
    wires = Wires(send, recv, local)
    greet([by_x, by_y, by_core, by_z])
    width = wexp.shape[0]
    block = lambda rel: pl.ds(512 * rel, 512)
    sec_core = wires.go(second, s.at[block(1)], by_core)
    sec_z = wires.go(second, s.at[block(2)], by_z)
    quarter = reduce_shard.at[rows16(400 * quad, 400)]
    spot = lambda rank: rows16(400 * rank, 400)
    red_x = wires.go(quarter, wred.at[spot(group)], by_x)
    red_y = wires.go(quarter, wred.at[spot(group)], by_y)
    load_s = wires.here(second, s.at[block(0)])
    load_e = wires.here(expand_part, wexp)
    load_r = wires.here(quarter, wred.at[spot(group)])
    load_m = wires.here(middle_in, gs_out)
    load_c = [wires.here(cot_in, c.at[block(0)])] + [wires.here(cots.at[i], c.at[block(i + 1)]) for i in range(3)]
    sum_out[...] = jnp.zeros_like(sum_out)
    root = 0.7978845608028654

    def gelu(u):
        square = u * u
        t = jnp.tanh(root * u * (1.0 + 0.044715 * square))
        half = 0.5 * (1.0 + t)
        slope = half + (0.5 * root) * u * (1.0 - t * t) * (1.0 + (3.0 * 0.044715) * square)
        return u * half, slope

    def steps(rel, body):
        def one(i, carry):
            body(pl.ds(pl.multiple_of(512 * rel + 256 * i, 256), 256))
            return carry

        lax.fori_loop(0, 2, one, 0)

    def keep_back(rows, low_at, high_at, back):
        back = back.astype(jnp.bfloat16)
        b[rows, low_at:high_at] = back
        sum_out[:, low_at:high_at] += jnp.sum(back.astype(jnp.float32).reshape(32, 8, high_at - low_at), axis=0)

    def up_only(rows):
        entries = s[rows, :width]
        for low_at, high_at in PIECES:
            act, slope = gelu(dot_nn(entries, wexp[:, low_at:high_at]) + bias[:, low_at:high_at])
            a[rows, low_at:high_at] = act.astype(jnp.bfloat16)
            b[rows, low_at:high_at] = slope.astype(jnp.bfloat16)

    def finish_rows(rows):
        gs[rows, width:] = jnp.zeros((256, gs.shape[1] - width), jnp.bfloat16)
        gs[rows, :width] = dot_nt(b[rows, :], wexp[...]).astype(jnp.bfloat16)

    def back_only(rows):
        cot = c[rows, :]
        for low_at, high_at in PIECES:
            keep_back(rows, low_at, high_at, dot_nt(cot, wred[low_at:high_at, :]) * b[rows, low_at:high_at].astype(jnp.float32))
        finish_rows(rows)

    def both(rows):
        entries = s[rows, :width]
        cot = c[rows, :]
        for low_at, high_at in PIECES:
            act, slope = gelu(dot_nn(entries, wexp[:, low_at:high_at]) + bias[:, low_at:high_at])
            a[rows, low_at:high_at] = act.astype(jnp.bfloat16)
            keep_back(rows, low_at, high_at, dot_nt(cot, wred[low_at:high_at, :]) * slope)
        finish_rows(rows)

    load_s.wait()
    load_e.wait()
    steps(0, up_only)
    sec_core.wait_recv()
    steps(1, up_only)
    red_x.wait_recv()
    more_y = wires.go(wred.at[rows16(400 * slot_x, HALF)], wred.at[rows16(400 * slot_x, HALF)], by_y)
    red_y.wait_recv()
    more_x = wires.go(wred.at[rows16(400 * slot_y + HALF, 400 - HALF)], wred.at[rows16(400 * slot_y + HALF, 400 - HALF)], by_x)
    sec_z.wait_recv()
    sec_both = wires.go(s.at[block(2)], s.at[block(3)], by_core)
    load_r.wait()
    for copy in load_c:
        copy.wait()
    more_x.wait_recv()
    more_y.wait_recv()
    wires.keep(wred, reduce_out)
    sec_both.wait_recv()
    wires.keep(s, second_out)
    steps(3, both)
    gs_both = wires.go(gs.at[block(3)], got_core.at[1], by_core)
    steps(2, both)
    gs_both.wait_recv()
    gs[block(2), :] = add_low(gs[block(2), :], got_core[1])
    gs_z = wires.go(gs.at[block(2)], got_z, by_z)
    wires.keep(a, act_out)
    weight_sum(a, c, rg)
    x_copies = [wires.go(rg.at[rows16(400 * slot, HALF)], got_x.at[i], by_x) for i, slot in enumerate((slot_x, slot_both))]
    y_copies = [wires.go(rg.at[rows16(400 * slot + HALF, 400 - HALF)], got_y.at[i], by_y) for i, slot in enumerate((slot_y, slot_both))]
    steps(1, back_only)
    gs_core = wires.go(gs.at[block(1)], got_core.at[0], by_core)
    steps(0, back_only)
    wires.keep(b, back_out)
    load_w = wires.here(out_in, wexp)
    load_m.wait()
    gs_core.wait_recv()
    wires.drain([gs_both])
    gs_z.wait_recv()
    load_w.wait()
    norm_sums[...] = jnp.zeros_like(norm_sums)
    lanes = lax.broadcasted_iota(jnp.int32, (1, 128), 1)
    for seq in range(2):
        stage = got_core.at[1 - seq]

        def norm_back(j, carry):
            rows = pl.ds(pl.multiple_of(256 * seq + 128 * j, 128), 128)
            first = pl.ds(pl.multiple_of(128 * j, 128), 128)
            other = pl.ds(pl.multiple_of(256 + 128 * j, 128), 128)
            grad = gs[rows, :width].astype(jnp.float32) + got_core[0, rows, :width].astype(jnp.float32) + got_z[rows, :width].astype(jnp.float32)
            middle = gs_out[rows, :]
            center = middle - jnp.mean(middle, axis=-1, keepdims=True)
            scale = lax.rsqrt(jnp.mean(center * center, axis=-1, keepdims=True) + epsilon)
            unit = center * scale
            q = grad * rows_ref[6:7, :width]
            grad_middle = c[rows, :].astype(jnp.float32) + scale * (
                q - jnp.mean(q, axis=-1, keepdims=True) - unit * jnp.mean(q * unit, axis=-1, keepdims=True)
            )
            gs_out[rows, :] = grad_middle
            grad_low = grad_middle.astype(jnp.bfloat16)
            gs[rows, :width] = grad_low
            norm_sums[0:1, :] += jnp.sum(grad * unit, axis=0, keepdims=True)
            norm_sums[1:2, :] += jnp.sum(grad, axis=0, keepdims=True)
            norm_sums[2:3, :] += jnp.sum(grad_low.astype(jnp.float32), axis=0, keepdims=True)
            att = dot_nt(grad_low, wexp[...]).astype(jnp.bfloat16)
            stage[first, 0:768] = att[:, 0:768]
            stage[first, 768:896] = jnp.where(lanes < 64, att[:, 768:896], jnp.bfloat16(0))
            stage[other, 0:128] = jnp.where(lanes >= 64, att[:, 768:896], jnp.bfloat16(0))
            stage[other, 128 : width - 768] = att[:, 896:width]
            stage[other, width - 768 : 896] = jnp.zeros((128, 896 + 768 - width), jnp.bfloat16)
            return carry

        lax.fori_loop(0, 2, norm_back, 0)
        for half in range(2):
            wires.keep(stage.at[pl.ds(256 * half, 256), pl.ds(0, 896)], att_out.at[seq, half])
    wires.keep(gs.at[block(0)], low_out)
    for copy in x_copies + y_copies:
        copy.wait_recv()
    own_out[:HALF] = add_low(rg[rows16(400 * group, HALF), :], got_x[0])
    own_out[HALF:] = add_low(rg[rows16(400 * group + HALF, 400 - HALF), :], got_y[0])
    pass_out[:HALF] = add_low(rg[rows16(400 * slot_y, HALF), :], got_x[1])
    pass_out[HALF:] = add_low(rg[rows16(400 * slot_x + HALF, 400 - HALF), :], got_y[1])
    wires.finish()


def feed_all(second, cot, cots, expand_part, reduce_shard, middle, full_out, bias, rows_in):
    any_space = pl.BlockSpec(memory_space=pl.ANY)
    vmem = pl.BlockSpec(memory_space=pltpu.VMEM)
    shape = jax.ShapeDtypeStruct
    kind = jnp.bfloat16
    rows, full = second.shape
    width = expand_part.shape[0]
    buf = lambda *dims: pltpu.VMEM(dims, kind)
    return pl.pallas_call(
        feed_all_kernel,
        in_specs=[any_space] * 7 + [vmem, vmem],
        out_specs=[any_space] * 6 + [vmem] * 5,
        out_shape=[
            shape((4 * rows, width), kind),
            shape((4 * rows, width), kind),
            shape((4 * rows, full), kind),
            shape((width, width), kind),
            shape((rows, full), kind),
            shape((2, 2, 256, 896), kind),
            shape((rows, width), jnp.float32),
            shape((400, width), kind),
            shape((400, width), kind),
            shape((8, width), jnp.float32),
            shape((8, width), jnp.float32),
        ],
        scratch_shapes=[
            buf(width, width),
            buf(width, width),
            buf(4 * rows, full),
            buf(4 * rows, width),
            buf(4 * rows, width),
            buf(4 * rows, width),
            buf(4 * rows, full),
            buf(2, rows, full),
            buf(rows, full),
            buf(width, width),
            buf(2, HALF, width),
            buf(2, 400 - HALF, width),
            pltpu.SemaphoreType.DMA((16,)),
            pltpu.SemaphoreType.DMA((16,)),
            pltpu.SemaphoreType.DMA((20,)),
        ],
        compiler_params=pltpu.CompilerParams(collective_id=5, has_side_effects=True, vmem_limit_bytes=63 * 2**20),
        cost_estimate=pl.CostEstimate(flops=10**11, bytes_accessed=2**26, transcendentals=0),
        name="feed_all",
    )(second, cot, cots, expand_part, reduce_shard, middle, full_out, bias, rows_in)


def turn_more_kernel(grad_att, back, second, act, wred_in, pass_in, att_in, grad_in, own_in, heads_out, result_out, share_out, first_out, own_out, pass_out, core_out, att, grad, stage, b, s, a, wred, rg, result, got_core, got_z, got, got_x, got_y, pair, send, recv, local):
    replica = lax.axis_index("replica")
    group = lax.axis_index("group")
    core = lax.rem(replica, 2)
    y = lax.div(group, 2)
    x = lax.rem(group, 2)
    by_x, by_y, by_both, by_core, by_z = partners(replica, group)
    by_pair = (lax.rem(replica + 4, 8), group)
    slot_x, slot_y, slot_both = by_x[1], by_y[1], by_both[1]
    wires = Wires(send, recv, local)
    load_a = wires.here(act, a)
    load_w = wires.here(wred_in, wred)
    load_own = wires.here(grad_att.at[x, y], stage)
    load_s = wires.here(second, s)
    load_b = wires.here(back, b)
    load_att = wires.here(att_in, att)
    load_grad = wires.here(grad_in, grad)
    greet([by_x, by_y, by_both, by_core, by_z, by_pair])
    width = wred.shape[0]
    block = lambda rel: pl.ds(512 * rel, 512)
    pass_y = wires.go(pass_in.at[pl.ds(0, HALF)], got.at[pl.ds(0, HALF)], by_y)
    pass_x = wires.go(pass_in.at[pl.ds(HALF, 400 - HALF)], got.at[pl.ds(HALF, 400 - HALF)], by_x)
    load_a.wait()
    load_w.wait()

    def rows_out(rel):
        def one(i, carry):
            rows = pl.ds(pl.multiple_of(512 * rel + 256 * i, 256), 256)
            result[rows, :] = dot_nn(a[rows, :], wred[...]).astype(jnp.bfloat16)
            return carry

        lax.fori_loop(0, 2, one, 0)

    rows_out(3)
    to_both = wires.go(result.at[block(3)], got_core.at[1], by_core)
    rows_out(2)
    wires.drain([pass_y, pass_x])
    turns = []
    for device in (by_both, by_x, by_y):
        there = device[1]
        turns.append(wires.go(grad_att.at[lax.rem(there, 2), lax.div(there, 2)], heads_out.at[group], device))
    to_both.wait_recv()
    result[block(2), :] = add_low(result[block(2), :], got_core[1])
    to_z = wires.go(result.at[block(2)], got_z, by_z)
    pass_y.wait_recv()
    pass_x.wait_recv()
    share_out[...] = add_low(own_in[...], got[...])
    pair_upper = wires.go(share_out.at[pl.ds(0, HALF)], pair, by_pair)
    load_own.wait()
    wires.keep(stage, heads_out.at[group])
    load_s.wait()
    load_b.wait()
    weight_sum(s, b, rg)
    x_copies = [wires.go(rg.at[rows16(400 * slot, HALF)], got_x.at[i], by_x) for i, slot in enumerate((slot_x, slot_both))]
    y_copies = [wires.go(rg.at[rows16(400 * slot + HALF, 400 - HALF)], got_y.at[i], by_y) for i, slot in enumerate((slot_y, slot_both))]
    rows_out(1)
    to_core = wires.go(result.at[block(1)], got_core.at[0], by_core)
    rows_out(0)
    load_att.wait()
    load_grad.wait()
    weight_sum(att, grad, wred)
    out_core = [wires.go(wred.at[rows16(400 * r + 192 * (1 - core), 208)], core_out.at[r], by_core) for r in range(4)]
    for r in range(4):
        out_core[r].wait_recv()
        core_out[r] = add_low(wred[rows16(400 * r + 192 * core, 208), :], core_out[r])
    to_core.wait_recv()
    to_z.wait_recv()
    result_out[...] = result[block(0), :].astype(jnp.float32) + got_core[0].astype(jnp.float32) + got_z[...].astype(jnp.float32)
    pair_upper.wait_recv()
    first_out[...] = add_low(share_out[:HALF, :], pair[...])
    for copy in x_copies + y_copies:
        copy.wait_recv()
    own_out[:HALF] = add_low(rg[rows16(400 * group, HALF), :], got_x[0])
    own_out[HALF:] = add_low(rg[rows16(400 * group + HALF, 400 - HALF), :], got_y[0])
    pass_out[:HALF] = add_low(rg[rows16(400 * slot_y, HALF), :], got_x[1])
    pass_out[HALF:] = add_low(rg[rows16(400 * slot_x + HALF, 400 - HALF), :], got_y[1])
    for copy in turns:
        copy.wait_recv()
    wires.finish()


def turn_more(grad_att, back, second, act, wred, passed, att, grad, own):
    any_space = pl.BlockSpec(memory_space=pl.ANY)
    vmem = pl.BlockSpec(memory_space=pltpu.VMEM)
    shape = jax.ShapeDtypeStruct
    kind = jnp.bfloat16
    width = wred.shape[0]
    rows = act.shape[0] // 4
    buf = lambda *dims: pltpu.VMEM(dims, kind)
    return pl.pallas_call(
        turn_more_kernel,
        in_specs=[any_space] * 8 + [vmem],
        out_specs=[any_space] + [vmem] * 6,
        out_shape=[
            shape((4,) + grad_att.shape[2:], kind),
            shape((rows, width), jnp.float32),
            shape((400, width), kind),
            shape((HALF, width), kind),
            shape((400, width), kind),
            shape((400, width), kind),
            shape((4, 208, width), kind),
        ],
        scratch_shapes=[
            buf(rows, width),
            buf(*grad.shape),
            buf(*grad_att.shape[2:]),
            buf(4 * rows, width),
            buf(*second.shape),
            buf(4 * rows, width),
            buf(width, width),
            buf(width, width),
            buf(4 * rows, width),
            buf(2, rows, width),
            buf(rows, width),
            buf(400, width),
            buf(2, HALF, width),
            buf(2, 400 - HALF, width),
            buf(HALF, width),
            pltpu.SemaphoreType.DMA((18,)),
            pltpu.SemaphoreType.DMA((18,)),
            pltpu.SemaphoreType.DMA((10,)),
        ],
        compiler_params=pltpu.CompilerParams(collective_id=2, has_side_effects=True, vmem_limit_bytes=63 * 2**20),
        cost_estimate=pl.CostEstimate(flops=3 * 10**10, bytes_accessed=2**26, transcendentals=0),
        name="turn_more",
    )(grad_att, back, second, act, wred, passed, att, grad, own)


def arrive(here, there, total, lane, k, y, mine):
    first = jnp.where(y == 0, here, there)
    other = jnp.where(y == 0, there, here)
    rows = pl.ds(mine, 208)
    total[k, rows, 0:768] = first[:, 0:768]
    total[k, rows, 768:896] = jnp.where(lane < 64, first[:, 768:896], other[:, 0:128])
    total[k, rows, 896:1664] = other[:, 128:896]


def last_kernel(dq, dk, dv, grad_in, unit_in, w_in, share_in, share_expand, first_expand, vec, gm_in, inp_in, gain, total, grad_out, vec_total, wide_total, quads, d, unit_rows, w, part, c_buf, x_buf, y_buf, line_buf, line_mid, gn, gn_y, gn_cross, inp, pair_buf, vec_got, vec_own, vec_core, vec_z, more_got, more_core, more_z, send, recv, local):
    replica = lax.axis_index("replica")
    group = lax.axis_index("group")
    core = lax.rem(replica, 2)
    quad = lax.rem(replica, 4)
    quad_z = lax.rem(quad + 2, 4)
    z = lax.div(replica, 2)
    y = lax.div(group, 2)
    x = lax.rem(group, 2)
    by_x, by_y, by_both, by_core, by_z = partners(replica, group)
    outer = (z == 0) | (z == 3)
    inner = jnp.logical_not(outer)
    by_line = (jnp.where(z == 0, replica + 2, jnp.where(z == 3, replica - 2, jnp.where(z == 1, replica - 2, replica + 2))), group)
    by_middle = (jnp.where(z == 1, replica + 2, replica - 2), group)
    lines_z = [(lax.rem(replica + 2 * k, 8), group) for k in (1, 2, 3)]
    by_pair = lines_z[1]
    wires = Wires(send, recv, local)
    greet([by_x, by_y, by_both, by_core] + lines_z)
    mine = pl.multiple_of(192 * core, 16)
    theirs = pl.multiple_of(192 * (1 - core), 16)
    other_x = 1 - x
    other_y = 1 - y
    far = 2 * other_y
    near = 2 * y
    width = w.shape[0]
    lane = lax.broadcasted_iota(jnp.int32, (1, 128), 1)
    halves = [(pl.ds(mine + 112 * m, 112 - 16 * m), pl.ds(112 * m, 112 - 16 * m)) for m in range(2)]
    pieces = [pl.ds(0, 208), pl.ds(208, 192)]

    pair_lower = wires.go(share_expand.at[pieces[1]], pair_buf, by_pair)
    c_copies = []
    part_loads = []
    for k in range(3):
        c_copies.append([wires.go(grad_in.at[k, rows16(400 * r + theirs, 208)], c_buf.at[k, r], by_core) for r in range(4)])
        part_loads.append([wires.here(grad_in.at[k, pl.ds(400 * r + mine, 208)], part.at[k, r]) for r in range(4)])
    loads = [wires.here(part, d.at[k]) for k, part in enumerate((dq, dk, dv))]
    load_w = [wires.here(w_in, w), wires.here(unit_in, unit_rows)]
    load_share = wires.here(share_in, total.at[3, pl.ds(mine, 208)])
    vec_group = [wires.go(vec.at[device[1]], vec_got.at[group], device) for device in (by_x, by_y, by_both)]

    def spread(value, rows):
        wires.keep(value, quads.at[quad, rows])
        over = wires.go(value, quads.at[quad, rows], by_z)
        return over, wires.go(value, quads.at[quad, rows], by_core)

    def spread_on(over, rows):
        over.wait_recv()
        return wires.go(quads.at[quad_z, rows], quads.at[quad_z, rows], by_core)

    load_gm = wires.here(gm_in, grad_out)
    load_inp = wires.here(inp_in, inp)

    def line_start(k, m):
        rows, merge = halves[m]
        into = wires.make(total.at[k, rows], line_buf.at[k, merge], by_line)
        middle = wires.make(total.at[k, rows], line_mid.at[k, merge], by_middle)
        back = wires.make(total.at[k, rows], line_buf.at[k, merge], by_line)

        @pl.when(outer)
        def _():
            if m == 1:
                lines[k, 0][0].wait_send()
            into.start()

        lines[k, m] = into, middle, back

    def line_second(k, m):
        rows, merge = halves[m]
        into, middle, back = lines[k, m]

        @pl.when(inner)
        def _():
            into.wait_recv()
            total[k, rows] = add_low(total[k, rows], line_buf[k, merge])
            middle.start()

    def line_third(k, m):
        rows, merge = halves[m]
        into, middle, back = lines[k, m]

        @pl.when(inner)
        def _():
            middle.wait_recv()
            middle.wait_send()
            total[k, rows] = add_low(total[k, rows], line_mid[k, merge])
            back.start()

    def line_fourth(k, m):
        rows, merge = halves[m]
        into, middle, back = lines[k, m]

        @pl.when(outer)
        def _():
            if m == 1:
                into.wait_send()
            back.wait_recv()
            total[k, rows] = line_buf[k, merge]

        @pl.when(inner)
        def _():
            back.wait_send()

    lines = {}
    x_copies = {}
    y_copies = {}

    def core_sum(k):
        for r in range(4):
            part_loads[k][r].wait()
            c_copies[k][r].wait_recv()
            c_buf[k, r] = add_low(c_buf[k, r], part[k, r])

    def x_go(k, i):
        row = (other_y, y)[i]
        x_copies[k, i] = wires.go(c_buf.at[k, 2 * row + other_x], x_buf.at[k, i], by_x)

    def x_next(k, i, after):
        wires.drain([x_copies[k, i]])
        if after is not None:
            x_go(*after)
        x_copies[k, i].wait_recv()
        spot = (far, near)[i] + x
        c_buf[k, spot] = add_low(c_buf[k, spot], x_buf[k, i])
        if i == 0:
            y_copies[k] = wires.go(c_buf.at[k, spot], y_buf.at[k], by_y)

    def y_done(k):
        y_copies[k].wait_recv()
        arrive(c_buf[k, near + x], y_buf[k], total, lane, k, y, mine)
        line_start(k, 0)

    def normed_grad(b):
        rows = pl.ds(pl.multiple_of(256 * b, 256), 256)
        value = dot_nt(d[0, rows, :], w[:, 0:896]) + dot_nt(d[1, rows, :], w[:, 896:1792]) + dot_nt(d[2, rows, :], w[:, 1792:2688])
        gn[b] = value.astype(jnp.bfloat16)
        more_got[group, 0:1, 0:width] += jnp.sum(value * unit_rows[rows, :].astype(jnp.float32), axis=0, keepdims=True)
        more_got[group, 1:2, 0:width] += jnp.sum(value, axis=0, keepdims=True)

    spread_expand = [spread(first_expand, pieces[0])]
    core_sum(0)
    x_go(0, 0)
    x_go(0, 1)
    core_sum(1)
    core_sum(2)
    load_share.wait()
    line_start(3, 0)
    more_got[group] = jnp.zeros(more_got.shape[1:], jnp.float32)
    for copy in loads + load_w:
        copy.wait()
    normed_grad(far + other_x)
    y_pass = wires.go(gn.at[far + other_x], gn_y.at[0], by_y)
    normed_grad(near + other_x)
    x_next(0, 0, (1, 0))
    x_next(0, 1, (1, 1))
    line_start(3, 1)
    line_second(3, 0)
    normed_grad(far + x)
    y_done(0)
    normed_grad(near + x)
    more_group = [wires.go(more_got.at[group], more_got.at[group], device) for device in (by_x, by_y, by_both)]
    for copy in vec_group:
        copy.wait_recv()
    vec_got[group] = vec[group]
    vec_own[...] = (vec_got[0] + vec_got[1]) + (vec_got[2] + vec_got[3])
    vec_pass = wires.go(vec_own, vec_core, by_core)
    x_next(1, 0, (2, 0))
    line_start(0, 1)
    line_second(3, 1)
    y_pass.wait_recv()
    gn_y[0] = add_low(gn_y[0], gn[near + other_x])
    line_second(0, 0)
    x_next(1, 1, (2, 1))
    y_done(1)
    for copy in more_group:
        copy.wait_recv()
    more_z[z] = (more_got[0] + more_got[1]) + (more_got[2] + more_got[3])
    more_pass = wires.go(more_z.at[z], more_core, by_core)
    line_third(3, 0)
    line_second(0, 1)
    vec_pass.wait_recv()
    vec_z[z] = vec_own[...] + vec_core[...]
    vec_line = [wires.go(vec_z.at[z], vec_z.at[z], device) for device in lines_z]
    line_start(1, 1)
    x_next(2, 0, None)
    cross = wires.go(gn_y.at[0], gn_cross, by_x)
    y_keep = wires.go(gn.at[far + x], gn_y.at[1], by_y)
    line_second(1, 0)
    line_third(3, 1)
    x_next(2, 1, None)
    y_done(2)
    pair_lower.wait_recv()
    pair_buf[...] = add_low(pair_buf[...], share_expand[HALF:, :])
    spread_expand.append(spread(pair_buf, pieces[1]))
    line_third(0, 0)
    line_second(1, 1)
    line_start(2, 1)
    more_pass.wait_recv()
    wires.drain([more_pass])
    more_z[z] = more_z[z] + more_core[...]
    more_line = [wires.go(more_z.at[z], more_z.at[z], device) for device in lines_z]
    line_third(0, 1)
    line_second(2, 0)
    line_third(1, 0)
    passes = [spread_on(spread_expand[0][0], pieces[0])]
    line_second(2, 1)
    line_third(1, 1)

    load_gm.wait()
    load_inp.wait()

    def norm_back(seq, grad):
        entries = inp[seq].astype(jnp.float32)
        center = entries - jnp.mean(entries, axis=-1, keepdims=True)
        scale = lax.rsqrt(jnp.mean(center * center, axis=-1, keepdims=True) + epsilon)
        unit = center * scale
        q = grad * gain[...]
        grad_out[seq] += scale * (q - jnp.mean(q, axis=-1, keepdims=True) - unit * jnp.mean(q * unit, axis=-1, keepdims=True))

    y_keep.wait_recv()
    norm_back(x, gn_y[1].astype(jnp.float32) + gn[near + x].astype(jnp.float32))
    cross.wait_recv()
    norm_back(other_x, gn_cross[...].astype(jnp.float32))
    line_third(2, 0)
    line_third(2, 1)
    for copy in vec_line:
        copy.wait_recv()
    vec_total[...] = (vec_z[0] + vec_z[1]) + (vec_z[2] + vec_z[3])
    passes.append(spread_on(spread_expand[1][0], pieces[1]))
    last = []
    for k in (3, 0, 1, 2):
        line_fourth(k, 0)
        line_fourth(k, 1)
        rows = pl.ds(pl.multiple_of(208 * core, 16), 192)
        last.append(wires.go(total.at[k, rows], total.at[k, rows], by_core))
    for copy in more_line:
        copy.wait_recv()
    wide_total[...] = (more_z[0] + more_z[1]) + (more_z[2] + more_z[3])
    for copy in last + passes + [both for over, both in spread_expand]:
        copy.wait_recv()
    wires.finish()


def last_sums(dq, dk, dv, in_grad, unit, w_half, out_share, share_expand, first_expand, vec, grad_middle, inputs, gain):
    any_space = pl.BlockSpec(memory_space=pl.ANY)
    vmem = pl.BlockSpec(memory_space=pltpu.VMEM)
    shape = jax.ShapeDtypeStruct
    kind = jnp.bfloat16
    width = w_half.shape[0]
    buf = lambda *dims: pltpu.VMEM(dims, kind)
    flat = lambda *dims: pltpu.VMEM(dims, jnp.float32)
    return pl.pallas_call(
        last_kernel,
        in_specs=[any_space] * 7 + [vmem, vmem, vmem, any_space, any_space, vmem],
        out_specs=[vmem, vmem, vmem, vmem, any_space],
        out_shape=[
            shape((4, 400, 1664), kind),
            shape(grad_middle.shape, jnp.float32),
            shape(vec.shape[1:], vec.dtype),
            shape((8, 1664), jnp.float32),
            shape((4,) + share_expand.shape, kind),
        ],
        scratch_shapes=[
            buf(3, 1024, 896),
            buf(*unit.shape),
            buf(*w_half.shape),
            buf(3, 4, 208, 896),
            buf(3, 4, 208, 896),
            buf(3, 2, 208, 896),
            buf(3, 208, 896),
            buf(4, 208, 1664),
            buf(4, 208, 1664),
            buf(4, 256, width),
            buf(2, 256, width),
            buf(256, width),
            buf(*inputs.shape),
            buf(400 - HALF, width),
            flat(*vec.shape),
            flat(*vec.shape[1:]),
            flat(*vec.shape[1:]),
            flat(*vec.shape),
            flat(4, 8, 1664),
            flat(8, 1664),
            flat(4, 8, 1664),
            pltpu.SemaphoreType.DMA((88,)),
            pltpu.SemaphoreType.DMA((88,)),
            pltpu.SemaphoreType.DMA((24,)),
        ],
        compiler_params=pltpu.CompilerParams(collective_id=3, has_side_effects=True, vmem_limit_bytes=63 * 2**20),
        cost_estimate=pl.CostEstimate(flops=10**11, bytes_accessed=2**26, transcendentals=0),
        name="last_sums",
    )(dq, dk, dv, in_grad, unit, w_half, out_share, share_expand, first_expand, vec, grad_middle, inputs, gain)


def on_device(
    inputs,
    segments,
    cotangent,
    project_in,
    project_out,
    expand_weight,
    reduce_weight,
    query_bias,
    value_bias,
    project_bias,
    expand_bias,
    reduce_bias,
    first_gain,
    first_shift,
    second_gain,
    second_shift,
):
    replica, group, z, core, y, x = place()
    quad = lax.rem(replica, 4)
    width = 1600
    rows = 512

    names = (query_bias, value_bias, project_bias, reduce_bias, first_gain, first_shift, second_gain, second_shift)
    index = lax.broadcasted_iota(jnp.int32, (16, 400), 0)
    vec = jnp.pad(expand_bias.reshape(4, 400), ((8, 4), (0, 0)))
    for k, name in enumerate(names):
        vec = jnp.where(index == k, name[None, :], vec)
    x_seq, w_half, vecs, segs, quarter_expand = first_exchange(inputs, project_in, vec, segments[:, None, :], expand_weight)
    row_vectors = padded(jnp.swapaxes(wide(vecs), 0, 1).reshape(16, width))
    bias_reduce = row_vectors[3:4, :width]
    bias_expand = lax.dynamic_index_in_dim(wide(vecs), 8 + quad, 1, False).reshape(1, width)
    segs = segs.reshape(1024)

    w_half = w_half.reshape(width, 2688)
    segc = segs[:, None]
    segr = segs[None]
    own_cot = cotangent.reshape(rows, width)
    mixture, normed, unit_seq, attended, lse, full_out, expand_part, cots = mix_heads(
        x_seq.reshape(1024, width), w_half, row_vectors, segc, segr, project_out, quarter_expand, own_cot
    )
    full_out = full_out.reshape(width, width)
    att_tokens, middle, second = turn_middle(attended.reshape(4, 256, 896), full_out, inputs, row_vectors)
    (
        activated,
        grad_expanded,
        second_all,
        reduce_part,
        grad_middle_low,
        grad_att,
        grad_middle,
        own_reduce,
        pass_reduce,
        expand_sums,
        norm_sums,
    ) = feed_all(
        second, own_cot, cots, expand_part.reshape(width, width), reduce_weight, middle, full_out, bias_expand, row_vectors
    )

    grad_heads, result, share_reduce, first_reduce, own_expand, pass_expand, out_core = turn_more(
        grad_att, grad_expanded, second_all, activated, reduce_part, pass_reduce, att_tokens, grad_middle_low, own_reduce
    )
    out_share = padded(lax.psum_scatter(out_core, "group", scatter_dimension=0, tiled=False))
    outputs = low(result + middle + bias_reduce).reshape(2, 256, width)
    dq, dk, dv, bias_sums, in_grad, share_expand, first_expand, quads_reduce = heads_back(
        mixture, grad_heads.reshape(1024, 896), attended, lse, segc, segr, normed, share_reduce, first_reduce, own_expand, pass_expand
    )

    def spread(columns):
        lower = jnp.concatenate([columns[:832], jnp.zeros((768,), jnp.float32)])
        upper = jnp.concatenate([jnp.zeros((832,), jnp.float32), columns[64:832]])
        return jnp.where(y == 0, lower, upper)

    expand_bias_part = jnp.sum(expand_sums, axis=0).reshape(4, 400)
    expand_bias_wide = lax.dynamic_update_slice_in_dim(jnp.zeros((4, width), jnp.float32), expand_bias_part, 400 * quad, 1)
    vectors = jnp.concatenate(
        [
            spread(bias_sums[0]).reshape(4, 400),
            spread(bias_sums[1]).reshape(4, 400),
            norm_sums[2].reshape(4, 400),
            column_sum(cotangent.reshape(rows, width)).reshape(4, 400),
            norm_sums[0].reshape(4, 400),
            norm_sums[1].reshape(4, 400),
            expand_bias_wide,
        ],
        axis=1,
    )
    vectors = jnp.pad(vectors, ((0, 0), (0, 96))).reshape(4, 32, 128)
    grad_total, input_grad, vec_total, wide_total, quads_expand = last_sums(
        dq, dk, dv, in_grad, unit_seq, w_half, out_share, share_expand, first_expand, vectors, grad_middle.reshape(2, 256, width), inputs, row_vectors[4:5, :width]
    )
    vec_total = vec_total.reshape(4096)
    pieces = [vec_total[400 * k : 400 * k + 400] for k in range(6)]
    first_sums = lax.dynamic_index_in_dim(wide_total[:2, :width].reshape(2, 4, 400), group, 1, False)
    total_reduce = wide(quads_reduce.reshape(width, width))
    total_expand = finish_feed(quads_expand)
    total_in, total_out = finish_mixer(grad_total)
    return (
        outputs,
        input_grad,
        total_in,
        total_out,
        total_expand,
        total_reduce,
        pieces[0],
        pieces[1],
        pieces[2],
        vec_total[2400:4000],
        pieces[3],
        first_sums[0],
        first_sums[1],
        pieces[4],
        pieces[5],
    )


def solution(mesh):
    placed = (
        P("replica", "group", None),
        P("replica", "group"),
        P("replica", "group", None),
        P("group", None),
        P("group", None),
        P("group", None),
        P("group", None),
        P("group"),
        P("group"),
        P("group"),
        P("group"),
        P("group"),
        P("group"),
        P("group"),
        P("group"),
        P("group"),
    )
    return jax.shard_map(
        on_device if dict(mesh.shape) == {"replica": 8, "group": 4} else on_device_any,
        mesh=mesh,
        in_specs=placed,
        out_specs=(
            P("replica", "group", None),
            P("replica", "group", None),
            P("group", None),
            P("group", None),
            P("group", None),
            P("group", None),
            P("group"),
            P("group"),
            P("group"),
            P("group"),
            P("group"),
            P("group"),
            P("group"),
            P("group"),
            P("group"),
        ),
        check_vma=False,
    )
```

```python
import functools
import math

import jax
import jax.numpy as jnp
from jax import lax
from jax.sharding import PartitionSpec as P

from jax.experimental import pallas as pl
from jax.experimental.pallas import tpu as pltpu

HEADS = 25
HEAD_DIM = 64


epsilon = 1e-05
very_low = -1e30


def carried_in(part, axis, combine, identity):
    place = lax.axis_index(axis)
    gathered = lax.all_gather(part, axis)
    state = jnp.zeros_like(part) + jnp.asarray(identity, part.dtype)

    def one(hop, state):
        return combine(state, lax.dynamic_index_in_dim(gathered, hop, 0, False))

    return lax.fori_loop(0, place, one, state)


def layer_norm(entries, gain, shift):
    center = entries - jnp.mean(entries, axis=-1, keepdims=True)
    spread = jnp.mean(center * center, axis=-1, keepdims=True)
    return center * lax.rsqrt(spread + epsilon) * gain + shift


def product(left, right):
    return jnp.dot(left, right, preferred_element_type=jnp.float32)


def product_back(left, right):
    return lax.dot_general(
        left, right, (((1,), (1,)), ((), ())), preferred_element_type=jnp.float32
    )


def weight_term(left, right):
    return lax.dot_general(
        left, right, (((0,), (0,)), ((), ())), preferred_element_type=jnp.float32
    )


def column_sum(entries):
    return jnp.sum(entries.astype(jnp.float32), axis=0)


def block_scores(queries, key_block, offset, query_pos, doc_start):
    block_count = key_block.shape[0]
    key_count = key_block.shape[2]
    scaling = 1.0 / math.sqrt(HEAD_DIM)
    scores = (
        jnp.einsum("schd,pskhd->shcpk", queries, key_block, preferred_element_type=jnp.float32)
        * scaling
    )
    key_pos = (offset + jnp.arange(block_count, dtype=jnp.int32))[:, None] * key_count + jnp.arange(
        key_count, dtype=jnp.int32
    )[None, :]
    allowed = (key_pos[None, None] <= query_pos[None, :, None, None]) & (
        key_pos[None, None] >= doc_start[:, :, None, None]
    )
    allowed = allowed[:, None]
    return (jnp.where(allowed, scores, very_low), allowed)


def attend(running, key_block, value_block, offset, queries, query_pos, doc_start):
    largest, denominator, summed = running
    masked, allowed = block_scores(queries, key_block, offset, query_pos, doc_start)
    fresh = jnp.maximum(largest, jnp.max(masked, axis=(3, 4)))
    shares = jnp.where(allowed, jnp.exp(masked - fresh[..., None, None]), 0.0)
    rescale = jnp.exp(largest - fresh)
    denominator = denominator * rescale + jnp.sum(shares, axis=(3, 4))
    added = jnp.einsum(
        "shcpk,pskhd->schd",
        shares.astype(jnp.bfloat16),
        value_block,
        preferred_element_type=jnp.float32,
    )
    summed = summed * jnp.transpose(rescale, (0, 2, 1))[..., None] + added
    return (fresh, denominator, summed)


def attend_back(
    grad_query,
    key_block,
    value_block,
    offset,
    queries,
    query_pos,
    doc_start,
    log_total,
    grad_low,
    row_dot,
):
    masked, allowed = block_scores(queries, key_block, offset, query_pos, doc_start)
    shares = jnp.where(allowed, jnp.exp(masked - log_total[..., None, None]), 0.0)
    grad_value = jnp.einsum(
        "shcpk,schd->pskhd",
        shares.astype(jnp.bfloat16),
        grad_low,
        preferred_element_type=jnp.float32,
    )
    grad_share = jnp.einsum(
        "schd,pskhd->shcpk", grad_low, value_block, preferred_element_type=jnp.float32
    )
    grad_score = (shares * (grad_share - row_dot[..., None, None])).astype(jnp.bfloat16)
    grad_query = grad_query + jnp.einsum(
        "shcpk,pskhd->schd", grad_score, key_block, preferred_element_type=jnp.float32
    )
    grad_key = jnp.einsum(
        "shcpk,schd->pskhd", grad_score, queries, preferred_element_type=jnp.float32
    )
    return (grad_query, (grad_key, grad_value))


def on_device_any(
    inputs,
    segments,
    cotangent,
    project_in,
    project_out,
    expand_weight,
    reduce_weight,
    query_bias,
    value_bias,
    project_bias,
    expand_bias,
    reduce_bias,
    first_gain,
    first_shift,
    second_gain,
    second_shift,
):
    seq_here, local_len, width = inputs.shape
    groups = lax.axis_size("group")
    total_rows = seq_here * local_len
    head_shape = (seq_here, local_len, HEADS, HEAD_DIM)
    shards = (
        project_in,
        project_out,
        expand_weight,
        reduce_weight,
        query_bias,
        value_bias,
        project_bias,
        expand_bias,
        reduce_bias,
        first_gain,
        first_shift,
        second_gain,
        second_shift,
    )
    whole = (
        lax.all_gather(shards[0], "group", axis=0, tiled=True),
        lax.all_gather(shards[1], "group", axis=0, tiled=True),
        lax.all_gather(shards[2], "group", axis=0, tiled=True),
        lax.all_gather(shards[3], "group", axis=0, tiled=True),
        lax.all_gather(shards[4], "group", axis=0, tiled=True),
        lax.all_gather(shards[5], "group", axis=0, tiled=True),
        lax.all_gather(shards[6], "group", axis=0, tiled=True),
        lax.all_gather(shards[7], "group", axis=0, tiled=True),
        lax.all_gather(shards[8], "group", axis=0, tiled=True),
        lax.all_gather(shards[9], "group", axis=0, tiled=True),
        lax.all_gather(shards[10], "group", axis=0, tiled=True),
        lax.all_gather(shards[11], "group", axis=0, tiled=True),
        lax.all_gather(shards[12], "group", axis=0, tiled=True),
    )
    (
        full_in,
        full_out,
        full_expand,
        full_reduce,
        bias_query,
        bias_value,
        bias_project,
        bias_expand,
        bias_reduce,
        gain_first,
        shift_first,
        gain_second,
        shift_second,
    ) = whole
    group_rank = lax.axis_index("group")
    query_pos = group_rank * local_len + jnp.arange(local_len, dtype=jnp.int32)
    positions = jnp.broadcast_to(query_pos[None, :], (seq_here, local_len))
    end_marks = jnp.where(segments == positions, positions + 1, 0)
    before = carried_in(
        jnp.max(end_marks, axis=1), "group", jnp.maximum, jnp.zeros((seq_here,), jnp.int32)
    )
    inside = lax.cummax(end_marks, axis=1)
    inside = jnp.concatenate([jnp.zeros((seq_here, 1), jnp.int32), inside[:, :-1]], axis=1)
    doc_start = jnp.maximum(before[:, None], inside)
    flat_input = inputs.reshape(total_rows, width).astype(jnp.float32)
    normed_low = layer_norm(
        flat_input, gain_first.astype(jnp.float32), shift_first.astype(jnp.float32)
    ).astype(jnp.bfloat16)
    mixture = product(normed_low, full_in)
    queries = (
        (mixture[:, :width] + bias_query.astype(jnp.float32))
        .astype(jnp.bfloat16)
        .reshape(head_shape)
    )
    key_rows = (
        mixture[:, width : 2 * width].astype(jnp.bfloat16).reshape(seq_here, local_len, width)
    )
    value_rows = (
        (mixture[:, 2 * width :] + bias_value.astype(jnp.float32))
        .astype(jnp.bfloat16)
        .reshape(seq_here, local_len, width)
    )
    initial = (
        jnp.full((seq_here, HEADS, local_len), very_low, jnp.float32),
        jnp.zeros((seq_here, HEADS, local_len), jnp.float32),
        jnp.zeros(head_shape, jnp.float32),
    )
    block_ids = jnp.arange(groups, dtype=jnp.int32)
    running = initial
    pieces = (
        lax.all_gather(key_rows[None], "group", axis=0, tiled=True),
        lax.all_gather(value_rows[None], "group", axis=0, tiled=True),
    )
    piece_count = pieces[0].shape[0]

    def one_piece(state, members):
        key_piece, value_piece, index = members
        updated = attend(
            state,
            key_piece.reshape((1,) + head_shape),
            value_piece.reshape((1,) + head_shape),
            index,
            queries,
            query_pos,
            doc_start,
        )
        return (updated, None)

    running, unused_steps = lax.scan(
        one_piece, running, (pieces[0], pieces[1], jnp.arange(piece_count, dtype=jnp.int32))
    )
    largest, denominator, summed = running
    attended = summed / jnp.transpose(denominator, (0, 2, 1))[..., None]
    log_total = largest + jnp.log(denominator)
    attended_low = attended.reshape(total_rows, width).astype(jnp.bfloat16)
    middle = flat_input + product(attended_low, full_out) + bias_project.astype(jnp.float32)
    second_low = layer_norm(
        middle, gain_second.astype(jnp.float32), shift_second.astype(jnp.float32)
    ).astype(jnp.bfloat16)
    expanded = product(second_low, full_expand) + bias_expand.astype(jnp.float32)
    activated_low = jax.nn.gelu(expanded, approximate=True).astype(jnp.bfloat16)
    result = middle + product(activated_low, full_reduce) + bias_reduce.astype(jnp.float32)
    outputs = result.astype(jnp.bfloat16).reshape(seq_here, local_len, width)
    whole_back = (
        lax.all_gather(shards[0], "group", axis=0, tiled=True),
        lax.all_gather(shards[1], "group", axis=0, tiled=True),
        lax.all_gather(shards[2], "group", axis=0, tiled=True),
        lax.all_gather(shards[3], "group", axis=0, tiled=True),
        lax.all_gather(shards[4], "group", axis=0, tiled=True),
        lax.all_gather(shards[5], "group", axis=0, tiled=True),
        lax.all_gather(shards[6], "group", axis=0, tiled=True),
        lax.all_gather(shards[7], "group", axis=0, tiled=True),
        lax.all_gather(shards[8], "group", axis=0, tiled=True),
        lax.all_gather(shards[9], "group", axis=0, tiled=True),
        lax.all_gather(shards[10], "group", axis=0, tiled=True),
        lax.all_gather(shards[11], "group", axis=0, tiled=True),
        lax.all_gather(shards[12], "group", axis=0, tiled=True),
    )
    keys_back = (
        lax.all_gather(key_rows[None], "group", axis=0, tiled=True),
        lax.all_gather(value_rows[None], "group", axis=0, tiled=True),
    )
    (
        back_in,
        back_out,
        back_expand,
        back_reduce,
        unused_query,
        unused_value,
        unused_project,
        unused_expand,
        unused_reduce,
        back_gain_first,
        back_shift_first,
        back_gain_second,
        back_shift_second,
    ) = whole_back
    grad_rows = cotangent.reshape(total_rows, width).astype(jnp.float32)
    grad_result_low = cotangent.reshape(total_rows, width)
    reduce_bias_grad = column_sum(grad_result_low)
    grad_activated = product_back(grad_result_low, back_reduce)
    unused_gelu, gelu_back = jax.vjp(lambda entry: jax.nn.gelu(entry, approximate=True), expanded)
    grad_expanded_low = gelu_back(grad_activated)[0].astype(jnp.bfloat16)
    expand_bias_grad = column_sum(grad_expanded_low)
    grad_second = product_back(grad_expanded_low, back_expand)
    unused_second, second_back = jax.vjp(
        layer_norm,
        middle,
        back_gain_second.astype(jnp.float32),
        back_shift_second.astype(jnp.float32),
    )
    grad_middle, second_gain_grad, second_shift_grad = second_back(grad_second)
    grad_middle = grad_middle + grad_rows
    reduce_weight_grad = weight_term(activated_low, grad_result_low)
    expand_weight_grad = weight_term(second_low, grad_expanded_low)
    feed_parts = (
        lax.psum_scatter(
            expand_weight_grad.astype(jnp.bfloat16), "group", scatter_dimension=0, tiled=True
        ).astype(jnp.float32),
        lax.psum_scatter(
            reduce_weight_grad.astype(jnp.bfloat16), "group", scatter_dimension=0, tiled=True
        ).astype(jnp.float32),
        lax.psum_scatter(
            expand_bias_grad.astype(jnp.bfloat16), "group", scatter_dimension=0, tiled=True
        ).astype(jnp.float32),
        lax.psum_scatter(
            reduce_bias_grad.astype(jnp.bfloat16), "group", scatter_dimension=0, tiled=True
        ).astype(jnp.float32),
        lax.psum_scatter(
            second_gain_grad.astype(jnp.bfloat16), "group", scatter_dimension=0, tiled=True
        ).astype(jnp.float32),
        lax.psum_scatter(
            second_shift_grad.astype(jnp.bfloat16), "group", scatter_dimension=0, tiled=True
        ).astype(jnp.float32),
    )
    grad_middle_low = grad_middle.astype(jnp.bfloat16)
    project_bias_grad = column_sum(grad_middle_low)
    grad_attended_low = (
        product_back(grad_middle_low, back_out).astype(jnp.bfloat16).reshape(head_shape)
    )
    row_dot = jnp.einsum("schd,schd->shc", grad_attended_low.astype(jnp.float32), attended)

    def back_step(grad_query, members):
        key_piece, value_piece, offset = members
        return attend_back(
            grad_query,
            key_piece.reshape((1,) + head_shape),
            value_piece.reshape((1,) + head_shape),
            offset,
            queries,
            query_pos,
            doc_start,
            log_total,
            grad_attended_low,
            row_dot,
        )

    grad_query, terms = lax.scan(
        back_step, jnp.zeros(head_shape, jnp.float32), (keys_back[0], keys_back[1], block_ids)
    )
    key_terms = terms[0].reshape(groups, seq_here, local_len, width)
    value_terms = terms[1].reshape(groups, seq_here, local_len, width)
    key_grad, value_grad = (
        lax.psum_scatter(
            key_terms.astype(jnp.bfloat16), "group", scatter_dimension=0, tiled=True
        ).astype(jnp.float32),
        lax.psum_scatter(
            value_terms.astype(jnp.bfloat16), "group", scatter_dimension=0, tiled=True
        ).astype(jnp.float32),
    )
    scaling = 1.0 / math.sqrt(HEAD_DIM)
    grad_query_low = (grad_query * scaling).reshape(total_rows, width).astype(jnp.bfloat16)
    grad_key_low = (key_grad * scaling).reshape(total_rows, width).astype(jnp.bfloat16)
    grad_value_low = value_grad.reshape(total_rows, width).astype(jnp.bfloat16)
    query_bias_grad = column_sum(grad_query_low)
    value_bias_grad = column_sum(grad_value_low)
    grad_mixture_low = jnp.concatenate([grad_query_low, grad_key_low, grad_value_low], axis=1)
    grad_normed = product_back(grad_mixture_low, back_in)
    unused_first, first_back = jax.vjp(
        layer_norm,
        flat_input,
        back_gain_first.astype(jnp.float32),
        back_shift_first.astype(jnp.float32),
    )
    grad_entry, first_gain_grad, first_shift_grad = first_back(grad_normed)
    input_grad = (grad_entry + grad_middle).reshape(seq_here, local_len, width)
    project_weight_grad = weight_term(attended_low, grad_middle_low)
    in_weight_grad = weight_term(normed_low, grad_mixture_low)
    mixer_parts = (
        lax.psum_scatter(
            in_weight_grad.astype(jnp.bfloat16), "group", scatter_dimension=0, tiled=True
        ).astype(jnp.float32),
        lax.psum_scatter(
            project_weight_grad.astype(jnp.bfloat16), "group", scatter_dimension=0, tiled=True
        ).astype(jnp.float32),
        lax.psum_scatter(
            query_bias_grad.astype(jnp.bfloat16), "group", scatter_dimension=0, tiled=True
        ).astype(jnp.float32),
        lax.psum_scatter(
            value_bias_grad.astype(jnp.bfloat16), "group", scatter_dimension=0, tiled=True
        ).astype(jnp.float32),
        lax.psum_scatter(
            project_bias_grad.astype(jnp.bfloat16), "group", scatter_dimension=0, tiled=True
        ).astype(jnp.float32),
        lax.psum_scatter(
            first_gain_grad.astype(jnp.bfloat16), "group", scatter_dimension=0, tiled=True
        ).astype(jnp.float32),
        lax.psum_scatter(
            first_shift_grad.astype(jnp.bfloat16), "group", scatter_dimension=0, tiled=True
        ).astype(jnp.float32),
    )
    share_in, share_out, share_expand, share_reduce = (
        mixer_parts[0],
        mixer_parts[1],
        feed_parts[0],
        feed_parts[1],
    )
    share_query, share_value, share_project = (mixer_parts[2], mixer_parts[3], mixer_parts[4])
    share_expand_bias, share_reduce_bias = (feed_parts[2], feed_parts[3])
    share_first_gain, share_first_shift = (mixer_parts[5], mixer_parts[6])
    share_second_gain, share_second_shift = (feed_parts[4], feed_parts[5])
    totals = (
        lax.psum(share_in.astype(jnp.bfloat16), "replica").astype(jnp.float32),
        lax.psum(share_out.astype(jnp.bfloat16), "replica").astype(jnp.float32),
        lax.psum(share_expand.astype(jnp.bfloat16), "replica").astype(jnp.float32),
        lax.psum(share_reduce.astype(jnp.bfloat16), "replica").astype(jnp.float32),
        lax.psum(share_query.astype(jnp.bfloat16), "replica").astype(jnp.float32),
        lax.psum(share_value.astype(jnp.bfloat16), "replica").astype(jnp.float32),
        lax.psum(share_project.astype(jnp.bfloat16), "replica").astype(jnp.float32),
        lax.psum(share_expand_bias.astype(jnp.bfloat16), "replica").astype(jnp.float32),
        lax.psum(share_reduce_bias.astype(jnp.bfloat16), "replica").astype(jnp.float32),
        lax.psum(share_first_gain.astype(jnp.bfloat16), "replica").astype(jnp.float32),
        lax.psum(share_first_shift.astype(jnp.bfloat16), "replica").astype(jnp.float32),
        lax.psum(share_second_gain.astype(jnp.bfloat16), "replica").astype(jnp.float32),
        lax.psum(share_second_shift.astype(jnp.bfloat16), "replica").astype(jnp.float32),
    )
    return (
        outputs,
        input_grad,
        totals[0],
        totals[1],
        totals[2],
        totals[3],
        totals[4],
        totals[5],
        totals[6],
        totals[7],
        totals[8],
        totals[9],
        totals[10],
        totals[11],
        totals[12],
    )


MESH = pl.DeviceIdType.MESH


def flipped(z=0, core=0, y=0, x=0):
    pairs = []
    for me in range(32):
        pairs.append((me, me ^ (8 * z + 4 * core + 2 * y + x)))
    return pairs


FLIP_X = flipped(x=1)
FLIP_Y = flipped(y=1)
FLIP_CORE = flipped(core=1)
FLIP_Z = flipped(z=1)
FLIP_PAIR = flipped(z=2)
INWARD = [(me, me + 8) for me in range(8)] + [(me, me - 8) for me in range(24, 32)]
MIDDLE = [(me, me + 8) for me in range(8, 16)] + [(me, me - 8) for me in range(16, 24)]
OUTWARD = [(me, me - 8) for me in range(8, 16)] + [(me, me + 8) for me in range(16, 24)]


def moved(entries, pairs):
    return lax.ppermute(entries, ("replica", "group"), pairs)


def low(entries):
    return entries.astype(jnp.bfloat16)


def wide(entries):
    return entries.astype(jnp.float32)


def at(entries, index):
    return lax.dynamic_index_in_dim(entries, index, 0, False)


def place():
    replica = lax.axis_index("replica")
    group = lax.axis_index("group")
    core = lax.rem(replica, 2)
    z = lax.div(replica, 2)
    return replica, group, z, core, lax.div(group, 2), lax.rem(group, 2)


def partners(replica, group):
    core = lax.rem(replica, 2)
    z = lax.rem(lax.div(replica, 2), 2)
    y = lax.div(group, 2)
    x = lax.rem(group, 2)
    by_x = (replica, group + 1 - 2 * x)
    by_y = (replica, group + 2 - 4 * y)
    by_both = (replica, group + 3 - 4 * y - 2 * x)
    by_core = (replica + 1 - 2 * core, group)
    by_z = (replica + 2 - 4 * z, group)
    return by_x, by_y, by_both, by_core, by_z


def greet(devices):
    barrier = pltpu.get_barrier_semaphore()
    for device in devices:
        pl.semaphore_signal(barrier, inc=1, device_id=device, device_id_type=MESH)
    pl.semaphore_wait(barrier, len(devices))


def first_exchange_kernel(inp, weights, vec, seg, expand, x_seq, w_full, vecs, segs, quarter, wide_raw, raw, halves, x_stage, vec_stage, seg_stage, send, recv, local):
    replica = lax.axis_index("replica")
    group = lax.axis_index("group")
    core = lax.rem(replica, 2)
    level = lax.rem(lax.div(replica, 2), 2)
    y = lax.div(group, 2)
    x = lax.rem(group, 2)
    by_x, by_y, by_both, by_core, by_z = partners(replica, group)
    slot_x, slot_y, slot_both = by_x[1], by_y[1], by_both[1]
    other_x = 1 - x
    other_y = 1 - y
    wires = Wires(send, recv, local)
    load_raw = wires.here(weights, raw)
    load_wide = wires.here(expand, wide_raw)
    greet((by_x, by_y, by_both, by_core, by_z))
    small = [wires.go(vec, vecs.at[group], device) for device in (by_x, by_y, by_both)]
    small += [wires.go(seg.at[pick], segs.at[group], device) for pick, device in ((other_x, by_x), (x, by_y), (other_x, by_both))]
    loads = [wires.here(here, there) for here, there in ((inp.at[x], x_stage), (vec, vec_stage), (seg.at[x], seg_stage))]
    load_raw.wait()
    for half in range(2):
        for k in range(3):
            first = 1600 * k + 768 * half
            halves[half, :, 896 * k : 896 * k + 832] = raw[:, first : first + 832]
            halves[half, :, 896 * k + 832 : 896 * k + 896] = jnp.zeros((halves.shape[1], 64), halves.dtype)

    part = 2 * level + core
    mine = rows16(96 * part, 112)
    to_core = rows16(96 * part + 16 * core, 96)
    to_z = rows16(96 * part + 16 * level, 96)
    passed = rows16(96 * (part + 2 - 4 * level) + 16 * (1 - level), 96)
    w_x = wires.go(halves.at[y, mine], w_full.at[group, mine], by_x)
    w_y = wires.go(halves.at[other_y, mine], w_full.at[group, mine], by_y)
    wires.keep(halves.at[y], w_full.at[group])
    for load, here, there in zip(loads, (x_stage, vec_stage, seg_stage), (x_seq, vecs, segs)):
        load.wait()
        wires.keep(here, there.at[group])
    shares = []
    over_z = []

    def share(slot):
        shares.append(wires.go(w_full.at[slot, to_core], w_full.at[slot, to_core], by_core))
        over_z.append((slot, wires.go(w_full.at[slot, to_z], w_full.at[slot, to_z], by_z)))

    wires.drain([w_x, w_y])
    x_block = wires.go(inp.at[other_x], x_seq.at[group], by_x)
    y_block = wires.go(inp.at[x], x_seq.at[group], by_y)
    w_y.wait_recv()
    share(slot_y)
    w_x.wait_recv()
    share(slot_x)
    load_wide.wait()
    quad = lax.rem(replica, 4)
    for pick in range(4):

        @pl.when(quad == pick)
        def _():
            for k in range(4):
                first = 1600 * k + 400 * pick
                quarter[:, 400 * k : 400 * k + 400] = wide_raw[:, first : first + 400]

    wires.drain([x_block])
    w_more = wires.go(w_full.at[slot_y, mine], w_full.at[slot_y, mine], by_x)
    x_block.wait_recv()
    y_more = wires.go(x_seq.at[slot_x], x_seq.at[slot_x], by_y)
    w_more.wait_recv()
    share(slot_both)
    for slot, copy in over_z:
        copy.wait_recv()
        shares.append(wires.go(w_full.at[slot, passed], w_full.at[slot, passed], by_core))
    for copy in small + shares + [y_block, y_more]:
        copy.wait_recv()
    wires.finish()


def first_exchange(inp, weights, vec, seg, expand):
    any_space = pl.BlockSpec(memory_space=pl.ANY)
    shape = jax.ShapeDtypeStruct
    rows = weights.shape[0]
    return pl.pallas_call(
        first_exchange_kernel,
        in_specs=[any_space] * 5,
        out_specs=[any_space] * 4 + [pl.BlockSpec(memory_space=pltpu.VMEM)],
        out_shape=[
            shape((4,) + inp.shape[1:], inp.dtype),
            shape((4, rows, 2688), weights.dtype),
            shape((4,) + vec.shape, vec.dtype),
            shape((4,) + seg.shape[1:], seg.dtype),
            shape((rows, 1600), expand.dtype),
        ],
        scratch_shapes=[
            pltpu.VMEM(expand.shape, expand.dtype),
            pltpu.VMEM(weights.shape, weights.dtype),
            pltpu.VMEM((2, rows, 2688), weights.dtype),
            pltpu.VMEM(inp.shape[1:], inp.dtype),
            pltpu.VMEM(vec.shape, vec.dtype),
            pltpu.VMEM(seg.shape[1:], seg.dtype),
            pltpu.SemaphoreType.DMA((24,)),
            pltpu.SemaphoreType.DMA((24,)),
            pltpu.SemaphoreType.DMA((12,)),
        ],
        compiler_params=pltpu.CompilerParams(collective_id=0, has_side_effects=True, vmem_limit_bytes=40 * 2**20),
        name="first_exchange",
    )(inp, weights, vec, seg, expand)


def turn_middle_kernel(src, out_in, inp_in, rows_ref, att_out, middle_out, second_out, att, w, inp, send, recv, local):
    replica = lax.axis_index("replica")
    group = lax.axis_index("group")
    y = lax.div(group, 2)
    x = lax.rem(group, 2)
    by_x, by_y, by_both, by_core, by_z = partners(replica, group)
    others = (by_both, by_x, by_y)
    wires = Wires(send, recv, local)
    greet(others)
    copies = [wires.go(src.at[device[1]], att.at[x, y], device) for device in others]
    own = wires.here(src.at[group], att.at[x, y])
    load_w = wires.here(out_in, w)
    load_inp = wires.here(inp_in, inp)
    width = w.shape[0]
    lane = lax.broadcasted_iota(jnp.int32, (1, 128), 1)
    for copy in (own, load_w, load_inp):
        copy.wait()
    for copy in copies:
        copy.wait_recv()
    for seq in range(2):
        rows = pl.ds(256 * seq, 256)
        att_out[rows, 0:768] = att[seq, 0, :, 0:768]
        att_out[rows, 768:896] = jnp.where(lane < 64, att[seq, 0, :, 768:896], att[seq, 1, :, 0:128])
        att_out[rows, 896:width] = att[seq, 1, :, 128 : width - 768]
        middle = inp[seq].astype(jnp.float32) + dot_nn(att_out[rows, :], w[...]) + rows_ref[2:3, :width]
        middle_out[rows, :] = middle
        center = middle - jnp.mean(middle, axis=-1, keepdims=True)
        spread = jnp.mean(center * center, axis=-1, keepdims=True)
        second = center * lax.rsqrt(spread + epsilon) * rows_ref[6:7, :width] + rows_ref[7:8, :width]
        second_out[rows, :width] = second.astype(jnp.bfloat16)
        second_out[rows, width:] = jnp.zeros((256, second_out.shape[1] - width), jnp.bfloat16)
    wires.finish()


def turn_middle(entries, full_out, inputs, rows):
    any_space = pl.BlockSpec(memory_space=pl.ANY)
    vmem = pl.BlockSpec(memory_space=pltpu.VMEM)
    shape = jax.ShapeDtypeStruct
    width = full_out.shape[0]
    return pl.pallas_call(
        turn_middle_kernel,
        in_specs=[any_space, any_space, any_space, vmem],
        out_specs=[vmem, vmem, vmem],
        out_shape=[shape((512, width), jnp.bfloat16), shape((512, width), jnp.float32), shape((512, width + 64), jnp.bfloat16)],
        scratch_shapes=[
            pltpu.VMEM((2, 2) + entries.shape[1:], jnp.bfloat16),
            pltpu.VMEM(full_out.shape, jnp.bfloat16),
            pltpu.VMEM(inputs.shape, jnp.bfloat16),
            pltpu.SemaphoreType.DMA((3,)),
            pltpu.SemaphoreType.DMA((3,)),
            pltpu.SemaphoreType.DMA((3,)),
        ],
        compiler_params=pltpu.CompilerParams(collective_id=1, has_side_effects=True, vmem_limit_bytes=40 * 2**20),
        cost_estimate=pl.CostEstimate(flops=0, bytes_accessed=60 * 2**20, transcendentals=0),
        name="turn_middle",
    )(entries, full_out, inputs, rows)


def padded(entries):
    return jnp.pad(entries, [(0, 0)] * (entries.ndim - 1) + [(0, 64)])


def joined(first, other):
    lane = lax.broadcasted_iota(jnp.int32, (1, 128), 1)
    middle = jnp.where(lane < 64, first[..., 768:896], other[..., 0:128])
    return jnp.concatenate([first[..., :768], middle, other[..., 128:]], axis=-1)


def hold(entries, *until):
    return lax.optimization_barrier((entries,) + until)[0]


def finish_feed_kernel(quads_ref, out_expand):
    for k in range(4):
        piece = quads_ref[k].astype(jnp.float32)
        for r in range(4):
            out_expand[:, 1600 * r + 400 * k : 1600 * r + 400 * k + 400] = piece[:, 400 * r : 400 * r + 400]


def finish_feed(quads):
    rows, width = quads.shape[1:]
    step = 80
    return pl.pallas_call(
        finish_feed_kernel,
        grid=(rows // step,),
        in_specs=[pl.BlockSpec((4, step, width), lambda i: (0, i, 0))],
        out_specs=pl.BlockSpec((step, 4 * width), lambda i: (i, 0)),
        out_shape=jax.ShapeDtypeStruct((rows, 4 * width), jnp.float32),
        compiler_params=pltpu.CompilerParams(vmem_limit_bytes=48 * 2**20),
        name="finish_feed",
    )(quads)


def finish_mixer_kernel(total_ref, in_ref, out_ref):
    for k in range(3):
        in_ref[:, 1600 * k : 1600 * k + 1600] = total_ref[k, :, :1600].astype(jnp.float32)
    out_ref[...] = total_ref[3, :, :1600].astype(jnp.float32)


def finish_mixer(total):
    rows = total.shape[1]
    step = 80
    return pl.pallas_call(
        finish_mixer_kernel,
        grid=(rows // step,),
        in_specs=[pl.BlockSpec((4, step, total.shape[2]), lambda i: (0, i, 0))],
        out_specs=[pl.BlockSpec((step, 4800), lambda i: (i, 0)), pl.BlockSpec((step, 1600), lambda i: (i, 0))],
        out_shape=[jax.ShapeDtypeStruct((rows, 4800), jnp.float32), jax.ShapeDtypeStruct((rows, 1600), jnp.float32)],
        compiler_params=pltpu.CompilerParams(vmem_limit_bytes=48 * 2**20),
        name="finish_mixer",
    )(total)


PIECES = ((0, 512), (512, 1024), (1024, 1600))
HALF = 208


class Wires:
    def __init__(self, send, recv, local):
        self.send, self.recv, self.local = send, recv, local
        self.remotes = self.locals = 0
        self.sent = []
        self.kept = []

    def make(self, src, dst, device):
        i = self.remotes
        assert i < self.send.shape[0]
        self.remotes = i + 1
        return pltpu.make_async_remote_copy(src_ref=src, dst_ref=dst, send_sem=self.send.at[i], recv_sem=self.recv.at[i], device_id=device, device_id_type=MESH)

    def go(self, src, dst, device):
        copy = self.make(src, dst, device)
        copy.start()
        self.sent.append(copy)
        return copy

    def here(self, src, dst):
        i = self.locals
        assert i < self.local.shape[0]
        self.locals = i + 1
        copy = pltpu.make_async_copy(src, dst, self.local.at[i])
        copy.start()
        return copy

    def keep(self, src, dst):
        self.kept.append(self.here(src, dst))

    def drain(self, copies):
        for copy in copies:
            copy.wait_send()
        self.sent = [copy for copy in self.sent if all(copy is not done for done in copies)]

    def finish(self):
        for copy in self.sent:
            copy.wait_send()
        for copy in self.kept:
            copy.wait()


def rows16(start, size):
    return pl.ds(pl.multiple_of(start, 16), size)


def dot_tn(a, b):
    return lax.dot_general(a, b, (((0,), (0,)), ((), ())), preferred_element_type=jnp.float32)


def add_low(a, b):
    return (a.astype(jnp.float32) + b.astype(jnp.float32)).astype(jnp.bfloat16)


def weight_sum(a, b, out):
    width = out.shape[0]
    whole = width // 256

    def chunk(j, carry):
        lanes = pl.ds(pl.multiple_of(256 * j, 256), 256)
        out[lanes, :] = dot_tn(a[:, lanes], b[:, : out.shape[1]]).astype(jnp.bfloat16)
        return carry

    lax.fori_loop(0, whole, chunk, 0)
    if width > 256 * whole:
        out[256 * whole :, :] = dot_tn(a[:, 256 * whole : width], b[:, : out.shape[1]]).astype(jnp.bfloat16)


NT = (((1,), (1,)), ((), ()))

def dot_nt(a, b):
    return lax.dot_general(a, b, NT, preferred_element_type=jnp.float32)

def dot_nn(a, b):
    return jnp.dot(a, b, preferred_element_type=jnp.float32)

BLOCK = 256

def mix_heads_kernel(x_seq, w_in, rows_ref, segc_ref, segr_ref, out_shard, expand_shard, cot, mix, normed, unit_out, o_ref, lse_ref, full_out, full_expand, cots, x_buf, w, stage_out, stage_expand, ot_ref, vt_ref, send, recv, local):
    replica = lax.axis_index("replica")
    group = lax.axis_index("group")
    core = lax.rem(replica, 2)
    y = lax.div(group, 2)
    x = lax.rem(group, 2)
    by_x, by_y, by_both, by_core, by_z = partners(replica, group)
    slot_x, slot_y, slot_both = by_x[1], by_y[1], by_both[1]
    wires = Wires(send, recv, local)
    greet([by_x, by_y, by_core, by_z])
    level = lax.rem(lax.div(replica, 2), 2)
    part = 2 * level + core
    mine = rows16(96 * part, 112)
    to_core = rows16(96 * part + 16 * core, 96)
    to_z = rows16(96 * part + 16 * level, 96)
    passed = rows16(96 * (part + 2 - 4 * level) + 16 * (1 - level), 96)
    out_x = wires.go(out_shard.at[mine], full_out.at[group, mine], by_x)
    out_y = wires.go(out_shard.at[mine], full_out.at[group, mine], by_y)
    expand_x = wires.go(expand_shard, full_expand.at[group], by_x)
    expand_y = wires.go(expand_shard, full_expand.at[group], by_y)
    cot_core = wires.go(cot, cots.at[0], by_core)
    cot_z = wires.go(cot, cots.at[1], by_z)
    load_x = wires.here(x_seq, x_buf)
    load_w = wires.here(w_in, w)
    load_out = wires.here(out_shard, stage_out)
    load_expand = wires.here(expand_shard, stage_expand)
    length = mix.shape[0]
    blocks = length // BLOCK
    lane = lax.broadcasted_iota(jnp.int32, (1, 128), 1)
    lse_ref[...] = jnp.zeros_like(lse_ref)
    half_lanes = pl.ds(pl.multiple_of(768 * y, 128), 896)
    load_x.wait()
    load_w.wait()

    def mix_rows(i, carry):
        rows = pl.ds(pl.multiple_of(256 * i, 256), 256)
        width = x_buf.shape[1]
        entries = x_buf[rows, :].astype(jnp.float32)
        center = entries - jnp.mean(entries, axis=-1, keepdims=True)
        spread = jnp.mean(center * center, axis=-1, keepdims=True)
        unit = center * lax.rsqrt(spread + epsilon)
        unit_out[rows, :] = unit.astype(jnp.bfloat16)
        low_rows = (unit * rows_ref[4:5, :width] + rows_ref[5:6, :width]).astype(jnp.bfloat16)
        normed[rows, :] = low_rows
        mix[rows, 0:896] = (dot_nn(low_rows, w[:, 0:896]) + rows_ref[0:1, half_lanes]).astype(jnp.bfloat16)
        mix[rows, 896:1792] = dot_nn(low_rows, w[:, 896:1792]).astype(jnp.bfloat16)
        mix[rows, 1792:2688] = (dot_nn(low_rows, w[:, 1792:2688]) + rows_ref[1:2, half_lanes]).astype(jnp.bfloat16)
        return carry

    lax.fori_loop(0, 4, mix_rows, 0)
    load_out.wait()
    wires.keep(stage_out, full_out.at[group])
    load_expand.wait()
    wires.keep(stage_expand, full_expand.at[group])
    upper = rows16(96 * part, 64)
    lower = rows16(96 * part + 64, 48)
    top = pl.ds(0, HALF)
    bottom = pl.ds(HALF, 400 - HALF)
    spot = lambda slot, rows: full_out.at[slot, rows]
    more = [wires.make(spot(slot_x, upper), spot(slot_x, upper), by_y), wires.make(spot(slot_y, lower), spot(slot_y, lower), by_x)]
    slots = (slot_x, slot_y, slot_both)
    cores = [wires.make(spot(slot, to_core), spot(slot, to_core), by_core) for slot in slots]
    overs = [wires.make(spot(slot, to_z), spot(slot, to_z), by_z) for slot in slots]
    passes = [wires.make(spot(slot, passed), spot(slot, passed), by_core) for slot in slots]
    expand_more = [wires.make(full_expand.at[slot_x, top], full_expand.at[slot_x, top], by_y), wires.make(full_expand.at[slot_y, bottom], full_expand.at[slot_y, bottom], by_x)]
    cot_both = wires.make(cots.at[1], cots.at[2], by_core)

    def tile_heads(tile, carry):
        at_lanes = lambda off: pl.ds(pl.multiple_of(128 * tile + off, 128), 128)
        ot_ref[...] = jnp.zeros_like(ot_ref)
        vt_ref[...] = mix[:, at_lanes(1792)].T

        def head(h):
            k = jnp.where((lane >= 64 * h) & (lane < 64 * h + 64), mix[:, at_lanes(896)], jnp.bfloat16(0))
            for i in range(blocks):
                low_at, high_at = i * BLOCK, (i + 1) * BLOCK
                q = mix[low_at:high_at, at_lanes(0)] * jnp.bfloat16(0.125)
                s = dot_nt(k[:high_at], q)
                same = segc_ref[:high_at, :] == segr_ref[:, low_at:high_at]
                kpos = lax.broadcasted_iota(jnp.int32, (high_at, BLOCK), 0)
                qpos = lax.broadcasted_iota(jnp.int32, (high_at, BLOCK), 1) + low_at
                s = jnp.where(same & (kpos <= qpos), s, -1e30)
                m = jnp.max(s, axis=0, keepdims=True)
                p = jnp.exp(s - m)
                l = jnp.sum(p, axis=0, keepdims=True)
                ot = dot_nn(vt_ref[64 * h : 64 * h + 64, :high_at], p.astype(jnp.bfloat16))
                ot_ref[64 * h : 64 * h + 64, low_at:high_at] = ot / l
                lse_ref[tile, h : h + 1, low_at:high_at] = m + jnp.log(l)

        head(0)

        @pl.when(tile < 6)
        def _():
            head(1)

        @pl.when(tile == 2)
        def _():
            out_x.wait_recv()
            out_y.wait_recv()
            for copy in more + cores[:2] + overs[:2]:
                copy.start()

        @pl.when(tile == 4)
        def _():
            expand_x.wait_recv()
            expand_y.wait_recv()
            for copy in expand_more:
                copy.start()
            for copy in more:
                copy.wait_recv()
            cores[2].start()
            overs[2].start()

        o_ref[:, at_lanes(0)] = ot_ref[...].T.astype(jnp.bfloat16)
        return carry

    lax.fori_loop(0, 7, tile_heads, 0)
    cot_z.wait_recv()
    cot_both.start()
    for i in range(3):
        overs[i].wait_recv()
        passes[i].start()
    for copy in expand_more + cores + passes + [cot_core, cot_both]:
        copy.wait_recv()
    for copy in more + cores + overs + passes + expand_more + [cot_both]:
        copy.wait_send()
    wires.finish()


def mix_heads(x_seq, w_in, rows, segc, segr, out_shard, expand_shard, cot):
    any_space = pl.BlockSpec(memory_space=pl.ANY)
    vmem = pl.BlockSpec(memory_space=pltpu.VMEM)
    shape = jax.ShapeDtypeStruct
    kind = jnp.bfloat16
    length = x_seq.shape[0]
    buf = lambda *dims: pltpu.VMEM(dims, kind)
    return pl.pallas_call(
        mix_heads_kernel,
        in_specs=[any_space, any_space, vmem, vmem, vmem, any_space, any_space, any_space],
        out_specs=[vmem] * 5 + [any_space] * 3,
        out_shape=[
            shape((length, 2688), kind),
            shape(x_seq.shape, kind),
            shape(x_seq.shape, kind),
            shape((length, 896), kind),
            shape((7, 8, length), jnp.float32),
            shape((4,) + out_shard.shape, kind),
            shape((4,) + expand_shard.shape, kind),
            shape((3,) + cot.shape, kind),
        ],
        scratch_shapes=[
            buf(*x_seq.shape),
            buf(*w_in.shape),
            buf(*out_shard.shape),
            buf(*expand_shard.shape),
            pltpu.VMEM((128, length), jnp.float32),
            buf(128, length),
            pltpu.SemaphoreType.DMA((24,)),
            pltpu.SemaphoreType.DMA((24,)),
            pltpu.SemaphoreType.DMA((8,)),
        ],
        compiler_params=pltpu.CompilerParams(collective_id=6, has_side_effects=True, vmem_limit_bytes=56 * 2**20),
        cost_estimate=pl.CostEstimate(flops=5 * 10**10, bytes_accessed=2**26, transcendentals=0),
        name="mix_heads",
    )(x_seq, w_in, rows, segc, segr, out_shard, expand_shard, cot)


def heads_back_kernel(q_ref, k_ref, v_ref, do_ref, o_ref, lse_ref, segc_ref, segr_ref, normed_ref, share_ref, first_ref, own_ref, pass_ref, result_ref, middle_ref, cot_ref, rows_ref, core_ref, dq_ref, dk_ref, dv_ref, sums_ref, grad_ref, share_out, first_out, result_out, cot_sums, core_out, quads, dqt_ref, odt_ref, pair, own, share_own, got, pair_next, normed_t, result, middle, cot, core_own, core_x, core_y, send, recv, local):
    tile = pl.program_id(0)
    replica = lax.axis_index("replica")
    group = lax.axis_index("group")
    quad = lax.rem(replica, 4)
    quad_z = lax.rem(quad + 2, 4)
    by_x, by_y, by_both, by_core, by_z = partners(replica, group)
    by_pair = (lax.rem(replica + 4, 8), group)
    wires = Wires(send, recv, local)
    pieces = [pl.ds(0, HALF), pl.ds(HALF, 400 - HALF)]
    pass_y = wires.make(pass_ref.at[pieces[0]], got.at[pieces[0]], by_y)
    pass_x = wires.make(pass_ref.at[pieces[1]], got.at[pieces[1]], by_x)
    pair_lower = wires.make(share_ref.at[pieces[1]], pair.at[pieces[1]], by_pair)
    pair_upper = wires.make(own.at[pieces[0]], pair_next, by_pair)
    loads = [
        pltpu.make_async_copy(first_ref, pair.at[pieces[0]], local.at[0]),
        pltpu.make_async_copy(own_ref, own, local.at[1]),
        pltpu.make_async_copy(share_ref, share_own, local.at[2]),
    ]
    x = lax.rem(group, 2)
    y = lax.div(group, 2)
    out_rows = (1 - y, y)
    out_x = [wires.make(core_ref.at[2 * row + 1 - x], core_x.at[i], by_x) for i, row in enumerate(out_rows)]
    out_y = wires.make(core_own.at[0], core_y, by_y)
    more_loads = [pltpu.make_async_copy(core_ref.at[2 * row + x], core_own.at[i], local.at[8 + i]) for i, row in enumerate(out_rows)]
    more_loads += [
        pltpu.make_async_copy(result_ref, result, local.at[5]),
        pltpu.make_async_copy(middle_ref, middle, local.at[6]),
        pltpu.make_async_copy(cot_ref, cot, local.at[7]),
    ]
    keeps = [pltpu.make_async_copy(pair.at[rows], quads.at[quad, rows], local.at[3 + i]) for i, rows in enumerate(pieces)]
    overs = [wires.make(pair.at[rows], quads.at[quad, rows], by_z) for rows in pieces]
    cores = [wires.make(pair.at[rows], quads.at[quad, rows], by_core) for rows in pieces]
    passes = [wires.make(quads.at[quad_z, rows], quads.at[quad_z, rows], by_core) for rows in pieces]

    def spread(i):
        keeps[i].start()
        overs[i].start()
        cores[i].start()

    @pl.when(tile == 0)
    def _():
        greet([by_pair, by_x, by_y, by_core, by_z])
        for copy in [pass_y, pass_x, pair_lower] + loads + more_loads:
            copy.start()
        normed_t[...] = normed_ref[...].T

    @pl.when(tile == 1)
    def _():
        for copy in loads:
            copy.wait()
        spread(0)

    @pl.when(tile == 2)
    def _():
        pass_y.wait()
        pass_x.wait()
        own[...] = add_low(own[...], got[...])
        for copy in out_x:
            copy.start()

    @pl.when(tile == 3)
    def _():
        for copy in more_loads:
            copy.wait()
        cot_sums[...] = jnp.zeros_like(cot_sums)
        for seq in range(2):
            rows = pl.ds(256 * seq, 256)
            final = result[rows, :] + middle[rows, :] + rows_ref[3:4, : result.shape[1]]
            result_out[seq] = final.astype(jnp.bfloat16)
            cot_sums[0:1, :] += jnp.sum(cot[rows, :].astype(jnp.float32), axis=0, keepdims=True)

    @pl.when(tile == 4)
    def _():
        pair_lower.wait()
        pair_upper.start()
        pair[HALF:, :] = add_low(pair[HALF:, :], share_own[HALF:, :])
        spread(1)
        overs[0].wait_recv()
        passes[0].start()

    @pl.when(tile == 5)
    def _():
        for i in range(2):
            out_x[i].wait()
            core_own[i] = add_low(core_own[i], core_x[i])
        out_y.start()

    length = q_ref.shape[0]
    blocks = length // BLOCK
    lane = lax.broadcasted_iota(jnp.int32, (1, 128), 1)
    dqt_ref[...] = jnp.zeros_like(dqt_ref)
    odt_ref[...] = (do_ref[...].astype(jnp.float32) * o_ref[...].astype(jnp.float32)).T

    def head(h):
        mine = (lane >= 64 * h) & (lane < 64 * h + 64)
        dot_row = jnp.sum(odt_ref[64 * h : 64 * h + 64, :], axis=0, keepdims=True)
        for j in range(blocks):
            low, high = j * BLOCK, (j + 1) * BLOCK
            rest = length - low
            q = q_ref[low:, :] * jnp.bfloat16(0.125)
            do = do_ref[low:, :]
            k = jnp.where(mine, k_ref[low:high, :], jnp.bfloat16(0))
            v = jnp.where(mine, v_ref[low:high, :], jnp.bfloat16(0))
            s = dot_nt(k, q)
            same = segc_ref[low:high, :] == segr_ref[:, low:]
            kpos = lax.broadcasted_iota(jnp.int32, (BLOCK, rest), 0)
            qpos = lax.broadcasted_iota(jnp.int32, (BLOCK, rest), 1)
            p = jnp.where(same & (kpos <= qpos), jnp.exp(s - lse_ref[0, h : h + 1, low:]), 0.0)
            dp = dot_nt(v, do)
            ds = (p * (dp - dot_row[:, low:])).astype(jnp.bfloat16)
            dv = dot_nn(p.astype(jnp.bfloat16), do)
            dk = dot_nn(ds, q)
            if h == 0:
                dv_ref[low:high, :] = jnp.where(mine, dv, 0.0).astype(jnp.bfloat16)
                dk_ref[low:high, :] = jnp.where(mine, dk, 0.0).astype(jnp.bfloat16)
            else:
                dv_ref[low:high, :] = jnp.where(mine, dv.astype(jnp.bfloat16), dv_ref[low:high, :])
                dk_ref[low:high, :] = jnp.where(mine, dk.astype(jnp.bfloat16), dk_ref[low:high, :])
            dqt_ref[:, low:] += dot_nn(k.T, ds)

    head(0)

    @pl.when(tile < 6)
    def _():
        head(1)

    dq_ref[...] = (dqt_ref[...].T * 0.125).astype(jnp.bfloat16)

    row = lax.broadcasted_iota(jnp.int32, (8, 128), 0)
    sum_q = jnp.sum(dq_ref[...].astype(jnp.float32), axis=0, keepdims=True)
    sum_v = jnp.sum(dv_ref[...].astype(jnp.float32), axis=0, keepdims=True)
    sums_ref[...] = jnp.where(row == 0, sum_q, jnp.where(row == 1, sum_v, 0.0))

    grads = jnp.concatenate([dq_ref[...], dk_ref[...], dv_ref[...]], axis=1)
    weights = dot_nn(normed_t[...], grads).astype(jnp.bfloat16)
    for i in range(3):
        grad_ref[i] = weights[:, 128 * i : 128 * i + 128]

    @pl.when(tile == 6)
    def _():
        overs[1].wait_recv()
        passes[1].start()
        share_out[...] = own[...]
        out_y.wait()
        width = core_own.shape[2]
        core_out[:, :width] = add_low(core_own[1], core_y[...])
        core_out[:, width:] = jnp.zeros((core_out.shape[0], core_out.shape[1] - width), jnp.bfloat16)
        pair_upper.wait()
        first_out[...] = add_low(own[:HALF, :], pair_next[...])
        for copy in cores + passes + keeps:
            copy.wait()
        for copy in overs:
            copy.wait_send()


def heads_back(qkv, grad, out, lse, segc, segr, normed, share, first, own, passed, result, middle, cot, rows, out_core):
    length = qkv.shape[0]
    width = share.shape[1]
    buf = lambda *dims: pltpu.VMEM(dims, jnp.bfloat16)
    still = lambda *dims: pl.BlockSpec(dims, lambda t: (0,) * len(dims))
    spec = lambda off: pl.BlockSpec((length, 128), lambda t: (0, t + off))
    one = pl.BlockSpec((length, 128), lambda t: (0, t))
    shape = jax.ShapeDtypeStruct((length, 896), jnp.bfloat16)
    return pl.pallas_call(
        heads_back_kernel,
        grid=(7,),
        in_specs=[spec(0), spec(7), spec(14), one, one, pl.BlockSpec((1, 8, length), lambda t: (t, 0, 0)), pl.BlockSpec((length, 1), lambda t: (0, 0)), pl.BlockSpec((1, length), lambda t: (0, 0)), still(*normed.shape)] + [pl.BlockSpec(memory_space=pl.ANY)] * 7 + [still(*rows.shape), pl.BlockSpec(memory_space=pl.ANY)],
        out_specs=[one, one, one, pl.BlockSpec((8, 128), lambda t: (0, t)), pl.BlockSpec((3, width, 128), lambda t: (0, 0, t)), still(*share.shape), still(*first.shape), still(2, 256, width), still(8, width), still(208, width + 64), pl.BlockSpec(memory_space=pl.ANY)],
        out_shape=[
            shape,
            shape,
            shape,
            jax.ShapeDtypeStruct((8, 896), jnp.float32),
            jax.ShapeDtypeStruct((3, width, 896), jnp.bfloat16),
            jax.ShapeDtypeStruct(share.shape, share.dtype),
            jax.ShapeDtypeStruct(first.shape, share.dtype),
            jax.ShapeDtypeStruct((2, 256, width), share.dtype),
            jax.ShapeDtypeStruct((8, width), jnp.float32),
            jax.ShapeDtypeStruct((208, width + 64), share.dtype),
            jax.ShapeDtypeStruct((4,) + share.shape, share.dtype),
        ],
        scratch_shapes=[pltpu.VMEM((128, length), jnp.float32), pltpu.VMEM((128, length), jnp.float32), buf(400, width), buf(400, width), buf(400, width), buf(400, width), buf(HALF, width), buf(width, length), pltpu.VMEM(result.shape, jnp.float32), pltpu.VMEM(middle.shape, jnp.float32), buf(*cot.shape), buf(2, 208, width), buf(2, 208, width), buf(208, width), pltpu.SemaphoreType.DMA((16,)), pltpu.SemaphoreType.DMA((16,)), pltpu.SemaphoreType.DMA((10,))],
        compiler_params=pltpu.CompilerParams(vmem_limit_bytes=56 * 2**20, collective_id=4, has_side_effects=True),
        cost_estimate=pl.CostEstimate(flops=int(13 * 5 * 2 * length * length * 64 * 2), bytes_accessed=16 * length * 896, transcendentals=13 * length * length // 2),
        name="heads_back",
    )(qkv, qkv, qkv, grad, out, lse, segc, segr, normed, share, first, own, passed, result, middle, cot, rows, out_core)

def feed_all_kernel(second, cot_in, cots, expand_part, reduce_shard, middle_in, out_in, bias, rows_ref, act_out, back_out, second_out, reduce_out, low_out, att_out, gs_out, own_out, pass_out, sum_out, norm_sums, wexp, wred, s, c, a, b, gs, got_core, got_z, rg, got_x, got_y, send, recv, local):
    replica = lax.axis_index("replica")
    group = lax.axis_index("group")
    quad = lax.rem(replica, 4)
    y = lax.div(group, 2)
    x = lax.rem(group, 2)
    by_x, by_y, by_both, by_core, by_z = partners(replica, group)
    slot_x, slot_y, slot_both = by_x[1], by_y[1], by_both[1]
    wires = Wires(send, recv, local)
    greet([by_x, by_y, by_core, by_z])
    width = wexp.shape[0]
    block = lambda rel: pl.ds(512 * rel, 512)
    sec_core = wires.go(second, s.at[block(1)], by_core)
    sec_z = wires.go(second, s.at[block(2)], by_z)
    quarter = reduce_shard.at[rows16(400 * quad, 400)]
    spot = lambda rank: rows16(400 * rank, 400)
    red_x = wires.go(quarter, wred.at[spot(group)], by_x)
    red_y = wires.go(quarter, wred.at[spot(group)], by_y)
    load_s = wires.here(second, s.at[block(0)])
    load_e = wires.here(expand_part, wexp)
    load_r = wires.here(quarter, wred.at[spot(group)])
    load_m = wires.here(middle_in, gs_out)
    load_c = [wires.here(cot_in, c.at[block(0)])] + [wires.here(cots.at[i], c.at[block(i + 1)]) for i in range(3)]
    sum_out[...] = jnp.zeros_like(sum_out)
    root = 0.7978845608028654

    def gelu(u):
        square = u * u
        t = jnp.tanh(root * u * (1.0 + 0.044715 * square))
        half = 0.5 * (1.0 + t)
        slope = half + (0.5 * root) * u * (1.0 - t * t) * (1.0 + (3.0 * 0.044715) * square)
        return u * half, slope

    def steps(rel, body):
        def one(i, carry):
            body(pl.ds(pl.multiple_of(512 * rel + 256 * i, 256), 256))
            return carry

        lax.fori_loop(0, 2, one, 0)

    def keep_back(rows, low_at, high_at, back):
        back = back.astype(jnp.bfloat16)
        b[rows, low_at:high_at] = back
        sum_out[:, low_at:high_at] += jnp.sum(back.astype(jnp.float32).reshape(32, 8, high_at - low_at), axis=0)

    def up_only(rows):
        entries = s[rows, :width]
        for low_at, high_at in PIECES:
            act, slope = gelu(dot_nn(entries, wexp[:, low_at:high_at]) + bias[:, low_at:high_at])
            a[rows, low_at:high_at] = act.astype(jnp.bfloat16)
            b[rows, low_at:high_at] = slope.astype(jnp.bfloat16)

    def finish_rows(rows):
        gs[rows, width:] = jnp.zeros((256, gs.shape[1] - width), jnp.bfloat16)
        gs[rows, :width] = dot_nt(b[rows, :], wexp[...]).astype(jnp.bfloat16)

    def back_only(rows):
        cot = c[rows, :]
        for low_at, high_at in PIECES:
            keep_back(rows, low_at, high_at, dot_nt(cot, wred[low_at:high_at, :]) * b[rows, low_at:high_at].astype(jnp.float32))
        finish_rows(rows)

    def both(rows):
        entries = s[rows, :width]
        cot = c[rows, :]
        for low_at, high_at in PIECES:
            act, slope = gelu(dot_nn(entries, wexp[:, low_at:high_at]) + bias[:, low_at:high_at])
            a[rows, low_at:high_at] = act.astype(jnp.bfloat16)
            keep_back(rows, low_at, high_at, dot_nt(cot, wred[low_at:high_at, :]) * slope)
        finish_rows(rows)

    load_s.wait()
    load_e.wait()
    steps(0, up_only)
    sec_core.wait_recv()
    steps(1, up_only)
    red_x.wait_recv()
    more_y = wires.go(wred.at[rows16(400 * slot_x, HALF)], wred.at[rows16(400 * slot_x, HALF)], by_y)
    red_y.wait_recv()
    more_x = wires.go(wred.at[rows16(400 * slot_y + HALF, 400 - HALF)], wred.at[rows16(400 * slot_y + HALF, 400 - HALF)], by_x)
    sec_z.wait_recv()
    sec_both = wires.go(s.at[block(2)], s.at[block(3)], by_core)
    load_r.wait()
    for copy in load_c:
        copy.wait()
    more_x.wait_recv()
    more_y.wait_recv()
    wires.keep(wred, reduce_out)
    sec_both.wait_recv()
    wires.keep(s, second_out)
    base = wires.remotes
    wires.remotes = base + 4

    def far_copies(half):
        piece = pl.ds(pl.multiple_of(256 * half, 256), 256)
        third = pl.ds(pl.multiple_of(1536 + 256 * half, 256), 256)
        second_rows = pl.ds(pl.multiple_of(1024 + 256 * half, 256), 256)
        near = pltpu.make_async_remote_copy(src_ref=gs.at[third], dst_ref=got_core.at[1, piece], send_sem=send.at[base + half], recv_sem=recv.at[base + half], device_id=by_core, device_id_type=MESH)
        over = pltpu.make_async_remote_copy(src_ref=gs.at[second_rows], dst_ref=got_z.at[piece], send_sem=send.at[base + 2 + half], recv_sem=recv.at[base + 2 + half], device_id=by_z, device_id_type=MESH)
        return third, second_rows, piece, near, over

    def far_half(half, carry):
        third, second_rows, piece, near, over = far_copies(half)
        both(third)
        near.start()
        both(second_rows)
        near.wait_recv()
        gs[second_rows, :] = add_low(gs[second_rows, :], got_core[1, piece, :])
        over.start()
        return carry

    lax.fori_loop(0, 2, far_half, 0)
    wires.keep(a, act_out)
    weight_sum(a, c, rg)
    x_copies = [wires.go(rg.at[rows16(400 * slot, HALF)], got_x.at[i], by_x) for i, slot in enumerate((slot_x, slot_both))]
    y_copies = [wires.go(rg.at[rows16(400 * slot + HALF, 400 - HALF)], got_y.at[i], by_y) for i, slot in enumerate((slot_y, slot_both))]
    steps(1, back_only)
    gs_core = wires.go(gs.at[block(1)], got_core.at[0], by_core)
    steps(0, back_only)
    wires.keep(b, back_out)
    load_w = wires.here(out_in, wexp)
    load_m.wait()
    gs_core.wait_recv()
    for half in range(2):
        third, second_rows, piece, near, over = far_copies(half)
        over.wait_recv()
        over.wait_send()
        near.wait_send()
    load_w.wait()
    norm_sums[...] = jnp.zeros_like(norm_sums)
    lanes = lax.broadcasted_iota(jnp.int32, (1, 128), 1)
    for seq in range(2):
        stage = got_core.at[1 - seq]

        def norm_back(j, carry):
            rows = pl.ds(pl.multiple_of(256 * seq + 128 * j, 128), 128)
            first = pl.ds(pl.multiple_of(128 * j, 128), 128)
            other = pl.ds(pl.multiple_of(256 + 128 * j, 128), 128)
            grad = gs[rows, :width].astype(jnp.float32) + got_core[0, rows, :width].astype(jnp.float32) + got_z[rows, :width].astype(jnp.float32)
            middle = gs_out[rows, :]
            center = middle - jnp.mean(middle, axis=-1, keepdims=True)
            scale = lax.rsqrt(jnp.mean(center * center, axis=-1, keepdims=True) + epsilon)
            unit = center * scale
            q = grad * rows_ref[6:7, :width]
            grad_middle = c[rows, :].astype(jnp.float32) + scale * (
                q - jnp.mean(q, axis=-1, keepdims=True) - unit * jnp.mean(q * unit, axis=-1, keepdims=True)
            )
            gs_out[rows, :] = grad_middle
            grad_low = grad_middle.astype(jnp.bfloat16)
            gs[rows, :width] = grad_low
            norm_sums[0:1, :] += jnp.sum(grad * unit, axis=0, keepdims=True)
            norm_sums[1:2, :] += jnp.sum(grad, axis=0, keepdims=True)
            norm_sums[2:3, :] += jnp.sum(grad_low.astype(jnp.float32), axis=0, keepdims=True)
            att = dot_nt(grad_low, wexp[...]).astype(jnp.bfloat16)
            stage[first, 0:768] = att[:, 0:768]
            stage[first, 768:896] = jnp.where(lanes < 64, att[:, 768:896], jnp.bfloat16(0))
            stage[other, 0:128] = jnp.where(lanes >= 64, att[:, 768:896], jnp.bfloat16(0))
            stage[other, 128 : width - 768] = att[:, 896:width]
            stage[other, width - 768 : 896] = jnp.zeros((128, 896 + 768 - width), jnp.bfloat16)
            return carry

        lax.fori_loop(0, 2, norm_back, 0)
        for half in range(2):
            wires.keep(stage.at[pl.ds(256 * half, 256), pl.ds(0, 896)], att_out.at[seq, half])
    wires.keep(gs.at[block(0)], low_out)
    for copy in x_copies + y_copies:
        copy.wait_recv()
    own_out[:HALF] = add_low(rg[rows16(400 * group, HALF), :], got_x[0])
    own_out[HALF:] = add_low(rg[rows16(400 * group + HALF, 400 - HALF), :], got_y[0])
    pass_out[:HALF] = add_low(rg[rows16(400 * slot_y, HALF), :], got_x[1])
    pass_out[HALF:] = add_low(rg[rows16(400 * slot_x + HALF, 400 - HALF), :], got_y[1])
    wires.finish()


def feed_all(second, cot, cots, expand_part, reduce_shard, middle, full_out, bias, rows_in):
    any_space = pl.BlockSpec(memory_space=pl.ANY)
    vmem = pl.BlockSpec(memory_space=pltpu.VMEM)
    shape = jax.ShapeDtypeStruct
    kind = jnp.bfloat16
    rows, full = second.shape
    width = expand_part.shape[0]
    buf = lambda *dims: pltpu.VMEM(dims, kind)
    return pl.pallas_call(
        feed_all_kernel,
        in_specs=[any_space] * 7 + [vmem, vmem],
        out_specs=[any_space] * 6 + [vmem] * 5,
        out_shape=[
            shape((4 * rows, width), kind),
            shape((4 * rows, width), kind),
            shape((4 * rows, full), kind),
            shape((width, width), kind),
            shape((rows, full), kind),
            shape((2, 2, 256, 896), kind),
            shape((rows, width), jnp.float32),
            shape((400, width), kind),
            shape((400, width), kind),
            shape((8, width), jnp.float32),
            shape((8, width), jnp.float32),
        ],
        scratch_shapes=[
            buf(width, width),
            buf(width, width),
            buf(4 * rows, full),
            buf(4 * rows, width),
            buf(4 * rows, width),
            buf(4 * rows, width),
            buf(4 * rows, full),
            buf(2, rows, full),
            buf(rows, full),
            buf(width, width),
            buf(2, HALF, width),
            buf(2, 400 - HALF, width),
            pltpu.SemaphoreType.DMA((16,)),
            pltpu.SemaphoreType.DMA((16,)),
            pltpu.SemaphoreType.DMA((20,)),
        ],
        compiler_params=pltpu.CompilerParams(collective_id=5, has_side_effects=True, vmem_limit_bytes=63 * 2**20),
        cost_estimate=pl.CostEstimate(flops=10**11, bytes_accessed=2**26, transcendentals=0),
        name="feed_all",
    )(second, cot, cots, expand_part, reduce_shard, middle, full_out, bias, rows_in)


def turn_more_kernel(grad_att, back, second, act, wred_in, pass_in, att_in, grad_in, own_in, heads_out, result_out, share_out, first_out, own_out, pass_out, core_out, att, grad, stage, b, s, a, wred, rg, result, got_core, got_z, got, got_x, got_y, pair, send, recv, local):
    replica = lax.axis_index("replica")
    group = lax.axis_index("group")
    core = lax.rem(replica, 2)
    y = lax.div(group, 2)
    x = lax.rem(group, 2)
    by_x, by_y, by_both, by_core, by_z = partners(replica, group)
    by_pair = (lax.rem(replica + 4, 8), group)
    slot_x, slot_y, slot_both = by_x[1], by_y[1], by_both[1]
    wires = Wires(send, recv, local)
    load_a = wires.here(act, a)
    load_w = wires.here(wred_in, wred)
    load_own = wires.here(grad_att.at[x, y], stage)
    load_s = wires.here(second, s)
    load_b = wires.here(back, b)
    load_att = wires.here(att_in, att)
    load_grad = wires.here(grad_in, grad)
    greet([by_x, by_y, by_both, by_core, by_z, by_pair])
    width = wred.shape[0]
    block = lambda rel: pl.ds(512 * rel, 512)
    pass_y = wires.go(pass_in.at[pl.ds(0, HALF)], got.at[pl.ds(0, HALF)], by_y)
    pass_x = wires.go(pass_in.at[pl.ds(HALF, 400 - HALF)], got.at[pl.ds(HALF, 400 - HALF)], by_x)
    load_a.wait()
    load_w.wait()

    def rows_out(rel):
        def one(i, carry):
            rows = pl.ds(pl.multiple_of(512 * rel + 256 * i, 256), 256)
            result[rows, :] = dot_nn(a[rows, :], wred[...]).astype(jnp.bfloat16)
            return carry

        lax.fori_loop(0, 2, one, 0)

    rows_out(3)
    to_both = wires.go(result.at[block(3)], got_core.at[1], by_core)
    rows_out(2)
    wires.drain([pass_y, pass_x])
    turns = []
    for device in (by_both, by_x, by_y):
        there = device[1]
        turns.append(wires.go(grad_att.at[lax.rem(there, 2), lax.div(there, 2)], heads_out.at[group], device))
    to_both.wait_recv()
    result[block(2), :] = add_low(result[block(2), :], got_core[1])
    to_z = wires.go(result.at[block(2)], got_z, by_z)
    pass_y.wait_recv()
    pass_x.wait_recv()
    share_out[...] = add_low(own_in[...], got[...])
    pair_upper = wires.go(share_out.at[pl.ds(0, HALF)], pair, by_pair)
    load_own.wait()
    wires.keep(stage, heads_out.at[group])
    load_s.wait()
    load_b.wait()
    weight_sum(s, b, rg)
    x_copies = [wires.go(rg.at[rows16(400 * slot, HALF)], got_x.at[i], by_x) for i, slot in enumerate((slot_x, slot_both))]
    y_copies = [wires.go(rg.at[rows16(400 * slot + HALF, 400 - HALF)], got_y.at[i], by_y) for i, slot in enumerate((slot_y, slot_both))]
    rows_out(1)
    to_core = wires.go(result.at[block(1)], got_core.at[0], by_core)
    rows_out(0)
    load_att.wait()
    load_grad.wait()
    weight_sum(att, grad, wred)
    out_core = [wires.go(wred.at[rows16(400 * r + 192 * (1 - core), 208)], core_out.at[r], by_core) for r in range(4)]
    for r in range(4):
        out_core[r].wait_recv()
        core_out[r] = add_low(wred[rows16(400 * r + 192 * core, 208), :], core_out[r])
    to_core.wait_recv()
    to_z.wait_recv()
    result_out[...] = result[block(0), :].astype(jnp.float32) + got_core[0].astype(jnp.float32) + got_z[...].astype(jnp.float32)
    pair_upper.wait_recv()
    first_out[...] = add_low(share_out[:HALF, :], pair[...])
    for copy in x_copies + y_copies:
        copy.wait_recv()
    own_out[:HALF] = add_low(rg[rows16(400 * group, HALF), :], got_x[0])
    own_out[HALF:] = add_low(rg[rows16(400 * group + HALF, 400 - HALF), :], got_y[0])
    pass_out[:HALF] = add_low(rg[rows16(400 * slot_y, HALF), :], got_x[1])
    pass_out[HALF:] = add_low(rg[rows16(400 * slot_x + HALF, 400 - HALF), :], got_y[1])
    for copy in turns:
        copy.wait_recv()
    wires.finish()


def turn_more(grad_att, back, second, act, wred, passed, att, grad, own):
    any_space = pl.BlockSpec(memory_space=pl.ANY)
    vmem = pl.BlockSpec(memory_space=pltpu.VMEM)
    shape = jax.ShapeDtypeStruct
    kind = jnp.bfloat16
    width = wred.shape[0]
    rows = act.shape[0] // 4
    buf = lambda *dims: pltpu.VMEM(dims, kind)
    return pl.pallas_call(
        turn_more_kernel,
        in_specs=[any_space] * 8 + [vmem],
        out_specs=[any_space] + [vmem] * 6,
        out_shape=[
            shape((4,) + grad_att.shape[2:], kind),
            shape((rows, width), jnp.float32),
            shape((400, width), kind),
            shape((HALF, width), kind),
            shape((400, width), kind),
            shape((400, width), kind),
            shape((4, 208, width), kind),
        ],
        scratch_shapes=[
            buf(rows, width),
            buf(*grad.shape),
            buf(*grad_att.shape[2:]),
            buf(4 * rows, width),
            buf(*second.shape),
            buf(4 * rows, width),
            buf(width, width),
            buf(width, width),
            buf(4 * rows, width),
            buf(2, rows, width),
            buf(rows, width),
            buf(400, width),
            buf(2, HALF, width),
            buf(2, 400 - HALF, width),
            buf(HALF, width),
            pltpu.SemaphoreType.DMA((18,)),
            pltpu.SemaphoreType.DMA((18,)),
            pltpu.SemaphoreType.DMA((10,)),
        ],
        compiler_params=pltpu.CompilerParams(collective_id=2, has_side_effects=True, vmem_limit_bytes=63 * 2**20),
        cost_estimate=pl.CostEstimate(flops=3 * 10**10, bytes_accessed=2**26, transcendentals=0),
        name="turn_more",
    )(grad_att, back, second, act, wred, passed, att, grad, own)


def arrive(here, there, total, lane, k, y, mine):
    first = jnp.where(y == 0, here, there)
    other = jnp.where(y == 0, there, here)
    rows = pl.ds(mine, 208)
    total[k, rows, 0:768] = first[:, 0:768]
    total[k, rows, 768:896] = jnp.where(lane < 64, first[:, 768:896], other[:, 0:128])
    total[k, rows, 896:1664] = other[:, 128:896]


def last_kernel(dq, dk, dv, grad_in, unit_in, w_in, share_in, share_expand, first_expand, vec, gm_in, inp_in, gain, total, grad_out, vec_total, wide_total, quads, d, unit_rows, w, part, c_buf, x_buf, y_buf, line_buf, line_mid, gn, gn_y, gn_cross, inp, pair_buf, vec_got, vec_own, vec_core, vec_z, more_got, more_core, more_z, send, recv, local):
    replica = lax.axis_index("replica")
    group = lax.axis_index("group")
    core = lax.rem(replica, 2)
    quad = lax.rem(replica, 4)
    quad_z = lax.rem(quad + 2, 4)
    z = lax.div(replica, 2)
    y = lax.div(group, 2)
    x = lax.rem(group, 2)
    by_x, by_y, by_both, by_core, by_z = partners(replica, group)
    outer = (z == 0) | (z == 3)
    inner = jnp.logical_not(outer)
    by_line = (jnp.where(z == 0, replica + 2, jnp.where(z == 3, replica - 2, jnp.where(z == 1, replica - 2, replica + 2))), group)
    by_middle = (jnp.where(z == 1, replica + 2, replica - 2), group)
    lines_z = [(lax.rem(replica + 2 * k, 8), group) for k in (1, 2, 3)]
    by_pair = lines_z[1]
    wires = Wires(send, recv, local)
    greet([by_x, by_y, by_both, by_core] + lines_z)
    mine = pl.multiple_of(192 * core, 16)
    theirs = pl.multiple_of(192 * (1 - core), 16)
    other_x = 1 - x
    other_y = 1 - y
    far = 2 * other_y
    near = 2 * y
    width = w.shape[0]
    lane = lax.broadcasted_iota(jnp.int32, (1, 128), 1)
    halves = [(pl.ds(mine + 112 * m, 112 - 16 * m), pl.ds(112 * m, 112 - 16 * m)) for m in range(2)]
    pieces = [pl.ds(0, 208), pl.ds(208, 192)]

    pair_lower = wires.go(share_expand.at[pieces[1]], pair_buf, by_pair)
    c_copies = []
    part_loads = []
    for k in range(3):
        c_copies.append([wires.go(grad_in.at[k, rows16(400 * r + theirs, 208)], c_buf.at[k, r], by_core) for r in range(4)])
        part_loads.append([wires.here(grad_in.at[k, pl.ds(400 * r + mine, 208)], part.at[k, r]) for r in range(4)])
    loads = [wires.here(part, d.at[k]) for k, part in enumerate((dq, dk, dv))]
    load_w = [wires.here(w_in, w), wires.here(unit_in, unit_rows)]
    load_share = wires.here(share_in, total.at[3, pl.ds(mine, 208)])
    vec_group = [wires.go(vec.at[device[1]], vec_got.at[group], device) for device in (by_x, by_y, by_both)]

    def spread(value, rows):
        wires.keep(value, quads.at[quad, rows])
        over = wires.go(value, quads.at[quad, rows], by_z)
        return over, wires.go(value, quads.at[quad, rows], by_core)

    def spread_on(over, rows):
        over.wait_recv()
        return wires.go(quads.at[quad_z, rows], quads.at[quad_z, rows], by_core)

    load_gm = wires.here(gm_in, grad_out)
    load_inp = wires.here(inp_in, inp)

    def line_start(k, m):
        rows, merge = halves[m]
        into = wires.make(total.at[k, rows], line_buf.at[k, merge], by_line)
        middle = wires.make(total.at[k, rows], line_mid.at[k, merge], by_middle)
        back = wires.make(total.at[k, rows], line_buf.at[k, merge], by_line)

        @pl.when(outer)
        def _():
            if m == 1:
                lines[k, 0][0].wait_send()
            into.start()

        lines[k, m] = into, middle, back

    def line_second(k, m):
        rows, merge = halves[m]
        into, middle, back = lines[k, m]

        @pl.when(inner)
        def _():
            into.wait_recv()
            total[k, rows] = add_low(total[k, rows], line_buf[k, merge])
            middle.start()

    def line_third(k, m):
        rows, merge = halves[m]
        into, middle, back = lines[k, m]

        @pl.when(inner)
        def _():
            middle.wait_recv()
            middle.wait_send()
            total[k, rows] = add_low(total[k, rows], line_mid[k, merge])
            back.start()

    def line_fourth(k, m):
        rows, merge = halves[m]
        into, middle, back = lines[k, m]

        @pl.when(outer)
        def _():
            if m == 1:
                into.wait_send()
            back.wait_recv()
            total[k, rows] = line_buf[k, merge]

        @pl.when(inner)
        def _():
            back.wait_send()

    lines = {}
    x_copies = {}
    y_copies = {}

    def core_sum(k):
        for r in range(4):
            part_loads[k][r].wait()
            c_copies[k][r].wait_recv()
            c_buf[k, r] = add_low(c_buf[k, r], part[k, r])

    def x_go(k, i):
        row = (other_y, y)[i]
        x_copies[k, i] = wires.go(c_buf.at[k, 2 * row + other_x], x_buf.at[k, i], by_x)

    def x_next(k, i, after):
        wires.drain([x_copies[k, i]])
        if after is not None:
            x_go(*after)
        x_copies[k, i].wait_recv()
        spot = (far, near)[i] + x
        c_buf[k, spot] = add_low(c_buf[k, spot], x_buf[k, i])
        if i == 0:
            y_copies[k] = wires.go(c_buf.at[k, spot], y_buf.at[k], by_y)

    def y_done(k):
        y_copies[k].wait_recv()
        arrive(c_buf[k, near + x], y_buf[k], total, lane, k, y, mine)
        line_start(k, 0)

    def normed_grad(b):
        rows = pl.ds(pl.multiple_of(256 * b, 256), 256)
        value = dot_nt(d[0, rows, :], w[:, 0:896]) + dot_nt(d[1, rows, :], w[:, 896:1792]) + dot_nt(d[2, rows, :], w[:, 1792:2688])
        gn[b] = value.astype(jnp.bfloat16)
        more_got[group, 0:1, 0:width] += jnp.sum(value * unit_rows[rows, :].astype(jnp.float32), axis=0, keepdims=True)
        more_got[group, 1:2, 0:width] += jnp.sum(value, axis=0, keepdims=True)

    spread_expand = [spread(first_expand, pieces[0])]
    core_sum(0)
    x_go(0, 0)
    x_go(0, 1)
    core_sum(1)
    core_sum(2)
    load_share.wait()
    line_start(3, 0)
    more_got[group] = jnp.zeros(more_got.shape[1:], jnp.float32)
    for copy in loads + load_w:
        copy.wait()
    normed_grad(far + other_x)
    y_pass = wires.go(gn.at[far + other_x], gn_y.at[0], by_y)
    normed_grad(near + other_x)
    x_next(0, 0, (1, 0))
    x_next(0, 1, (1, 1))
    line_start(3, 1)
    line_second(3, 0)
    normed_grad(far + x)
    y_done(0)
    normed_grad(near + x)
    more_group = [wires.go(more_got.at[group], more_got.at[group], device) for device in (by_x, by_y, by_both)]
    for copy in vec_group:
        copy.wait_recv()
    vec_got[group] = vec[group]
    vec_own[...] = (vec_got[0] + vec_got[1]) + (vec_got[2] + vec_got[3])
    vec_pass = wires.go(vec_own, vec_core, by_core)
    x_next(1, 0, (2, 0))
    line_start(0, 1)
    line_second(3, 1)
    y_pass.wait_recv()
    gn_y[0] = add_low(gn_y[0], gn[near + other_x])
    line_second(0, 0)
    x_next(1, 1, (2, 1))
    y_done(1)
    for copy in more_group:
        copy.wait_recv()
    more_z[z] = (more_got[0] + more_got[1]) + (more_got[2] + more_got[3])
    more_pass = wires.go(more_z.at[z], more_core, by_core)
    pair_lower.wait_recv()
    pair_buf[...] = add_low(pair_buf[...], share_expand[HALF:, :])
    spread_expand.append(spread(pair_buf, pieces[1]))
    line_third(3, 0)
    line_second(0, 1)
    vec_pass.wait_recv()
    vec_z[z] = vec_own[...] + vec_core[...]
    vec_line = [wires.go(vec_z.at[z], vec_z.at[z], device) for device in lines_z]
    line_start(1, 1)
    x_next(2, 0, None)
    cross = wires.go(gn_y.at[0], gn_cross, by_x)
    y_keep = wires.go(gn.at[far + x], gn_y.at[1], by_y)
    line_second(1, 0)
    line_third(3, 1)
    x_next(2, 1, None)
    y_done(2)
    line_third(0, 0)
    line_second(1, 1)
    line_start(2, 1)
    more_pass.wait_recv()
    wires.drain([more_pass])
    more_z[z] = more_z[z] + more_core[...]
    more_line = [wires.go(more_z.at[z], more_z.at[z], device) for device in lines_z]
    line_third(0, 1)
    line_second(2, 0)
    line_third(1, 0)
    passes = [spread_on(spread_expand[0][0], pieces[0])]
    line_second(2, 1)
    line_third(1, 1)

    load_gm.wait()
    load_inp.wait()

    def norm_back(seq, grad):
        entries = inp[seq].astype(jnp.float32)
        center = entries - jnp.mean(entries, axis=-1, keepdims=True)
        scale = lax.rsqrt(jnp.mean(center * center, axis=-1, keepdims=True) + epsilon)
        unit = center * scale
        q = grad * gain[...]
        grad_out[seq] += scale * (q - jnp.mean(q, axis=-1, keepdims=True) - unit * jnp.mean(q * unit, axis=-1, keepdims=True))

    y_keep.wait_recv()
    norm_back(x, gn_y[1].astype(jnp.float32) + gn[near + x].astype(jnp.float32))
    cross.wait_recv()
    norm_back(other_x, gn_cross[...].astype(jnp.float32))
    line_third(2, 0)
    line_third(2, 1)
    for copy in vec_line:
        copy.wait_recv()
    vec_total[...] = (vec_z[0] + vec_z[1]) + (vec_z[2] + vec_z[3])
    passes.append(spread_on(spread_expand[1][0], pieces[1]))
    last = []
    for k in (3, 0, 1, 2):
        line_fourth(k, 0)
        line_fourth(k, 1)
        rows = pl.ds(pl.multiple_of(208 * core, 16), 192)
        last.append(wires.go(total.at[k, rows], total.at[k, rows], by_core))
    for copy in more_line:
        copy.wait_recv()
    wide_total[...] = (more_z[0] + more_z[1]) + (more_z[2] + more_z[3])
    for copy in last + passes + [both for over, both in spread_expand]:
        copy.wait_recv()
    wires.finish()


def last_sums(dq, dk, dv, in_grad, unit, w_half, out_share, share_expand, first_expand, vec, grad_middle, inputs, gain):
    any_space = pl.BlockSpec(memory_space=pl.ANY)
    vmem = pl.BlockSpec(memory_space=pltpu.VMEM)
    shape = jax.ShapeDtypeStruct
    kind = jnp.bfloat16
    width = w_half.shape[0]
    buf = lambda *dims: pltpu.VMEM(dims, kind)
    flat = lambda *dims: pltpu.VMEM(dims, jnp.float32)
    return pl.pallas_call(
        last_kernel,
        in_specs=[any_space] * 7 + [vmem, vmem, vmem, any_space, any_space, vmem],
        out_specs=[vmem, vmem, vmem, vmem, any_space],
        out_shape=[
            shape((4, 400, 1664), kind),
            shape(grad_middle.shape, jnp.float32),
            shape(vec.shape[1:], vec.dtype),
            shape((8, 1664), jnp.float32),
            shape((4,) + share_expand.shape, kind),
        ],
        scratch_shapes=[
            buf(3, 1024, 896),
            buf(*unit.shape),
            buf(*w_half.shape),
            buf(3, 4, 208, 896),
            buf(3, 4, 208, 896),
            buf(3, 2, 208, 896),
            buf(3, 208, 896),
            buf(4, 208, 1664),
            buf(4, 208, 1664),
            buf(4, 256, width),
            buf(2, 256, width),
            buf(256, width),
            buf(*inputs.shape),
            buf(400 - HALF, width),
            flat(*vec.shape),
            flat(*vec.shape[1:]),
            flat(*vec.shape[1:]),
            flat(*vec.shape),
            flat(4, 8, 1664),
            flat(8, 1664),
            flat(4, 8, 1664),
            pltpu.SemaphoreType.DMA((88,)),
            pltpu.SemaphoreType.DMA((88,)),
            pltpu.SemaphoreType.DMA((24,)),
        ],
        compiler_params=pltpu.CompilerParams(collective_id=3, has_side_effects=True, vmem_limit_bytes=63 * 2**20),
        cost_estimate=pl.CostEstimate(flops=10**11, bytes_accessed=2**26, transcendentals=0),
        name="last_sums",
    )(dq, dk, dv, in_grad, unit, w_half, out_share, share_expand, first_expand, vec, grad_middle, inputs, gain)


def on_device(
    inputs,
    segments,
    cotangent,
    project_in,
    project_out,
    expand_weight,
    reduce_weight,
    query_bias,
    value_bias,
    project_bias,
    expand_bias,
    reduce_bias,
    first_gain,
    first_shift,
    second_gain,
    second_shift,
):
    replica, group, z, core, y, x = place()
    quad = lax.rem(replica, 4)
    width = 1600
    rows = 512

    names = (query_bias, value_bias, project_bias, reduce_bias, first_gain, first_shift, second_gain, second_shift)
    index = lax.broadcasted_iota(jnp.int32, (16, 400), 0)
    vec = jnp.pad(expand_bias.reshape(4, 400), ((8, 4), (0, 0)))
    for k, name in enumerate(names):
        vec = jnp.where(index == k, name[None, :], vec)
    x_seq, w_half, vecs, segs, quarter_expand = first_exchange(inputs, project_in, vec, segments[:, None, :], expand_weight)
    row_vectors = padded(jnp.swapaxes(wide(vecs), 0, 1).reshape(16, width))
    bias_expand = lax.dynamic_index_in_dim(wide(vecs), 8 + quad, 1, False).reshape(1, width)
    segs = segs.reshape(1024)

    w_half = w_half.reshape(width, 2688)
    segc = segs[:, None]
    segr = segs[None]
    own_cot = cotangent.reshape(rows, width)
    mixture, normed, unit_seq, attended, lse, full_out, expand_part, cots = mix_heads(
        x_seq.reshape(1024, width), w_half, row_vectors, segc, segr, project_out, quarter_expand, own_cot
    )
    full_out = full_out.reshape(width, width)
    att_tokens, middle, second = turn_middle(attended.reshape(4, 256, 896), full_out, inputs, row_vectors)
    (
        activated,
        grad_expanded,
        second_all,
        reduce_part,
        grad_middle_low,
        grad_att,
        grad_middle,
        own_reduce,
        pass_reduce,
        expand_sums,
        norm_sums,
    ) = feed_all(
        second, own_cot, cots, expand_part.reshape(width, width), reduce_weight, middle, full_out, bias_expand, row_vectors
    )

    grad_heads, result, share_reduce, first_reduce, own_expand, pass_expand, out_core = turn_more(
        grad_att, grad_expanded, second_all, activated, reduce_part, pass_reduce, att_tokens, grad_middle_low, own_reduce
    )
    dq, dk, dv, bias_sums, in_grad, share_expand, first_expand, outputs, cot_sums, out_share, quads_reduce = heads_back(
        mixture,
        grad_heads.reshape(1024, 896),
        attended,
        lse,
        segc,
        segr,
        normed,
        share_reduce,
        first_reduce,
        own_expand,
        pass_expand,
        result,
        middle,
        own_cot,
        row_vectors,
        out_core,
    )

    def spread(columns):
        lower = jnp.concatenate([columns[:832], jnp.zeros((768,), jnp.float32)])
        upper = jnp.concatenate([jnp.zeros((832,), jnp.float32), columns[64:832]])
        return jnp.where(y == 0, lower, upper)

    expand_bias_part = jnp.sum(expand_sums, axis=0).reshape(4, 400)
    expand_bias_wide = lax.dynamic_update_slice_in_dim(jnp.zeros((4, width), jnp.float32), expand_bias_part, 400 * quad, 1)
    vectors = jnp.concatenate(
        [
            spread(bias_sums[0]).reshape(4, 400),
            spread(bias_sums[1]).reshape(4, 400),
            norm_sums[2].reshape(4, 400),
            cot_sums[0].reshape(4, 400),
            norm_sums[0].reshape(4, 400),
            norm_sums[1].reshape(4, 400),
            expand_bias_wide,
        ],
        axis=1,
    )
    vectors = jnp.pad(vectors, ((0, 0), (0, 96))).reshape(4, 32, 128)
    grad_total, input_grad, vec_total, wide_total, quads_expand = last_sums(
        dq, dk, dv, in_grad, unit_seq, w_half, out_share, share_expand, first_expand, vectors, grad_middle.reshape(2, 256, width), inputs, row_vectors[4:5, :width]
    )
    vec_total = vec_total.reshape(4096)
    pieces = [vec_total[400 * k : 400 * k + 400] for k in range(6)]
    first_sums = lax.dynamic_index_in_dim(wide_total[:2, :width].reshape(2, 4, 400), group, 1, False)
    total_reduce = wide(quads_reduce.reshape(width, width))
    total_expand = finish_feed(quads_expand)
    total_in, total_out = finish_mixer(grad_total)
    return (
        outputs,
        input_grad,
        total_in,
        total_out,
        total_expand,
        total_reduce,
        pieces[0],
        pieces[1],
        pieces[2],
        vec_total[2400:4000],
        pieces[3],
        first_sums[0],
        first_sums[1],
        pieces[4],
        pieces[5],
    )


def solution(mesh):
    placed = (
        P("replica", "group", None),
        P("replica", "group"),
        P("replica", "group", None),
        P("group", None),
        P("group", None),
        P("group", None),
        P("group", None),
        P("group"),
        P("group"),
        P("group"),
        P("group"),
        P("group"),
        P("group"),
        P("group"),
        P("group"),
        P("group"),
    )
    return jax.shard_map(
        on_device if dict(mesh.shape) == {"replica": 8, "group": 4} else on_device_any,
        mesh=mesh,
        in_specs=placed,
        out_specs=(
            P("replica", "group", None),
            P("replica", "group", None),
            P("group", None),
            P("group", None),
            P("group", None),
            P("group", None),
            P("group"),
            P("group"),
            P("group"),
            P("group"),
            P("group"),
            P("group"),
            P("group"),
            P("group"),
            P("group"),
        ),
        check_vma=False,
    )
```

```python
import functools
import math

import jax
import jax.numpy as jnp
from jax import lax
from jax.sharding import PartitionSpec as P

from jax.experimental import pallas as pl
from jax.experimental.pallas import tpu as pltpu

HEADS = 25
HEAD_DIM = 64


epsilon = 1e-05
very_low = -1e30


def carried_in(part, axis, combine, identity):
    place = lax.axis_index(axis)
    gathered = lax.all_gather(part, axis)
    state = jnp.zeros_like(part) + jnp.asarray(identity, part.dtype)

    def one(hop, state):
        return combine(state, lax.dynamic_index_in_dim(gathered, hop, 0, False))

    return lax.fori_loop(0, place, one, state)


def layer_norm(entries, gain, shift):
    center = entries - jnp.mean(entries, axis=-1, keepdims=True)
    spread = jnp.mean(center * center, axis=-1, keepdims=True)
    return center * lax.rsqrt(spread + epsilon) * gain + shift


def product(left, right):
    return jnp.dot(left, right, preferred_element_type=jnp.float32)


def product_back(left, right):
    return lax.dot_general(
        left, right, (((1,), (1,)), ((), ())), preferred_element_type=jnp.float32
    )


def weight_term(left, right):
    return lax.dot_general(
        left, right, (((0,), (0,)), ((), ())), preferred_element_type=jnp.float32
    )


def column_sum(entries):
    return jnp.sum(entries.astype(jnp.float32), axis=0)


def block_scores(queries, key_block, offset, query_pos, doc_start):
    block_count = key_block.shape[0]
    key_count = key_block.shape[2]
    scaling = 1.0 / math.sqrt(HEAD_DIM)
    scores = (
        jnp.einsum("schd,pskhd->shcpk", queries, key_block, preferred_element_type=jnp.float32)
        * scaling
    )
    key_pos = (offset + jnp.arange(block_count, dtype=jnp.int32))[:, None] * key_count + jnp.arange(
        key_count, dtype=jnp.int32
    )[None, :]
    allowed = (key_pos[None, None] <= query_pos[None, :, None, None]) & (
        key_pos[None, None] >= doc_start[:, :, None, None]
    )
    allowed = allowed[:, None]
    return (jnp.where(allowed, scores, very_low), allowed)


def attend(running, key_block, value_block, offset, queries, query_pos, doc_start):
    largest, denominator, summed = running
    masked, allowed = block_scores(queries, key_block, offset, query_pos, doc_start)
    fresh = jnp.maximum(largest, jnp.max(masked, axis=(3, 4)))
    shares = jnp.where(allowed, jnp.exp(masked - fresh[..., None, None]), 0.0)
    rescale = jnp.exp(largest - fresh)
    denominator = denominator * rescale + jnp.sum(shares, axis=(3, 4))
    added = jnp.einsum(
        "shcpk,pskhd->schd",
        shares.astype(jnp.bfloat16),
        value_block,
        preferred_element_type=jnp.float32,
    )
    summed = summed * jnp.transpose(rescale, (0, 2, 1))[..., None] + added
    return (fresh, denominator, summed)


def attend_back(
    grad_query,
    key_block,
    value_block,
    offset,
    queries,
    query_pos,
    doc_start,
    log_total,
    grad_low,
    row_dot,
):
    masked, allowed = block_scores(queries, key_block, offset, query_pos, doc_start)
    shares = jnp.where(allowed, jnp.exp(masked - log_total[..., None, None]), 0.0)
    grad_value = jnp.einsum(
        "shcpk,schd->pskhd",
        shares.astype(jnp.bfloat16),
        grad_low,
        preferred_element_type=jnp.float32,
    )
    grad_share = jnp.einsum(
        "schd,pskhd->shcpk", grad_low, value_block, preferred_element_type=jnp.float32
    )
    grad_score = (shares * (grad_share - row_dot[..., None, None])).astype(jnp.bfloat16)
    grad_query = grad_query + jnp.einsum(
        "shcpk,pskhd->schd", grad_score, key_block, preferred_element_type=jnp.float32
    )
    grad_key = jnp.einsum(
        "shcpk,schd->pskhd", grad_score, queries, preferred_element_type=jnp.float32
    )
    return (grad_query, (grad_key, grad_value))


def on_device_any(
    inputs,
    segments,
    cotangent,
    project_in,
    project_out,
    expand_weight,
    reduce_weight,
    query_bias,
    value_bias,
    project_bias,
    expand_bias,
    reduce_bias,
    first_gain,
    first_shift,
    second_gain,
    second_shift,
):
    seq_here, local_len, width = inputs.shape
    groups = lax.axis_size("group")
    total_rows = seq_here * local_len
    head_shape = (seq_here, local_len, HEADS, HEAD_DIM)
    shards = (
        project_in,
        project_out,
        expand_weight,
        reduce_weight,
        query_bias,
        value_bias,
        project_bias,
        expand_bias,
        reduce_bias,
        first_gain,
        first_shift,
        second_gain,
        second_shift,
    )
    whole = (
        lax.all_gather(shards[0], "group", axis=0, tiled=True),
        lax.all_gather(shards[1], "group", axis=0, tiled=True),
        lax.all_gather(shards[2], "group", axis=0, tiled=True),
        lax.all_gather(shards[3], "group", axis=0, tiled=True),
        lax.all_gather(shards[4], "group", axis=0, tiled=True),
        lax.all_gather(shards[5], "group", axis=0, tiled=True),
        lax.all_gather(shards[6], "group", axis=0, tiled=True),
        lax.all_gather(shards[7], "group", axis=0, tiled=True),
        lax.all_gather(shards[8], "group", axis=0, tiled=True),
        lax.all_gather(shards[9], "group", axis=0, tiled=True),
        lax.all_gather(shards[10], "group", axis=0, tiled=True),
        lax.all_gather(shards[11], "group", axis=0, tiled=True),
        lax.all_gather(shards[12], "group", axis=0, tiled=True),
    )
    (
        full_in,
        full_out,
        full_expand,
        full_reduce,
        bias_query,
        bias_value,
        bias_project,
        bias_expand,
        bias_reduce,
        gain_first,
        shift_first,
        gain_second,
        shift_second,
    ) = whole
    group_rank = lax.axis_index("group")
    query_pos = group_rank * local_len + jnp.arange(local_len, dtype=jnp.int32)
    positions = jnp.broadcast_to(query_pos[None, :], (seq_here, local_len))
    end_marks = jnp.where(segments == positions, positions + 1, 0)
    before = carried_in(
        jnp.max(end_marks, axis=1), "group", jnp.maximum, jnp.zeros((seq_here,), jnp.int32)
    )
    inside = lax.cummax(end_marks, axis=1)
    inside = jnp.concatenate([jnp.zeros((seq_here, 1), jnp.int32), inside[:, :-1]], axis=1)
    doc_start = jnp.maximum(before[:, None], inside)
    flat_input = inputs.reshape(total_rows, width).astype(jnp.float32)
    normed_low = layer_norm(
        flat_input, gain_first.astype(jnp.float32), shift_first.astype(jnp.float32)
    ).astype(jnp.bfloat16)
    mixture = product(normed_low, full_in)
    queries = (
        (mixture[:, :width] + bias_query.astype(jnp.float32))
        .astype(jnp.bfloat16)
        .reshape(head_shape)
    )
    key_rows = (
        mixture[:, width : 2 * width].astype(jnp.bfloat16).reshape(seq_here, local_len, width)
    )
    value_rows = (
        (mixture[:, 2 * width :] + bias_value.astype(jnp.float32))
        .astype(jnp.bfloat16)
        .reshape(seq_here, local_len, width)
    )
    initial = (
        jnp.full((seq_here, HEADS, local_len), very_low, jnp.float32),
        jnp.zeros((seq_here, HEADS, local_len), jnp.float32),
        jnp.zeros(head_shape, jnp.float32),
    )
    block_ids = jnp.arange(groups, dtype=jnp.int32)
    running = initial
    pieces = (
        lax.all_gather(key_rows[None], "group", axis=0, tiled=True),
        lax.all_gather(value_rows[None], "group", axis=0, tiled=True),
    )
    piece_count = pieces[0].shape[0]

    def one_piece(state, members):
        key_piece, value_piece, index = members
        updated = attend(
            state,
            key_piece.reshape((1,) + head_shape),
            value_piece.reshape((1,) + head_shape),
            index,
            queries,
            query_pos,
            doc_start,
        )
        return (updated, None)

    running, unused_steps = lax.scan(
        one_piece, running, (pieces[0], pieces[1], jnp.arange(piece_count, dtype=jnp.int32))
    )
    largest, denominator, summed = running
    attended = summed / jnp.transpose(denominator, (0, 2, 1))[..., None]
    log_total = largest + jnp.log(denominator)
    attended_low = attended.reshape(total_rows, width).astype(jnp.bfloat16)
    middle = flat_input + product(attended_low, full_out) + bias_project.astype(jnp.float32)
    second_low = layer_norm(
        middle, gain_second.astype(jnp.float32), shift_second.astype(jnp.float32)
    ).astype(jnp.bfloat16)
    expanded = product(second_low, full_expand) + bias_expand.astype(jnp.float32)
    activated_low = jax.nn.gelu(expanded, approximate=True).astype(jnp.bfloat16)
    result = middle + product(activated_low, full_reduce) + bias_reduce.astype(jnp.float32)
    outputs = result.astype(jnp.bfloat16).reshape(seq_here, local_len, width)
    whole_back = (
        lax.all_gather(shards[0], "group", axis=0, tiled=True),
        lax.all_gather(shards[1], "group", axis=0, tiled=True),
        lax.all_gather(shards[2], "group", axis=0, tiled=True),
        lax.all_gather(shards[3], "group", axis=0, tiled=True),
        lax.all_gather(shards[4], "group", axis=0, tiled=True),
        lax.all_gather(shards[5], "group", axis=0, tiled=True),
        lax.all_gather(shards[6], "group", axis=0, tiled=True),
        lax.all_gather(shards[7], "group", axis=0, tiled=True),
        lax.all_gather(shards[8], "group", axis=0, tiled=True),
        lax.all_gather(shards[9], "group", axis=0, tiled=True),
        lax.all_gather(shards[10], "group", axis=0, tiled=True),
        lax.all_gather(shards[11], "group", axis=0, tiled=True),
        lax.all_gather(shards[12], "group", axis=0, tiled=True),
    )
    keys_back = (
        lax.all_gather(key_rows[None], "group", axis=0, tiled=True),
        lax.all_gather(value_rows[None], "group", axis=0, tiled=True),
    )
    (
        back_in,
        back_out,
        back_expand,
        back_reduce,
        unused_query,
        unused_value,
        unused_project,
        unused_expand,
        unused_reduce,
        back_gain_first,
        back_shift_first,
        back_gain_second,
        back_shift_second,
    ) = whole_back
    grad_rows = cotangent.reshape(total_rows, width).astype(jnp.float32)
    grad_result_low = cotangent.reshape(total_rows, width)
    reduce_bias_grad = column_sum(grad_result_low)
    grad_activated = product_back(grad_result_low, back_reduce)
    unused_gelu, gelu_back = jax.vjp(lambda entry: jax.nn.gelu(entry, approximate=True), expanded)
    grad_expanded_low = gelu_back(grad_activated)[0].astype(jnp.bfloat16)
    expand_bias_grad = column_sum(grad_expanded_low)
    grad_second = product_back(grad_expanded_low, back_expand)
    unused_second, second_back = jax.vjp(
        layer_norm,
        middle,
        back_gain_second.astype(jnp.float32),
        back_shift_second.astype(jnp.float32),
    )
    grad_middle, second_gain_grad, second_shift_grad = second_back(grad_second)
    grad_middle = grad_middle + grad_rows
    reduce_weight_grad = weight_term(activated_low, grad_result_low)
    expand_weight_grad = weight_term(second_low, grad_expanded_low)
    feed_parts = (
        lax.psum_scatter(
            expand_weight_grad.astype(jnp.bfloat16), "group", scatter_dimension=0, tiled=True
        ).astype(jnp.float32),
        lax.psum_scatter(
            reduce_weight_grad.astype(jnp.bfloat16), "group", scatter_dimension=0, tiled=True
        ).astype(jnp.float32),
        lax.psum_scatter(
            expand_bias_grad.astype(jnp.bfloat16), "group", scatter_dimension=0, tiled=True
        ).astype(jnp.float32),
        lax.psum_scatter(
            reduce_bias_grad.astype(jnp.bfloat16), "group", scatter_dimension=0, tiled=True
        ).astype(jnp.float32),
        lax.psum_scatter(
            second_gain_grad.astype(jnp.bfloat16), "group", scatter_dimension=0, tiled=True
        ).astype(jnp.float32),
        lax.psum_scatter(
            second_shift_grad.astype(jnp.bfloat16), "group", scatter_dimension=0, tiled=True
        ).astype(jnp.float32),
    )
    grad_middle_low = grad_middle.astype(jnp.bfloat16)
    project_bias_grad = column_sum(grad_middle_low)
    grad_attended_low = (
        product_back(grad_middle_low, back_out).astype(jnp.bfloat16).reshape(head_shape)
    )
    row_dot = jnp.einsum("schd,schd->shc", grad_attended_low.astype(jnp.float32), attended)

    def back_step(grad_query, members):
        key_piece, value_piece, offset = members
        return attend_back(
            grad_query,
            key_piece.reshape((1,) + head_shape),
            value_piece.reshape((1,) + head_shape),
            offset,
            queries,
            query_pos,
            doc_start,
            log_total,
            grad_attended_low,
            row_dot,
        )

    grad_query, terms = lax.scan(
        back_step, jnp.zeros(head_shape, jnp.float32), (keys_back[0], keys_back[1], block_ids)
    )
    key_terms = terms[0].reshape(groups, seq_here, local_len, width)
    value_terms = terms[1].reshape(groups, seq_here, local_len, width)
    key_grad, value_grad = (
        lax.psum_scatter(
            key_terms.astype(jnp.bfloat16), "group", scatter_dimension=0, tiled=True
        ).astype(jnp.float32),
        lax.psum_scatter(
            value_terms.astype(jnp.bfloat16), "group", scatter_dimension=0, tiled=True
        ).astype(jnp.float32),
    )
    scaling = 1.0 / math.sqrt(HEAD_DIM)
    grad_query_low = (grad_query * scaling).reshape(total_rows, width).astype(jnp.bfloat16)
    grad_key_low = (key_grad * scaling).reshape(total_rows, width).astype(jnp.bfloat16)
    grad_value_low = value_grad.reshape(total_rows, width).astype(jnp.bfloat16)
    query_bias_grad = column_sum(grad_query_low)
    value_bias_grad = column_sum(grad_value_low)
    grad_mixture_low = jnp.concatenate([grad_query_low, grad_key_low, grad_value_low], axis=1)
    grad_normed = product_back(grad_mixture_low, back_in)
    unused_first, first_back = jax.vjp(
        layer_norm,
        flat_input,
        back_gain_first.astype(jnp.float32),
        back_shift_first.astype(jnp.float32),
    )
    grad_entry, first_gain_grad, first_shift_grad = first_back(grad_normed)
    input_grad = (grad_entry + grad_middle).reshape(seq_here, local_len, width)
    project_weight_grad = weight_term(attended_low, grad_middle_low)
    in_weight_grad = weight_term(normed_low, grad_mixture_low)
    mixer_parts = (
        lax.psum_scatter(
            in_weight_grad.astype(jnp.bfloat16), "group", scatter_dimension=0, tiled=True
        ).astype(jnp.float32),
        lax.psum_scatter(
            project_weight_grad.astype(jnp.bfloat16), "group", scatter_dimension=0, tiled=True
        ).astype(jnp.float32),
        lax.psum_scatter(
            query_bias_grad.astype(jnp.bfloat16), "group", scatter_dimension=0, tiled=True
        ).astype(jnp.float32),
        lax.psum_scatter(
            value_bias_grad.astype(jnp.bfloat16), "group", scatter_dimension=0, tiled=True
        ).astype(jnp.float32),
        lax.psum_scatter(
            project_bias_grad.astype(jnp.bfloat16), "group", scatter_dimension=0, tiled=True
        ).astype(jnp.float32),
        lax.psum_scatter(
            first_gain_grad.astype(jnp.bfloat16), "group", scatter_dimension=0, tiled=True
        ).astype(jnp.float32),
        lax.psum_scatter(
            first_shift_grad.astype(jnp.bfloat16), "group", scatter_dimension=0, tiled=True
        ).astype(jnp.float32),
    )
    share_in, share_out, share_expand, share_reduce = (
        mixer_parts[0],
        mixer_parts[1],
        feed_parts[0],
        feed_parts[1],
    )
    share_query, share_value, share_project = (mixer_parts[2], mixer_parts[3], mixer_parts[4])
    share_expand_bias, share_reduce_bias = (feed_parts[2], feed_parts[3])
    share_first_gain, share_first_shift = (mixer_parts[5], mixer_parts[6])
    share_second_gain, share_second_shift = (feed_parts[4], feed_parts[5])
    totals = (
        lax.psum(share_in.astype(jnp.bfloat16), "replica").astype(jnp.float32),
        lax.psum(share_out.astype(jnp.bfloat16), "replica").astype(jnp.float32),
        lax.psum(share_expand.astype(jnp.bfloat16), "replica").astype(jnp.float32),
        lax.psum(share_reduce.astype(jnp.bfloat16), "replica").astype(jnp.float32),
        lax.psum(share_query.astype(jnp.bfloat16), "replica").astype(jnp.float32),
        lax.psum(share_value.astype(jnp.bfloat16), "replica").astype(jnp.float32),
        lax.psum(share_project.astype(jnp.bfloat16), "replica").astype(jnp.float32),
        lax.psum(share_expand_bias.astype(jnp.bfloat16), "replica").astype(jnp.float32),
        lax.psum(share_reduce_bias.astype(jnp.bfloat16), "replica").astype(jnp.float32),
        lax.psum(share_first_gain.astype(jnp.bfloat16), "replica").astype(jnp.float32),
        lax.psum(share_first_shift.astype(jnp.bfloat16), "replica").astype(jnp.float32),
        lax.psum(share_second_gain.astype(jnp.bfloat16), "replica").astype(jnp.float32),
        lax.psum(share_second_shift.astype(jnp.bfloat16), "replica").astype(jnp.float32),
    )
    return (
        outputs,
        input_grad,
        totals[0],
        totals[1],
        totals[2],
        totals[3],
        totals[4],
        totals[5],
        totals[6],
        totals[7],
        totals[8],
        totals[9],
        totals[10],
        totals[11],
        totals[12],
    )


MESH = pl.DeviceIdType.MESH


def flipped(z=0, core=0, y=0, x=0):
    pairs = []
    for me in range(32):
        pairs.append((me, me ^ (8 * z + 4 * core + 2 * y + x)))
    return pairs


FLIP_X = flipped(x=1)
FLIP_Y = flipped(y=1)
FLIP_CORE = flipped(core=1)
FLIP_Z = flipped(z=1)
FLIP_PAIR = flipped(z=2)
INWARD = [(me, me + 8) for me in range(8)] + [(me, me - 8) for me in range(24, 32)]
MIDDLE = [(me, me + 8) for me in range(8, 16)] + [(me, me - 8) for me in range(16, 24)]
OUTWARD = [(me, me - 8) for me in range(8, 16)] + [(me, me + 8) for me in range(16, 24)]


def moved(entries, pairs):
    return lax.ppermute(entries, ("replica", "group"), pairs)


def low(entries):
    return entries.astype(jnp.bfloat16)


def wide(entries):
    return entries.astype(jnp.float32)


def at(entries, index):
    return lax.dynamic_index_in_dim(entries, index, 0, False)


def place():
    replica = lax.axis_index("replica")
    group = lax.axis_index("group")
    core = lax.rem(replica, 2)
    z = lax.div(replica, 2)
    return replica, group, z, core, lax.div(group, 2), lax.rem(group, 2)


def partners(replica, group):
    core = lax.rem(replica, 2)
    z = lax.rem(lax.div(replica, 2), 2)
    y = lax.div(group, 2)
    x = lax.rem(group, 2)
    by_x = (replica, group + 1 - 2 * x)
    by_y = (replica, group + 2 - 4 * y)
    by_both = (replica, group + 3 - 4 * y - 2 * x)
    by_core = (replica + 1 - 2 * core, group)
    by_z = (replica + 2 - 4 * z, group)
    return by_x, by_y, by_both, by_core, by_z


def greet(devices):
    barrier = pltpu.get_barrier_semaphore()
    for device in devices:
        pl.semaphore_signal(barrier, inc=1, device_id=device, device_id_type=MESH)
    pl.semaphore_wait(barrier, len(devices))


def first_exchange_kernel(inp_turned, weights, vec, seg, expand, cot_turned, x_seq, w_full, vecs, segs, inp_out, cot_out, quarter, wide_raw, inp_raw, cot_raw, inp, cot, raw, halves, vec_stage, seg_stage, send, recv, local):
    replica = lax.axis_index("replica")
    group = lax.axis_index("group")
    core = lax.rem(replica, 2)
    level = lax.rem(lax.div(replica, 2), 2)
    y = lax.div(group, 2)
    x = lax.rem(group, 2)
    by_x, by_y, by_both, by_core, by_z = partners(replica, group)
    slot_x, slot_y, slot_both = by_x[1], by_y[1], by_both[1]
    other_x = 1 - x
    other_y = 1 - y
    wires = Wires(send, recv, local)
    load_raw = wires.here(weights, raw)
    load_inp = wires.here(inp_turned, inp_raw)
    load_wide = wires.here(expand, wide_raw)
    load_cot = wires.here(cot_turned, cot_raw)
    greet((by_x, by_y, by_both, by_core, by_z))
    small = [wires.go(vec, vecs.at[group], device) for device in (by_x, by_y, by_both)]
    small += [wires.go(seg.at[pick], segs.at[group], device) for pick, device in ((other_x, by_x), (x, by_y), (other_x, by_both))]
    loads = [wires.here(here, there) for here, there in ((vec, vec_stage), (seg.at[x], seg_stage))]
    load_raw.wait()
    for half in range(2):
        for k in range(3):
            first = 1600 * k + 768 * half
            halves[half, :, 896 * k : 896 * k + 832] = raw[:, first : first + 832]
            halves[half, :, 896 * k + 832 : 896 * k + 896] = jnp.zeros((halves.shape[1], 64), halves.dtype)

    part = 2 * level + core
    mine = rows16(96 * part, 112)
    to_core = rows16(96 * part + 16 * core, 96)
    to_z = rows16(96 * part + 16 * level, 96)
    passed = rows16(96 * (part + 2 - 4 * level) + 16 * (1 - level), 96)
    w_x = wires.go(halves.at[y, mine], w_full.at[group, mine], by_x)
    w_y = wires.go(halves.at[other_y, mine], w_full.at[group, mine], by_y)
    wires.keep(halves.at[y], w_full.at[group])
    load_inp.wait()
    for seq in range(2):
        inp[seq] = inp_raw[seq].T
    wires.keep(inp, inp_out)
    wires.keep(inp.at[x], x_seq.at[group])
    for load, here, there in zip(loads, (vec_stage, seg_stage), (vecs, segs)):
        load.wait()
        wires.keep(here, there.at[group])
    shares = []
    over_z = []

    def share(slot):
        shares.append(wires.go(w_full.at[slot, to_core], w_full.at[slot, to_core], by_core))
        over_z.append((slot, wires.go(w_full.at[slot, to_z], w_full.at[slot, to_z], by_z)))

    wires.drain([w_x, w_y])
    x_block = wires.go(inp.at[other_x], x_seq.at[group], by_x)
    y_block = wires.go(inp.at[x], x_seq.at[group], by_y)
    w_y.wait_recv()
    share(slot_y)
    w_x.wait_recv()
    share(slot_x)
    load_wide.wait()
    quad = lax.rem(replica, 4)
    for pick in range(4):

        @pl.when(quad == pick)
        def _():
            for k in range(4):
                first = 1600 * k + 400 * pick
                quarter[:, 400 * k : 400 * k + 400] = wide_raw[:, first : first + 400]

    load_cot.wait()
    for seq in range(2):
        cot[seq] = cot_raw[seq].T
    wires.keep(cot, cot_out)
    wires.drain([x_block])
    w_more = wires.go(w_full.at[slot_y, mine], w_full.at[slot_y, mine], by_x)
    x_block.wait_recv()
    y_more = wires.go(x_seq.at[slot_x], x_seq.at[slot_x], by_y)
    w_more.wait_recv()
    share(slot_both)
    for slot, copy in over_z:
        copy.wait_recv()
        shares.append(wires.go(w_full.at[slot, passed], w_full.at[slot, passed], by_core))
    for copy in small + shares + [y_block, y_more]:
        copy.wait_recv()
    wires.finish()


def first_exchange(inp, weights, vec, seg, expand, cot):
    any_space = pl.BlockSpec(memory_space=pl.ANY)
    shape = jax.ShapeDtypeStruct
    rows = weights.shape[0]
    turned = inp.shape[:0:-1]
    return pl.pallas_call(
        first_exchange_kernel,
        in_specs=[any_space] * 6,
        out_specs=[any_space] * 6 + [pl.BlockSpec(memory_space=pltpu.VMEM)],
        out_shape=[
            shape((4,) + turned, inp.dtype),
            shape((4, rows, 2688), weights.dtype),
            shape((4,) + vec.shape, vec.dtype),
            shape((4,) + seg.shape[1:], seg.dtype),
            shape((2,) + turned, inp.dtype),
            shape((2,) + turned, cot.dtype),
            shape((rows, 1600), expand.dtype),
        ],
        scratch_shapes=[
            pltpu.VMEM(expand.shape, expand.dtype),
            pltpu.VMEM(inp.shape, inp.dtype),
            pltpu.VMEM(cot.shape, cot.dtype),
            pltpu.VMEM((2,) + turned, inp.dtype),
            pltpu.VMEM((2,) + turned, cot.dtype),
            pltpu.VMEM(weights.shape, weights.dtype),
            pltpu.VMEM((2, rows, 2688), weights.dtype),
            pltpu.VMEM(vec.shape, vec.dtype),
            pltpu.VMEM(seg.shape[1:], seg.dtype),
            pltpu.SemaphoreType.DMA((24,)),
            pltpu.SemaphoreType.DMA((24,)),
            pltpu.SemaphoreType.DMA((16,)),
        ],
        compiler_params=pltpu.CompilerParams(collective_id=0, has_side_effects=True, vmem_limit_bytes=63 * 2**20),
        name="first_exchange",
    )(inp, weights, vec, seg, expand, cot)


def turn_middle_kernel(src, out_in, inp_in, rows_ref, att_out, middle_out, second_out, att, w, inp, send, recv, local):
    replica = lax.axis_index("replica")
    group = lax.axis_index("group")
    y = lax.div(group, 2)
    x = lax.rem(group, 2)
    by_x, by_y, by_both, by_core, by_z = partners(replica, group)
    others = (by_both, by_x, by_y)
    wires = Wires(send, recv, local)
    greet(others)
    copies = [wires.go(src.at[device[1]], att.at[x, y], device) for device in others]
    own = wires.here(src.at[group], att.at[x, y])
    load_w = wires.here(out_in, w)
    load_inp = wires.here(inp_in, inp)
    width = w.shape[0]
    lane = lax.broadcasted_iota(jnp.int32, (1, 128), 1)
    for copy in (own, load_w, load_inp):
        copy.wait()
    for copy in copies:
        copy.wait_recv()
    for seq in range(2):
        rows = pl.ds(256 * seq, 256)
        att_out[rows, 0:768] = att[seq, 0, :, 0:768]
        att_out[rows, 768:896] = jnp.where(lane < 64, att[seq, 0, :, 768:896], att[seq, 1, :, 0:128])
        att_out[rows, 896:width] = att[seq, 1, :, 128 : width - 768]
        middle = inp[seq].astype(jnp.float32) + dot_nn(att_out[rows, :], w[...]) + rows_ref[2:3, :width]
        middle_out[rows, :] = middle
        center = middle - jnp.mean(middle, axis=-1, keepdims=True)
        spread = jnp.mean(center * center, axis=-1, keepdims=True)
        second = center * lax.rsqrt(spread + epsilon) * rows_ref[6:7, :width] + rows_ref[7:8, :width]
        second_out[rows, :width] = second.astype(jnp.bfloat16)
        second_out[rows, width:] = jnp.zeros((256, second_out.shape[1] - width), jnp.bfloat16)
    wires.finish()


def turn_middle(entries, full_out, inputs, rows):
    any_space = pl.BlockSpec(memory_space=pl.ANY)
    vmem = pl.BlockSpec(memory_space=pltpu.VMEM)
    shape = jax.ShapeDtypeStruct
    width = full_out.shape[0]
    return pl.pallas_call(
        turn_middle_kernel,
        in_specs=[any_space, any_space, any_space, vmem],
        out_specs=[vmem, vmem, vmem],
        out_shape=[shape((512, width), jnp.bfloat16), shape((512, width), jnp.float32), shape((512, width + 64), jnp.bfloat16)],
        scratch_shapes=[
            pltpu.VMEM((2, 2) + entries.shape[1:], jnp.bfloat16),
            pltpu.VMEM(full_out.shape, jnp.bfloat16),
            pltpu.VMEM(inputs.shape, jnp.bfloat16),
            pltpu.SemaphoreType.DMA((3,)),
            pltpu.SemaphoreType.DMA((3,)),
            pltpu.SemaphoreType.DMA((3,)),
        ],
        compiler_params=pltpu.CompilerParams(collective_id=1, has_side_effects=True, vmem_limit_bytes=63 * 2**20),
        cost_estimate=pl.CostEstimate(flops=0, bytes_accessed=60 * 2**20, transcendentals=0),
        name="turn_middle",
    )(entries, full_out, inputs, rows)


def padded(entries):
    return jnp.pad(entries, [(0, 0)] * (entries.ndim - 1) + [(0, 64)])


def joined(first, other):
    lane = lax.broadcasted_iota(jnp.int32, (1, 128), 1)
    middle = jnp.where(lane < 64, first[..., 768:896], other[..., 0:128])
    return jnp.concatenate([first[..., :768], middle, other[..., 128:]], axis=-1)


def hold(entries, *until):
    return lax.optimization_barrier((entries,) + until)[0]


def finish_kernel(expand_ref, total_ref, out_expand, in_ref, out_ref):
    for k in range(4):
        piece = expand_ref[k].astype(jnp.float32)
        for r in range(4):
            out_expand[:, 1600 * r + 400 * k : 1600 * r + 400 * k + 400] = piece[:, 400 * r : 400 * r + 400]
    for k in range(3):
        in_ref[:, 1600 * k : 1600 * k + 1600] = total_ref[k, :, :1600].astype(jnp.float32)
    out_ref[...] = total_ref[3, :, :1600].astype(jnp.float32)


def finish(quads, total):
    rows, width = quads.shape[1:]
    step = 80
    shape = lambda columns: jax.ShapeDtypeStruct((rows, columns), jnp.float32)
    spec = lambda columns: pl.BlockSpec((step, columns), lambda i: (i, 0))
    return pl.pallas_call(
        finish_kernel,
        grid=(rows // step,),
        in_specs=[pl.BlockSpec((4, step, width), lambda i: (0, i, 0)), pl.BlockSpec((4, step, total.shape[2]), lambda i: (0, i, 0))],
        out_specs=[spec(4 * width), spec(4800), spec(1600)],
        out_shape=[shape(4 * width), shape(4800), shape(1600)],
        compiler_params=pltpu.CompilerParams(vmem_limit_bytes=63 * 2**20),
        name="finish",
    )(quads, total)


PIECES = ((0, 512), (512, 1024), (1024, 1600))
HALF = 208


class Wires:
    def __init__(self, send, recv, local):
        self.send, self.recv, self.local = send, recv, local
        self.remotes = self.locals = 0
        self.sent = []
        self.kept = []

    def make(self, src, dst, device):
        i = self.remotes
        assert i < self.send.shape[0]
        self.remotes = i + 1
        return pltpu.make_async_remote_copy(src_ref=src, dst_ref=dst, send_sem=self.send.at[i], recv_sem=self.recv.at[i], device_id=device, device_id_type=MESH)

    def go(self, src, dst, device):
        copy = self.make(src, dst, device)
        copy.start()
        self.sent.append(copy)
        return copy

    def here(self, src, dst):
        i = self.locals
        assert i < self.local.shape[0]
        self.locals = i + 1
        copy = pltpu.make_async_copy(src, dst, self.local.at[i])
        copy.start()
        return copy

    def keep(self, src, dst):
        self.kept.append(self.here(src, dst))

    def drain(self, copies):
        for copy in copies:
            copy.wait_send()
        self.sent = [copy for copy in self.sent if all(copy is not done for done in copies)]

    def finish(self):
        for copy in self.sent:
            copy.wait_send()
        for copy in self.kept:
            copy.wait()


def rows16(start, size):
    return pl.ds(pl.multiple_of(start, 16), size)


def dot_tn(a, b):
    return lax.dot_general(a, b, (((0,), (0,)), ((), ())), preferred_element_type=jnp.float32)


def add_low(a, b):
    return (a.astype(jnp.float32) + b.astype(jnp.float32)).astype(jnp.bfloat16)


def weight_sum(a, b, out):
    width = out.shape[0]
    whole = width // 256

    def chunk(j, carry):
        lanes = pl.ds(pl.multiple_of(256 * j, 256), 256)
        out[lanes, :] = dot_tn(a[:, lanes], b[:, : out.shape[1]]).astype(jnp.bfloat16)
        return carry

    lax.fori_loop(0, whole, chunk, 0)
    if width > 256 * whole:
        out[256 * whole :, :] = dot_tn(a[:, 256 * whole : width], b[:, : out.shape[1]]).astype(jnp.bfloat16)


NT = (((1,), (1,)), ((), ()))

def dot_nt(a, b):
    return lax.dot_general(a, b, NT, preferred_element_type=jnp.float32)

def dot_nn(a, b):
    return jnp.dot(a, b, preferred_element_type=jnp.float32)

BLOCK = 256

def mix_heads_kernel(x_seq, w_in, rows_ref, segc_ref, segr_ref, out_shard, expand_shard, cot, mix, normed, unit_out, o_ref, lse_ref, full_out, full_expand, cots, x_buf, w, stage_out, stage_expand, ot_ref, vt_ref, send, recv, local):
    replica = lax.axis_index("replica")
    group = lax.axis_index("group")
    core = lax.rem(replica, 2)
    y = lax.div(group, 2)
    x = lax.rem(group, 2)
    by_x, by_y, by_both, by_core, by_z = partners(replica, group)
    slot_x, slot_y, slot_both = by_x[1], by_y[1], by_both[1]
    wires = Wires(send, recv, local)
    greet([by_x, by_y, by_core, by_z])
    level = lax.rem(lax.div(replica, 2), 2)
    part = 2 * level + core
    mine = rows16(96 * part, 112)
    to_core = rows16(96 * part + 16 * core, 96)
    to_z = rows16(96 * part + 16 * level, 96)
    passed = rows16(96 * (part + 2 - 4 * level) + 16 * (1 - level), 96)
    out_x = wires.go(out_shard.at[mine], full_out.at[group, mine], by_x)
    out_y = wires.go(out_shard.at[mine], full_out.at[group, mine], by_y)
    expand_x = wires.go(expand_shard, full_expand.at[group], by_x)
    expand_y = wires.go(expand_shard, full_expand.at[group], by_y)
    cot_core = wires.go(cot, cots.at[0], by_core)
    cot_z = wires.go(cot, cots.at[1], by_z)
    load_x = wires.here(x_seq, x_buf)
    load_w = wires.here(w_in, w)
    load_out = wires.here(out_shard, stage_out)
    load_expand = wires.here(expand_shard, stage_expand)
    length = mix.shape[0]
    blocks = length // BLOCK
    lane = lax.broadcasted_iota(jnp.int32, (1, 128), 1)
    lse_ref[...] = jnp.zeros_like(lse_ref)
    half_lanes = pl.ds(pl.multiple_of(768 * y, 128), 896)
    load_x.wait()
    load_w.wait()

    def mix_rows(i, carry):
        rows = pl.ds(pl.multiple_of(256 * i, 256), 256)
        width = x_buf.shape[1]
        entries = x_buf[rows, :].astype(jnp.float32)
        center = entries - jnp.mean(entries, axis=-1, keepdims=True)
        spread = jnp.mean(center * center, axis=-1, keepdims=True)
        unit = center * lax.rsqrt(spread + epsilon)
        unit_out[rows, :] = unit.astype(jnp.bfloat16)
        low_rows = (unit * rows_ref[4:5, :width] + rows_ref[5:6, :width]).astype(jnp.bfloat16)
        normed[rows, :] = low_rows
        mix[rows, 0:896] = (dot_nn(low_rows, w[:, 0:896]) + rows_ref[0:1, half_lanes]).astype(jnp.bfloat16)
        mix[rows, 896:1792] = dot_nn(low_rows, w[:, 896:1792]).astype(jnp.bfloat16)
        mix[rows, 1792:2688] = (dot_nn(low_rows, w[:, 1792:2688]) + rows_ref[1:2, half_lanes]).astype(jnp.bfloat16)
        return carry

    lax.fori_loop(0, 4, mix_rows, 0)
    load_out.wait()
    wires.keep(stage_out, full_out.at[group])
    load_expand.wait()
    wires.keep(stage_expand, full_expand.at[group])
    upper = rows16(96 * part, 64)
    lower = rows16(96 * part + 64, 48)
    top = pl.ds(0, HALF)
    bottom = pl.ds(HALF, 400 - HALF)
    spot = lambda slot, rows: full_out.at[slot, rows]
    more = [wires.make(spot(slot_x, upper), spot(slot_x, upper), by_y), wires.make(spot(slot_y, lower), spot(slot_y, lower), by_x)]
    slots = (slot_x, slot_y, slot_both)
    cores = [wires.make(spot(slot, to_core), spot(slot, to_core), by_core) for slot in slots]
    overs = [wires.make(spot(slot, to_z), spot(slot, to_z), by_z) for slot in slots]
    passes = [wires.make(spot(slot, passed), spot(slot, passed), by_core) for slot in slots]
    expand_more = [wires.make(full_expand.at[slot_x, top], full_expand.at[slot_x, top], by_y), wires.make(full_expand.at[slot_y, bottom], full_expand.at[slot_y, bottom], by_x)]
    cot_both = wires.make(cots.at[1], cots.at[2], by_core)

    def tile_heads(tile, carry):
        at_lanes = lambda off: pl.ds(pl.multiple_of(128 * tile + off, 128), 128)
        ot_ref[...] = jnp.zeros_like(ot_ref)
        vt_ref[...] = mix[:, at_lanes(1792)].T

        def head(h):
            k = jnp.where((lane >= 64 * h) & (lane < 64 * h + 64), mix[:, at_lanes(896)], jnp.bfloat16(0))
            for i in range(blocks):
                low_at, high_at = i * BLOCK, (i + 1) * BLOCK
                q = mix[low_at:high_at, at_lanes(0)] * jnp.bfloat16(0.125)
                s = dot_nt(k[:high_at], q)
                same = segc_ref[:high_at, :] == segr_ref[:, low_at:high_at]
                kpos = lax.broadcasted_iota(jnp.int32, (high_at, BLOCK), 0)
                qpos = lax.broadcasted_iota(jnp.int32, (high_at, BLOCK), 1) + low_at
                s = jnp.where(same & (kpos <= qpos), s, -1e30)
                m = jnp.max(s, axis=0, keepdims=True)
                p = jnp.exp(s - m)
                l = jnp.sum(p, axis=0, keepdims=True)
                ot = dot_nn(vt_ref[64 * h : 64 * h + 64, :high_at], p.astype(jnp.bfloat16))
                ot_ref[64 * h : 64 * h + 64, low_at:high_at] = ot / l
                lse_ref[tile, h : h + 1, low_at:high_at] = m + jnp.log(l)

        head(0)

        @pl.when(tile < 6)
        def _():
            head(1)

        @pl.when(tile == 2)
        def _():
            out_x.wait_recv()
            out_y.wait_recv()
            for copy in more + cores[:2] + overs[:2]:
                copy.start()

        @pl.when(tile == 4)
        def _():
            expand_x.wait_recv()
            expand_y.wait_recv()
            for copy in expand_more:
                copy.start()
            for copy in more:
                copy.wait_recv()
            cores[2].start()
            overs[2].start()

        o_ref[:, at_lanes(0)] = ot_ref[...].T.astype(jnp.bfloat16)
        return carry

    lax.fori_loop(0, 7, tile_heads, 0)
    cot_z.wait_recv()
    cot_both.start()
    for i in range(3):
        overs[i].wait_recv()
        passes[i].start()
    for copy in expand_more + cores + passes + [cot_core, cot_both]:
        copy.wait_recv()
    for copy in more + cores + overs + passes + expand_more + [cot_both]:
        copy.wait_send()
    wires.finish()


def mix_heads(x_seq, w_in, rows, segc, segr, out_shard, expand_shard, cot):
    any_space = pl.BlockSpec(memory_space=pl.ANY)
    vmem = pl.BlockSpec(memory_space=pltpu.VMEM)
    shape = jax.ShapeDtypeStruct
    kind = jnp.bfloat16
    length = x_seq.shape[0]
    buf = lambda *dims: pltpu.VMEM(dims, kind)
    return pl.pallas_call(
        mix_heads_kernel,
        in_specs=[any_space, any_space, vmem, vmem, vmem, any_space, any_space, any_space],
        out_specs=[vmem] * 5 + [any_space] * 3,
        out_shape=[
            shape((length, 2688), kind),
            shape(x_seq.shape, kind),
            shape(x_seq.shape, kind),
            shape((length, 896), kind),
            shape((7, 8, length), jnp.float32),
            shape((4,) + out_shard.shape, kind),
            shape((4,) + expand_shard.shape, kind),
            shape((3,) + cot.shape, kind),
        ],
        scratch_shapes=[
            buf(*x_seq.shape),
            buf(*w_in.shape),
            buf(*out_shard.shape),
            buf(*expand_shard.shape),
            pltpu.VMEM((128, length), jnp.float32),
            buf(128, length),
            pltpu.SemaphoreType.DMA((24,)),
            pltpu.SemaphoreType.DMA((24,)),
            pltpu.SemaphoreType.DMA((8,)),
        ],
        compiler_params=pltpu.CompilerParams(collective_id=6, has_side_effects=True, vmem_limit_bytes=63 * 2**20),
        cost_estimate=pl.CostEstimate(flops=5 * 10**10, bytes_accessed=2**26, transcendentals=0),
        name="mix_heads",
    )(x_seq, w_in, rows, segc, segr, out_shard, expand_shard, cot)


def heads_back_kernel(q_ref, k_ref, v_ref, do_ref, o_ref, lse_ref, segc_ref, segr_ref, normed_ref, share_ref, first_ref, own_ref, pass_ref, result_ref, middle_ref, cot_ref, rows_ref, core_ref, dq_ref, dk_ref, dv_ref, sums_ref, grad_ref, share_out, first_out, result_out, cot_sums, core_out, quads, dqt_ref, odt_ref, pair, own, share_own, got, pair_next, normed_t, result, middle, cot, core_own, core_x, core_y, send, recv, local):
    tile = pl.program_id(0)
    replica = lax.axis_index("replica")
    group = lax.axis_index("group")
    quad = lax.rem(replica, 4)
    quad_z = lax.rem(quad + 2, 4)
    by_x, by_y, by_both, by_core, by_z = partners(replica, group)
    by_pair = (lax.rem(replica + 4, 8), group)
    wires = Wires(send, recv, local)
    pieces = [pl.ds(0, HALF), pl.ds(HALF, 400 - HALF)]
    pass_y = wires.make(pass_ref.at[pieces[0]], got.at[pieces[0]], by_y)
    pass_x = wires.make(pass_ref.at[pieces[1]], got.at[pieces[1]], by_x)
    pair_lower = wires.make(share_ref.at[pieces[1]], pair.at[pieces[1]], by_pair)
    pair_upper = wires.make(own.at[pieces[0]], pair_next, by_pair)
    loads = [
        pltpu.make_async_copy(first_ref, pair.at[pieces[0]], local.at[0]),
        pltpu.make_async_copy(own_ref, own, local.at[1]),
        pltpu.make_async_copy(share_ref, share_own, local.at[2]),
    ]
    x = lax.rem(group, 2)
    y = lax.div(group, 2)
    out_rows = (1 - y, y)
    out_x = [wires.make(core_ref.at[2 * row + 1 - x], core_x.at[i], by_x) for i, row in enumerate(out_rows)]
    out_y = wires.make(core_own.at[0], core_y, by_y)
    more_loads = [pltpu.make_async_copy(core_ref.at[2 * row + x], core_own.at[i], local.at[8 + i]) for i, row in enumerate(out_rows)]
    more_loads += [
        pltpu.make_async_copy(result_ref, result, local.at[5]),
        pltpu.make_async_copy(middle_ref, middle, local.at[6]),
        pltpu.make_async_copy(cot_ref, cot, local.at[7]),
    ]
    keeps = [pltpu.make_async_copy(pair.at[rows], quads.at[quad, rows], local.at[3 + i]) for i, rows in enumerate(pieces)]
    overs = [wires.make(pair.at[rows], quads.at[quad, rows], by_z) for rows in pieces]
    cores = [wires.make(pair.at[rows], quads.at[quad, rows], by_core) for rows in pieces]
    passes = [wires.make(quads.at[quad_z, rows], quads.at[quad_z, rows], by_core) for rows in pieces]

    def spread(i):
        keeps[i].start()
        overs[i].start()
        cores[i].start()

    @pl.when(tile == 0)
    def _():
        greet([by_pair, by_x, by_y, by_core, by_z])
        for copy in [pass_y, pass_x, pair_lower] + loads + more_loads:
            copy.start()
        normed_t[...] = normed_ref[...].T

    @pl.when(tile == 1)
    def _():
        for copy in loads:
            copy.wait()
        spread(0)

    @pl.when(tile == 2)
    def _():
        pass_y.wait()
        pass_x.wait()
        own[...] = add_low(own[...], got[...])
        for copy in out_x:
            copy.start()

    @pl.when(tile == 3)
    def _():
        for copy in more_loads:
            copy.wait()
        cot_sums[...] = jnp.zeros_like(cot_sums)
        for seq in range(2):
            rows = pl.ds(256 * seq, 256)
            final = result[rows, :] + middle[rows, :] + rows_ref[3:4, : result.shape[1]]
            result_out[seq] = final.astype(jnp.bfloat16).T
            cot_sums[0:1, :] += jnp.sum(cot[rows, :].astype(jnp.float32), axis=0, keepdims=True)

    @pl.when(tile == 4)
    def _():
        pair_lower.wait()
        pair_upper.start()
        pair[HALF:, :] = add_low(pair[HALF:, :], share_own[HALF:, :])
        spread(1)
        overs[0].wait_recv()
        passes[0].start()

    @pl.when(tile == 5)
    def _():
        for i in range(2):
            out_x[i].wait()
            core_own[i] = add_low(core_own[i], core_x[i])
        out_y.start()

    length = q_ref.shape[0]
    blocks = length // BLOCK
    lane = lax.broadcasted_iota(jnp.int32, (1, 128), 1)
    dqt_ref[...] = jnp.zeros_like(dqt_ref)
    odt_ref[...] = (do_ref[...].astype(jnp.float32) * o_ref[...].astype(jnp.float32)).T

    def head(h):
        mine = (lane >= 64 * h) & (lane < 64 * h + 64)
        dot_row = jnp.sum(odt_ref[64 * h : 64 * h + 64, :], axis=0, keepdims=True)
        for j in range(blocks):
            low, high = j * BLOCK, (j + 1) * BLOCK
            rest = length - low
            q = q_ref[low:, :] * jnp.bfloat16(0.125)
            do = do_ref[low:, :]
            k = jnp.where(mine, k_ref[low:high, :], jnp.bfloat16(0))
            v = jnp.where(mine, v_ref[low:high, :], jnp.bfloat16(0))
            s = dot_nt(k, q)
            same = segc_ref[low:high, :] == segr_ref[:, low:]
            kpos = lax.broadcasted_iota(jnp.int32, (BLOCK, rest), 0)
            qpos = lax.broadcasted_iota(jnp.int32, (BLOCK, rest), 1)
            p = jnp.where(same & (kpos <= qpos), jnp.exp(s - lse_ref[0, h : h + 1, low:]), 0.0)
            dp = dot_nt(v, do)
            ds = (p * (dp - dot_row[:, low:])).astype(jnp.bfloat16)
            dv = dot_nn(p.astype(jnp.bfloat16), do)
            dk = dot_nn(ds, q)
            if h == 0:
                dv_ref[low:high, :] = jnp.where(mine, dv, 0.0).astype(jnp.bfloat16)
                dk_ref[low:high, :] = jnp.where(mine, dk, 0.0).astype(jnp.bfloat16)
            else:
                dv_ref[low:high, :] = jnp.where(mine, dv.astype(jnp.bfloat16), dv_ref[low:high, :])
                dk_ref[low:high, :] = jnp.where(mine, dk.astype(jnp.bfloat16), dk_ref[low:high, :])
            dqt_ref[:, low:] += dot_nn(k.T, ds)

    head(0)

    @pl.when(tile < 6)
    def _():
        head(1)

    dq_ref[...] = (dqt_ref[...].T * 0.125).astype(jnp.bfloat16)

    row = lax.broadcasted_iota(jnp.int32, (8, 128), 0)
    sum_q = jnp.sum(dq_ref[...].astype(jnp.float32), axis=0, keepdims=True)
    sum_v = jnp.sum(dv_ref[...].astype(jnp.float32), axis=0, keepdims=True)
    sums_ref[...] = jnp.where(row == 0, sum_q, jnp.where(row == 1, sum_v, 0.0))

    grads = jnp.concatenate([dq_ref[...], dk_ref[...], dv_ref[...]], axis=1)
    weights = dot_nn(normed_t[...], grads).astype(jnp.bfloat16)
    for i in range(3):
        grad_ref[i] = weights[:, 128 * i : 128 * i + 128]

    @pl.when(tile == 6)
    def _():
        overs[1].wait_recv()
        passes[1].start()
        share_out[...] = own[...]
        out_y.wait()
        width = core_own.shape[2]
        core_out[:, :width] = add_low(core_own[1], core_y[...])
        core_out[:, width:] = jnp.zeros((core_out.shape[0], core_out.shape[1] - width), jnp.bfloat16)
        pair_upper.wait()
        first_out[...] = add_low(own[:HALF, :], pair_next[...])
        for copy in cores + passes + keeps:
            copy.wait()
        for copy in overs:
            copy.wait_send()


def heads_back(qkv, grad, out, lse, segc, segr, normed, share, first, own, passed, result, middle, cot, rows, out_core):
    length = qkv.shape[0]
    width = share.shape[1]
    buf = lambda *dims: pltpu.VMEM(dims, jnp.bfloat16)
    still = lambda *dims: pl.BlockSpec(dims, lambda t: (0,) * len(dims))
    spec = lambda off: pl.BlockSpec((length, 128), lambda t: (0, t + off))
    one = pl.BlockSpec((length, 128), lambda t: (0, t))
    shape = jax.ShapeDtypeStruct((length, 896), jnp.bfloat16)
    return pl.pallas_call(
        heads_back_kernel,
        grid=(7,),
        in_specs=[spec(0), spec(7), spec(14), one, one, pl.BlockSpec((1, 8, length), lambda t: (t, 0, 0)), pl.BlockSpec((length, 1), lambda t: (0, 0)), pl.BlockSpec((1, length), lambda t: (0, 0)), still(*normed.shape)] + [pl.BlockSpec(memory_space=pl.ANY)] * 7 + [still(*rows.shape), pl.BlockSpec(memory_space=pl.ANY)],
        out_specs=[one, one, one, pl.BlockSpec((8, 128), lambda t: (0, t)), pl.BlockSpec((3, width, 128), lambda t: (0, 0, t)), still(*share.shape), still(*first.shape), still(2, width, 256), still(8, width), still(208, width + 64), pl.BlockSpec(memory_space=pl.ANY)],
        out_shape=[
            shape,
            shape,
            shape,
            jax.ShapeDtypeStruct((8, 896), jnp.float32),
            jax.ShapeDtypeStruct((3, width, 896), jnp.bfloat16),
            jax.ShapeDtypeStruct(share.shape, share.dtype),
            jax.ShapeDtypeStruct(first.shape, share.dtype),
            jax.ShapeDtypeStruct((2, width, 256), share.dtype),
            jax.ShapeDtypeStruct((8, width), jnp.float32),
            jax.ShapeDtypeStruct((208, width + 64), share.dtype),
            jax.ShapeDtypeStruct((4,) + share.shape, share.dtype),
        ],
        scratch_shapes=[pltpu.VMEM((128, length), jnp.float32), pltpu.VMEM((128, length), jnp.float32), buf(400, width), buf(400, width), buf(400, width), buf(400, width), buf(HALF, width), buf(width, length), pltpu.VMEM(result.shape, jnp.float32), pltpu.VMEM(middle.shape, jnp.float32), buf(*cot.shape), buf(2, 208, width), buf(2, 208, width), buf(208, width), pltpu.SemaphoreType.DMA((16,)), pltpu.SemaphoreType.DMA((16,)), pltpu.SemaphoreType.DMA((10,))],
        compiler_params=pltpu.CompilerParams(vmem_limit_bytes=63 * 2**20, collective_id=4, has_side_effects=True),
        cost_estimate=pl.CostEstimate(flops=int(13 * 5 * 2 * length * length * 64 * 2), bytes_accessed=16 * length * 896, transcendentals=13 * length * length // 2),
        name="heads_back",
    )(qkv, qkv, qkv, grad, out, lse, segc, segr, normed, share, first, own, passed, result, middle, cot, rows, out_core)

def feed_all_kernel(second, cot_in, cots, expand_part, reduce_shard, middle_in, out_in, bias, rows_ref, act_out, back_out, second_out, reduce_out, low_out, att_out, gs_out, own_out, pass_out, sum_out, norm_sums, wexp, wred, s, c, a, b, gs, got_core, got_z, rg, got_x, got_y, send, recv, local):
    replica = lax.axis_index("replica")
    group = lax.axis_index("group")
    quad = lax.rem(replica, 4)
    y = lax.div(group, 2)
    x = lax.rem(group, 2)
    by_x, by_y, by_both, by_core, by_z = partners(replica, group)
    slot_x, slot_y, slot_both = by_x[1], by_y[1], by_both[1]
    wires = Wires(send, recv, local)
    greet([by_x, by_y, by_core, by_z])
    width = wexp.shape[0]
    block = lambda rel: pl.ds(512 * rel, 512)
    sec_core = wires.go(second, s.at[block(1)], by_core)
    sec_z = wires.go(second, s.at[block(2)], by_z)
    quarter = reduce_shard.at[rows16(400 * quad, 400)]
    spot = lambda rank: rows16(400 * rank, 400)
    red_x = wires.go(quarter, wred.at[spot(group)], by_x)
    red_y = wires.go(quarter, wred.at[spot(group)], by_y)
    load_s = wires.here(second, s.at[block(0)])
    load_e = wires.here(expand_part, wexp)
    load_r = wires.here(quarter, wred.at[spot(group)])
    load_m = wires.here(middle_in, gs_out)
    load_c = [wires.here(cot_in, c.at[block(0)])] + [wires.here(cots.at[i], c.at[block(i + 1)]) for i in range(3)]
    sum_out[...] = jnp.zeros_like(sum_out)
    root = 0.7978845608028654

    def gelu(u):
        square = u * u
        t = jnp.tanh(root * u * (1.0 + 0.044715 * square))
        half = 0.5 * (1.0 + t)
        slope = half + (0.5 * root) * u * (1.0 - t * t) * (1.0 + (3.0 * 0.044715) * square)
        return u * half, slope

    def steps(rel, body):
        def one(i, carry):
            body(pl.ds(pl.multiple_of(512 * rel + 256 * i, 256), 256))
            return carry

        lax.fori_loop(0, 2, one, 0)

    def keep_back(rows, low_at, high_at, back):
        back = back.astype(jnp.bfloat16)
        b[rows, low_at:high_at] = back
        sum_out[:, low_at:high_at] += jnp.sum(back.astype(jnp.float32).reshape(32, 8, high_at - low_at), axis=0)

    def up_only(rows):
        entries = s[rows, :width]
        for low_at, high_at in PIECES:
            act, slope = gelu(dot_nn(entries, wexp[:, low_at:high_at]) + bias[:, low_at:high_at])
            a[rows, low_at:high_at] = act.astype(jnp.bfloat16)
            b[rows, low_at:high_at] = slope.astype(jnp.bfloat16)

    def finish_rows(rows):
        gs[rows, width:] = jnp.zeros((256, gs.shape[1] - width), jnp.bfloat16)
        gs[rows, :width] = dot_nt(b[rows, :], wexp[...]).astype(jnp.bfloat16)

    def back_only(rows):
        cot = c[rows, :]
        for low_at, high_at in PIECES:
            keep_back(rows, low_at, high_at, dot_nt(cot, wred[low_at:high_at, :]) * b[rows, low_at:high_at].astype(jnp.float32))
        finish_rows(rows)

    def both(rows):
        entries = s[rows, :width]
        cot = c[rows, :]
        for low_at, high_at in PIECES:
            act, slope = gelu(dot_nn(entries, wexp[:, low_at:high_at]) + bias[:, low_at:high_at])
            a[rows, low_at:high_at] = act.astype(jnp.bfloat16)
            keep_back(rows, low_at, high_at, dot_nt(cot, wred[low_at:high_at, :]) * slope)
        finish_rows(rows)

    load_s.wait()
    load_e.wait()
    steps(0, up_only)
    sec_core.wait_recv()
    steps(1, up_only)
    red_x.wait_recv()
    more_y = wires.go(wred.at[rows16(400 * slot_x, HALF)], wred.at[rows16(400 * slot_x, HALF)], by_y)
    red_y.wait_recv()
    more_x = wires.go(wred.at[rows16(400 * slot_y + HALF, 400 - HALF)], wred.at[rows16(400 * slot_y + HALF, 400 - HALF)], by_x)
    sec_z.wait_recv()
    sec_both = wires.go(s.at[block(2)], s.at[block(3)], by_core)
    load_r.wait()
    for copy in load_c:
        copy.wait()
    more_x.wait_recv()
    more_y.wait_recv()
    wires.keep(wred, reduce_out)
    sec_both.wait_recv()
    wires.keep(s, second_out)
    base = wires.remotes
    wires.remotes = base + 4

    def far_copies(half):
        piece = pl.ds(pl.multiple_of(256 * half, 256), 256)
        third = pl.ds(pl.multiple_of(1536 + 256 * half, 256), 256)
        second_rows = pl.ds(pl.multiple_of(1024 + 256 * half, 256), 256)
        near = pltpu.make_async_remote_copy(src_ref=gs.at[third], dst_ref=got_core.at[1, piece], send_sem=send.at[base + half], recv_sem=recv.at[base + half], device_id=by_core, device_id_type=MESH)
        over = pltpu.make_async_remote_copy(src_ref=gs.at[second_rows], dst_ref=got_z.at[piece], send_sem=send.at[base + 2 + half], recv_sem=recv.at[base + 2 + half], device_id=by_z, device_id_type=MESH)
        return third, second_rows, piece, near, over

    def far_half(half, carry):
        third, second_rows, piece, near, over = far_copies(half)
        both(third)
        near.start()
        both(second_rows)
        near.wait_recv()
        gs[second_rows, :] = add_low(gs[second_rows, :], got_core[1, piece, :])
        over.start()
        return carry

    lax.fori_loop(0, 2, far_half, 0)
    wires.keep(a, act_out)
    weight_sum(a, c, rg)
    x_copies = [wires.go(rg.at[rows16(400 * slot, HALF)], got_x.at[i], by_x) for i, slot in enumerate((slot_x, slot_both))]
    y_copies = [wires.go(rg.at[rows16(400 * slot + HALF, 400 - HALF)], got_y.at[i], by_y) for i, slot in enumerate((slot_y, slot_both))]
    steps(1, back_only)
    gs_core = wires.go(gs.at[block(1)], got_core.at[0], by_core)
    steps(0, back_only)
    wires.keep(b, back_out)
    load_w = wires.here(out_in, wexp)
    load_m.wait()
    gs_core.wait_recv()
    for half in range(2):
        third, second_rows, piece, near, over = far_copies(half)
        over.wait_recv()
        over.wait_send()
        near.wait_send()
    load_w.wait()
    norm_sums[...] = jnp.zeros_like(norm_sums)
    lanes = lax.broadcasted_iota(jnp.int32, (1, 128), 1)
    for seq in range(2):
        stage = got_core.at[1 - seq]

        def norm_back(j, carry):
            rows = pl.ds(pl.multiple_of(256 * seq + 128 * j, 128), 128)
            first = pl.ds(pl.multiple_of(128 * j, 128), 128)
            other = pl.ds(pl.multiple_of(256 + 128 * j, 128), 128)
            grad = gs[rows, :width].astype(jnp.float32) + got_core[0, rows, :width].astype(jnp.float32) + got_z[rows, :width].astype(jnp.float32)
            middle = gs_out[rows, :]
            center = middle - jnp.mean(middle, axis=-1, keepdims=True)
            scale = lax.rsqrt(jnp.mean(center * center, axis=-1, keepdims=True) + epsilon)
            unit = center * scale
            q = grad * rows_ref[6:7, :width]
            grad_middle = c[rows, :].astype(jnp.float32) + scale * (
                q - jnp.mean(q, axis=-1, keepdims=True) - unit * jnp.mean(q * unit, axis=-1, keepdims=True)
            )
            gs_out[rows, :] = grad_middle
            grad_low = grad_middle.astype(jnp.bfloat16)
            gs[rows, :width] = grad_low
            norm_sums[0:1, :] += jnp.sum(grad * unit, axis=0, keepdims=True)
            norm_sums[1:2, :] += jnp.sum(grad, axis=0, keepdims=True)
            norm_sums[2:3, :] += jnp.sum(grad_low.astype(jnp.float32), axis=0, keepdims=True)
            att = dot_nt(grad_low, wexp[...]).astype(jnp.bfloat16)
            stage[first, 0:768] = att[:, 0:768]
            stage[first, 768:896] = jnp.where(lanes < 64, att[:, 768:896], jnp.bfloat16(0))
            stage[other, 0:128] = jnp.where(lanes >= 64, att[:, 768:896], jnp.bfloat16(0))
            stage[other, 128 : width - 768] = att[:, 896:width]
            stage[other, width - 768 : 896] = jnp.zeros((128, 896 + 768 - width), jnp.bfloat16)
            return carry

        lax.fori_loop(0, 2, norm_back, 0)
        for half in range(2):
            wires.keep(stage.at[pl.ds(256 * half, 256), pl.ds(0, 896)], att_out.at[seq, half])
    wires.keep(gs.at[block(0)], low_out)
    for copy in x_copies + y_copies:
        copy.wait_recv()
    own_out[:HALF] = add_low(rg[rows16(400 * group, HALF), :], got_x[0])
    own_out[HALF:] = add_low(rg[rows16(400 * group + HALF, 400 - HALF), :], got_y[0])
    pass_out[:HALF] = add_low(rg[rows16(400 * slot_y, HALF), :], got_x[1])
    pass_out[HALF:] = add_low(rg[rows16(400 * slot_x + HALF, 400 - HALF), :], got_y[1])
    wires.finish()


def feed_all(second, cot, cots, expand_part, reduce_shard, middle, full_out, bias, rows_in):
    any_space = pl.BlockSpec(memory_space=pl.ANY)
    vmem = pl.BlockSpec(memory_space=pltpu.VMEM)
    shape = jax.ShapeDtypeStruct
    kind = jnp.bfloat16
    rows, full = second.shape
    width = expand_part.shape[0]
    buf = lambda *dims: pltpu.VMEM(dims, kind)
    return pl.pallas_call(
        feed_all_kernel,
        in_specs=[any_space] * 7 + [vmem, vmem],
        out_specs=[any_space] * 6 + [vmem] * 5,
        out_shape=[
            shape((4 * rows, width), kind),
            shape((4 * rows, width), kind),
            shape((4 * rows, full), kind),
            shape((width, width), kind),
            shape((rows, full), kind),
            shape((2, 2, 256, 896), kind),
            shape((rows, width), jnp.float32),
            shape((400, width), kind),
            shape((400, width), kind),
            shape((8, width), jnp.float32),
            shape((8, width), jnp.float32),
        ],
        scratch_shapes=[
            buf(width, width),
            buf(width, width),
            buf(4 * rows, full),
            buf(4 * rows, width),
            buf(4 * rows, width),
            buf(4 * rows, width),
            buf(4 * rows, full),
            buf(2, rows, full),
            buf(rows, full),
            buf(width, width),
            buf(2, HALF, width),
            buf(2, 400 - HALF, width),
            pltpu.SemaphoreType.DMA((16,)),
            pltpu.SemaphoreType.DMA((16,)),
            pltpu.SemaphoreType.DMA((20,)),
        ],
        compiler_params=pltpu.CompilerParams(collective_id=5, has_side_effects=True, vmem_limit_bytes=63 * 2**20),
        cost_estimate=pl.CostEstimate(flops=10**11, bytes_accessed=2**26, transcendentals=0),
        name="feed_all",
    )(second, cot, cots, expand_part, reduce_shard, middle, full_out, bias, rows_in)


def turn_more_kernel(grad_att, back, second, act, wred_in, pass_in, att_in, grad_in, own_in, heads_out, result_out, share_out, first_out, own_out, pass_out, core_out, att, grad, stage, b, s, a, wred, rg, result, got_core, got_z, got, got_x, got_y, pair, send, recv, local):
    replica = lax.axis_index("replica")
    group = lax.axis_index("group")
    core = lax.rem(replica, 2)
    y = lax.div(group, 2)
    x = lax.rem(group, 2)
    by_x, by_y, by_both, by_core, by_z = partners(replica, group)
    by_pair = (lax.rem(replica + 4, 8), group)
    slot_x, slot_y, slot_both = by_x[1], by_y[1], by_both[1]
    wires = Wires(send, recv, local)
    load_a = wires.here(act, a)
    load_w = wires.here(wred_in, wred)
    load_own = wires.here(grad_att.at[x, y], stage)
    load_s = wires.here(second, s)
    load_b = wires.here(back, b)
    load_att = wires.here(att_in, att)
    load_grad = wires.here(grad_in, grad)
    greet([by_x, by_y, by_both, by_core, by_z, by_pair])
    width = wred.shape[0]
    block = lambda rel: pl.ds(512 * rel, 512)
    pass_y = wires.go(pass_in.at[pl.ds(0, HALF)], got.at[pl.ds(0, HALF)], by_y)
    pass_x = wires.go(pass_in.at[pl.ds(HALF, 400 - HALF)], got.at[pl.ds(HALF, 400 - HALF)], by_x)
    load_a.wait()
    load_w.wait()

    def rows_out(rel):
        def one(i, carry):
            rows = pl.ds(pl.multiple_of(512 * rel + 256 * i, 256), 256)
            result[rows, :] = dot_nn(a[rows, :], wred[...]).astype(jnp.bfloat16)
            return carry

        lax.fori_loop(0, 2, one, 0)

    rows_out(3)
    to_both = wires.go(result.at[block(3)], got_core.at[1], by_core)
    rows_out(2)
    wires.drain([pass_y, pass_x])
    turns = []
    for device in (by_both, by_x, by_y):
        there = device[1]
        turns.append(wires.go(grad_att.at[lax.rem(there, 2), lax.div(there, 2)], heads_out.at[group], device))
    to_both.wait_recv()
    result[block(2), :] = add_low(result[block(2), :], got_core[1])
    to_z = wires.go(result.at[block(2)], got_z, by_z)
    pass_y.wait_recv()
    pass_x.wait_recv()
    share_out[...] = add_low(own_in[...], got[...])
    pair_upper = wires.go(share_out.at[pl.ds(0, HALF)], pair, by_pair)
    load_own.wait()
    wires.keep(stage, heads_out.at[group])
    load_s.wait()
    load_b.wait()
    weight_sum(s, b, rg)
    x_copies = [wires.go(rg.at[rows16(400 * slot, HALF)], got_x.at[i], by_x) for i, slot in enumerate((slot_x, slot_both))]
    y_copies = [wires.go(rg.at[rows16(400 * slot + HALF, 400 - HALF)], got_y.at[i], by_y) for i, slot in enumerate((slot_y, slot_both))]
    rows_out(1)
    to_core = wires.go(result.at[block(1)], got_core.at[0], by_core)
    rows_out(0)
    load_att.wait()
    load_grad.wait()
    weight_sum(att, grad, wred)
    out_core = [wires.go(wred.at[rows16(400 * r + 192 * (1 - core), 208)], core_out.at[r], by_core) for r in range(4)]
    for r in range(4):
        out_core[r].wait_recv()
        core_out[r] = add_low(wred[rows16(400 * r + 192 * core, 208), :], core_out[r])
    to_core.wait_recv()
    to_z.wait_recv()
    result_out[...] = result[block(0), :].astype(jnp.float32) + got_core[0].astype(jnp.float32) + got_z[...].astype(jnp.float32)
    pair_upper.wait_recv()
    first_out[...] = add_low(share_out[:HALF, :], pair[...])
    for copy in x_copies + y_copies:
        copy.wait_recv()
    own_out[:HALF] = add_low(rg[rows16(400 * group, HALF), :], got_x[0])
    own_out[HALF:] = add_low(rg[rows16(400 * group + HALF, 400 - HALF), :], got_y[0])
    pass_out[:HALF] = add_low(rg[rows16(400 * slot_y, HALF), :], got_x[1])
    pass_out[HALF:] = add_low(rg[rows16(400 * slot_x + HALF, 400 - HALF), :], got_y[1])
    for copy in turns:
        copy.wait_recv()
    wires.finish()


def turn_more(grad_att, back, second, act, wred, passed, att, grad, own):
    any_space = pl.BlockSpec(memory_space=pl.ANY)
    vmem = pl.BlockSpec(memory_space=pltpu.VMEM)
    shape = jax.ShapeDtypeStruct
    kind = jnp.bfloat16
    width = wred.shape[0]
    rows = act.shape[0] // 4
    buf = lambda *dims: pltpu.VMEM(dims, kind)
    return pl.pallas_call(
        turn_more_kernel,
        in_specs=[any_space] * 8 + [vmem],
        out_specs=[any_space] + [vmem] * 6,
        out_shape=[
            shape((4,) + grad_att.shape[2:], kind),
            shape((rows, width), jnp.float32),
            shape((400, width), kind),
            shape((HALF, width), kind),
            shape((400, width), kind),
            shape((400, width), kind),
            shape((4, 208, width), kind),
        ],
        scratch_shapes=[
            buf(rows, width),
            buf(*grad.shape),
            buf(*grad_att.shape[2:]),
            buf(4 * rows, width),
            buf(*second.shape),
            buf(4 * rows, width),
            buf(width, width),
            buf(width, width),
            buf(4 * rows, width),
            buf(2, rows, width),
            buf(rows, width),
            buf(400, width),
            buf(2, HALF, width),
            buf(2, 400 - HALF, width),
            buf(HALF, width),
            pltpu.SemaphoreType.DMA((18,)),
            pltpu.SemaphoreType.DMA((18,)),
            pltpu.SemaphoreType.DMA((10,)),
        ],
        compiler_params=pltpu.CompilerParams(collective_id=2, has_side_effects=True, vmem_limit_bytes=63 * 2**20),
        cost_estimate=pl.CostEstimate(flops=3 * 10**10, bytes_accessed=2**26, transcendentals=0),
        name="turn_more",
    )(grad_att, back, second, act, wred, passed, att, grad, own)


def arrive(here, there, total, lane, k, y, mine):
    first = jnp.where(y == 0, here, there)
    other = jnp.where(y == 0, there, here)
    rows = pl.ds(mine, 208)
    total[k, rows, 0:768] = first[:, 0:768]
    total[k, rows, 768:896] = jnp.where(lane < 64, first[:, 768:896], other[:, 0:128])
    total[k, rows, 896:1664] = other[:, 128:896]


def last_kernel(dq, dk, dv, grad_in, unit_in, w_in, share_in, share_expand, first_expand, vec, gm_in, inp_in, gain, total, grad_turned, vec_total, wide_total, quads, grad_out, d, unit_rows, w, part, c_buf, x_buf, y_buf, line_buf, line_mid, gn, gn_y, gn_cross, inp, pair_buf, vec_got, vec_own, vec_core, vec_z, more_got, more_core, more_z, send, recv, local):
    replica = lax.axis_index("replica")
    group = lax.axis_index("group")
    core = lax.rem(replica, 2)
    quad = lax.rem(replica, 4)
    quad_z = lax.rem(quad + 2, 4)
    z = lax.div(replica, 2)
    y = lax.div(group, 2)
    x = lax.rem(group, 2)
    by_x, by_y, by_both, by_core, by_z = partners(replica, group)
    outer = (z == 0) | (z == 3)
    inner = jnp.logical_not(outer)
    by_line = (jnp.where(z == 0, replica + 2, jnp.where(z == 3, replica - 2, jnp.where(z == 1, replica - 2, replica + 2))), group)
    by_middle = (jnp.where(z == 1, replica + 2, replica - 2), group)
    lines_z = [(lax.rem(replica + 2 * k, 8), group) for k in (1, 2, 3)]
    by_pair = lines_z[1]
    wires = Wires(send, recv, local)
    greet([by_x, by_y, by_both, by_core] + lines_z)
    mine = pl.multiple_of(192 * core, 16)
    theirs = pl.multiple_of(192 * (1 - core), 16)
    other_x = 1 - x
    other_y = 1 - y
    far = 2 * other_y
    near = 2 * y
    width = w.shape[0]
    lane = lax.broadcasted_iota(jnp.int32, (1, 128), 1)
    halves = [(pl.ds(mine + 112 * m, 112 - 16 * m), pl.ds(112 * m, 112 - 16 * m)) for m in range(2)]
    pieces = [pl.ds(0, 208), pl.ds(208, 192)]

    pair_lower = wires.go(share_expand.at[pieces[1]], pair_buf, by_pair)
    c_copies = []
    part_loads = []
    for k in range(3):
        c_copies.append([wires.go(grad_in.at[k, rows16(400 * r + theirs, 208)], c_buf.at[k, r], by_core) for r in range(4)])
        part_loads.append([wires.here(grad_in.at[k, pl.ds(400 * r + mine, 208)], part.at[k, r]) for r in range(4)])
    loads = [wires.here(part, d.at[k]) for k, part in enumerate((dq, dk, dv))]
    load_w = [wires.here(w_in, w), wires.here(unit_in, unit_rows)]
    load_share = wires.here(share_in, total.at[3, pl.ds(mine, 208)])
    vec_group = [wires.go(vec.at[device[1]], vec_got.at[group], device) for device in (by_x, by_y, by_both)]

    def spread(value, rows):
        wires.keep(value, quads.at[quad, rows])
        over = wires.go(value, quads.at[quad, rows], by_z)
        return over, wires.go(value, quads.at[quad, rows], by_core)

    def spread_on(over, rows):
        over.wait_recv()
        return wires.go(quads.at[quad_z, rows], quads.at[quad_z, rows], by_core)

    load_gm = wires.here(gm_in, grad_out)
    load_inp = wires.here(inp_in, inp)

    def line_start(k, m):
        rows, merge = halves[m]
        into = wires.make(total.at[k, rows], line_buf.at[k, merge], by_line)
        middle = wires.make(total.at[k, rows], line_mid.at[k, merge], by_middle)
        back = wires.make(total.at[k, rows], line_buf.at[k, merge], by_line)

        @pl.when(outer)
        def _():
            if m == 1:
                lines[k, 0][0].wait_send()
            into.start()

        lines[k, m] = into, middle, back

    def line_second(k, m):
        rows, merge = halves[m]
        into, middle, back = lines[k, m]

        @pl.when(inner)
        def _():
            into.wait_recv()
            total[k, rows] = add_low(total[k, rows], line_buf[k, merge])
            middle.start()

    def line_third(k, m):
        rows, merge = halves[m]
        into, middle, back = lines[k, m]

        @pl.when(inner)
        def _():
            middle.wait_recv()
            middle.wait_send()
            total[k, rows] = add_low(total[k, rows], line_mid[k, merge])
            back.start()

    def line_fourth(k, m):
        rows, merge = halves[m]
        into, middle, back = lines[k, m]

        @pl.when(outer)
        def _():
            if m == 1:
                into.wait_send()
            back.wait_recv()
            total[k, rows] = line_buf[k, merge]

        @pl.when(inner)
        def _():
            back.wait_send()

    lines = {}
    x_copies = {}
    y_copies = {}

    def core_sum(k):
        for r in range(4):
            part_loads[k][r].wait()
            c_copies[k][r].wait_recv()
            c_buf[k, r] = add_low(c_buf[k, r], part[k, r])

    def x_go(k, i):
        row = (other_y, y)[i]
        x_copies[k, i] = wires.go(c_buf.at[k, 2 * row + other_x], x_buf.at[k, i], by_x)

    def x_next(k, i, after):
        wires.drain([x_copies[k, i]])
        if after is not None:
            x_go(*after)
        x_copies[k, i].wait_recv()
        spot = (far, near)[i] + x
        c_buf[k, spot] = add_low(c_buf[k, spot], x_buf[k, i])
        if i == 0:
            y_copies[k] = wires.go(c_buf.at[k, spot], y_buf.at[k], by_y)

    def y_done(k):
        y_copies[k].wait_recv()
        arrive(c_buf[k, near + x], y_buf[k], total, lane, k, y, mine)
        line_start(k, 0)

    def normed_grad(b):
        rows = pl.ds(pl.multiple_of(256 * b, 256), 256)
        value = dot_nt(d[0, rows, :], w[:, 0:896]) + dot_nt(d[1, rows, :], w[:, 896:1792]) + dot_nt(d[2, rows, :], w[:, 1792:2688])
        gn[b] = value.astype(jnp.bfloat16)
        more_got[group, 0:1, 0:width] += jnp.sum(value * unit_rows[rows, :].astype(jnp.float32), axis=0, keepdims=True)
        more_got[group, 1:2, 0:width] += jnp.sum(value, axis=0, keepdims=True)

    spread_expand = [spread(first_expand, pieces[0])]
    core_sum(0)
    x_go(0, 0)
    x_go(0, 1)
    core_sum(1)
    core_sum(2)
    load_share.wait()
    line_start(3, 0)
    more_got[group] = jnp.zeros(more_got.shape[1:], jnp.float32)
    for copy in loads + load_w:
        copy.wait()
    normed_grad(far + other_x)
    y_pass = wires.go(gn.at[far + other_x], gn_y.at[0], by_y)
    normed_grad(near + other_x)
    x_next(0, 0, (1, 0))
    x_next(0, 1, (1, 1))
    line_start(3, 1)
    line_second(3, 0)
    normed_grad(far + x)
    y_done(0)
    normed_grad(near + x)
    more_group = [wires.go(more_got.at[group], more_got.at[group], device) for device in (by_x, by_y, by_both)]
    for copy in vec_group:
        copy.wait_recv()
    vec_got[group] = vec[group]
    vec_own[...] = (vec_got[0] + vec_got[1]) + (vec_got[2] + vec_got[3])
    vec_pass = wires.go(vec_own, vec_core, by_core)
    x_next(1, 0, (2, 0))
    line_start(0, 1)
    line_second(3, 1)
    y_pass.wait_recv()
    gn_y[0] = add_low(gn_y[0], gn[near + other_x])
    line_second(0, 0)
    x_next(1, 1, (2, 1))
    y_done(1)
    for copy in more_group:
        copy.wait_recv()
    more_z[z] = (more_got[0] + more_got[1]) + (more_got[2] + more_got[3])
    more_pass = wires.go(more_z.at[z], more_core, by_core)
    pair_lower.wait_recv()
    pair_buf[...] = add_low(pair_buf[...], share_expand[HALF:, :])
    spread_expand.append(spread(pair_buf, pieces[1]))
    line_third(3, 0)
    line_second(0, 1)
    vec_pass.wait_recv()
    vec_z[z] = vec_own[...] + vec_core[...]
    vec_line = [wires.go(vec_z.at[z], vec_z.at[z], device) for device in lines_z]
    line_start(1, 1)
    x_next(2, 0, None)
    cross = wires.go(gn_y.at[0], gn_cross, by_x)
    y_keep = wires.go(gn.at[far + x], gn_y.at[1], by_y)
    line_second(1, 0)
    line_third(3, 1)
    x_next(2, 1, None)
    y_done(2)
    line_third(0, 0)
    line_second(1, 1)
    line_start(2, 1)
    more_pass.wait_recv()
    wires.drain([more_pass])
    more_z[z] = more_z[z] + more_core[...]
    more_line = [wires.go(more_z.at[z], more_z.at[z], device) for device in lines_z]
    line_third(0, 1)
    line_second(2, 0)
    line_third(1, 0)
    passes = [spread_on(spread_expand[0][0], pieces[0])]
    line_second(2, 1)
    line_third(1, 1)

    load_gm.wait()
    load_inp.wait()

    def norm_back(seq, grad):
        entries = inp[seq].astype(jnp.float32)
        center = entries - jnp.mean(entries, axis=-1, keepdims=True)
        scale = lax.rsqrt(jnp.mean(center * center, axis=-1, keepdims=True) + epsilon)
        unit = center * scale
        q = grad * gain[...]
        grad_out[seq] += scale * (q - jnp.mean(q, axis=-1, keepdims=True) - unit * jnp.mean(q * unit, axis=-1, keepdims=True))
        grad_turned[seq] = grad_out[seq].T

    y_keep.wait_recv()
    norm_back(x, gn_y[1].astype(jnp.float32) + gn[near + x].astype(jnp.float32))
    cross.wait_recv()
    norm_back(other_x, gn_cross[...].astype(jnp.float32))
    line_third(2, 0)
    line_third(2, 1)
    for copy in vec_line:
        copy.wait_recv()
    vec_total[...] = (vec_z[0] + vec_z[1]) + (vec_z[2] + vec_z[3])
    passes.append(spread_on(spread_expand[1][0], pieces[1]))
    last = []
    for k in (3, 0, 1, 2):
        line_fourth(k, 0)
        line_fourth(k, 1)
        rows = pl.ds(pl.multiple_of(208 * core, 16), 192)
        last.append(wires.go(total.at[k, rows], total.at[k, rows], by_core))
    for copy in more_line:
        copy.wait_recv()
    wide_total[...] = (more_z[0] + more_z[1]) + (more_z[2] + more_z[3])
    for copy in last + passes + [both for over, both in spread_expand]:
        copy.wait_recv()
    wires.finish()


def last_sums(dq, dk, dv, in_grad, unit, w_half, out_share, share_expand, first_expand, vec, grad_middle, inputs, gain):
    any_space = pl.BlockSpec(memory_space=pl.ANY)
    vmem = pl.BlockSpec(memory_space=pltpu.VMEM)
    shape = jax.ShapeDtypeStruct
    kind = jnp.bfloat16
    width = w_half.shape[0]
    buf = lambda *dims: pltpu.VMEM(dims, kind)
    flat = lambda *dims: pltpu.VMEM(dims, jnp.float32)
    return pl.pallas_call(
        last_kernel,
        in_specs=[any_space] * 7 + [vmem, vmem, vmem, any_space, any_space, vmem],
        out_specs=[vmem, vmem, vmem, vmem, any_space],
        out_shape=[
            shape((4, 400, 1664), kind),
            shape((2, width, 256), jnp.float32),
            shape(vec.shape[1:], vec.dtype),
            shape((8, 1664), jnp.float32),
            shape((4,) + share_expand.shape, kind),
        ],
        scratch_shapes=[
            flat(*grad_middle.shape),
            buf(3, 1024, 896),
            buf(*unit.shape),
            buf(*w_half.shape),
            buf(3, 4, 208, 896),
            buf(3, 4, 208, 896),
            buf(3, 2, 208, 896),
            buf(3, 208, 896),
            buf(4, 208, 1664),
            buf(4, 208, 1664),
            buf(4, 256, width),
            buf(2, 256, width),
            buf(256, width),
            buf(*inputs.shape),
            buf(400 - HALF, width),
            flat(*vec.shape),
            flat(*vec.shape[1:]),
            flat(*vec.shape[1:]),
            flat(*vec.shape),
            flat(4, 8, 1664),
            flat(8, 1664),
            flat(4, 8, 1664),
            pltpu.SemaphoreType.DMA((88,)),
            pltpu.SemaphoreType.DMA((88,)),
            pltpu.SemaphoreType.DMA((24,)),
        ],
        compiler_params=pltpu.CompilerParams(collective_id=3, has_side_effects=True, vmem_limit_bytes=63 * 2**20),
        cost_estimate=pl.CostEstimate(flops=10**11, bytes_accessed=2**26, transcendentals=0),
        name="last_sums",
    )(dq, dk, dv, in_grad, unit, w_half, out_share, share_expand, first_expand, vec, grad_middle, inputs, gain)


def on_device(
    inputs,
    segments,
    cotangent,
    project_in,
    project_out,
    expand_weight,
    reduce_weight,
    query_bias,
    value_bias,
    project_bias,
    expand_bias,
    reduce_bias,
    first_gain,
    first_shift,
    second_gain,
    second_shift,
):
    replica, group, z, core, y, x = place()
    quad = lax.rem(replica, 4)
    width = 1600
    rows = 512

    names = (query_bias, value_bias, project_bias, reduce_bias, first_gain, first_shift, second_gain, second_shift)
    index = lax.broadcasted_iota(jnp.int32, (16, 400), 0)
    vec = jnp.pad(expand_bias.reshape(4, 400), ((8, 4), (0, 0)))
    for k, name in enumerate(names):
        vec = jnp.where(index == k, name[None, :], vec)
    turned = lambda entries: jnp.swapaxes(entries, 1, 2)
    x_seq, w_half, vecs, segs, own_inputs, own_cot, quarter_expand = first_exchange(
        turned(inputs), project_in, vec, segments[:, None, :], expand_weight, turned(cotangent)
    )
    row_vectors = padded(jnp.swapaxes(wide(vecs), 0, 1).reshape(16, width))
    bias_expand = lax.dynamic_index_in_dim(wide(vecs), 8 + quad, 1, False).reshape(1, width)
    segs = segs.reshape(1024)

    w_half = w_half.reshape(width, 2688)
    segc = segs[:, None]
    segr = segs[None]
    own_cot = own_cot.reshape(rows, width)
    mixture, normed, unit_seq, attended, lse, full_out, expand_part, cots = mix_heads(
        x_seq.reshape(1024, width), w_half, row_vectors, segc, segr, project_out, quarter_expand, own_cot
    )
    full_out = full_out.reshape(width, width)
    att_tokens, middle, second = turn_middle(attended.reshape(4, 256, 896), full_out, own_inputs, row_vectors)
    (
        activated,
        grad_expanded,
        second_all,
        reduce_part,
        grad_middle_low,
        grad_att,
        grad_middle,
        own_reduce,
        pass_reduce,
        expand_sums,
        norm_sums,
    ) = feed_all(
        second, own_cot, cots, expand_part.reshape(width, width), reduce_weight, middle, full_out, bias_expand, row_vectors
    )

    grad_heads, result, share_reduce, first_reduce, own_expand, pass_expand, out_core = turn_more(
        grad_att, grad_expanded, second_all, activated, reduce_part, pass_reduce, att_tokens, grad_middle_low, own_reduce
    )
    dq, dk, dv, bias_sums, in_grad, share_expand, first_expand, outputs, cot_sums, out_share, quads_reduce = heads_back(
        mixture,
        grad_heads.reshape(1024, 896),
        attended,
        lse,
        segc,
        segr,
        normed,
        share_reduce,
        first_reduce,
        own_expand,
        pass_expand,
        result,
        middle,
        own_cot,
        row_vectors,
        out_core,
    )

    def spread(columns):
        lower = jnp.concatenate([columns[:832], jnp.zeros((768,), jnp.float32)])
        upper = jnp.concatenate([jnp.zeros((832,), jnp.float32), columns[64:832]])
        return jnp.where(y == 0, lower, upper)

    expand_bias_part = jnp.sum(expand_sums, axis=0).reshape(4, 400)
    expand_bias_wide = lax.dynamic_update_slice_in_dim(jnp.zeros((4, width), jnp.float32), expand_bias_part, 400 * quad, 1)
    vectors = jnp.concatenate(
        [
            spread(bias_sums[0]).reshape(4, 400),
            spread(bias_sums[1]).reshape(4, 400),
            norm_sums[2].reshape(4, 400),
            cot_sums[0].reshape(4, 400),
            norm_sums[0].reshape(4, 400),
            norm_sums[1].reshape(4, 400),
            expand_bias_wide,
        ],
        axis=1,
    )
    vectors = jnp.pad(vectors, ((0, 0), (0, 96))).reshape(4, 32, 128)
    grad_total, input_grad, vec_total, wide_total, quads_expand = last_sums(
        dq, dk, dv, in_grad, unit_seq, w_half, out_share, share_expand, first_expand, vectors, grad_middle.reshape(2, 256, width), own_inputs, row_vectors[4:5, :width]
    )
    vec_total = vec_total.reshape(4096)
    pieces = [vec_total[400 * k : 400 * k + 400] for k in range(6)]
    first_sums = lax.dynamic_index_in_dim(wide_total[:2, :width].reshape(2, 4, 400), group, 1, False)
    total_reduce = wide(quads_reduce.reshape(width, width))
    total_expand, total_in, total_out = finish(quads_expand, grad_total)
    return (
        turned(outputs),
        turned(input_grad),
        total_in,
        total_out,
        total_expand,
        total_reduce,
        pieces[0],
        pieces[1],
        pieces[2],
        vec_total[2400:4000],
        pieces[3],
        first_sums[0],
        first_sums[1],
        pieces[4],
        pieces[5],
    )


def solution(mesh):
    placed = (
        P("replica", "group", None),
        P("replica", "group"),
        P("replica", "group", None),
        P("group", None),
        P("group", None),
        P("group", None),
        P("group", None),
        P("group"),
        P("group"),
        P("group"),
        P("group"),
        P("group"),
        P("group"),
        P("group"),
        P("group"),
        P("group"),
    )
    return jax.shard_map(
        on_device if dict(mesh.shape) == {"replica": 8, "group": 4} else on_device_any,
        mesh=mesh,
        in_specs=placed,
        out_specs=(
            P("replica", "group", None),
            P("replica", "group", None),
            P("group", None),
            P("group", None),
            P("group", None),
            P("group", None),
            P("group"),
            P("group"),
            P("group"),
            P("group"),
            P("group"),
            P("group"),
            P("group"),
            P("group"),
            P("group"),
        ),
        check_vma=False,
    )
```

```python
import functools
import math

import jax
import jax.numpy as jnp
from jax import lax
from jax.sharding import PartitionSpec as P

from jax.experimental import pallas as pl
from jax.experimental.pallas import tpu as pltpu

HEADS = 25
HEAD_DIM = 64


epsilon = 1e-05
very_low = -1e30


def carried_in(part, axis, combine, identity):
    place = lax.axis_index(axis)
    gathered = lax.all_gather(part, axis)
    state = jnp.zeros_like(part) + jnp.asarray(identity, part.dtype)

    def one(hop, state):
        return combine(state, lax.dynamic_index_in_dim(gathered, hop, 0, False))

    return lax.fori_loop(0, place, one, state)


def layer_norm(entries, gain, shift):
    center = entries - jnp.mean(entries, axis=-1, keepdims=True)
    spread = jnp.mean(center * center, axis=-1, keepdims=True)
    return center * lax.rsqrt(spread + epsilon) * gain + shift


def product(left, right):
    return jnp.dot(left, right, preferred_element_type=jnp.float32)


def product_back(left, right):
    return lax.dot_general(
        left, right, (((1,), (1,)), ((), ())), preferred_element_type=jnp.float32
    )


def weight_term(left, right):
    return lax.dot_general(
        left, right, (((0,), (0,)), ((), ())), preferred_element_type=jnp.float32
    )


def column_sum(entries):
    return jnp.sum(entries.astype(jnp.float32), axis=0)


def block_scores(queries, key_block, offset, query_pos, doc_start):
    block_count = key_block.shape[0]
    key_count = key_block.shape[2]
    scaling = 1.0 / math.sqrt(HEAD_DIM)
    scores = (
        jnp.einsum("schd,pskhd->shcpk", queries, key_block, preferred_element_type=jnp.float32)
        * scaling
    )
    key_pos = (offset + jnp.arange(block_count, dtype=jnp.int32))[:, None] * key_count + jnp.arange(
        key_count, dtype=jnp.int32
    )[None, :]
    allowed = (key_pos[None, None] <= query_pos[None, :, None, None]) & (
        key_pos[None, None] >= doc_start[:, :, None, None]
    )
    allowed = allowed[:, None]
    return (jnp.where(allowed, scores, very_low), allowed)


def attend(running, key_block, value_block, offset, queries, query_pos, doc_start):
    largest, denominator, summed = running
    masked, allowed = block_scores(queries, key_block, offset, query_pos, doc_start)
    fresh = jnp.maximum(largest, jnp.max(masked, axis=(3, 4)))
    shares = jnp.where(allowed, jnp.exp(masked - fresh[..., None, None]), 0.0)
    rescale = jnp.exp(largest - fresh)
    denominator = denominator * rescale + jnp.sum(shares, axis=(3, 4))
    added = jnp.einsum(
        "shcpk,pskhd->schd",
        shares.astype(jnp.bfloat16),
        value_block,
        preferred_element_type=jnp.float32,
    )
    summed = summed * jnp.transpose(rescale, (0, 2, 1))[..., None] + added
    return (fresh, denominator, summed)


def attend_back(
    grad_query,
    key_block,
    value_block,
    offset,
    queries,
    query_pos,
    doc_start,
    log_total,
    grad_low,
    row_dot,
):
    masked, allowed = block_scores(queries, key_block, offset, query_pos, doc_start)
    shares = jnp.where(allowed, jnp.exp(masked - log_total[..., None, None]), 0.0)
    grad_value = jnp.einsum(
        "shcpk,schd->pskhd",
        shares.astype(jnp.bfloat16),
        grad_low,
        preferred_element_type=jnp.float32,
    )
    grad_share = jnp.einsum(
        "schd,pskhd->shcpk", grad_low, value_block, preferred_element_type=jnp.float32
    )
    grad_score = (shares * (grad_share - row_dot[..., None, None])).astype(jnp.bfloat16)
    grad_query = grad_query + jnp.einsum(
        "shcpk,pskhd->schd", grad_score, key_block, preferred_element_type=jnp.float32
    )
    grad_key = jnp.einsum(
        "shcpk,schd->pskhd", grad_score, queries, preferred_element_type=jnp.float32
    )
    return (grad_query, (grad_key, grad_value))


def on_device_any(
    inputs,
    segments,
    cotangent,
    project_in,
    project_out,
    expand_weight,
    reduce_weight,
    query_bias,
    value_bias,
    project_bias,
    expand_bias,
    reduce_bias,
    first_gain,
    first_shift,
    second_gain,
    second_shift,
):
    seq_here, local_len, width = inputs.shape
    groups = lax.axis_size("group")
    total_rows = seq_here * local_len
    head_shape = (seq_here, local_len, HEADS, HEAD_DIM)
    shards = (
        project_in,
        project_out,
        expand_weight,
        reduce_weight,
        query_bias,
        value_bias,
        project_bias,
        expand_bias,
        reduce_bias,
        first_gain,
        first_shift,
        second_gain,
        second_shift,
    )
    whole = (
        lax.all_gather(shards[0], "group", axis=0, tiled=True),
        lax.all_gather(shards[1], "group", axis=0, tiled=True),
        lax.all_gather(shards[2], "group", axis=0, tiled=True),
        lax.all_gather(shards[3], "group", axis=0, tiled=True),
        lax.all_gather(shards[4], "group", axis=0, tiled=True),
        lax.all_gather(shards[5], "group", axis=0, tiled=True),
        lax.all_gather(shards[6], "group", axis=0, tiled=True),
        lax.all_gather(shards[7], "group", axis=0, tiled=True),
        lax.all_gather(shards[8], "group", axis=0, tiled=True),
        lax.all_gather(shards[9], "group", axis=0, tiled=True),
        lax.all_gather(shards[10], "group", axis=0, tiled=True),
        lax.all_gather(shards[11], "group", axis=0, tiled=True),
        lax.all_gather(shards[12], "group", axis=0, tiled=True),
    )
    (
        full_in,
        full_out,
        full_expand,
        full_reduce,
        bias_query,
        bias_value,
        bias_project,
        bias_expand,
        bias_reduce,
        gain_first,
        shift_first,
        gain_second,
        shift_second,
    ) = whole
    group_rank = lax.axis_index("group")
    query_pos = group_rank * local_len + jnp.arange(local_len, dtype=jnp.int32)
    positions = jnp.broadcast_to(query_pos[None, :], (seq_here, local_len))
    end_marks = jnp.where(segments == positions, positions + 1, 0)
    before = carried_in(
        jnp.max(end_marks, axis=1), "group", jnp.maximum, jnp.zeros((seq_here,), jnp.int32)
    )
    inside = lax.cummax(end_marks, axis=1)
    inside = jnp.concatenate([jnp.zeros((seq_here, 1), jnp.int32), inside[:, :-1]], axis=1)
    doc_start = jnp.maximum(before[:, None], inside)
    flat_input = inputs.reshape(total_rows, width).astype(jnp.float32)
    normed_low = layer_norm(
        flat_input, gain_first.astype(jnp.float32), shift_first.astype(jnp.float32)
    ).astype(jnp.bfloat16)
    mixture = product(normed_low, full_in)
    queries = (
        (mixture[:, :width] + bias_query.astype(jnp.float32))
        .astype(jnp.bfloat16)
        .reshape(head_shape)
    )
    key_rows = (
        mixture[:, width : 2 * width].astype(jnp.bfloat16).reshape(seq_here, local_len, width)
    )
    value_rows = (
        (mixture[:, 2 * width :] + bias_value.astype(jnp.float32))
        .astype(jnp.bfloat16)
        .reshape(seq_here, local_len, width)
    )
    initial = (
        jnp.full((seq_here, HEADS, local_len), very_low, jnp.float32),
        jnp.zeros((seq_here, HEADS, local_len), jnp.float32),
        jnp.zeros(head_shape, jnp.float32),
    )
    block_ids = jnp.arange(groups, dtype=jnp.int32)
    running = initial
    pieces = (
        lax.all_gather(key_rows[None], "group", axis=0, tiled=True),
        lax.all_gather(value_rows[None], "group", axis=0, tiled=True),
    )
    piece_count = pieces[0].shape[0]

    def one_piece(state, members):
        key_piece, value_piece, index = members
        updated = attend(
            state,
            key_piece.reshape((1,) + head_shape),
            value_piece.reshape((1,) + head_shape),
            index,
            queries,
            query_pos,
            doc_start,
        )
        return (updated, None)

    running, unused_steps = lax.scan(
        one_piece, running, (pieces[0], pieces[1], jnp.arange(piece_count, dtype=jnp.int32))
    )
    largest, denominator, summed = running
    attended = summed / jnp.transpose(denominator, (0, 2, 1))[..., None]
    log_total = largest + jnp.log(denominator)
    attended_low = attended.reshape(total_rows, width).astype(jnp.bfloat16)
    middle = flat_input + product(attended_low, full_out) + bias_project.astype(jnp.float32)
    second_low = layer_norm(
        middle, gain_second.astype(jnp.float32), shift_second.astype(jnp.float32)
    ).astype(jnp.bfloat16)
    expanded = product(second_low, full_expand) + bias_expand.astype(jnp.float32)
    activated_low = jax.nn.gelu(expanded, approximate=True).astype(jnp.bfloat16)
    result = middle + product(activated_low, full_reduce) + bias_reduce.astype(jnp.float32)
    outputs = result.astype(jnp.bfloat16).reshape(seq_here, local_len, width)
    whole_back = (
        lax.all_gather(shards[0], "group", axis=0, tiled=True),
        lax.all_gather(shards[1], "group", axis=0, tiled=True),
        lax.all_gather(shards[2], "group", axis=0, tiled=True),
        lax.all_gather(shards[3], "group", axis=0, tiled=True),
        lax.all_gather(shards[4], "group", axis=0, tiled=True),
        lax.all_gather(shards[5], "group", axis=0, tiled=True),
        lax.all_gather(shards[6], "group", axis=0, tiled=True),
        lax.all_gather(shards[7], "group", axis=0, tiled=True),
        lax.all_gather(shards[8], "group", axis=0, tiled=True),
        lax.all_gather(shards[9], "group", axis=0, tiled=True),
        lax.all_gather(shards[10], "group", axis=0, tiled=True),
        lax.all_gather(shards[11], "group", axis=0, tiled=True),
        lax.all_gather(shards[12], "group", axis=0, tiled=True),
    )
    keys_back = (
        lax.all_gather(key_rows[None], "group", axis=0, tiled=True),
        lax.all_gather(value_rows[None], "group", axis=0, tiled=True),
    )
    (
        back_in,
        back_out,
        back_expand,
        back_reduce,
        unused_query,
        unused_value,
        unused_project,
        unused_expand,
        unused_reduce,
        back_gain_first,
        back_shift_first,
        back_gain_second,
        back_shift_second,
    ) = whole_back
    grad_rows = cotangent.reshape(total_rows, width).astype(jnp.float32)
    grad_result_low = cotangent.reshape(total_rows, width)
    reduce_bias_grad = column_sum(grad_result_low)
    grad_activated = product_back(grad_result_low, back_reduce)
    unused_gelu, gelu_back = jax.vjp(lambda entry: jax.nn.gelu(entry, approximate=True), expanded)
    grad_expanded_low = gelu_back(grad_activated)[0].astype(jnp.bfloat16)
    expand_bias_grad = column_sum(grad_expanded_low)
    grad_second = product_back(grad_expanded_low, back_expand)
    unused_second, second_back = jax.vjp(
        layer_norm,
        middle,
        back_gain_second.astype(jnp.float32),
        back_shift_second.astype(jnp.float32),
    )
    grad_middle, second_gain_grad, second_shift_grad = second_back(grad_second)
    grad_middle = grad_middle + grad_rows
    reduce_weight_grad = weight_term(activated_low, grad_result_low)
    expand_weight_grad = weight_term(second_low, grad_expanded_low)
    feed_parts = (
        lax.psum_scatter(
            expand_weight_grad.astype(jnp.bfloat16), "group", scatter_dimension=0, tiled=True
        ).astype(jnp.float32),
        lax.psum_scatter(
            reduce_weight_grad.astype(jnp.bfloat16), "group", scatter_dimension=0, tiled=True
        ).astype(jnp.float32),
        lax.psum_scatter(
            expand_bias_grad.astype(jnp.bfloat16), "group", scatter_dimension=0, tiled=True
        ).astype(jnp.float32),
        lax.psum_scatter(
            reduce_bias_grad.astype(jnp.bfloat16), "group", scatter_dimension=0, tiled=True
        ).astype(jnp.float32),
        lax.psum_scatter(
            second_gain_grad.astype(jnp.bfloat16), "group", scatter_dimension=0, tiled=True
        ).astype(jnp.float32),
        lax.psum_scatter(
            second_shift_grad.astype(jnp.bfloat16), "group", scatter_dimension=0, tiled=True
        ).astype(jnp.float32),
    )
    grad_middle_low = grad_middle.astype(jnp.bfloat16)
    project_bias_grad = column_sum(grad_middle_low)
    grad_attended_low = (
        product_back(grad_middle_low, back_out).astype(jnp.bfloat16).reshape(head_shape)
    )
    row_dot = jnp.einsum("schd,schd->shc", grad_attended_low.astype(jnp.float32), attended)

    def back_step(grad_query, members):
        key_piece, value_piece, offset = members
        return attend_back(
            grad_query,
            key_piece.reshape((1,) + head_shape),
            value_piece.reshape((1,) + head_shape),
            offset,
            queries,
            query_pos,
            doc_start,
            log_total,
            grad_attended_low,
            row_dot,
        )

    grad_query, terms = lax.scan(
        back_step, jnp.zeros(head_shape, jnp.float32), (keys_back[0], keys_back[1], block_ids)
    )
    key_terms = terms[0].reshape(groups, seq_here, local_len, width)
    value_terms = terms[1].reshape(groups, seq_here, local_len, width)
    key_grad, value_grad = (
        lax.psum_scatter(
            key_terms.astype(jnp.bfloat16), "group", scatter_dimension=0, tiled=True
        ).astype(jnp.float32),
        lax.psum_scatter(
            value_terms.astype(jnp.bfloat16), "group", scatter_dimension=0, tiled=True
        ).astype(jnp.float32),
    )
    scaling = 1.0 / math.sqrt(HEAD_DIM)
    grad_query_low = (grad_query * scaling).reshape(total_rows, width).astype(jnp.bfloat16)
    grad_key_low = (key_grad * scaling).reshape(total_rows, width).astype(jnp.bfloat16)
    grad_value_low = value_grad.reshape(total_rows, width).astype(jnp.bfloat16)
    query_bias_grad = column_sum(grad_query_low)
    value_bias_grad = column_sum(grad_value_low)
    grad_mixture_low = jnp.concatenate([grad_query_low, grad_key_low, grad_value_low], axis=1)
    grad_normed = product_back(grad_mixture_low, back_in)
    unused_first, first_back = jax.vjp(
        layer_norm,
        flat_input,
        back_gain_first.astype(jnp.float32),
        back_shift_first.astype(jnp.float32),
    )
    grad_entry, first_gain_grad, first_shift_grad = first_back(grad_normed)
    input_grad = (grad_entry + grad_middle).reshape(seq_here, local_len, width)
    project_weight_grad = weight_term(attended_low, grad_middle_low)
    in_weight_grad = weight_term(normed_low, grad_mixture_low)
    mixer_parts = (
        lax.psum_scatter(
            in_weight_grad.astype(jnp.bfloat16), "group", scatter_dimension=0, tiled=True
        ).astype(jnp.float32),
        lax.psum_scatter(
            project_weight_grad.astype(jnp.bfloat16), "group", scatter_dimension=0, tiled=True
        ).astype(jnp.float32),
        lax.psum_scatter(
            query_bias_grad.astype(jnp.bfloat16), "group", scatter_dimension=0, tiled=True
        ).astype(jnp.float32),
        lax.psum_scatter(
            value_bias_grad.astype(jnp.bfloat16), "group", scatter_dimension=0, tiled=True
        ).astype(jnp.float32),
        lax.psum_scatter(
            project_bias_grad.astype(jnp.bfloat16), "group", scatter_dimension=0, tiled=True
        ).astype(jnp.float32),
        lax.psum_scatter(
            first_gain_grad.astype(jnp.bfloat16), "group", scatter_dimension=0, tiled=True
        ).astype(jnp.float32),
        lax.psum_scatter(
            first_shift_grad.astype(jnp.bfloat16), "group", scatter_dimension=0, tiled=True
        ).astype(jnp.float32),
    )
    share_in, share_out, share_expand, share_reduce = (
        mixer_parts[0],
        mixer_parts[1],
        feed_parts[0],
        feed_parts[1],
    )
    share_query, share_value, share_project = (mixer_parts[2], mixer_parts[3], mixer_parts[4])
    share_expand_bias, share_reduce_bias = (feed_parts[2], feed_parts[3])
    share_first_gain, share_first_shift = (mixer_parts[5], mixer_parts[6])
    share_second_gain, share_second_shift = (feed_parts[4], feed_parts[5])
    totals = (
        lax.psum(share_in.astype(jnp.bfloat16), "replica").astype(jnp.float32),
        lax.psum(share_out.astype(jnp.bfloat16), "replica").astype(jnp.float32),
        lax.psum(share_expand.astype(jnp.bfloat16), "replica").astype(jnp.float32),
        lax.psum(share_reduce.astype(jnp.bfloat16), "replica").astype(jnp.float32),
        lax.psum(share_query.astype(jnp.bfloat16), "replica").astype(jnp.float32),
        lax.psum(share_value.astype(jnp.bfloat16), "replica").astype(jnp.float32),
        lax.psum(share_project.astype(jnp.bfloat16), "replica").astype(jnp.float32),
        lax.psum(share_expand_bias.astype(jnp.bfloat16), "replica").astype(jnp.float32),
        lax.psum(share_reduce_bias.astype(jnp.bfloat16), "replica").astype(jnp.float32),
        lax.psum(share_first_gain.astype(jnp.bfloat16), "replica").astype(jnp.float32),
        lax.psum(share_first_shift.astype(jnp.bfloat16), "replica").astype(jnp.float32),
        lax.psum(share_second_gain.astype(jnp.bfloat16), "replica").astype(jnp.float32),
        lax.psum(share_second_shift.astype(jnp.bfloat16), "replica").astype(jnp.float32),
    )
    return (
        outputs,
        input_grad,
        totals[0],
        totals[1],
        totals[2],
        totals[3],
        totals[4],
        totals[5],
        totals[6],
        totals[7],
        totals[8],
        totals[9],
        totals[10],
        totals[11],
        totals[12],
    )


MESH = pl.DeviceIdType.MESH


def flipped(z=0, core=0, y=0, x=0):
    pairs = []
    for me in range(32):
        pairs.append((me, me ^ (8 * z + 4 * core + 2 * y + x)))
    return pairs


FLIP_X = flipped(x=1)
FLIP_Y = flipped(y=1)
FLIP_CORE = flipped(core=1)
FLIP_Z = flipped(z=1)
FLIP_PAIR = flipped(z=2)
INWARD = [(me, me + 8) for me in range(8)] + [(me, me - 8) for me in range(24, 32)]
MIDDLE = [(me, me + 8) for me in range(8, 16)] + [(me, me - 8) for me in range(16, 24)]
OUTWARD = [(me, me - 8) for me in range(8, 16)] + [(me, me + 8) for me in range(16, 24)]


def moved(entries, pairs):
    return lax.ppermute(entries, ("replica", "group"), pairs)


def low(entries):
    return entries.astype(jnp.bfloat16)


def wide(entries):
    return entries.astype(jnp.float32)


def at(entries, index):
    return lax.dynamic_index_in_dim(entries, index, 0, False)


def place():
    replica = lax.axis_index("replica")
    group = lax.axis_index("group")
    core = lax.rem(replica, 2)
    z = lax.div(replica, 2)
    return replica, group, z, core, lax.div(group, 2), lax.rem(group, 2)


def partners(replica, group):
    core = lax.rem(replica, 2)
    z = lax.rem(lax.div(replica, 2), 2)
    y = lax.div(group, 2)
    x = lax.rem(group, 2)
    by_x = (replica, group + 1 - 2 * x)
    by_y = (replica, group + 2 - 4 * y)
    by_both = (replica, group + 3 - 4 * y - 2 * x)
    by_core = (replica + 1 - 2 * core, group)
    by_z = (replica + 2 - 4 * z, group)
    return by_x, by_y, by_both, by_core, by_z


def greet(devices):
    barrier = pltpu.get_barrier_semaphore()
    for device in devices:
        pl.semaphore_signal(barrier, inc=1, device_id=device, device_id_type=MESH)
    pl.semaphore_wait(barrier, len(devices))


def first_exchange_kernel(inp_turned, weights, vec, seg, expand, cot_turned, x_seq, w_full, vecs, segs, inp_out, cot_out, quarter, wide_raw, inp_raw, cot_raw, inp, cot, raw, halves, vec_stage, seg_stage, send, recv, local):
    replica = lax.axis_index("replica")
    group = lax.axis_index("group")
    core = lax.rem(replica, 2)
    level = lax.rem(lax.div(replica, 2), 2)
    y = lax.div(group, 2)
    x = lax.rem(group, 2)
    by_x, by_y, by_both, by_core, by_z = partners(replica, group)
    slot_x, slot_y, slot_both = by_x[1], by_y[1], by_both[1]
    other_x = 1 - x
    other_y = 1 - y
    wires = Wires(send, recv, local)
    load_raw = wires.here(weights, raw)
    load_inp = wires.here(inp_turned, inp_raw)
    load_wide = wires.here(expand, wide_raw)
    load_cot = wires.here(cot_turned, cot_raw)
    greet((by_x, by_y, by_both, by_core, by_z))
    small = [wires.go(vec, vecs.at[group], device) for device in (by_x, by_y, by_both)]
    small += [wires.go(seg.at[pick], segs.at[group], device) for pick, device in ((other_x, by_x), (x, by_y), (other_x, by_both))]
    loads = [wires.here(here, there) for here, there in ((vec, vec_stage), (seg.at[x], seg_stage))]
    load_raw.wait()
    for half in range(2):
        for k in range(3):
            first = 1600 * k + 768 * half
            halves[half, :, 896 * k : 896 * k + 832] = raw[:, first : first + 832]
            halves[half, :, 896 * k + 832 : 896 * k + 896] = jnp.zeros((halves.shape[1], 64), halves.dtype)

    part = 2 * level + core
    mine = rows16(96 * part, 112)
    to_core = rows16(96 * part + 16 * core, 96)
    to_z = rows16(96 * part + 16 * level, 96)
    passed = rows16(96 * (part + 2 - 4 * level) + 16 * (1 - level), 96)
    w_x = wires.go(halves.at[y, mine], w_full.at[group, mine], by_x)
    w_y = wires.go(halves.at[other_y, mine], w_full.at[group, mine], by_y)
    wires.keep(halves.at[y], w_full.at[group])
    load_inp.wait()
    for seq in range(2):
        inp[seq] = inp_raw[seq].T
    wires.keep(inp, inp_out)
    wires.keep(inp.at[x], x_seq.at[group])
    for load, here, there in zip(loads, (vec_stage, seg_stage), (vecs, segs)):
        load.wait()
        wires.keep(here, there.at[group])
    shares = []
    over_z = []

    def share(slot):
        shares.append(wires.go(w_full.at[slot, to_core], w_full.at[slot, to_core], by_core))
        over_z.append((slot, wires.go(w_full.at[slot, to_z], w_full.at[slot, to_z], by_z)))

    wires.drain([w_x, w_y])
    x_block = wires.go(inp.at[other_x], x_seq.at[group], by_x)
    y_block = wires.go(inp.at[x], x_seq.at[group], by_y)
    w_y.wait_recv()
    share(slot_y)
    w_x.wait_recv()
    share(slot_x)
    load_wide.wait()
    quad = lax.rem(replica, 4)
    for pick in range(4):

        @pl.when(quad == pick)
        def _():
            for k in range(4):
                first = 1600 * k + 400 * pick
                quarter[:, 400 * k : 400 * k + 400] = wide_raw[:, first : first + 400]

    load_cot.wait()
    for seq in range(2):
        cot[seq] = cot_raw[seq].T
    wires.keep(cot, cot_out)
    wires.drain([x_block])
    w_more = wires.go(w_full.at[slot_y, mine], w_full.at[slot_y, mine], by_x)
    x_block.wait_recv()
    y_more = wires.go(x_seq.at[slot_x], x_seq.at[slot_x], by_y)
    w_more.wait_recv()
    share(slot_both)
    for slot, copy in over_z:
        copy.wait_recv()
        shares.append(wires.go(w_full.at[slot, passed], w_full.at[slot, passed], by_core))
    for copy in small + shares + [y_block, y_more]:
        copy.wait_recv()
    wires.finish()


def first_exchange(inp, weights, vec, seg, expand, cot):
    any_space = pl.BlockSpec(memory_space=pl.ANY)
    shape = jax.ShapeDtypeStruct
    rows = weights.shape[0]
    turned = inp.shape[:0:-1]
    return pl.pallas_call(
        first_exchange_kernel,
        in_specs=[any_space] * 6,
        out_specs=[any_space] * 6 + [pl.BlockSpec(memory_space=pltpu.VMEM)],
        out_shape=[
            shape((4,) + turned, inp.dtype),
            shape((4, rows, 2688), weights.dtype),
            shape((4,) + vec.shape, vec.dtype),
            shape((4,) + seg.shape[1:], seg.dtype),
            shape((2,) + turned, inp.dtype),
            shape((2,) + turned, cot.dtype),
            shape((rows, 1600), expand.dtype),
        ],
        scratch_shapes=[
            pltpu.VMEM(expand.shape, expand.dtype),
            pltpu.VMEM(inp.shape, inp.dtype),
            pltpu.VMEM(cot.shape, cot.dtype),
            pltpu.VMEM((2,) + turned, inp.dtype),
            pltpu.VMEM((2,) + turned, cot.dtype),
            pltpu.VMEM(weights.shape, weights.dtype),
            pltpu.VMEM((2, rows, 2688), weights.dtype),
            pltpu.VMEM(vec.shape, vec.dtype),
            pltpu.VMEM(seg.shape[1:], seg.dtype),
            pltpu.SemaphoreType.DMA((24,)),
            pltpu.SemaphoreType.DMA((24,)),
            pltpu.SemaphoreType.DMA((16,)),
        ],
        compiler_params=pltpu.CompilerParams(collective_id=0, has_side_effects=True, vmem_limit_bytes=63 * 2**20),
        name="first_exchange",
    )(inp, weights, vec, seg, expand, cot)


def turn_middle_kernel(src, out_in, inp_in, rows_ref, att_out, middle_out, second_out, att, w, inp, send, recv, local):
    replica = lax.axis_index("replica")
    group = lax.axis_index("group")
    y = lax.div(group, 2)
    x = lax.rem(group, 2)
    by_x, by_y, by_both, by_core, by_z = partners(replica, group)
    others = (by_both, by_x, by_y)
    wires = Wires(send, recv, local)
    greet(others)
    copies = [wires.go(src.at[device[1]], att.at[x, y], device) for device in others]
    own = wires.here(src.at[group], att.at[x, y])
    load_w = wires.here(out_in, w)
    load_inp = wires.here(inp_in, inp)
    width = w.shape[0]
    lane = lax.broadcasted_iota(jnp.int32, (1, 128), 1)
    for copy in (own, load_w, load_inp):
        copy.wait()
    for copy in copies:
        copy.wait_recv()
    for seq in range(2):
        rows = pl.ds(256 * seq, 256)
        att_out[rows, 0:768] = att[seq, 0, :, 0:768]
        att_out[rows, 768:896] = jnp.where(lane < 64, att[seq, 0, :, 768:896], att[seq, 1, :, 0:128])
        att_out[rows, 896:width] = att[seq, 1, :, 128 : width - 768]
        middle = inp[seq].astype(jnp.float32) + dot_nn(att_out[rows, :], w[...]) + rows_ref[2:3, :width]
        middle_out[rows, :] = middle
        center = middle - jnp.mean(middle, axis=-1, keepdims=True)
        spread = jnp.mean(center * center, axis=-1, keepdims=True)
        second = center * lax.rsqrt(spread + epsilon) * rows_ref[6:7, :width] + rows_ref[7:8, :width]
        second_out[rows, :width] = second.astype(jnp.bfloat16)
        second_out[rows, width:] = jnp.zeros((256, second_out.shape[1] - width), jnp.bfloat16)
    wires.finish()


def turn_middle(entries, full_out, inputs, rows):
    any_space = pl.BlockSpec(memory_space=pl.ANY)
    vmem = pl.BlockSpec(memory_space=pltpu.VMEM)
    shape = jax.ShapeDtypeStruct
    width = full_out.shape[0]
    return pl.pallas_call(
        turn_middle_kernel,
        in_specs=[any_space, any_space, any_space, vmem],
        out_specs=[vmem, vmem, vmem],
        out_shape=[shape((512, width), jnp.bfloat16), shape((512, width), jnp.float32), shape((512, width + 64), jnp.bfloat16)],
        scratch_shapes=[
            pltpu.VMEM((2, 2) + entries.shape[1:], jnp.bfloat16),
            pltpu.VMEM(full_out.shape, jnp.bfloat16),
            pltpu.VMEM(inputs.shape, jnp.bfloat16),
            pltpu.SemaphoreType.DMA((3,)),
            pltpu.SemaphoreType.DMA((3,)),
            pltpu.SemaphoreType.DMA((3,)),
        ],
        compiler_params=pltpu.CompilerParams(collective_id=1, has_side_effects=True, vmem_limit_bytes=63 * 2**20),
        cost_estimate=pl.CostEstimate(flops=0, bytes_accessed=60 * 2**20, transcendentals=0),
        name="turn_middle",
    )(entries, full_out, inputs, rows)


def padded(entries):
    return jnp.pad(entries, [(0, 0)] * (entries.ndim - 1) + [(0, 64)])


def joined(first, other):
    lane = lax.broadcasted_iota(jnp.int32, (1, 128), 1)
    middle = jnp.where(lane < 64, first[..., 768:896], other[..., 0:128])
    return jnp.concatenate([first[..., :768], middle, other[..., 128:]], axis=-1)


def hold(entries, *until):
    return lax.optimization_barrier((entries,) + until)[0]


def finish_kernel(reduce_ref, expand_ref, total_ref, out_reduce, out_expand, in_ref, out_ref):
    out_reduce[...] = reduce_ref[...].astype(jnp.float32)
    for k in range(4):
        piece = expand_ref[k].astype(jnp.float32)
        for r in range(4):
            out_expand[:, 1600 * r + 400 * k : 1600 * r + 400 * k + 400] = piece[:, 400 * r : 400 * r + 400]
    for k in range(3):
        in_ref[:, 1600 * k : 1600 * k + 1600] = total_ref[k, :, :1600].astype(jnp.float32)
    out_ref[...] = total_ref[3, :, :1600].astype(jnp.float32)


def finish(reduce_quads, quads, total):
    rows, width = quads.shape[1:]
    step = 80
    shape = lambda columns: jax.ShapeDtypeStruct((rows, columns), jnp.float32)
    spec = lambda columns: pl.BlockSpec((step, columns), lambda i: (i, 0))
    return pl.pallas_call(
        finish_kernel,
        grid=(rows // step,),
        in_specs=[pl.BlockSpec((4, step, width), lambda i: (0, i, 0))] * 2 + [pl.BlockSpec((4, step, total.shape[2]), lambda i: (0, i, 0))],
        out_specs=[pl.BlockSpec((4, step, width), lambda i: (0, i, 0)), spec(4 * width), spec(4800), spec(1600)],
        out_shape=[jax.ShapeDtypeStruct(quads.shape, jnp.float32), shape(4 * width), shape(4800), shape(1600)],
        compiler_params=pltpu.CompilerParams(vmem_limit_bytes=63 * 2**20),
        name="finish",
    )(reduce_quads, quads, total)


PIECES = ((0, 512), (512, 1024), (1024, 1600))
HALF = 208


class Wires:
    def __init__(self, send, recv, local):
        self.send, self.recv, self.local = send, recv, local
        self.remotes = self.locals = 0
        self.sent = []
        self.kept = []

    def make(self, src, dst, device):
        i = self.remotes
        assert i < self.send.shape[0]
        self.remotes = i + 1
        return pltpu.make_async_remote_copy(src_ref=src, dst_ref=dst, send_sem=self.send.at[i], recv_sem=self.recv.at[i], device_id=device, device_id_type=MESH)

    def go(self, src, dst, device):
        copy = self.make(src, dst, device)
        copy.start()
        self.sent.append(copy)
        return copy

    def here(self, src, dst):
        i = self.locals
        assert i < self.local.shape[0]
        self.locals = i + 1
        copy = pltpu.make_async_copy(src, dst, self.local.at[i])
        copy.start()
        return copy

    def keep(self, src, dst):
        self.kept.append(self.here(src, dst))

    def drain(self, copies):
        for copy in copies:
            copy.wait_send()
        self.sent = [copy for copy in self.sent if all(copy is not done for done in copies)]

    def finish(self):
        for copy in self.sent:
            copy.wait_send()
        for copy in self.kept:
            copy.wait()


def rows16(start, size):
    return pl.ds(pl.multiple_of(start, 16), size)


def dot_tn(a, b):
    return lax.dot_general(a, b, (((0,), (0,)), ((), ())), preferred_element_type=jnp.float32)


def add_low(a, b):
    return (a.astype(jnp.float32) + b.astype(jnp.float32)).astype(jnp.bfloat16)


def weight_sum(a, b, out):
    width = out.shape[0]
    whole = width // 256

    def chunk(j, carry):
        lanes = pl.ds(pl.multiple_of(256 * j, 256), 256)
        out[lanes, :] = dot_tn(a[:, lanes], b[:, : out.shape[1]]).astype(jnp.bfloat16)
        return carry

    lax.fori_loop(0, whole, chunk, 0)
    if width > 256 * whole:
        out[256 * whole :, :] = dot_tn(a[:, 256 * whole : width], b[:, : out.shape[1]]).astype(jnp.bfloat16)


NT = (((1,), (1,)), ((), ()))

def dot_nt(a, b):
    return lax.dot_general(a, b, NT, preferred_element_type=jnp.float32)

def dot_nn(a, b):
    return jnp.dot(a, b, preferred_element_type=jnp.float32)

BLOCK = 256

def mix_heads_kernel(x_seq, w_in, rows_ref, segc_ref, segr_ref, out_shard, expand_shard, cot, mix, normed, unit_out, o_ref, lse_ref, full_out, full_expand, cots, x_buf, w, stage_out, stage_expand, ot_ref, vt_ref, send, recv, local):
    replica = lax.axis_index("replica")
    group = lax.axis_index("group")
    core = lax.rem(replica, 2)
    y = lax.div(group, 2)
    x = lax.rem(group, 2)
    by_x, by_y, by_both, by_core, by_z = partners(replica, group)
    slot_x, slot_y, slot_both = by_x[1], by_y[1], by_both[1]
    wires = Wires(send, recv, local)
    greet([by_x, by_y, by_core, by_z])
    level = lax.rem(lax.div(replica, 2), 2)
    part = 2 * level + core
    mine = rows16(96 * part, 112)
    to_core = rows16(96 * part + 16 * core, 96)
    to_z = rows16(96 * part + 16 * level, 96)
    passed = rows16(96 * (part + 2 - 4 * level) + 16 * (1 - level), 96)
    out_x = wires.go(out_shard.at[mine], full_out.at[group, mine], by_x)
    out_y = wires.go(out_shard.at[mine], full_out.at[group, mine], by_y)
    expand_x = wires.go(expand_shard, full_expand.at[group], by_x)
    expand_y = wires.go(expand_shard, full_expand.at[group], by_y)
    cot_core = wires.go(cot, cots.at[0], by_core)
    cot_z = wires.go(cot, cots.at[1], by_z)
    load_x = wires.here(x_seq, x_buf)
    load_w = wires.here(w_in, w)
    load_out = wires.here(out_shard, stage_out)
    load_expand = wires.here(expand_shard, stage_expand)
    length = mix.shape[0]
    blocks = length // BLOCK
    lane = lax.broadcasted_iota(jnp.int32, (1, 128), 1)
    lse_ref[...] = jnp.zeros_like(lse_ref)
    half_lanes = pl.ds(pl.multiple_of(768 * y, 128), 896)
    load_x.wait()
    load_w.wait()

    def mix_rows(i, carry):
        rows = pl.ds(pl.multiple_of(256 * i, 256), 256)
        width = x_buf.shape[1]
        entries = x_buf[rows, :].astype(jnp.float32)
        center = entries - jnp.mean(entries, axis=-1, keepdims=True)
        spread = jnp.mean(center * center, axis=-1, keepdims=True)
        unit = center * lax.rsqrt(spread + epsilon)
        unit_out[rows, :] = unit.astype(jnp.bfloat16)
        low_rows = (unit * rows_ref[4:5, :width] + rows_ref[5:6, :width]).astype(jnp.bfloat16)
        normed[rows, :] = low_rows
        mix[rows, 0:896] = (dot_nn(low_rows, w[:, 0:896]) + rows_ref[0:1, half_lanes]).astype(jnp.bfloat16)
        mix[rows, 896:1792] = dot_nn(low_rows, w[:, 896:1792]).astype(jnp.bfloat16)
        mix[rows, 1792:2688] = (dot_nn(low_rows, w[:, 1792:2688]) + rows_ref[1:2, half_lanes]).astype(jnp.bfloat16)
        return carry

    lax.fori_loop(0, 4, mix_rows, 0)
    load_out.wait()
    wires.keep(stage_out, full_out.at[group])
    load_expand.wait()
    wires.keep(stage_expand, full_expand.at[group])
    upper = rows16(96 * part, 64)
    lower = rows16(96 * part + 64, 48)
    top = pl.ds(0, HALF)
    bottom = pl.ds(HALF, 400 - HALF)
    spot = lambda slot, rows: full_out.at[slot, rows]
    more = [wires.make(spot(slot_x, upper), spot(slot_x, upper), by_y), wires.make(spot(slot_y, lower), spot(slot_y, lower), by_x)]
    slots = (slot_x, slot_y, slot_both)
    cores = [wires.make(spot(slot, to_core), spot(slot, to_core), by_core) for slot in slots]
    overs = [wires.make(spot(slot, to_z), spot(slot, to_z), by_z) for slot in slots]
    passes = [wires.make(spot(slot, passed), spot(slot, passed), by_core) for slot in slots]
    expand_more = [wires.make(full_expand.at[slot_x, top], full_expand.at[slot_x, top], by_y), wires.make(full_expand.at[slot_y, bottom], full_expand.at[slot_y, bottom], by_x)]
    cot_both = wires.make(cots.at[1], cots.at[2], by_core)

    def tile_heads(tile, carry):
        at_lanes = lambda off: pl.ds(pl.multiple_of(128 * tile + off, 128), 128)
        ot_ref[...] = jnp.zeros_like(ot_ref)
        vt_ref[...] = mix[:, at_lanes(1792)].T

        def head(h):
            k = jnp.where((lane >= 64 * h) & (lane < 64 * h + 64), mix[:, at_lanes(896)], jnp.bfloat16(0))
            for i in range(blocks):
                low_at, high_at = i * BLOCK, (i + 1) * BLOCK
                q = mix[low_at:high_at, at_lanes(0)] * jnp.bfloat16(0.125)
                s = dot_nt(k[:high_at], q)
                same = segc_ref[:high_at, :] == segr_ref[:, low_at:high_at]
                kpos = lax.broadcasted_iota(jnp.int32, (high_at, BLOCK), 0)
                qpos = lax.broadcasted_iota(jnp.int32, (high_at, BLOCK), 1) + low_at
                s = jnp.where(same & (kpos <= qpos), s, -1e30)
                m = jnp.max(s, axis=0, keepdims=True)
                p = jnp.exp(s - m)
                l = jnp.sum(p, axis=0, keepdims=True)
                ot = dot_nn(vt_ref[64 * h : 64 * h + 64, :high_at], p.astype(jnp.bfloat16))
                ot_ref[64 * h : 64 * h + 64, low_at:high_at] = ot / l
                lse_ref[tile, h : h + 1, low_at:high_at] = m + jnp.log(l)

        head(0)

        @pl.when(tile < 6)
        def _():
            head(1)

        @pl.when(tile == 2)
        def _():
            out_x.wait_recv()
            out_y.wait_recv()
            for copy in more + cores[:2] + overs[:2]:
                copy.start()

        @pl.when(tile == 4)
        def _():
            expand_x.wait_recv()
            expand_y.wait_recv()
            for copy in expand_more:
                copy.start()
            for copy in more:
                copy.wait_recv()
            cores[2].start()
            overs[2].start()

        o_ref[:, at_lanes(0)] = ot_ref[...].T.astype(jnp.bfloat16)
        return carry

    lax.fori_loop(0, 7, tile_heads, 0)
    cot_z.wait_recv()
    cot_both.start()
    for i in range(3):
        overs[i].wait_recv()
        passes[i].start()
    for copy in expand_more + cores + passes + [cot_core, cot_both]:
        copy.wait_recv()
    for copy in more + cores + overs + passes + expand_more + [cot_both]:
        copy.wait_send()
    wires.finish()


def mix_heads(x_seq, w_in, rows, segc, segr, out_shard, expand_shard, cot):
    any_space = pl.BlockSpec(memory_space=pl.ANY)
    vmem = pl.BlockSpec(memory_space=pltpu.VMEM)
    shape = jax.ShapeDtypeStruct
    kind = jnp.bfloat16
    length = x_seq.shape[0]
    buf = lambda *dims: pltpu.VMEM(dims, kind)
    return pl.pallas_call(
        mix_heads_kernel,
        in_specs=[any_space, any_space, vmem, vmem, vmem, any_space, any_space, any_space],
        out_specs=[vmem] * 5 + [any_space] * 3,
        out_shape=[
            shape((length, 2688), kind),
            shape(x_seq.shape, kind),
            shape(x_seq.shape, kind),
            shape((length, 896), kind),
            shape((7, 8, length), jnp.float32),
            shape((4,) + out_shard.shape, kind),
            shape((4,) + expand_shard.shape, kind),
            shape((3,) + cot.shape, kind),
        ],
        scratch_shapes=[
            buf(*x_seq.shape),
            buf(*w_in.shape),
            buf(*out_shard.shape),
            buf(*expand_shard.shape),
            pltpu.VMEM((128, length), jnp.float32),
            buf(128, length),
            pltpu.SemaphoreType.DMA((24,)),
            pltpu.SemaphoreType.DMA((24,)),
            pltpu.SemaphoreType.DMA((8,)),
        ],
        compiler_params=pltpu.CompilerParams(collective_id=6, has_side_effects=True, vmem_limit_bytes=63 * 2**20),
        cost_estimate=pl.CostEstimate(flops=5 * 10**10, bytes_accessed=2**26, transcendentals=0),
        name="mix_heads",
    )(x_seq, w_in, rows, segc, segr, out_shard, expand_shard, cot)


def heads_back_kernel(q_ref, k_ref, v_ref, do_ref, o_ref, lse_ref, segc_ref, segr_ref, normed_ref, share_ref, first_ref, own_ref, pass_ref, result_ref, middle_ref, cot_ref, rows_ref, core_ref, dq_ref, dk_ref, dv_ref, sums_ref, grad_ref, share_out, first_out, result_out, cot_sums, core_out, quads, dqt_ref, odt_ref, pair, own, share_own, got, pair_next, normed_t, result, middle, cot, core_own, core_x, core_y, send, recv, local):
    tile = pl.program_id(0)
    replica = lax.axis_index("replica")
    group = lax.axis_index("group")
    quad = lax.rem(replica, 4)
    quad_z = lax.rem(quad + 2, 4)
    by_x, by_y, by_both, by_core, by_z = partners(replica, group)
    by_pair = (lax.rem(replica + 4, 8), group)
    wires = Wires(send, recv, local)
    pieces = [pl.ds(0, HALF), pl.ds(HALF, 400 - HALF)]
    pass_y = wires.make(pass_ref.at[pieces[0]], got.at[pieces[0]], by_y)
    pass_x = wires.make(pass_ref.at[pieces[1]], got.at[pieces[1]], by_x)
    pair_lower = wires.make(share_ref.at[pieces[1]], pair.at[pieces[1]], by_pair)
    pair_upper = wires.make(own.at[pieces[0]], pair_next, by_pair)
    loads = [
        pltpu.make_async_copy(first_ref, pair.at[pieces[0]], local.at[0]),
        pltpu.make_async_copy(own_ref, own, local.at[1]),
        pltpu.make_async_copy(share_ref, share_own, local.at[2]),
    ]
    x = lax.rem(group, 2)
    y = lax.div(group, 2)
    out_rows = (1 - y, y)
    out_x = [wires.make(core_ref.at[2 * row + 1 - x], core_x.at[i], by_x) for i, row in enumerate(out_rows)]
    out_y = wires.make(core_own.at[0], core_y, by_y)
    more_loads = [pltpu.make_async_copy(core_ref.at[2 * row + x], core_own.at[i], local.at[8 + i]) for i, row in enumerate(out_rows)]
    more_loads += [
        pltpu.make_async_copy(result_ref, result, local.at[5]),
        pltpu.make_async_copy(middle_ref, middle, local.at[6]),
        pltpu.make_async_copy(cot_ref, cot, local.at[7]),
    ]
    keeps = [pltpu.make_async_copy(pair.at[rows], quads.at[quad, rows], local.at[3 + i]) for i, rows in enumerate(pieces)]
    overs = [wires.make(pair.at[rows], quads.at[quad, rows], by_z) for rows in pieces]
    cores = [wires.make(pair.at[rows], quads.at[quad, rows], by_core) for rows in pieces]
    passes = [wires.make(quads.at[quad_z, rows], quads.at[quad_z, rows], by_core) for rows in pieces]

    def spread(i):
        keeps[i].start()
        overs[i].start()
        cores[i].start()

    @pl.when(tile == 0)
    def _():
        greet([by_pair, by_x, by_y, by_core, by_z])
        for copy in [pass_y, pass_x, pair_lower] + loads + more_loads:
            copy.start()
        normed_t[...] = normed_ref[...].T

    @pl.when(tile == 1)
    def _():
        for copy in loads:
            copy.wait()
        spread(0)

    @pl.when(tile == 2)
    def _():
        pass_y.wait()
        pass_x.wait()
        own[...] = add_low(own[...], got[...])
        for copy in out_x:
            copy.start()

    @pl.when(tile == 3)
    def _():
        for copy in more_loads:
            copy.wait()
        cot_sums[...] = jnp.zeros_like(cot_sums)
        for seq in range(2):
            rows = pl.ds(256 * seq, 256)
            final = result[rows, :] + middle[rows, :] + rows_ref[3:4, : result.shape[1]]
            result_out[seq] = final.astype(jnp.bfloat16).T
            cot_sums[0:1, :] += jnp.sum(cot[rows, :].astype(jnp.float32), axis=0, keepdims=True)

    @pl.when(tile == 4)
    def _():
        pair_lower.wait()
        pair_upper.start()
        pair[HALF:, :] = add_low(pair[HALF:, :], share_own[HALF:, :])
        spread(1)
        overs[0].wait_recv()
        passes[0].start()

    @pl.when(tile == 5)
    def _():
        for i in range(2):
            out_x[i].wait()
            core_own[i] = add_low(core_own[i], core_x[i])
        out_y.start()

    length = q_ref.shape[0]
    blocks = length // BLOCK
    lane = lax.broadcasted_iota(jnp.int32, (1, 128), 1)
    dqt_ref[...] = jnp.zeros_like(dqt_ref)
    odt_ref[...] = (do_ref[...].astype(jnp.float32) * o_ref[...].astype(jnp.float32)).T

    def head(h):
        mine = (lane >= 64 * h) & (lane < 64 * h + 64)
        dot_row = jnp.sum(odt_ref[64 * h : 64 * h + 64, :], axis=0, keepdims=True)
        for j in range(blocks):
            low, high = j * BLOCK, (j + 1) * BLOCK
            rest = length - low
            q = q_ref[low:, :] * jnp.bfloat16(0.125)
            do = do_ref[low:, :]
            k = jnp.where(mine, k_ref[low:high, :], jnp.bfloat16(0))
            v = jnp.where(mine, v_ref[low:high, :], jnp.bfloat16(0))
            s = dot_nt(k, q)
            same = segc_ref[low:high, :] == segr_ref[:, low:]
            kpos = lax.broadcasted_iota(jnp.int32, (BLOCK, rest), 0)
            qpos = lax.broadcasted_iota(jnp.int32, (BLOCK, rest), 1)
            p = jnp.where(same & (kpos <= qpos), jnp.exp(s - lse_ref[0, h : h + 1, low:]), 0.0)
            dp = dot_nt(v, do)
            ds = (p * (dp - dot_row[:, low:])).astype(jnp.bfloat16)
            dv = dot_nn(p.astype(jnp.bfloat16), do)
            dk = dot_nn(ds, q)
            if h == 0:
                dv_ref[low:high, :] = jnp.where(mine, dv, 0.0).astype(jnp.bfloat16)
                dk_ref[low:high, :] = jnp.where(mine, dk, 0.0).astype(jnp.bfloat16)
            else:
                dv_ref[low:high, :] = jnp.where(mine, dv.astype(jnp.bfloat16), dv_ref[low:high, :])
                dk_ref[low:high, :] = jnp.where(mine, dk.astype(jnp.bfloat16), dk_ref[low:high, :])
            dqt_ref[:, low:] += dot_nn(k.T, ds)

    head(0)

    @pl.when(tile < 6)
    def _():
        head(1)

    dq_ref[...] = (dqt_ref[...].T * 0.125).astype(jnp.bfloat16)

    row = lax.broadcasted_iota(jnp.int32, (8, 128), 0)
    sum_q = jnp.sum(dq_ref[...].astype(jnp.float32), axis=0, keepdims=True)
    sum_v = jnp.sum(dv_ref[...].astype(jnp.float32), axis=0, keepdims=True)
    sums_ref[...] = jnp.where(row == 0, sum_q, jnp.where(row == 1, sum_v, 0.0))

    grads = jnp.concatenate([dq_ref[...], dk_ref[...], dv_ref[...]], axis=1)
    weights = dot_nn(normed_t[...], grads).astype(jnp.bfloat16)
    for i in range(3):
        grad_ref[i] = weights[:, 128 * i : 128 * i + 128]

    @pl.when(tile == 6)
    def _():
        overs[1].wait_recv()
        passes[1].start()
        share_out[...] = own[...]
        out_y.wait()
        width = core_own.shape[2]
        core_out[:, :width] = add_low(core_own[1], core_y[...])
        core_out[:, width:] = jnp.zeros((core_out.shape[0], core_out.shape[1] - width), jnp.bfloat16)
        pair_upper.wait()
        first_out[...] = add_low(own[:HALF, :], pair_next[...])
        for copy in cores + passes + keeps:
            copy.wait()
        for copy in overs:
            copy.wait_send()


def heads_back(qkv, grad, out, lse, segc, segr, normed, share, first, own, passed, result, middle, cot, rows, out_core):
    length = qkv.shape[0]
    width = share.shape[1]
    buf = lambda *dims: pltpu.VMEM(dims, jnp.bfloat16)
    still = lambda *dims: pl.BlockSpec(dims, lambda t: (0,) * len(dims))
    spec = lambda off: pl.BlockSpec((length, 128), lambda t: (0, t + off))
    one = pl.BlockSpec((length, 128), lambda t: (0, t))
    shape = jax.ShapeDtypeStruct((length, 896), jnp.bfloat16)
    return pl.pallas_call(
        heads_back_kernel,
        grid=(7,),
        in_specs=[spec(0), spec(7), spec(14), one, one, pl.BlockSpec((1, 8, length), lambda t: (t, 0, 0)), pl.BlockSpec((length, 1), lambda t: (0, 0)), pl.BlockSpec((1, length), lambda t: (0, 0)), still(*normed.shape)] + [pl.BlockSpec(memory_space=pl.ANY)] * 7 + [still(*rows.shape), pl.BlockSpec(memory_space=pl.ANY)],
        out_specs=[one, one, one, pl.BlockSpec((8, 128), lambda t: (0, t)), pl.BlockSpec((3, width, 128), lambda t: (0, 0, t)), still(*share.shape), still(*first.shape), still(2, width, 256), still(8, width), still(208, width + 64), pl.BlockSpec(memory_space=pl.ANY)],
        out_shape=[
            shape,
            shape,
            shape,
            jax.ShapeDtypeStruct((8, 896), jnp.float32),
            jax.ShapeDtypeStruct((3, width, 896), jnp.bfloat16),
            jax.ShapeDtypeStruct(share.shape, share.dtype),
            jax.ShapeDtypeStruct(first.shape, share.dtype),
            jax.ShapeDtypeStruct((2, width, 256), share.dtype),
            jax.ShapeDtypeStruct((8, width), jnp.float32),
            jax.ShapeDtypeStruct((208, width + 64), share.dtype),
            jax.ShapeDtypeStruct((4,) + share.shape, share.dtype),
        ],
        scratch_shapes=[pltpu.VMEM((128, length), jnp.float32), pltpu.VMEM((128, length), jnp.float32), buf(400, width), buf(400, width), buf(400, width), buf(400, width), buf(HALF, width), buf(width, length), pltpu.VMEM(result.shape, jnp.float32), pltpu.VMEM(middle.shape, jnp.float32), buf(*cot.shape), buf(2, 208, width), buf(2, 208, width), buf(208, width), pltpu.SemaphoreType.DMA((16,)), pltpu.SemaphoreType.DMA((16,)), pltpu.SemaphoreType.DMA((10,))],
        compiler_params=pltpu.CompilerParams(vmem_limit_bytes=63 * 2**20, collective_id=4, has_side_effects=True),
        cost_estimate=pl.CostEstimate(flops=int(13 * 5 * 2 * length * length * 64 * 2), bytes_accessed=16 * length * 896, transcendentals=13 * length * length // 2),
        name="heads_back",
    )(qkv, qkv, qkv, grad, out, lse, segc, segr, normed, share, first, own, passed, result, middle, cot, rows, out_core)

def feed_all_kernel(second, cot_in, cots, expand_part, reduce_shard, middle_in, out_in, bias, rows_ref, act_out, back_out, second_out, reduce_out, low_out, att_out, gs_out, own_out, pass_out, sum_out, norm_sums, wexp, wred, s, c, a, b, gs, got_core, got_z, rg, got_x, got_y, send, recv, local):
    replica = lax.axis_index("replica")
    group = lax.axis_index("group")
    quad = lax.rem(replica, 4)
    y = lax.div(group, 2)
    x = lax.rem(group, 2)
    by_x, by_y, by_both, by_core, by_z = partners(replica, group)
    slot_x, slot_y, slot_both = by_x[1], by_y[1], by_both[1]
    wires = Wires(send, recv, local)
    greet([by_x, by_y, by_core, by_z])
    width = wexp.shape[0]
    block = lambda rel: pl.ds(512 * rel, 512)
    sec_core = wires.go(second, s.at[block(1)], by_core)
    sec_z = wires.go(second, s.at[block(2)], by_z)
    quarter = reduce_shard.at[rows16(400 * quad, 400)]
    spot = lambda rank: rows16(400 * rank, 400)
    red_x = wires.go(quarter, wred.at[spot(group)], by_x)
    red_y = wires.go(quarter, wred.at[spot(group)], by_y)
    load_s = wires.here(second, s.at[block(0)])
    load_e = wires.here(expand_part, wexp)
    load_r = wires.here(quarter, wred.at[spot(group)])
    load_m = wires.here(middle_in, gs_out)
    load_c = [wires.here(cot_in, c.at[block(0)])] + [wires.here(cots.at[i], c.at[block(i + 1)]) for i in range(3)]
    sum_out[...] = jnp.zeros_like(sum_out)
    root = 0.7978845608028654

    def gelu(u):
        square = u * u
        t = jnp.tanh(root * u * (1.0 + 0.044715 * square))
        half = 0.5 * (1.0 + t)
        slope = half + (0.5 * root) * u * (1.0 - t * t) * (1.0 + (3.0 * 0.044715) * square)
        return u * half, slope

    def steps(rel, body):
        def one(i, carry):
            body(pl.ds(pl.multiple_of(512 * rel + 256 * i, 256), 256))
            return carry

        lax.fori_loop(0, 2, one, 0)

    def keep_back(rows, low_at, high_at, back):
        back = back.astype(jnp.bfloat16)
        b[rows, low_at:high_at] = back
        sum_out[:, low_at:high_at] += jnp.sum(back.astype(jnp.float32).reshape(32, 8, high_at - low_at), axis=0)

    def up_only(rows):
        entries = s[rows, :width]
        for low_at, high_at in PIECES:
            act, slope = gelu(dot_nn(entries, wexp[:, low_at:high_at]) + bias[:, low_at:high_at])
            a[rows, low_at:high_at] = act.astype(jnp.bfloat16)
            b[rows, low_at:high_at] = slope.astype(jnp.bfloat16)

    def finish_rows(rows):
        gs[rows, width:] = jnp.zeros((256, gs.shape[1] - width), jnp.bfloat16)
        gs[rows, :width] = dot_nt(b[rows, :], wexp[...]).astype(jnp.bfloat16)

    def back_only(rows):
        cot = c[rows, :]
        for low_at, high_at in PIECES:
            keep_back(rows, low_at, high_at, dot_nt(cot, wred[low_at:high_at, :]) * b[rows, low_at:high_at].astype(jnp.float32))
        finish_rows(rows)

    def both(rows):
        entries = s[rows, :width]
        cot = c[rows, :]
        for low_at, high_at in PIECES:
            act, slope = gelu(dot_nn(entries, wexp[:, low_at:high_at]) + bias[:, low_at:high_at])
            a[rows, low_at:high_at] = act.astype(jnp.bfloat16)
            keep_back(rows, low_at, high_at, dot_nt(cot, wred[low_at:high_at, :]) * slope)
        finish_rows(rows)

    load_s.wait()
    load_e.wait()
    steps(0, up_only)
    sec_core.wait_recv()
    steps(1, up_only)
    red_x.wait_recv()
    more_y = wires.go(wred.at[rows16(400 * slot_x, HALF)], wred.at[rows16(400 * slot_x, HALF)], by_y)
    red_y.wait_recv()
    more_x = wires.go(wred.at[rows16(400 * slot_y + HALF, 400 - HALF)], wred.at[rows16(400 * slot_y + HALF, 400 - HALF)], by_x)
    sec_z.wait_recv()
    sec_both = wires.go(s.at[block(2)], s.at[block(3)], by_core)
    load_r.wait()
    for copy in load_c:
        copy.wait()
    more_x.wait_recv()
    more_y.wait_recv()
    wires.keep(wred, reduce_out)
    sec_both.wait_recv()
    wires.keep(s, second_out)
    base = wires.remotes
    wires.remotes = base + 4

    def far_copies(half):
        piece = pl.ds(pl.multiple_of(256 * half, 256), 256)
        third = pl.ds(pl.multiple_of(1536 + 256 * half, 256), 256)
        second_rows = pl.ds(pl.multiple_of(1024 + 256 * half, 256), 256)
        near = pltpu.make_async_remote_copy(src_ref=gs.at[third], dst_ref=got_core.at[1, piece], send_sem=send.at[base + half], recv_sem=recv.at[base + half], device_id=by_core, device_id_type=MESH)
        over = pltpu.make_async_remote_copy(src_ref=gs.at[second_rows], dst_ref=got_z.at[piece], send_sem=send.at[base + 2 + half], recv_sem=recv.at[base + 2 + half], device_id=by_z, device_id_type=MESH)
        return third, second_rows, piece, near, over

    def far_half(half, carry):
        third, second_rows, piece, near, over = far_copies(half)
        both(third)
        near.start()
        both(second_rows)
        near.wait_recv()
        gs[second_rows, :] = add_low(gs[second_rows, :], got_core[1, piece, :])
        over.start()
        return carry

    lax.fori_loop(0, 2, far_half, 0)
    wires.keep(a, act_out)
    weight_sum(a, c, rg)
    x_copies = [wires.go(rg.at[rows16(400 * slot, HALF)], got_x.at[i], by_x) for i, slot in enumerate((slot_x, slot_both))]
    y_copies = [wires.go(rg.at[rows16(400 * slot + HALF, 400 - HALF)], got_y.at[i], by_y) for i, slot in enumerate((slot_y, slot_both))]
    steps(1, back_only)
    gs_core = wires.go(gs.at[block(1)], got_core.at[0], by_core)
    steps(0, back_only)
    wires.keep(b, back_out)
    load_w = wires.here(out_in, wexp)
    load_m.wait()
    gs_core.wait_recv()
    for half in range(2):
        third, second_rows, piece, near, over = far_copies(half)
        over.wait_recv()
        over.wait_send()
        near.wait_send()
    load_w.wait()
    norm_sums[...] = jnp.zeros_like(norm_sums)
    lanes = lax.broadcasted_iota(jnp.int32, (1, 128), 1)
    for seq in range(2):
        stage = got_core.at[1 - seq]

        def norm_back(j, carry):
            rows = pl.ds(pl.multiple_of(256 * seq + 128 * j, 128), 128)
            first = pl.ds(pl.multiple_of(128 * j, 128), 128)
            other = pl.ds(pl.multiple_of(256 + 128 * j, 128), 128)
            grad = gs[rows, :width].astype(jnp.float32) + got_core[0, rows, :width].astype(jnp.float32) + got_z[rows, :width].astype(jnp.float32)
            middle = gs_out[rows, :]
            center = middle - jnp.mean(middle, axis=-1, keepdims=True)
            scale = lax.rsqrt(jnp.mean(center * center, axis=-1, keepdims=True) + epsilon)
            unit = center * scale
            q = grad * rows_ref[6:7, :width]
            grad_middle = c[rows, :].astype(jnp.float32) + scale * (
                q - jnp.mean(q, axis=-1, keepdims=True) - unit * jnp.mean(q * unit, axis=-1, keepdims=True)
            )
            gs_out[rows, :] = grad_middle
            grad_low = grad_middle.astype(jnp.bfloat16)
            gs[rows, :width] = grad_low
            norm_sums[0:1, :] += jnp.sum(grad * unit, axis=0, keepdims=True)
            norm_sums[1:2, :] += jnp.sum(grad, axis=0, keepdims=True)
            norm_sums[2:3, :] += jnp.sum(grad_low.astype(jnp.float32), axis=0, keepdims=True)
            att = dot_nt(grad_low, wexp[...]).astype(jnp.bfloat16)
            stage[first, 0:768] = att[:, 0:768]
            stage[first, 768:896] = jnp.where(lanes < 64, att[:, 768:896], jnp.bfloat16(0))
            stage[other, 0:128] = jnp.where(lanes >= 64, att[:, 768:896], jnp.bfloat16(0))
            stage[other, 128 : width - 768] = att[:, 896:width]
            stage[other, width - 768 : 896] = jnp.zeros((128, 896 + 768 - width), jnp.bfloat16)
            return carry

        lax.fori_loop(0, 2, norm_back, 0)
        for half in range(2):
            wires.keep(stage.at[pl.ds(256 * half, 256), pl.ds(0, 896)], att_out.at[seq, half])
    wires.keep(gs.at[block(0)], low_out)
    for copy in x_copies + y_copies:
        copy.wait_recv()
    own_out[:HALF] = add_low(rg[rows16(400 * group, HALF), :], got_x[0])
    own_out[HALF:] = add_low(rg[rows16(400 * group + HALF, 400 - HALF), :], got_y[0])
    pass_out[:HALF] = add_low(rg[rows16(400 * slot_y, HALF), :], got_x[1])
    pass_out[HALF:] = add_low(rg[rows16(400 * slot_x + HALF, 400 - HALF), :], got_y[1])
    wires.finish()


def feed_all(second, cot, cots, expand_part, reduce_shard, middle, full_out, bias, rows_in):
    any_space = pl.BlockSpec(memory_space=pl.ANY)
    vmem = pl.BlockSpec(memory_space=pltpu.VMEM)
    shape = jax.ShapeDtypeStruct
    kind = jnp.bfloat16
    rows, full = second.shape
    width = expand_part.shape[0]
    buf = lambda *dims: pltpu.VMEM(dims, kind)
    return pl.pallas_call(
        feed_all_kernel,
        in_specs=[any_space] * 7 + [vmem, vmem],
        out_specs=[any_space] * 6 + [vmem] * 5,
        out_shape=[
            shape((4 * rows, width), kind),
            shape((4 * rows, width), kind),
            shape((4 * rows, full), kind),
            shape((width, width), kind),
            shape((rows, full), kind),
            shape((2, 2, 256, 896), kind),
            shape((rows, width), jnp.float32),
            shape((400, width), kind),
            shape((400, width), kind),
            shape((8, width), jnp.float32),
            shape((8, width), jnp.float32),
        ],
        scratch_shapes=[
            buf(width, width),
            buf(width, width),
            buf(4 * rows, full),
            buf(4 * rows, width),
            buf(4 * rows, width),
            buf(4 * rows, width),
            buf(4 * rows, full),
            buf(2, rows, full),
            buf(rows, full),
            buf(width, width),
            buf(2, HALF, width),
            buf(2, 400 - HALF, width),
            pltpu.SemaphoreType.DMA((16,)),
            pltpu.SemaphoreType.DMA((16,)),
            pltpu.SemaphoreType.DMA((20,)),
        ],
        compiler_params=pltpu.CompilerParams(collective_id=5, has_side_effects=True, vmem_limit_bytes=63 * 2**20),
        cost_estimate=pl.CostEstimate(flops=10**11, bytes_accessed=2**26, transcendentals=0),
        name="feed_all",
    )(second, cot, cots, expand_part, reduce_shard, middle, full_out, bias, rows_in)


def turn_more_kernel(grad_att, back, second, act, wred_in, pass_in, att_in, grad_in, own_in, heads_out, result_out, share_out, first_out, own_out, pass_out, core_out, att, grad, stage, b, s, a, wred, rg, result, got_core, got_z, got, got_x, got_y, pair, send, recv, local):
    replica = lax.axis_index("replica")
    group = lax.axis_index("group")
    core = lax.rem(replica, 2)
    y = lax.div(group, 2)
    x = lax.rem(group, 2)
    by_x, by_y, by_both, by_core, by_z = partners(replica, group)
    by_pair = (lax.rem(replica + 4, 8), group)
    slot_x, slot_y, slot_both = by_x[1], by_y[1], by_both[1]
    wires = Wires(send, recv, local)
    load_a = wires.here(act, a)
    load_w = wires.here(wred_in, wred)
    load_own = wires.here(grad_att.at[x, y], stage)
    load_s = wires.here(second, s)
    load_b = wires.here(back, b)
    load_att = wires.here(att_in, att)
    load_grad = wires.here(grad_in, grad)
    greet([by_x, by_y, by_both, by_core, by_z, by_pair])
    width = wred.shape[0]
    block = lambda rel: pl.ds(512 * rel, 512)
    pass_y = wires.go(pass_in.at[pl.ds(0, HALF)], got.at[pl.ds(0, HALF)], by_y)
    pass_x = wires.go(pass_in.at[pl.ds(HALF, 400 - HALF)], got.at[pl.ds(HALF, 400 - HALF)], by_x)
    load_a.wait()
    load_w.wait()

    def rows_out(rel):
        def one(i, carry):
            rows = pl.ds(pl.multiple_of(512 * rel + 256 * i, 256), 256)
            result[rows, :] = dot_nn(a[rows, :], wred[...]).astype(jnp.bfloat16)
            return carry

        lax.fori_loop(0, 2, one, 0)

    rows_out(3)
    to_both = wires.go(result.at[block(3)], got_core.at[1], by_core)
    rows_out(2)
    wires.drain([pass_y, pass_x])
    turns = []
    for device in (by_both, by_x, by_y):
        there = device[1]
        turns.append(wires.go(grad_att.at[lax.rem(there, 2), lax.div(there, 2)], heads_out.at[group], device))
    to_both.wait_recv()
    result[block(2), :] = add_low(result[block(2), :], got_core[1])
    to_z = wires.go(result.at[block(2)], got_z, by_z)
    pass_y.wait_recv()
    pass_x.wait_recv()
    share_out[...] = add_low(own_in[...], got[...])
    pair_upper = wires.go(share_out.at[pl.ds(0, HALF)], pair, by_pair)
    load_own.wait()
    wires.keep(stage, heads_out.at[group])
    load_s.wait()
    load_b.wait()
    weight_sum(s, b, rg)
    x_copies = [wires.go(rg.at[rows16(400 * slot, HALF)], got_x.at[i], by_x) for i, slot in enumerate((slot_x, slot_both))]
    y_copies = [wires.go(rg.at[rows16(400 * slot + HALF, 400 - HALF)], got_y.at[i], by_y) for i, slot in enumerate((slot_y, slot_both))]
    rows_out(1)
    to_core = wires.go(result.at[block(1)], got_core.at[0], by_core)
    rows_out(0)
    load_att.wait()
    load_grad.wait()
    weight_sum(att, grad, wred)
    out_core = [wires.go(wred.at[rows16(400 * r + 192 * (1 - core), 208)], core_out.at[r], by_core) for r in range(4)]
    for r in range(4):
        out_core[r].wait_recv()
        core_out[r] = add_low(wred[rows16(400 * r + 192 * core, 208), :], core_out[r])
    to_core.wait_recv()
    to_z.wait_recv()
    result_out[...] = result[block(0), :].astype(jnp.float32) + got_core[0].astype(jnp.float32) + got_z[...].astype(jnp.float32)
    pair_upper.wait_recv()
    first_out[...] = add_low(share_out[:HALF, :], pair[...])
    for copy in x_copies + y_copies:
        copy.wait_recv()
    own_out[:HALF] = add_low(rg[rows16(400 * group, HALF), :], got_x[0])
    own_out[HALF:] = add_low(rg[rows16(400 * group + HALF, 400 - HALF), :], got_y[0])
    pass_out[:HALF] = add_low(rg[rows16(400 * slot_y, HALF), :], got_x[1])
    pass_out[HALF:] = add_low(rg[rows16(400 * slot_x + HALF, 400 - HALF), :], got_y[1])
    for copy in turns:
        copy.wait_recv()
    wires.finish()


def turn_more(grad_att, back, second, act, wred, passed, att, grad, own):
    any_space = pl.BlockSpec(memory_space=pl.ANY)
    vmem = pl.BlockSpec(memory_space=pltpu.VMEM)
    shape = jax.ShapeDtypeStruct
    kind = jnp.bfloat16
    width = wred.shape[0]
    rows = act.shape[0] // 4
    buf = lambda *dims: pltpu.VMEM(dims, kind)
    return pl.pallas_call(
        turn_more_kernel,
        in_specs=[any_space] * 8 + [vmem],
        out_specs=[any_space] + [vmem] * 6,
        out_shape=[
            shape((4,) + grad_att.shape[2:], kind),
            shape((rows, width), jnp.float32),
            shape((400, width), kind),
            shape((HALF, width), kind),
            shape((400, width), kind),
            shape((400, width), kind),
            shape((4, 208, width), kind),
        ],
        scratch_shapes=[
            buf(rows, width),
            buf(*grad.shape),
            buf(*grad_att.shape[2:]),
            buf(4 * rows, width),
            buf(*second.shape),
            buf(4 * rows, width),
            buf(width, width),
            buf(width, width),
            buf(4 * rows, width),
            buf(2, rows, width),
            buf(rows, width),
            buf(400, width),
            buf(2, HALF, width),
            buf(2, 400 - HALF, width),
            buf(HALF, width),
            pltpu.SemaphoreType.DMA((18,)),
            pltpu.SemaphoreType.DMA((18,)),
            pltpu.SemaphoreType.DMA((10,)),
        ],
        compiler_params=pltpu.CompilerParams(collective_id=2, has_side_effects=True, vmem_limit_bytes=63 * 2**20),
        cost_estimate=pl.CostEstimate(flops=3 * 10**10, bytes_accessed=2**26, transcendentals=0),
        name="turn_more",
    )(grad_att, back, second, act, wred, passed, att, grad, own)


def arrive(here, there, total, lane, k, y, mine):
    first = jnp.where(y == 0, here, there)
    other = jnp.where(y == 0, there, here)
    rows = pl.ds(mine, 208)
    total[k, rows, 0:768] = first[:, 0:768]
    total[k, rows, 768:896] = jnp.where(lane < 64, first[:, 768:896], other[:, 0:128])
    total[k, rows, 896:1664] = other[:, 128:896]


def last_kernel(dq, dk, dv, grad_in, unit_in, w_in, share_in, share_expand, first_expand, vec, gm_in, inp_in, gain, total, grad_turned, vec_total, wide_total, quads, grad_out, d, unit_rows, w, part, c_buf, x_buf, y_buf, line_buf, line_mid, gn, gn_y, gn_cross, inp, pair_buf, vec_got, vec_own, vec_core, vec_z, more_got, more_core, more_z, send, recv, local):
    replica = lax.axis_index("replica")
    group = lax.axis_index("group")
    core = lax.rem(replica, 2)
    quad = lax.rem(replica, 4)
    quad_z = lax.rem(quad + 2, 4)
    z = lax.div(replica, 2)
    y = lax.div(group, 2)
    x = lax.rem(group, 2)
    by_x, by_y, by_both, by_core, by_z = partners(replica, group)
    outer = (z == 0) | (z == 3)
    inner = jnp.logical_not(outer)
    by_line = (jnp.where(z == 0, replica + 2, jnp.where(z == 3, replica - 2, jnp.where(z == 1, replica - 2, replica + 2))), group)
    by_middle = (jnp.where(z == 1, replica + 2, replica - 2), group)
    lines_z = [(lax.rem(replica + 2 * k, 8), group) for k in (1, 2, 3)]
    by_pair = lines_z[1]
    wires = Wires(send, recv, local)
    greet([by_x, by_y, by_both, by_core] + lines_z)
    mine = pl.multiple_of(192 * core, 16)
    theirs = pl.multiple_of(192 * (1 - core), 16)
    other_x = 1 - x
    other_y = 1 - y
    far = 2 * other_y
    near = 2 * y
    width = w.shape[0]
    lane = lax.broadcasted_iota(jnp.int32, (1, 128), 1)
    halves = [(pl.ds(mine + 112 * m, 112 - 16 * m), pl.ds(112 * m, 112 - 16 * m)) for m in range(2)]
    pieces = [pl.ds(0, 208), pl.ds(208, 192)]

    pair_lower = wires.go(share_expand.at[pieces[1]], pair_buf, by_pair)
    c_copies = []
    part_loads = []
    for k in range(3):
        c_copies.append([wires.go(grad_in.at[k, rows16(400 * r + theirs, 208)], c_buf.at[k, r], by_core) for r in range(4)])
        part_loads.append([wires.here(grad_in.at[k, pl.ds(400 * r + mine, 208)], part.at[k, r]) for r in range(4)])
    loads = [wires.here(part, d.at[k]) for k, part in enumerate((dq, dk, dv))]
    load_w = [wires.here(w_in, w), wires.here(unit_in, unit_rows)]
    load_share = wires.here(share_in, total.at[3, pl.ds(mine, 208)])
    vec_group = [wires.go(vec.at[device[1]], vec_got.at[group], device) for device in (by_x, by_y, by_both)]

    def spread(value, rows):
        wires.keep(value, quads.at[quad, rows])
        over = wires.go(value, quads.at[quad, rows], by_z)
        return over, wires.go(value, quads.at[quad, rows], by_core)

    def spread_on(over, rows):
        over.wait_recv()
        return wires.go(quads.at[quad_z, rows], quads.at[quad_z, rows], by_core)

    load_gm = wires.here(gm_in, grad_out)
    load_inp = wires.here(inp_in, inp)

    def line_start(k, m):
        rows, merge = halves[m]
        into = wires.make(total.at[k, rows], line_buf.at[k, merge], by_line)
        middle = wires.make(total.at[k, rows], line_mid.at[k, merge], by_middle)
        back = wires.make(total.at[k, rows], line_buf.at[k, merge], by_line)

        @pl.when(outer)
        def _():
            if m == 1:
                lines[k, 0][0].wait_send()
            into.start()

        lines[k, m] = into, middle, back

    def line_second(k, m):
        rows, merge = halves[m]
        into, middle, back = lines[k, m]

        @pl.when(inner)
        def _():
            into.wait_recv()
            total[k, rows] = add_low(total[k, rows], line_buf[k, merge])
            middle.start()

    def line_third(k, m):
        rows, merge = halves[m]
        into, middle, back = lines[k, m]

        @pl.when(inner)
        def _():
            middle.wait_recv()
            middle.wait_send()
            total[k, rows] = add_low(total[k, rows], line_mid[k, merge])
            back.start()

    def line_fourth(k, m):
        rows, merge = halves[m]
        into, middle, back = lines[k, m]

        @pl.when(outer)
        def _():
            if m == 1:
                into.wait_send()
            back.wait_recv()
            total[k, rows] = line_buf[k, merge]

        @pl.when(inner)
        def _():
            back.wait_send()

    lines = {}
    x_copies = {}
    y_copies = {}

    def core_sum(k):
        for r in range(4):
            part_loads[k][r].wait()
            c_copies[k][r].wait_recv()
            c_buf[k, r] = add_low(c_buf[k, r], part[k, r])

    def x_go(k, i):
        row = (other_y, y)[i]
        x_copies[k, i] = wires.go(c_buf.at[k, 2 * row + other_x], x_buf.at[k, i], by_x)

    def x_next(k, i, after):
        wires.drain([x_copies[k, i]])
        if after is not None:
            x_go(*after)
        x_copies[k, i].wait_recv()
        spot = (far, near)[i] + x
        c_buf[k, spot] = add_low(c_buf[k, spot], x_buf[k, i])
        if i == 0:
            y_copies[k] = wires.go(c_buf.at[k, spot], y_buf.at[k], by_y)

    def y_done(k):
        y_copies[k].wait_recv()
        arrive(c_buf[k, near + x], y_buf[k], total, lane, k, y, mine)
        line_start(k, 0)

    def normed_grad(b):
        rows = pl.ds(pl.multiple_of(256 * b, 256), 256)
        value = dot_nt(d[0, rows, :], w[:, 0:896]) + dot_nt(d[1, rows, :], w[:, 896:1792]) + dot_nt(d[2, rows, :], w[:, 1792:2688])
        gn[b] = value.astype(jnp.bfloat16)
        more_got[group, 0:1, 0:width] += jnp.sum(value * unit_rows[rows, :].astype(jnp.float32), axis=0, keepdims=True)
        more_got[group, 1:2, 0:width] += jnp.sum(value, axis=0, keepdims=True)

    spread_expand = [spread(first_expand, pieces[0])]
    core_sum(0)
    x_go(0, 0)
    x_go(0, 1)
    core_sum(1)
    core_sum(2)
    load_share.wait()
    line_start(3, 0)
    more_got[group] = jnp.zeros(more_got.shape[1:], jnp.float32)
    for copy in loads + load_w:
        copy.wait()
    normed_grad(far + other_x)
    y_pass = wires.go(gn.at[far + other_x], gn_y.at[0], by_y)
    normed_grad(near + other_x)
    x_next(0, 0, (1, 0))
    x_next(0, 1, (1, 1))
    line_start(3, 1)
    line_second(3, 0)
    normed_grad(far + x)
    y_done(0)
    normed_grad(near + x)
    more_group = [wires.go(more_got.at[group], more_got.at[group], device) for device in (by_x, by_y, by_both)]
    for copy in vec_group:
        copy.wait_recv()
    vec_got[group] = vec[group]
    vec_own[...] = (vec_got[0] + vec_got[1]) + (vec_got[2] + vec_got[3])
    vec_pass = wires.go(vec_own, vec_core, by_core)
    x_next(1, 0, (2, 0))
    line_start(0, 1)
    line_second(3, 1)
    y_pass.wait_recv()
    gn_y[0] = add_low(gn_y[0], gn[near + other_x])
    line_second(0, 0)
    x_next(1, 1, (2, 1))
    y_done(1)
    for copy in more_group:
        copy.wait_recv()
    more_z[z] = (more_got[0] + more_got[1]) + (more_got[2] + more_got[3])
    more_pass = wires.go(more_z.at[z], more_core, by_core)
    pair_lower.wait_recv()
    pair_buf[...] = add_low(pair_buf[...], share_expand[HALF:, :])
    spread_expand.append(spread(pair_buf, pieces[1]))
    line_third(3, 0)
    line_second(0, 1)
    vec_pass.wait_recv()
    vec_z[z] = vec_own[...] + vec_core[...]
    vec_line = [wires.go(vec_z.at[z], vec_z.at[z], device) for device in lines_z]
    line_start(1, 1)
    x_next(2, 0, None)
    cross = wires.go(gn_y.at[0], gn_cross, by_x)
    y_keep = wires.go(gn.at[far + x], gn_y.at[1], by_y)
    line_second(1, 0)
    line_third(3, 1)
    x_next(2, 1, None)
    y_done(2)
    line_third(0, 0)
    line_second(1, 1)
    line_start(2, 1)
    more_pass.wait_recv()
    wires.drain([more_pass])
    more_z[z] = more_z[z] + more_core[...]
    more_line = [wires.go(more_z.at[z], more_z.at[z], device) for device in lines_z]
    line_third(0, 1)
    line_second(2, 0)
    line_third(1, 0)
    passes = [spread_on(spread_expand[0][0], pieces[0])]
    line_second(2, 1)
    line_third(1, 1)

    load_gm.wait()
    load_inp.wait()

    def norm_back(seq, grad):
        entries = inp[seq].astype(jnp.float32)
        center = entries - jnp.mean(entries, axis=-1, keepdims=True)
        scale = lax.rsqrt(jnp.mean(center * center, axis=-1, keepdims=True) + epsilon)
        unit = center * scale
        q = grad * gain[...]
        grad_out[seq] += scale * (q - jnp.mean(q, axis=-1, keepdims=True) - unit * jnp.mean(q * unit, axis=-1, keepdims=True))
        grad_turned[seq] = grad_out[seq].T

    y_keep.wait_recv()
    norm_back(x, gn_y[1].astype(jnp.float32) + gn[near + x].astype(jnp.float32))
    cross.wait_recv()
    norm_back(other_x, gn_cross[...].astype(jnp.float32))
    line_third(2, 0)
    line_third(2, 1)
    for copy in vec_line:
        copy.wait_recv()
    vec_total[...] = (vec_z[0] + vec_z[1]) + (vec_z[2] + vec_z[3])
    passes.append(spread_on(spread_expand[1][0], pieces[1]))
    last = []
    for k in (3, 0, 1, 2):
        line_fourth(k, 0)
        line_fourth(k, 1)
        rows = pl.ds(pl.multiple_of(208 * core, 16), 192)
        last.append(wires.go(total.at[k, rows], total.at[k, rows], by_core))
    for copy in more_line:
        copy.wait_recv()
    wide_total[...] = (more_z[0] + more_z[1]) + (more_z[2] + more_z[3])
    for copy in last + passes + [both for over, both in spread_expand]:
        copy.wait_recv()
    wires.finish()


def last_sums(dq, dk, dv, in_grad, unit, w_half, out_share, share_expand, first_expand, vec, grad_middle, inputs, gain):
    any_space = pl.BlockSpec(memory_space=pl.ANY)
    vmem = pl.BlockSpec(memory_space=pltpu.VMEM)
    shape = jax.ShapeDtypeStruct
    kind = jnp.bfloat16
    width = w_half.shape[0]
    buf = lambda *dims: pltpu.VMEM(dims, kind)
    flat = lambda *dims: pltpu.VMEM(dims, jnp.float32)
    return pl.pallas_call(
        last_kernel,
        in_specs=[any_space] * 7 + [vmem, vmem, vmem, any_space, any_space, vmem],
        out_specs=[vmem, vmem, vmem, vmem, any_space],
        out_shape=[
            shape((4, 400, 1664), kind),
            shape((2, width, 256), jnp.float32),
            shape(vec.shape[1:], vec.dtype),
            shape((8, 1664), jnp.float32),
            shape((4,) + share_expand.shape, kind),
        ],
        scratch_shapes=[
            flat(*grad_middle.shape),
            buf(3, 1024, 896),
            buf(*unit.shape),
            buf(*w_half.shape),
            buf(3, 4, 208, 896),
            buf(3, 4, 208, 896),
            buf(3, 2, 208, 896),
            buf(3, 208, 896),
            buf(4, 208, 1664),
            buf(4, 208, 1664),
            buf(4, 256, width),
            buf(2, 256, width),
            buf(256, width),
            buf(*inputs.shape),
            buf(400 - HALF, width),
            flat(*vec.shape),
            flat(*vec.shape[1:]),
            flat(*vec.shape[1:]),
            flat(*vec.shape),
            flat(4, 8, 1664),
            flat(8, 1664),
            flat(4, 8, 1664),
            pltpu.SemaphoreType.DMA((88,)),
            pltpu.SemaphoreType.DMA((88,)),
            pltpu.SemaphoreType.DMA((24,)),
        ],
        compiler_params=pltpu.CompilerParams(collective_id=3, has_side_effects=True, vmem_limit_bytes=63 * 2**20),
        cost_estimate=pl.CostEstimate(flops=10**11, bytes_accessed=2**26, transcendentals=0),
        name="last_sums",
    )(dq, dk, dv, in_grad, unit, w_half, out_share, share_expand, first_expand, vec, grad_middle, inputs, gain)


def on_device(
    inputs,
    segments,
    cotangent,
    project_in,
    project_out,
    expand_weight,
    reduce_weight,
    query_bias,
    value_bias,
    project_bias,
    expand_bias,
    reduce_bias,
    first_gain,
    first_shift,
    second_gain,
    second_shift,
):
    replica, group, z, core, y, x = place()
    quad = lax.rem(replica, 4)
    width = 1600
    rows = 512

    names = (query_bias, value_bias, project_bias, reduce_bias, first_gain, first_shift, second_gain, second_shift)
    index = lax.broadcasted_iota(jnp.int32, (16, 400), 0)
    vec = jnp.pad(expand_bias.reshape(4, 400), ((8, 4), (0, 0)))
    for k, name in enumerate(names):
        vec = jnp.where(index == k, name[None, :], vec)
    turned = lambda entries: jnp.swapaxes(entries, 1, 2)
    x_seq, w_half, vecs, segs, own_inputs, own_cot, quarter_expand = first_exchange(
        turned(inputs), project_in, vec, segments[:, None, :], expand_weight, turned(cotangent)
    )
    row_vectors = padded(jnp.swapaxes(wide(vecs), 0, 1).reshape(16, width))
    bias_expand = lax.dynamic_index_in_dim(wide(vecs), 8 + quad, 1, False).reshape(1, width)
    segs = segs.reshape(1024)

    w_half = w_half.reshape(width, 2688)
    segc = segs[:, None]
    segr = segs[None]
    own_cot = own_cot.reshape(rows, width)
    mixture, normed, unit_seq, attended, lse, full_out, expand_part, cots = mix_heads(
        x_seq.reshape(1024, width), w_half, row_vectors, segc, segr, project_out, quarter_expand, own_cot
    )
    full_out = full_out.reshape(width, width)
    att_tokens, middle, second = turn_middle(attended.reshape(4, 256, 896), full_out, own_inputs, row_vectors)
    (
        activated,
        grad_expanded,
        second_all,
        reduce_part,
        grad_middle_low,
        grad_att,
        grad_middle,
        own_reduce,
        pass_reduce,
        expand_sums,
        norm_sums,
    ) = feed_all(
        second, own_cot, cots, expand_part.reshape(width, width), reduce_weight, middle, full_out, bias_expand, row_vectors
    )

    grad_heads, result, share_reduce, first_reduce, own_expand, pass_expand, out_core = turn_more(
        grad_att, grad_expanded, second_all, activated, reduce_part, pass_reduce, att_tokens, grad_middle_low, own_reduce
    )
    dq, dk, dv, bias_sums, in_grad, share_expand, first_expand, outputs, cot_sums, out_share, quads_reduce = heads_back(
        mixture,
        grad_heads.reshape(1024, 896),
        attended,
        lse,
        segc,
        segr,
        normed,
        share_reduce,
        first_reduce,
        own_expand,
        pass_expand,
        result,
        middle,
        own_cot,
        row_vectors,
        out_core,
    )

    def spread(columns):
        lower = jnp.concatenate([columns[:832], jnp.zeros((768,), jnp.float32)])
        upper = jnp.concatenate([jnp.zeros((832,), jnp.float32), columns[64:832]])
        return jnp.where(y == 0, lower, upper)

    expand_bias_part = jnp.sum(expand_sums, axis=0).reshape(4, 400)
    expand_bias_wide = lax.dynamic_update_slice_in_dim(jnp.zeros((4, width), jnp.float32), expand_bias_part, 400 * quad, 1)
    vectors = jnp.concatenate(
        [
            spread(bias_sums[0]).reshape(4, 400),
            spread(bias_sums[1]).reshape(4, 400),
            norm_sums[2].reshape(4, 400),
            cot_sums[0].reshape(4, 400),
            norm_sums[0].reshape(4, 400),
            norm_sums[1].reshape(4, 400),
            expand_bias_wide,
        ],
        axis=1,
    )
    vectors = jnp.pad(vectors, ((0, 0), (0, 96))).reshape(4, 32, 128)
    grad_total, input_grad, vec_total, wide_total, quads_expand = last_sums(
        dq, dk, dv, in_grad, unit_seq, w_half, out_share, share_expand, first_expand, vectors, grad_middle.reshape(2, 256, width), own_inputs, row_vectors[4:5, :width]
    )
    vec_total = vec_total.reshape(4096)
    pieces = [vec_total[400 * k : 400 * k + 400] for k in range(6)]
    first_sums = lax.dynamic_index_in_dim(wide_total[:2, :width].reshape(2, 4, 400), group, 1, False)
    total_reduce, total_expand, total_in, total_out = finish(quads_reduce, quads_expand, grad_total)
    total_reduce = total_reduce.reshape(width, width)
    return (
        turned(outputs),
        turned(input_grad),
        total_in,
        total_out,
        total_expand,
        total_reduce,
        pieces[0],
        pieces[1],
        pieces[2],
        vec_total[2400:4000],
        pieces[3],
        first_sums[0],
        first_sums[1],
        pieces[4],
        pieces[5],
    )


def solution(mesh):
    placed = (
        P("replica", "group", None),
        P("replica", "group"),
        P("replica", "group", None),
        P("group", None),
        P("group", None),
        P("group", None),
        P("group", None),
        P("group"),
        P("group"),
        P("group"),
        P("group"),
        P("group"),
        P("group"),
        P("group"),
        P("group"),
        P("group"),
    )
    return jax.shard_map(
        on_device if dict(mesh.shape) == {"replica": 8, "group": 4} else on_device_any,
        mesh=mesh,
        in_specs=placed,
        out_specs=(
            P("replica", "group", None),
            P("replica", "group", None),
            P("group", None),
            P("group", None),
            P("group", None),
            P("group", None),
            P("group"),
            P("group"),
            P("group"),
            P("group"),
            P("group"),
            P("group"),
            P("group"),
            P("group"),
            P("group"),
        ),
        check_vma=False,
    )
```
